32 devices in a mesh: seq: 8 (over y, x, core), tp: 4 (over z).
Axes of the slice: x: 2, y: 2, z: 4, core: 2. Of those that a mesh axis runs over, the one named last changes fastest.
Arguments:
- hidden_in: bfloat16 [16, 512, 1024], P(None, 'seq', 'tp'), may hold values from -6 to 6
- norm_gain: float32 [1024], replicated, may hold values from 0.25 to 1.75
- norm_shift: float32 [1024], replicated, may hold values from -3 to 3
- query_weight: bfloat16 [1024, 1024], P(None, 'tp'), may hold values from -0.375 to 0.375
- query_bias: float32 [1024], P('tp'), may hold values from -3 to 3
- key_weight: bfloat16 [1024, 1024], P(None, 'tp'), may hold values from -0.1875 to 0.1875
- value_weight: bfloat16 [1024, 1024], P(None, 'tp'), may hold values from -0.1875 to 0.1875
- value_bias: float32 [1024], P('tp'), may hold values from -3 to 3
- output_weight: bfloat16 [1024, 1024], P('tp'), may hold values from -4 to 4
- output_bias: float32 [1024], replicated, may hold values from -3 to 3
- feed_gain: float32 [1024], replicated, may hold values from 0.25 to 1.75
- feed_shift: float32 [1024], replicated, may hold values from -3 to 3
- inner_weight: bfloat16 [1024, 4096], P(None, 'tp'), may hold values from -0.1875 to 0.1875
- inner_bias: float32 [4096], P('tp'), may hold values from -3 to 3
- outer_weight: bfloat16 [4096, 1024], P('tp'), may hold values from -0.09375 to 0.09375
- outer_bias: float32 [1024], replicated, may hold values from -3 to 3
- doc_blocks: int32 [32], replicated, may hold values from 1 to 64, 128 in all
- doc_padding: int32 [32], replicated, may hold values from 0 to 31
- random_picks: int32 [128, 3], replicated, may hold values from 0 to 4095
- cotangent: bfloat16 [16, 512, 1024], P(None, 'seq', 'tp'), may hold values from -6 to 6
Outputs:
- layer_out: bfloat16 [16, 512, 1024], P(None, 'seq', 'tp')
- grad_input: float32 [16, 512, 1024], P(None, 'seq', 'tp')
- grad_norm_gain: float32 [1024], replicated
- grad_norm_shift: float32 [1024], replicated
- grad_query_weight: float32 [1024, 1024], P('seq', 'tp')
- grad_query_bias: float32 [1024], P('tp')
- grad_key_weight: float32 [1024, 1024], P('seq', 'tp')
- grad_value_weight: float32 [1024, 1024], P('seq', 'tp')
- grad_value_bias: float32 [1024], P('tp')
- grad_output_weight: float32 [1024, 1024], P('tp', 'seq')
- grad_output_bias: float32 [1024], replicated
- grad_feed_gain: float32 [1024], replicated
- grad_feed_shift: float32 [1024], replicated
- grad_inner_weight: float32 [1024, 4096], P('seq', 'tp')
- grad_inner_bias: float32 [4096], P('tp')
- grad_outer_weight: float32 [4096, 1024], P('tp', 'seq')
- grad_outer_bias: float32 [1024], replicated
The draws below stay inside these ranges and needn't reach their ends.
Inputs may be any that keep to these rules, and one draw needn't show every extreme that they name: `doc_blocks`: document lengths in blocks of 64 tokens; together they fill all 128 blocks.
All inputs are finite; a program needn't handle non-finite values.
Results may differ from the reference program's by a relative error of at most 0.02.
Values may be sent and summed in bfloat16 or wider, within the bound.
A program may use at most 192 MiB of HBM per device.

```python
import math
import jax
import jax.numpy as jnp
import numpy as np
from jax import lax

D = 1024
FF = 4096
HEAD_DIM = 64
BLK = 64
RAND = 3
GLOBAL = 2
BLK_DEV = 16
HEADS = 16
NBLK = 128
TOKENS = 8192
LONG_BLK = 64
NDOC = 32
N_SEQ = 8


def touch_ends(values, key, low, high):
    longest = values.shape.index(max(values.shape))
    spots = []
    for shift in (0, 1):
        where = [jax.random.randint(jax.random.fold_in(key, axis), (), 0, length) for axis, length in enumerate(values.shape)]
        where[longest] = (where[longest] + shift) % values.shape[longest]
        spots.append(tuple(where))
    return values.at[spots[0]].set(low).at[spots[1]].set(high)


def level_of(key, shape, pieces, least, top_value):
    level = 1.0
    for position, blocks in pieces:
        draws = jax.random.uniform(jax.random.fold_in(jax.random.fold_in(key, 6), position), (blocks,), jnp.float32, least / len(pieces), top_value / len(pieces))
        level = level * jnp.repeat(jnp.exp(draws), shape[position] // blocks).reshape((-1,) + (1,) * (len(shape) - 1 - position))
    return level


def length_profile(amount, total, reach, skew):
    loads = [(1 << 20) // math.isqrt(grade ** skew) + 1 for grade in range(2, amount + 1)]
    spare, holding = total - reach - (amount - 1), [1] * (amount - 1)
    while spare > 0:
        free = [i for i in range(amount - 1) if holding[i] < reach]
        pool, remaining = sum([loads[i] for i in free]), spare
        for i in free:
            more = min(reach - holding[i], max(1, remaining * loads[i] // pool), spare)
            holding[i] = holding[i] + more
            spare = spare - more
    return np.array([reach] + holding)


def uneven(stream_key, number_of, total, bound, skew):
    if number_of == 2:
        one = jax.random.randint(stream_key, (), max(1, total - bound), min(bound, total - 1) + 1)
        return jnp.stack([one, total - one])
    sizes = jnp.asarray(length_profile(number_of, total, bound, skew), jnp.int32)
    couples = (number_of - 1) // 2
    giver, sink = sizes[1:1 + 2 * couples:2], sizes[2:2 + 2 * couples:2]
    room = jnp.minimum(giver - 1, bound - sink)
    passed = jax.random.randint(jax.random.fold_in(stream_key, 1), (couples,), 0, 1 << 20) % (room + 1)
    sizes = sizes.at[1:1 + 2 * couples:2].set(giver - passed).at[2:2 + 2 * couples:2].set(sink + passed)
    return sizes[jax.random.permutation(jax.random.fold_in(stream_key, 2), number_of)]


def bell_draw(rng, dims, deviation, limit, split=(), held_as=jnp.bfloat16):
    level = level_of(rng, dims, split, -0.22, 0.18) if split else 1.0
    drawn = jax.random.normal(rng, dims, jnp.float32) * deviation * level
    return jnp.minimum(jnp.maximum(drawn, -limit), limit).astype(held_as)


def setup_inputs(seed: int = 0) -> dict:
    seeds = jax.random.split(jax.random.key(seed), 21)
    hidden_in = bell_draw(seeds[0], (BLK_DEV, N_SEQ * BLK, D), 1.0, 6.0, ((1, 8), (2, 4)))
    norm_gain = jnp.clip(1.0 + 0.15 * jax.random.normal(seeds[1], (D,), jnp.float32), 0.25, 1.75)
    norm_shift = bell_draw(seeds[2], (D,), 0.3, 3.0, (), jnp.float32)
    query_weight = bell_draw(seeds[3], (D, D), (D // 4) ** -0.5, 0.375, ((1, 4),))
    query_bias = bell_draw(seeds[4], (D,), 0.5, 3.0, ((0, 4),), jnp.float32)
    key_weight = bell_draw(seeds[5], (D, D), D ** -0.5, 0.1875, ((1, 4),))
    value_weight = bell_draw(seeds[6], (D, D), D ** -0.5, 0.1875, ((1, 4),))
    value_bias = bell_draw(seeds[7], (D,), 0.5, 3.0, ((0, 4),), jnp.float32)
    output_weight = bell_draw(seeds[8], (D, D), (max(D // 512, 1)) ** -0.5, 4.0, ((0, 4),))
    output_bias = bell_draw(seeds[9], (D,), 0.3, 3.0, (), jnp.float32)
    feed_gain = jnp.clip(1.0 + 0.15 * jax.random.normal(seeds[10], (D,), jnp.float32), 0.25, 1.75)
    feed_shift = bell_draw(seeds[11], (D,), 0.3, 3.0, (), jnp.float32)
    inner_weight = bell_draw(seeds[12], (D, FF), D ** -0.5, 0.1875, ((1, 4),))
    inner_bias = bell_draw(seeds[13], (FF,), 0.5, 3.0, ((0, 4),), jnp.float32)
    outer_weight = bell_draw(seeds[14], (FF, D), FF ** -0.5, 0.09375, ((0, 4),))
    outer_bias = bell_draw(seeds[15], (D,), 0.3, 3.0, (), jnp.float32)
    doc_blocks = uneven(seeds[16], NDOC, NBLK, LONG_BLK, 2).astype(jnp.int32)
    doc_padding = touch_ends(jax.random.randint(seeds[17], (NDOC,), 0, BLK // 2), jax.random.fold_in(seeds[17], 1), 0, (BLK // 2) - 1).astype(jnp.int32)
    random_picks = touch_ends(jax.random.randint(seeds[18], (NBLK, RAND), 0, 4096), jax.random.fold_in(seeds[18], 1), 0, 4095).astype(jnp.int32)
    cotangent = bell_draw(seeds[19], (BLK_DEV, N_SEQ * BLK, D), 1.0, 6.0, ((1, 8), (2, 4)))
    return {"hidden_in": hidden_in, "norm_gain": norm_gain, "norm_shift": norm_shift, "query_weight": query_weight, "query_bias": query_bias, "key_weight": key_weight, "value_weight": value_weight, "value_bias": value_bias, "output_weight": output_weight, "output_bias": output_bias, "feed_gain": feed_gain, "feed_shift": feed_shift, "inner_weight": inner_weight, "inner_bias": inner_bias, "outer_weight": outer_weight, "outer_bias": outer_bias, "doc_blocks": doc_blocks, "doc_padding": doc_padding, "random_picks": random_picks, "cotangent": cotangent}


@jax.custom_vjp
def low(v):
    return lax.optimization_barrier(v.astype(jnp.bfloat16)).astype(jnp.float32)

@jax.custom_vjp
def low_back(v):
    return v

def low_keep(v):
    return (low(v), None)

def low_pass(kept, grad):
    return (grad,)

def back_keep(v):
    return (v, None)

def back_low(kept, grad):
    return (low(grad),)
low.defvjp(low_keep, low_pass)
low_back.defvjp(back_keep, back_low)

def layer_norm(value, gain, shift):
    mean = lax.optimization_barrier(jnp.mean(value, axis=-1, keepdims=True))
    centered = value - mean
    spread = lax.optimization_barrier(jnp.mean(centered * centered, axis=-1, keepdims=True))
    return centered * lax.rsqrt(spread + 1e-05) * gain + shift

def block_tables(doc_blocks, doc_padding, random_picks, nblocks):
    ends = jnp.cumsum(doc_blocks).astype(jnp.int32)
    starts = (ends - doc_blocks).astype(jnp.int32)
    block_ids = jnp.arange(nblocks, dtype=jnp.int32)
    member = ((block_ids[:, None] >= starts[None, :]) & (block_ids[:, None] < ends[None, :])).astype(jnp.int32)
    doc_index = jnp.arange(doc_blocks.shape[0], dtype=jnp.int32)
    doc_of = lax.optimization_barrier(jnp.sum(member * doc_index[None, :], axis=1)).astype(jnp.int32)
    first = lax.optimization_barrier(jnp.sum(member * starts[None, :], axis=1)).astype(jnp.int32)
    length = lax.optimization_barrier(jnp.sum(member * doc_blocks[None, :], axis=1)).astype(jnp.int32)
    padding = lax.optimization_barrier(jnp.sum(member * doc_padding[None, :], axis=1)).astype(jnp.int32)
    last_block = block_ids == first + length - 1
    live = jnp.where(last_block, BLK - padding, BLK).astype(jnp.int32)
    partner = (first[:, None] + jnp.remainder(random_picks, length[:, None])).astype(jnp.int32)
    return (doc_of, first, live, partner)

def allowed_blocks(query_blocks, key_blocks, tables):
    doc_of, first, live, partner = tables
    same = doc_of[query_blocks][:, None] == doc_of[key_blocks][None, :]
    near = jnp.abs(query_blocks[:, None] - key_blocks[None, :]) <= 1
    glob = (key_blocks - first[key_blocks] < GLOBAL)[None, :] | (query_blocks - first[query_blocks] < GLOBAL)[:, None]
    chosen = jnp.any(partner[query_blocks][:, :, None] == key_blocks[None, None, :], axis=1)
    return same & (near | glob | chosen)

def attention(queries, keys, values, tables):
    tokens = queries.shape[0]
    nblocks = tokens // BLK
    group = min(512, tokens)
    group_blocks = group // BLK
    live = tables[2]
    key_live = jnp.arange(tokens, dtype=jnp.int32) % BLK < jnp.repeat(live, BLK)
    query_heads = queries.reshape(tokens // group, group, HEADS, HEAD_DIM)
    key_heads = keys.reshape(tokens, HEADS, HEAD_DIM)
    value_heads = values.reshape(tokens, HEADS, HEAD_DIM)
    key_blocks = jnp.arange(nblocks, dtype=jnp.int32)

    def one_group(pair):
        query_group, index = pair
        query_blocks = (index * group_blocks + jnp.arange(group_blocks, dtype=jnp.int32)).astype(jnp.int32)
        allow = allowed_blocks(query_blocks, key_blocks, tables)
        mask = jnp.repeat(jnp.repeat(allow, BLK, axis=0), BLK, axis=1) & key_live[None, :]
        scores = jnp.einsum('qhe,khe->hqk', query_group, key_heads, precision=lax.Precision.HIGHEST)
        scores = low_back(scores)
        scores = jnp.where(mask[None], scores, -1e+30)
        top = lax.optimization_barrier(jnp.max(scores, axis=-1, keepdims=True))
        weights = jnp.where(mask[None], jnp.exp(scores - top), 0.0)
        probs = low(weights / lax.optimization_barrier(jnp.sum(weights, axis=-1, keepdims=True)))
        return jnp.einsum('hqk,khe->qhe', probs, value_heads, precision=lax.Precision.HIGHEST)
    result = lax.map(jax.checkpoint(one_group), (query_heads, jnp.arange(tokens // group, dtype=jnp.int32)))
    return result.reshape(tokens, HEADS * HEAD_DIM)

def layer(x, norm_gain, norm_shift, query_weight, query_bias, key_weight, value_weight, value_bias, output_weight, output_bias, feed_gain, feed_shift, inner_weight, inner_bias, outer_weight, outer_bias, tables):
    best = lax.Precision.HIGHEST
    h1 = low(layer_norm(x, norm_gain, norm_shift))
    queries = low_back(low((jnp.dot(h1, query_weight, precision=best) + query_bias) * 0.125))
    keys = low_back(low(jnp.dot(h1, key_weight, precision=best)))
    values = low_back(low(jnp.dot(h1, value_weight, precision=best) + value_bias))
    mixed = low_back(low(attention(queries, keys, values, tables)))
    branch = low_back(jnp.dot(mixed, output_weight, precision=best) + output_bias)
    x1 = x + branch
    h2 = low(layer_norm(x1, feed_gain, feed_shift))
    pre = low_back(jnp.dot(h2, inner_weight, precision=best) + inner_bias)
    act = low(jax.nn.gelu(pre, approximate=True))
    return x1 + jnp.dot(act, outer_weight, precision=best) + outer_bias

def reference(hidden_in, norm_gain, norm_shift, query_weight, query_bias, key_weight, value_weight, value_bias, output_weight, output_bias, feed_gain, feed_shift, inner_weight, inner_bias, outer_weight, outer_bias, doc_blocks, doc_padding, random_picks, cotangent):
    tables = block_tables(doc_blocks, doc_padding, random_picks, TOKENS // BLK)
    flat = hidden_in.reshape(TOKENS, D).astype(jnp.float32)
    params = (norm_gain, norm_shift, query_weight, query_bias, key_weight, value_weight, value_bias, output_weight, output_bias, feed_gain, feed_shift, inner_weight, inner_bias, outer_weight, outer_bias)
    params = tuple((item.astype(jnp.float32) for item in params))

    def forward(*inputs):
        return layer(*inputs, tables)
    result, pull = jax.vjp(forward, flat, *params)
    grads = pull(cotangent.reshape(TOKENS, D).astype(jnp.float32))
    return (result.astype(jnp.bfloat16).reshape(hidden_in.shape), grads[0].reshape(hidden_in.shape), grads[1], grads[2], grads[3], grads[4], grads[5], grads[6], grads[7], grads[8], grads[9], grads[10], grads[11], grads[12], grads[13], grads[14], grads[15])
```

```python
import functools

import jax
import jax.numpy as jnp
from jax import lax
from jax.experimental import pallas as pl
from jax.experimental.pallas import tpu as pltpu
from jax.sharding import PartitionSpec as P

HEAD_DIM = 64
BLK = 64
GLOBAL = 2
SLOTS = 8
WIDE = 2 * HEAD_DIM
NEG = -1e30
NT = (((1,), (1,)), ((), ()))
TN = (((0,), (0,)), ((), ()))


def layer_norm(value, gain, shift):
    mean = jnp.mean(value, axis=-1, keepdims=True)
    centered = value - mean
    spread = jnp.mean(centered * centered, axis=-1, keepdims=True)
    return centered * lax.rsqrt(spread + 1e-05) * gain + shift


def gelu_tanh(value):
    return jax.nn.gelu(value, approximate=True)


def block_tables(doc_blocks, doc_padding, random_picks, nblocks):
    ends = jnp.cumsum(doc_blocks)
    starts = ends - doc_blocks
    block_ids = jnp.arange(nblocks, dtype=jnp.int32)
    member = (
        (block_ids[:, None] >= starts[None, :]) & (block_ids[:, None] < ends[None, :])
    ).astype(jnp.int32)
    first = jnp.sum(member * starts[None, :], axis=1)
    length = jnp.sum(member * doc_blocks[None, :], axis=1)
    padding = jnp.sum(member * doc_padding[None, :], axis=1)
    last_block = block_ids == first + length - 1
    live = jnp.where(last_block, BLK - padding, BLK)
    partner = first[:, None] + jnp.remainder(random_picks, length[:, None])
    return (first, length, live, partner)


def attention_tables(doc_blocks, doc_padding, random_picks, nrows, nseq, heads, part):
    share = nseq // heads
    nblocks = nrows * nseq
    first, length, live, partner = block_tables(doc_blocks, doc_padding, random_picks, nblocks)
    block = jnp.arange(nblocks, dtype=jnp.int32)
    holder = block % nseq
    slot_of = ((holder % share) * heads + holder // share) * nrows + block // nseq
    glob = block - first < GLOBAL
    last = first + length - 1
    step = jnp.arange(SLOTS, dtype=jnp.int32)
    near = jnp.stack([block - 1, block, block + 1, first, first + 1], axis=1)
    picks = jnp.concatenate([near, partner], axis=1)
    whole = first[:, None] + step[None, :]
    cand = jnp.where(glob[:, None], whole, picks)
    valid = (cand >= first[:, None]) & (cand <= last[:, None])
    same = (cand[:, :, None] == cand[:, None, :]) & valid[:, None, :]
    earlier = step[None, None, :] < step[None, :, None]
    valid = valid & ~jnp.any(same & earlier, axis=2)
    is_long = glob & (length > SLOTS)
    valid = valid & ~is_long[:, None]
    place = jnp.cumsum(valid.astype(jnp.int32), axis=1) - 1
    pick = (valid[:, :, None] & (place[:, :, None] == step[None, None, :])).astype(jnp.int32)
    order = jnp.sum(pick * cand[:, :, None], axis=1)
    filled = jnp.sum(pick, axis=1)
    onehot = (order[:, :, None] == block[None, None, :]).astype(jnp.int32)
    slots = jnp.sum(onehot * slot_of[None, None, :], axis=2) * BLK
    lives = filled * jnp.sum(onehot * live[None, None, :], axis=2)
    mine = lambda item: lax.dynamic_index_in_dim(
        jnp.moveaxis(item.reshape((nrows, heads, share) + item.shape[1:]), 2, 0), part, 0, False
    ).swapaxes(0, 1).reshape((nrows * heads,) + item.shape[1:])
    nquery = nrows * heads
    long_mine = mine(is_long.astype(jnp.int32))
    rank = jnp.cumsum(long_mine) - 1
    query = jnp.arange(nquery, dtype=jnp.int32)
    chosen = (long_mine[:, None] * (rank[:, None] == query[None, :])).astype(jnp.int32)
    long_query = jnp.sum(chosen * query[:, None], axis=0)
    long_first = jnp.sum(chosen * mine(first)[:, None], axis=0)
    long_len = jnp.sum(chosen * mine(length)[:, None], axis=0)
    near_table = jnp.concatenate([mine(slots).reshape(-1), mine(lives).reshape(-1)])
    long_table = jnp.concatenate([long_query, long_first, long_len, jnp.sum(long_mine)[None]])
    block_table = jnp.concatenate([slot_of * BLK, live])
    return near_table, long_table, block_table


def bias_row(lives):
    lane = lax.broadcasted_iota(jnp.int32, (1, WIDE), 1)
    parts = []
    for index in range(0, SLOTS, 2):
        bound = jnp.where(lane < BLK, lives[index], lives[index + 1] + BLK)
        parts.append(jnp.where(lane < bound, 0.0, NEG))
    return jnp.concatenate(parts, axis=1)


def near_slots(near_ref, query, nquery):
    base = query * SLOTS
    slots = [pl.multiple_of(near_ref[base + k], BLK) for k in range(SLOTS)]
    lives = [near_ref[nquery * SLOTS + base + k] for k in range(SLOTS)]
    return slots, lives


def long_slots(block_ref, nblocks, first, length, chunk):
    slots, lives = [], []
    for k in range(SLOTS):
        place = chunk * SLOTS + k
        block = first + jnp.minimum(place, length - 1)
        slots.append(pl.multiple_of(block_ref[block], BLK))
        lives.append(jnp.where(place < length, block_ref[nblocks + block], 0))
    return slots, lives


def take(ref, slots):
    return jnp.concatenate([ref[pl.ds(slot, BLK), :] for slot in slots], axis=0)


def forward_kernel(nquery, nblocks, unroll, near_ref, long_ref, block_ref, q_ref, kv_ref, out_ref):
    upper = lax.broadcasted_iota(jnp.int32, (BLK, WIDE), 1) >= HEAD_DIM

    def finish(query, top, total, accum):
        out_ref[pl.ds(query * BLK, BLK), :] = jnp.where(
            upper, accum / total, top + jnp.log(total)
        )

    def scores_of(query, slots, lives):
        kv = take(kv_ref, slots)
        scores = lax.dot_general(
            q_ref[pl.ds(query * BLK, BLK), :], kv, NT, preferred_element_type=jnp.float32
        )
        return kv, scores + bias_row(lives)

    def near_step(index, carry):
        for offset in range(unroll):
            query = index * unroll + offset
            kv, scores = scores_of(query, *near_slots(near_ref, query, nquery))
            top = jnp.max(scores, axis=1, keepdims=True)
            weights = jnp.exp(scores - top)
            total = jnp.sum(weights, axis=1, keepdims=True)
            accum = jnp.dot(weights.astype(jnp.bfloat16), kv, preferred_element_type=jnp.float32)
            finish(query, top, total, accum)
        return carry

    lax.fori_loop(0, nquery // unroll, near_step, 0)

    def long_step(index, carry):
        query = long_ref[index]
        first = long_ref[nquery + index]
        length = long_ref[2 * nquery + index]

        def chunk_step(chunk, state):
            top, total, accum = state
            kv, scores = scores_of(query, *long_slots(block_ref, nblocks, first, length, chunk))
            new_top = jnp.maximum(top, jnp.max(scores, axis=1, keepdims=True))
            weights = jnp.exp(scores - new_top)
            decay = jnp.exp(top - new_top)
            total = total * decay + jnp.sum(weights, axis=1, keepdims=True)
            accum = accum * decay + jnp.dot(
                weights.astype(jnp.bfloat16), kv, preferred_element_type=jnp.float32
            )
            return new_top, total, accum

        start = (
            jnp.full((BLK, 1), NEG, jnp.float32),
            jnp.zeros((BLK, 1), jnp.float32),
            jnp.zeros((BLK, WIDE), jnp.float32),
        )
        top, total, accum = lax.fori_loop(0, (length + SLOTS - 1) // SLOTS, chunk_step, start)
        finish(query, top, total, accum)
        return carry

    lax.fori_loop(0, long_ref[3 * nquery], long_step, 0)


def backward_kernel(
    nquery, nblocks, unroll,
    near_ref, long_ref, block_ref, q_ref, do_ref, res_ref, kv_ref, dq_ref, dkv_ref, sum_ref,
):
    sum_ref[...] = jnp.zeros_like(sum_ref)

    def load(query):
        rows = pl.ds(query * BLK, BLK)
        grad = do_ref[rows, :]
        both = jnp.concatenate([q_ref[rows, :], grad], axis=0)
        res = res_ref[rows, :]
        log_total = res[:, :1]
        delta = jnp.sum(res * grad.astype(jnp.float32), axis=1, keepdims=True)
        return both, log_total, delta

    def terms(both, log_total, delta, slots, lives):
        kv = take(kv_ref, slots)
        pair = lax.dot_general(both, kv, NT, preferred_element_type=jnp.float32)
        probs = jnp.exp(pair[:BLK] + bias_row(lives) - log_total)
        grad_scores = (probs * (pair[BLK:] - delta)).astype(jnp.bfloat16)
        weights = jnp.concatenate([grad_scores, probs.astype(jnp.bfloat16)], axis=0)
        dkv = lax.dot_general(weights, both, TN, preferred_element_type=jnp.float32)
        dq = jnp.dot(grad_scores, kv, preferred_element_type=jnp.float32)
        return dq, dkv

    def scatter(slots, dkv):
        for k, slot in enumerate(slots):
            sum_ref[pl.ds(slot, BLK), :] += dkv[k * BLK : (k + 1) * BLK]

    def near_step(index, carry):
        done = []
        for offset in range(unroll):
            query = index * unroll + offset
            slots, lives = near_slots(near_ref, query, nquery)
            dq, dkv = terms(*load(query), slots, lives)
            dq_ref[pl.ds(query * BLK, BLK), :] = dq.astype(jnp.bfloat16)
            done.append((slots, dkv))
        for slots, dkv in done:
            scatter(slots, dkv)
        return carry

    lax.fori_loop(0, nquery // unroll, near_step, 0)

    def long_step(index, carry):
        query = long_ref[index]
        first = long_ref[nquery + index]
        length = long_ref[2 * nquery + index]
        loaded = load(query)

        def chunk_step(chunk, total):
            slots, lives = long_slots(block_ref, nblocks, first, length, chunk)
            dq, dkv = terms(*loaded, slots, lives)
            scatter(slots, dkv)
            return total + dq

        total = lax.fori_loop(
            0, (length + SLOTS - 1) // SLOTS, chunk_step, jnp.zeros((BLK, WIDE), jnp.float32)
        )
        dq_ref[pl.ds(query * BLK, BLK), :] = total.astype(jnp.bfloat16)
        return carry

    lax.fori_loop(0, long_ref[3 * nquery], long_step, 0)
    dkv_ref[...] = sum_ref[...].astype(jnp.bfloat16)


def local_call(kernel, name, out_shape, nsmem, nvmem, scratch=(), flops=0):
    return pl.pallas_call(
        kernel,
        out_shape=out_shape,
        in_specs=[pl.BlockSpec(memory_space=pltpu.SMEM)] * nsmem
        + [pl.BlockSpec(memory_space=pltpu.VMEM)] * nvmem,
        out_specs=jax.tree.map(lambda _: pl.BlockSpec(memory_space=pltpu.VMEM), out_shape),
        scratch_shapes=list(scratch),
        name=name,
        cost_estimate=pl.CostEstimate(flops=flops, bytes_accessed=8 << 20, transcendentals=0),
        compiler_params=pltpu.CompilerParams(vmem_limit_bytes=56 << 20),
    )


def rows_product(left, right):
    return lax.dot_general(left, right, TN, preferred_element_type=jnp.float32)


def cols_product(left, right):
    return lax.dot_general(left, right, NT, preferred_element_type=jnp.float32)


def spread_heads(weight, heads, upper, axis):
    shape = weight.shape[:axis] + (heads, HEAD_DIM) + weight.shape[axis + 1 :]
    weight = weight.reshape(shape)
    pads = [(0, 0)] * len(shape)
    pads[axis + 1] = (HEAD_DIM, 0) if upper else (0, HEAD_DIM)
    weight = jnp.pad(weight, pads)
    return weight.reshape(shape[:axis] + (heads * WIDE,) + shape[axis + 2 :])


def pair_heads(left, right, heads):
    lead = left.shape[:-1]
    both = jnp.concatenate(
        [left.reshape(lead + (heads, HEAD_DIM)), right.reshape(lead + (heads, HEAD_DIM))], axis=-1
    )
    return both.reshape(lead + (heads * WIDE,))


def on_device(
    hidden_in,
    norm_gain,
    norm_shift,
    query_weight,
    query_bias,
    key_weight,
    value_weight,
    value_bias,
    output_weight,
    output_bias,
    feed_gain,
    feed_shift,
    inner_weight,
    inner_bias,
    outer_weight,
    outer_bias,
    doc_blocks,
    doc_padding,
    random_picks,
    cotangent,
):
    f32, bf16 = jnp.float32, jnp.bfloat16
    nrows, block_len, part_width = hidden_in.shape
    rows = nrows * block_len
    nseq, ntp = lax.axis_size("seq"), lax.axis_size("tp")
    seq_index, tp_index = lax.axis_index("seq"), lax.axis_index("tp")
    local_width = query_weight.shape[1]
    heads = local_width // HEAD_DIM
    share = nseq // heads
    nquery = nrows * heads
    nblocks = nrows * nseq
    tokens_part = rows // ntp
    across = [[h * share + r for h in range(heads)] for r in range(share)]
    within = [[h * share + r for r in range(share)] for h in range(heads)]

    def swap_heads(value):
        width = value.shape[1] // heads
        value = value.reshape(rows, heads, width).swapaxes(0, 1)
        value = lax.all_to_all(value, "seq", 0, 0, axis_index_groups=across, tiled=True)
        return value.reshape(heads * rows, width)

    def swap_back(value):
        width = value.shape[1]
        value = lax.all_to_all(
            value.reshape(heads, rows, width), "seq", 0, 0, axis_index_groups=across, tiled=True
        )
        return value.swapaxes(0, 1).reshape(rows, heads * width)

    tables = attention_tables(
        doc_blocks, doc_padding, random_picks, nrows, nseq, heads, seq_index % share
    )
    x_full = lax.all_gather(hidden_in.reshape(rows, part_width), "tp", axis=1, tiled=True).astype(f32)
    mean1 = jnp.mean(x_full, axis=-1, keepdims=True)
    centered = x_full - mean1
    scale1 = lax.rsqrt(jnp.mean(centered * centered, axis=-1, keepdims=True) + 1e-05)
    h1 = (centered * scale1 * norm_gain + norm_shift).astype(bf16)
    q_wide = (
        (
            jnp.dot(h1, spread_heads(query_weight, heads, False, 1), preferred_element_type=f32)
            + spread_heads(query_bias, heads, False, 0)
        )
        * 0.125
    ).astype(bf16)
    kv_bias = pair_heads(jnp.zeros_like(value_bias), value_bias, heads)
    kv = (
        jnp.dot(h1, pair_heads(key_weight, value_weight, heads), preferred_element_type=f32) + kv_bias
    ).astype(bf16)
    q_head = swap_heads(q_wide)
    kv_head = lax.all_gather(
        swap_heads(kv), "seq", axis=0, axis_index_groups=within, tiled=True
    )
    near_table, long_table, block_table = tables
    res = local_call(
        functools.partial(forward_kernel, nquery, nblocks, 2),
        "attention_forward",
        jax.ShapeDtypeStruct((nquery * BLK, WIDE), f32),
        3,
        2,
    )(near_table, long_table, block_table, q_head, kv_head)
    mixed = swap_back(res[:, HEAD_DIM:].astype(bf16))
    attn_part = jnp.dot(mixed, output_weight, preferred_element_type=f32).astype(bf16)
    attn = lax.psum_scatter(attn_part, "tp", scatter_dimension=0, tiled=True).astype(f32)
    token_start = tp_index * tokens_part
    x_part = lax.dynamic_slice_in_dim(x_full, token_start, tokens_part, 0)
    x1 = x_part + attn + output_bias
    h2_f, feed_pull = jax.vjp(layer_norm, x1, feed_gain, feed_shift)
    h2 = lax.all_gather(h2_f.astype(bf16), "tp", axis=0, tiled=True)
    pre = jnp.dot(h2, inner_weight, preferred_element_type=f32) + inner_bias
    act_f, gelu_pull = jax.vjp(gelu_tanh, pre)
    act = act_f.astype(bf16)
    ffn_part = jnp.dot(act, outer_weight, preferred_element_type=f32)
    own = lax.dynamic_slice_in_dim(ffn_part, token_start, tokens_part, 0) + x1
    ffn_part = lax.dynamic_update_slice_in_dim(ffn_part, own, token_start, 0).astype(bf16)
    result = lax.psum_scatter(ffn_part, "tp", scatter_dimension=1, tiled=True).astype(f32)
    bias_part = lax.dynamic_slice_in_dim(outer_bias, tp_index * part_width, part_width, 0)
    layer_out = (result + bias_part).astype(bf16).reshape(hidden_in.shape)

    cot = cotangent.reshape(rows, part_width)
    grad_out = lax.all_gather(cot, "tp", axis=1, tiled=True)
    grad_outer_bias_part = jnp.sum(cot.astype(f32), axis=0)
    grad_outer_weight = rows_product(act, grad_out)
    grad_act = cols_product(grad_out, outer_weight)
    grad_pre = gelu_pull(grad_act)[0].astype(bf16)
    grad_inner_bias = jnp.sum(grad_pre.astype(f32), axis=0)
    grad_inner_weight = rows_product(h2, grad_pre)
    grad_h2 = lax.psum_scatter(
        cols_product(grad_pre, inner_weight).astype(bf16), "tp", scatter_dimension=0, tiled=True
    ).astype(f32)
    grad_x1_norm, grad_feed_gain, grad_feed_shift = feed_pull(grad_h2)
    grad_out_part = lax.dynamic_slice_in_dim(grad_out, token_start, tokens_part, 0).astype(f32)
    grad_branch_part = (grad_out_part + grad_x1_norm).astype(bf16)
    grad_output_bias = jnp.sum(grad_branch_part.astype(f32), axis=0)
    grad_branch = lax.all_gather(grad_branch_part, "tp", axis=0, tiled=True)
    grad_output_weight = rows_product(mixed, grad_branch)
    do_wide = cols_product(grad_branch, spread_heads(output_weight, heads, True, 0)).astype(bf16)
    do_head = swap_heads(do_wide)
    dq_head, dkv_head = local_call(
        functools.partial(backward_kernel, nquery, nblocks, 2),
        "attention_backward",
        (
            jax.ShapeDtypeStruct((nquery * BLK, WIDE), bf16),
            jax.ShapeDtypeStruct((nblocks * BLK, WIDE), bf16),
        ),
        3,
        4,
        [pltpu.VMEM((nblocks * BLK, WIDE), f32)],
    )(near_table, long_table, block_table, q_head, do_head, res, kv_head)
    dq = swap_back(dq_head[:, :HEAD_DIM])
    dkv = swap_back(
        lax.psum_scatter(
            dkv_head, "seq", scatter_dimension=0, axis_index_groups=within, tiled=True
        )
    )
    split = dkv.reshape(rows, heads, 2, HEAD_DIM)
    dk, dv = (split[:, :, index].reshape(rows, local_width) for index in range(2))
    grad_query_bias = 0.125 * jnp.sum(dq.astype(f32), axis=0)
    grad_value_bias = jnp.sum(dv.astype(f32), axis=0)
    grad_query_weight = 0.125 * rows_product(h1, dq)
    grad_key_weight = rows_product(h1, dk)
    grad_value_weight = rows_product(h1, dv)
    grad_h1_part = (
        0.125 * cols_product(dq, query_weight)
        + cols_product(dk, key_weight)
        + cols_product(dv, value_weight)
    ).astype(bf16)
    grad_h1 = lax.psum_scatter(grad_h1_part, "tp", scatter_dimension=1, tiled=True).astype(f32)
    feature_start = tp_index * part_width
    my_gain = lax.dynamic_slice_in_dim(norm_gain, feature_start, part_width, 0)
    x_mine = hidden_in.reshape(rows, part_width).astype(f32)
    xhat = (x_mine - mean1) * scale1
    grad_hat = grad_h1 * my_gain
    sums = lax.psum(
        jnp.stack([jnp.sum(grad_hat, axis=1), jnp.sum(grad_hat * xhat, axis=1)]), "tp"
    ) * (1.0 / (part_width * ntp))
    grad_x_norm = scale1 * (grad_hat - sums[0][:, None] - xhat * sums[1][:, None])
    grad_x1_mine = lax.dynamic_slice_in_dim(grad_branch, feature_start, part_width, 1).astype(f32)
    grad_input = (grad_x1_mine + grad_x_norm).reshape(hidden_in.shape)

    def scatter_grad(value, dimension):
        return lax.psum_scatter(
            value.astype(bf16), "seq", scatter_dimension=dimension, tiled=True
        ).astype(f32)

    feature_sums = lax.all_gather(
        jnp.stack([jnp.sum(grad_h1 * xhat, axis=0), jnp.sum(grad_h1, axis=0), grad_outer_bias_part]),
        "tp",
        axis=1,
        tiled=True,
    )
    token_sums = lax.psum(jnp.stack([grad_output_bias, grad_feed_gain, grad_feed_shift]), "tp")
    vectors = lax.psum(
        jnp.concatenate(
            [
                feature_sums.reshape(-1),
                token_sums.reshape(-1),
                grad_query_bias,
                grad_value_bias,
                grad_inner_bias,
            ]
        ),
        "seq",
    )
    features = part_width * ntp
    wide = vectors[: 6 * features].reshape(6, features)
    rest = vectors[6 * features :]
    return (
        layer_out,
        grad_input,
        wide[0],
        wide[1],
        scatter_grad(grad_query_weight, 0),
        rest[:local_width],
        scatter_grad(grad_key_weight, 0),
        scatter_grad(grad_value_weight, 0),
        rest[local_width : 2 * local_width],
        scatter_grad(grad_output_weight, 1),
        wide[3],
        wide[4],
        wide[5],
        scatter_grad(grad_inner_weight, 0),
        rest[2 * local_width :],
        scatter_grad(grad_outer_weight, 1),
        wide[2],
    )


def solution(mesh):
    return jax.shard_map(
        on_device,
        mesh=mesh,
        in_specs=(
            P(None, "seq", "tp"),
            P(),
            P(),
            P(None, "tp"),
            P("tp"),
            P(None, "tp"),
            P(None, "tp"),
            P("tp"),
            P("tp", None),
            P(),
            P(),
            P(),
            P(None, "tp"),
            P("tp"),
            P("tp", None),
            P(),
            P(),
            P(),
            P(),
            P(None, "seq", "tp"),
        ),
        out_specs=(
            P(None, "seq", "tp"),
            P(None, "seq", "tp"),
            P(),
            P(),
            P("seq", "tp"),
            P("tp"),
            P("seq", "tp"),
            P("seq", "tp"),
            P("tp"),
            P("tp", "seq"),
            P(),
            P(),
            P(),
            P("seq", "tp"),
            P("tp"),
            P("tp", "seq"),
            P(),
        ),
        check_vma=False,
    )
```

```python
import functools

import jax
import jax.numpy as jnp
from jax import lax
from jax.experimental import pallas as pl
from jax.experimental.pallas import tpu as pltpu
from jax.sharding import PartitionSpec as P

HEAD_DIM = 64
BLK = 64
GLOBAL = 2
SLOTS = 8
WIDE = 2 * HEAD_DIM
NEG = -1e30
NT = (((1,), (1,)), ((), ()))
TN = (((0,), (0,)), ((), ()))


def layer_norm(value, gain, shift):
    mean = jnp.mean(value, axis=-1, keepdims=True)
    centered = value - mean
    spread = jnp.mean(centered * centered, axis=-1, keepdims=True)
    return centered * lax.rsqrt(spread + 1e-05) * gain + shift


def gelu_tanh(value):
    return jax.nn.gelu(value, approximate=True)


def block_tables(doc_blocks, doc_padding, random_picks, nblocks):
    ends = jnp.cumsum(doc_blocks)
    starts = ends - doc_blocks
    block_ids = jnp.arange(nblocks, dtype=jnp.int32)
    member = (
        (block_ids[:, None] >= starts[None, :]) & (block_ids[:, None] < ends[None, :])
    ).astype(jnp.int32)
    first = jnp.sum(member * starts[None, :], axis=1)
    length = jnp.sum(member * doc_blocks[None, :], axis=1)
    padding = jnp.sum(member * doc_padding[None, :], axis=1)
    last_block = block_ids == first + length - 1
    live = jnp.where(last_block, BLK - padding, BLK)
    partner = first[:, None] + jnp.remainder(random_picks, length[:, None])
    return (first, length, live, partner)


def attention_tables(doc_blocks, doc_padding, random_picks, nrows, nseq, heads, part):
    share = nseq // heads
    nblocks = nrows * nseq
    first, length, live, partner = block_tables(doc_blocks, doc_padding, random_picks, nblocks)
    block = jnp.arange(nblocks, dtype=jnp.int32)
    holder = block % nseq
    slot_of = ((holder % share) * heads + holder // share) * nrows + block // nseq
    glob = block - first < GLOBAL
    last = first + length - 1
    step = jnp.arange(SLOTS, dtype=jnp.int32)
    near = jnp.stack([block - 1, block, block + 1, first, first + 1], axis=1)
    picks = jnp.concatenate([near, partner], axis=1)
    whole = first[:, None] + step[None, :]
    cand = jnp.where(glob[:, None], whole, picks)
    valid = (cand >= first[:, None]) & (cand <= last[:, None])
    same = (cand[:, :, None] == cand[:, None, :]) & valid[:, None, :]
    earlier = step[None, None, :] < step[None, :, None]
    valid = valid & ~jnp.any(same & earlier, axis=2)
    is_long = glob & (length > SLOTS)
    valid = valid & ~is_long[:, None]
    place = jnp.cumsum(valid.astype(jnp.int32), axis=1) - 1
    pick = (valid[:, :, None] & (place[:, :, None] == step[None, None, :])).astype(jnp.int32)
    order = jnp.sum(pick * cand[:, :, None], axis=1)
    filled = jnp.sum(pick, axis=1)
    onehot = (order[:, :, None] == block[None, None, :]).astype(jnp.int32)
    slots = jnp.sum(onehot * slot_of[None, None, :], axis=2) * BLK
    lives = filled * jnp.sum(onehot * live[None, None, :], axis=2)
    mine = lambda item: lax.dynamic_index_in_dim(
        jnp.moveaxis(item.reshape((nrows, heads, share) + item.shape[1:]), 2, 0), part, 0, False
    ).swapaxes(0, 1).reshape((nrows * heads,) + item.shape[1:])
    nquery = nrows * heads
    long_mine = mine(is_long.astype(jnp.int32))
    rank = jnp.cumsum(long_mine) - 1
    query = jnp.arange(nquery, dtype=jnp.int32)
    chosen = (long_mine[:, None] * (rank[:, None] == query[None, :])).astype(jnp.int32)
    long_query = jnp.sum(chosen * query[:, None], axis=0)
    long_first = jnp.sum(chosen * mine(first)[:, None], axis=0)
    long_len = jnp.sum(chosen * mine(length)[:, None], axis=0)
    near_table = jnp.concatenate([mine(slots).reshape(-1), mine(lives).reshape(-1)])
    long_table = jnp.concatenate([long_query, long_first, long_len, jnp.sum(long_mine)[None]])
    block_table = jnp.concatenate([slot_of * BLK, live])
    return near_table, long_table, block_table


def bias_row(lives):
    lane = lax.broadcasted_iota(jnp.int32, (1, WIDE), 1)
    parts = []
    for index in range(0, SLOTS, 2):
        bound = jnp.where(lane < BLK, lives[index], lives[index + 1] + BLK)
        parts.append(jnp.where(lane < bound, 0.0, NEG))
    return jnp.concatenate(parts, axis=1)


def near_slots(near_ref, query, nquery):
    base = query * SLOTS
    slots = [pl.multiple_of(near_ref[base + k], BLK) for k in range(SLOTS)]
    lives = [near_ref[nquery * SLOTS + base + k] for k in range(SLOTS)]
    return slots, lives


def long_slots(block_ref, nblocks, first, length, chunk):
    slots, lives = [], []
    for k in range(SLOTS):
        place = chunk * SLOTS + k
        block = first + jnp.minimum(place, length - 1)
        slots.append(pl.multiple_of(block_ref[block], BLK))
        lives.append(jnp.where(place < length, block_ref[nblocks + block], 0))
    return slots, lives


def take(ref, slots):
    return jnp.concatenate([ref[pl.ds(slot, BLK), :] for slot in slots], axis=0)


def forward_kernel(nquery, nblocks, unroll, near_ref, long_ref, block_ref, q_ref, kv_ref, out_ref):
    upper = lax.broadcasted_iota(jnp.int32, (BLK, WIDE), 1) >= HEAD_DIM

    def finish(query, top, total, accum):
        out_ref[pl.ds(query * BLK, BLK), :] = jnp.where(
            upper, accum / total, top + jnp.log(total)
        )

    def scores_of(query, slots, lives):
        kv = take(kv_ref, slots)
        scores = lax.dot_general(
            q_ref[pl.ds(query * BLK, BLK), :], kv, NT, preferred_element_type=jnp.float32
        )
        return kv, scores + bias_row(lives)

    def near_step(index, carry):
        for offset in range(unroll):
            query = index * unroll + offset
            kv, scores = scores_of(query, *near_slots(near_ref, query, nquery))
            top = jnp.max(scores, axis=1, keepdims=True)
            weights = jnp.exp(scores - top)
            total = jnp.sum(weights, axis=1, keepdims=True)
            accum = jnp.dot(weights.astype(jnp.bfloat16), kv, preferred_element_type=jnp.float32)
            finish(query, top, total, accum)
        return carry

    lax.fori_loop(0, nquery // unroll, near_step, 0)

    def long_step(index, carry):
        query = long_ref[index]
        first = long_ref[nquery + index]
        length = long_ref[2 * nquery + index]

        def chunk_step(chunk, state):
            top, total, accum = state
            kv, scores = scores_of(query, *long_slots(block_ref, nblocks, first, length, chunk))
            new_top = jnp.maximum(top, jnp.max(scores, axis=1, keepdims=True))
            weights = jnp.exp(scores - new_top)
            decay = jnp.exp(top - new_top)
            total = total * decay + jnp.sum(weights, axis=1, keepdims=True)
            accum = accum * decay + jnp.dot(
                weights.astype(jnp.bfloat16), kv, preferred_element_type=jnp.float32
            )
            return new_top, total, accum

        start = (
            jnp.full((BLK, 1), NEG, jnp.float32),
            jnp.zeros((BLK, 1), jnp.float32),
            jnp.zeros((BLK, WIDE), jnp.float32),
        )
        top, total, accum = lax.fori_loop(0, (length + SLOTS - 1) // SLOTS, chunk_step, start)
        finish(query, top, total, accum)
        return carry

    lax.fori_loop(0, long_ref[3 * nquery], long_step, 0)


def backward_kernel(
    nquery, nblocks, unroll,
    near_ref, long_ref, block_ref, q_ref, do_ref, res_ref, kv_ref, dq_ref, dkv_ref, sum_ref,
):
    sum_ref[...] = jnp.zeros_like(sum_ref)

    def load(query):
        rows = pl.ds(query * BLK, BLK)
        grad = do_ref[rows, :]
        both = jnp.concatenate([q_ref[rows, :], grad], axis=0)
        res = res_ref[rows, :]
        log_total = res[:, :1]
        delta = jnp.sum(res * grad.astype(jnp.float32), axis=1, keepdims=True)
        return both, log_total, delta

    def terms(both, log_total, delta, slots, lives):
        kv = take(kv_ref, slots)
        pair = lax.dot_general(both, kv, NT, preferred_element_type=jnp.float32)
        probs = jnp.exp(pair[:BLK] + bias_row(lives) - log_total)
        grad_scores = (probs * (pair[BLK:] - delta)).astype(jnp.bfloat16)
        weights = jnp.concatenate([grad_scores, probs.astype(jnp.bfloat16)], axis=0)
        dkv = lax.dot_general(weights, both, TN, preferred_element_type=jnp.float32)
        dq = jnp.dot(grad_scores, kv, preferred_element_type=jnp.float32)
        return dq, dkv

    def scatter(slots, dkv):
        for k, slot in enumerate(slots):
            sum_ref[pl.ds(slot, BLK), :] += dkv[k * BLK : (k + 1) * BLK]

    def near_step(index, carry):
        done = []
        for offset in range(unroll):
            query = index * unroll + offset
            slots, lives = near_slots(near_ref, query, nquery)
            dq, dkv = terms(*load(query), slots, lives)
            dq_ref[pl.ds(query * BLK, BLK), :] = dq.astype(jnp.bfloat16)
            done.append((slots, dkv))
        for slots, dkv in done:
            scatter(slots, dkv)
        return carry

    lax.fori_loop(0, nquery // unroll, near_step, 0)

    def long_step(index, carry):
        query = long_ref[index]
        first = long_ref[nquery + index]
        length = long_ref[2 * nquery + index]
        loaded = load(query)

        def chunk_step(chunk, total):
            slots, lives = long_slots(block_ref, nblocks, first, length, chunk)
            dq, dkv = terms(*loaded, slots, lives)
            scatter(slots, dkv)
            return total + dq

        total = lax.fori_loop(
            0, (length + SLOTS - 1) // SLOTS, chunk_step, jnp.zeros((BLK, WIDE), jnp.float32)
        )
        dq_ref[pl.ds(query * BLK, BLK), :] = total.astype(jnp.bfloat16)
        return carry

    lax.fori_loop(0, long_ref[3 * nquery], long_step, 0)
    dkv_ref[...] = sum_ref[...].astype(jnp.bfloat16)


def local_call(kernel, name, out_shape, nsmem, nvmem, scratch=(), flops=0):
    return pl.pallas_call(
        kernel,
        out_shape=out_shape,
        in_specs=[pl.BlockSpec(memory_space=pltpu.SMEM)] * nsmem
        + [pl.BlockSpec(memory_space=pltpu.VMEM)] * nvmem,
        out_specs=jax.tree.map(lambda _: pl.BlockSpec(memory_space=pltpu.VMEM), out_shape),
        scratch_shapes=list(scratch),
        name=name,
        cost_estimate=pl.CostEstimate(flops=flops, bytes_accessed=8 << 20, transcendentals=0),
        compiler_params=pltpu.CompilerParams(vmem_limit_bytes=56 << 20),
    )


MESH = pl.DeviceIdType.MESH
CHUNKS = 4


def remote(src, dst, send_sem, recv_sem, device):
    return pltpu.make_async_remote_copy(
        src_ref=src, dst_ref=dst, send_sem=send_sem, recv_sem=recv_sem,
        device_id=device, device_id_type=MESH,
    )


def greet(seq, tp, nseq, ntp):
    barrier = pltpu.get_barrier_semaphore()
    for step in range(1, nseq):
        peer = (lax.rem(seq + step, nseq), tp)
        pl.semaphore_signal(barrier, inc=1, device_id=peer, device_id_type=MESH)
    for step in range(1, ntp):
        peer = (seq, lax.rem(tp + step, ntp))
        pl.semaphore_signal(barrier, inc=1, device_id=peer, device_id_type=MESH)
    pl.semaphore_wait(barrier, nseq + ntp - 2)


def add_bf16(*terms):
    total = terms[0].astype(jnp.float32)
    for term in terms[1:]:
        total = total + term.astype(jnp.float32)
    return total


class GradScatter:
    def __init__(self, dims, place, source, land, pair, far, sems):
        self.heads, self.share, self.nseq = dims
        self.seq, self.tp, self.head, self.part = place
        self.source, self.land, self.pair, self.far = source, land, pair, far
        self.send1, self.recv1, self.send2, self.recv2 = sems

    def near(self, step):
        other = lax.rem(self.part + step, self.share)
        return remote(
            self.source.at[:, other], self.land.at[step - 1],
            self.send1.at[step - 1], self.recv1.at[step - 1],
            (self.head * self.share + other, self.tp),
        )

    def across(self, step):
        other = lax.rem(self.head + step, self.heads)
        return remote(
            self.pair.at[other], self.far.at[step - 1],
            self.send2.at[step - 1], self.recv2.at[step - 1],
            (other * self.share + self.part, self.tp),
        )

    def start_near(self):
        for step in range(1, self.share):
            self.near(step).start()

    def start_across(self):
        for step in range(1, self.share):
            self.near(step).wait_recv()

        def body(head, carry):
            parts = [self.source[head, self.part]]
            parts += [self.land[step, head] for step in range(self.share - 1)]
            self.pair[head] = add_bf16(*parts).astype(jnp.bfloat16)
            return carry

        lax.fori_loop(0, self.heads, body, 0)
        for step in range(1, self.heads):
            self.across(step).start()

    def result(self):
        for step in range(1, self.heads):
            self.across(step).wait_recv()
        parts = [self.pair[self.head]] + [self.far[step] for step in range(self.heads - 1)]
        return add_bf16(*parts)

    def finish(self):
        for step in range(1, self.share):
            self.near(step).wait_send()
        for step in range(1, self.heads):
            self.across(step).wait_send()


def tail_kernel(
    dims,
    dq_ref, dkv_ref, h1_ref, x_ref, stat_ref, gain_ref, wq_ref, wkv_ref, da_ref,
    gi_ref, gu_ref, gw_ref, vec_ref,
    gx_ref, oi_ref, ou_ref, ow_ref, oq_ref, okv_ref, vout_ref,
    dq_in, dkv_in, dkv_land, dkv_sum, pbuf, from_left, from_right,
    sums, sums_land, vbuf, vec_land, vsum, vec_far, gq, gkv,
    *rest,
):
    heads, share, nseq, ntp = dims
    lands, sems = rest[:15], rest[15:]
    rows, features = h1_ref.shape
    part_width = features // ntp
    chunk_rows = rows // CHUNKS
    seq, tp = lax.axis_index("seq"), lax.axis_index("tp")
    head, part = seq // share, lax.rem(seq, share)
    place = (seq, tp, head, part)
    (dq_s, dq_r, kv1_s, kv1_r, kv2_s, kv2_r, right_s, right_r, left_s, left_r,
     st_s, st_r, v1_s, v1_r, v2_s, v2_r, g1_s, g1_r, g2_s, g2_r) = sems
    f32, bf16 = jnp.float32, jnp.bfloat16

    def chunk_of(chunk):
        return pl.ds(chunk * chunk_rows, chunk_rows)

    scatters = [
        GradScatter(
            (heads, share, nseq), place, source, *lands[3 * k : 3 * k + 3],
            (g1_s.at[k], g1_r.at[k], g2_s.at[k], g2_r.at[k]),
        )
        for k, source in enumerate((gi_ref, gu_ref, gw_ref, gq, gkv))
    ]

    def dq_copy(chunk, step):
        other = lax.rem(head + step, heads)
        return remote(
            dq_ref.at[other, chunk_of(chunk)], dq_in.at[head, chunk_of(chunk)],
            dq_s.at[chunk, step - 1], dq_r.at[chunk, step - 1], (other * share + part, tp),
        )

    def dkv_near(step):
        other = lax.rem(part + step, share)
        return remote(
            dkv_ref.at[other], dkv_land.at[step - 1], kv1_s.at[step - 1], kv1_r.at[step - 1],
            (head * share + other, tp),
        )

    def dkv_copy(chunk, step):
        other = lax.rem(head + step, heads)
        return remote(
            dkv_sum.at[other, chunk_of(chunk)], dkv_in.at[head, chunk_of(chunk)],
            kv2_s.at[chunk, step - 1], kv2_r.at[chunk, step - 1], (other * share + part, tp),
        )

    def rightward(chunk, index):
        return remote(
            pbuf.at[chunk, index], from_left.at[chunk, index],
            right_s.at[chunk, index], right_r.at[chunk, index], (seq, tp + 1),
        )

    def leftward(chunk, index):
        return remote(
            pbuf.at[chunk, index], from_right.at[chunk, index],
            left_s.at[chunk, index], left_r.at[chunk, index], (seq, tp - 1),
        )

    def sums_copy(step):
        return remote(
            sums, sums_land.at[step - 1], st_s.at[step - 1], st_r.at[step - 1],
            (seq, lax.rem(tp + step, ntp)),
        )

    def vec_copy(step):
        return remote(
            vbuf, vec_land.at[step - 1], v1_s.at[step - 1], v1_r.at[step - 1],
            (lax.rem(seq + step, nseq), tp),
        )

    def vec_far_copy(step):
        return remote(
            vsum, vec_far.at[step - 1], v2_s.at[step - 1], v2_r.at[step - 1],
            (seq, lax.rem(tp + step, ntp)),
        )

    greet(seq, tp, nseq, ntp)
    for step in range(1, share):
        dkv_near(step).start()
    for chunk in range(CHUNKS):
        for step in range(1, heads):
            dq_copy(chunk, step).start()
    for scatter in scatters[:3]:
        scatter.start_near()
    dq_in[head] = dq_ref[head]
    for step in range(1, share):
        dkv_near(step).wait_recv()
    for chunk in range(CHUNKS):
        for target in range(heads):
            where = (target, chunk_of(chunk))
            parts = [dkv_ref[(part,) + where]]
            parts += [dkv_land[(step,) + where] for step in range(share - 1)]
            dkv_sum[where] = add_bf16(*parts).astype(bf16)
        for step in range(1, heads):
            dkv_copy(chunk, step).start()
    dkv_in[head] = dkv_sum[head]
    for scatter in scatters[:3]:
        scatter.start_across()

    vbuf[...] = vec_ref[...]
    gain = gain_ref[...]
    lane = lax.broadcasted_iota(jnp.int32, (chunk_rows, WIDE), 1)
    per = features // WIDE

    def partial_step(chunk):
        here = chunk_of(chunk)
        for step in range(1, heads):
            dq_copy(chunk, step).wait_recv()
            dkv_copy(chunk, step).wait_recv()
        dq = jnp.concatenate([dq_in[index, here] for index in range(heads)], axis=1)
        dkv = jnp.concatenate([dkv_in[index, here] for index in range(heads)], axis=1)
        grad = lax.dot_general(dq, wq_ref[...], NT, preferred_element_type=f32)
        grad = grad + lax.dot_general(dkv, wkv_ref[...], NT, preferred_element_type=f32)
        mean, scale = stat_ref[here, 0:1], stat_ref[here, 1:2]
        sum0 = jnp.zeros((chunk_rows, 1), f32)
        sum1 = jnp.zeros((chunk_rows, 1), f32)
        for index in range(ntp):
            cols = slice(index * part_width, (index + 1) * part_width)
            piece = grad[:, cols]
            xhat = (x_ref[index, here].astype(f32) - mean) * scale
            weighted = piece * gain[:, cols]
            product = piece * xhat
            sum0 = sum0 + jnp.sum(weighted, axis=1, keepdims=True)
            sum1 = sum1 + jnp.sum(weighted * xhat, axis=1, keepdims=True)
            col0 = jnp.sum(product, axis=0, keepdims=True)
            col1 = jnp.sum(piece, axis=0, keepdims=True)
            for sub in range(part_width // WIDE):
                row = index * (part_width // WIDE) + sub
                lanes = slice(sub * WIDE, (sub + 1) * WIDE)
                vbuf[row : row + 1, :] += col0[:, lanes]
                vbuf[per + row : per + row + 1, :] += col1[:, lanes]
            pbuf[chunk, index] = piece.astype(bf16)
        both = jnp.where(lane == 0, sum0, jnp.where(lane == 1, sum1, 0.0))
        sums[:, here] = both.T[:8]
        base = 6 * per
        for index in range(heads):
            lanes = slice(index * WIDE, (index + 1) * WIDE)
            vbuf[base + index : base + index + 1, :] += jnp.sum(
                dq[:, lanes].astype(f32), axis=0, keepdims=True
            )
            vbuf[base + heads + index : base + heads + index + 1, :] += jnp.sum(
                dkv[:, lanes].astype(f32), axis=0, keepdims=True
            )

    def pass_on(chunk):
        for step in range(ntp - 1):
            far = ntp - 1 - step

            @pl.when(tp < far)
            def _():
                @pl.when(tp > 0)
                def _():
                    rightward(chunk, far).wait_recv()
                    pbuf[chunk, far] = add_bf16(pbuf[chunk, far], from_left[chunk, far]).astype(bf16)

                rightward(chunk, far).start()

            @pl.when(tp > step)
            def _():
                @pl.when(tp < ntp - 1)
                def _():
                    leftward(chunk, step).wait_recv()
                    pbuf[chunk, step] = add_bf16(pbuf[chunk, step], from_right[chunk, step]).astype(bf16)

                leftward(chunk, step).start()

    for chunk in range(CHUNKS):
        partial_step(chunk)
        if chunk > 0:
            pass_on(chunk - 1)
    for step in range(1, ntp):
        sums_copy(step).start()
    for step in range(1, nseq):
        vec_copy(step).start()

    halves = [dq_in[index][:, :HEAD_DIM] for index in range(heads)]
    dq_all = jnp.concatenate(halves, axis=1)
    dkv_all = jnp.concatenate([dkv_in[index] for index in range(heads)], axis=1)
    band = features // heads

    def grad_step(index, carry):
        left = h1_ref[:, pl.ds(pl.multiple_of(index * band, band), band)]
        shape = (share, band // share, -1)
        gq[index] = (
            0.125 * lax.dot_general(left, dq_all, TN, preferred_element_type=f32)
        ).astype(bf16).reshape(shape)
        gkv[index] = lax.dot_general(left, dkv_all, TN, preferred_element_type=f32).astype(
            bf16
        ).reshape(shape)
        return carry

    lax.fori_loop(0, heads, grad_step, 0)
    for scatter in scatters[3:]:
        scatter.start_near()
    pass_on(CHUNKS - 1)
    for step in range(1, nseq):
        vec_copy(step).wait_recv()
    total = vbuf[...]
    for step in range(nseq - 1):
        total = total + vec_land[step]
    vsum[...] = total
    for step in range(1, ntp):
        vec_far_copy(step).start()
    for scatter in scatters[3:]:
        scatter.start_across()

    for step in range(1, ntp):
        sums_copy(step).wait_recv()
    my_gain = gain_ref[:, pl.ds(pl.multiple_of(tp * part_width, part_width), part_width)]
    for chunk in range(CHUNKS):
        here = chunk_of(chunk)
        both = sums[:, here]
        for step in range(ntp - 1):
            both = both + sums_land[step, :, here]
        both = jnp.concatenate([both, jnp.zeros((WIDE - 8, chunk_rows), f32)], axis=0).T
        both = both * (1.0 / features)

        @pl.when(tp > 0)
        def _():
            rightward(chunk, tp).wait_recv()

        @pl.when(tp < ntp - 1)
        def _():
            leftward(chunk, tp).wait_recv()

        grad = pbuf[chunk, tp].astype(f32)
        grad = grad + jnp.where(tp > 0, from_left[chunk, tp].astype(f32), 0.0)
        grad = grad + jnp.where(tp < ntp - 1, from_right[chunk, tp].astype(f32), 0.0)
        mean, scale = stat_ref[here, 0:1], stat_ref[here, 1:2]
        xhat = (x_ref[tp, here].astype(f32) - mean) * scale
        inner = grad * my_gain - both[:, 0:1] - xhat * both[:, 1:2]
        gx_ref[here] = da_ref[here].astype(f32) + scale * inner
    for scatter, out in zip(scatters, (oi_ref, ou_ref, ow_ref, oq_ref, okv_ref)):
        out[...] = scatter.result()
    for step in range(1, ntp):
        vec_far_copy(step).wait_recv()
    vout_ref[...] = vsum[...]
    for step in range(ntp - 1):
        vout_ref[: 6 * per] += vec_far[step, : 6 * per]

    for step in range(1, share):
        dkv_near(step).wait_send()
    for chunk in range(CHUNKS):
        for step in range(1, heads):
            dq_copy(chunk, step).wait_send()
            dkv_copy(chunk, step).wait_send()
        for index in range(ntp):
            @pl.when(tp < index)
            def _():
                rightward(chunk, index).wait_send()

            @pl.when(tp > index)
            def _():
                leftward(chunk, index).wait_send()

    for step in range(1, ntp):
        sums_copy(step).wait_send()
        vec_far_copy(step).wait_send()
    for step in range(1, nseq):
        vec_copy(step).wait_send()
    for scatter in scatters:
        scatter.finish()


def run_tail(dims, dq, dkv, h1, x_parts, stats, gain, wq, wkv, da, grads, vec):
    heads, share, nseq, ntp = dims
    f32, bf16 = jnp.float32, jnp.bfloat16
    rows, features = h1.shape
    width = features // ntp
    band = features // nseq
    columns = [grad.shape[-1] for grad in grads] + [heads * HEAD_DIM, heads * WIDE]
    sds = jax.ShapeDtypeStruct
    outs = (
        [sds((rows, width), f32)]
        + [sds((band, cols), f32) for cols in columns]
        + [sds(vec.shape, f32)]
    )
    lands = []
    for cols in columns:
        lands += [
            pltpu.VMEM((max(share - 1, 1), heads, band, cols), bf16),
            pltpu.VMEM((heads, band, cols), bf16),
            pltpu.VMEM((max(heads - 1, 1), band, cols), bf16),
        ]
    pieces = (CHUNKS, ntp, rows // CHUNKS, width)
    scratch = [
        pltpu.VMEM((heads, rows, WIDE), bf16),
        pltpu.VMEM((heads, rows, WIDE), bf16),
        pltpu.VMEM((max(share - 1, 1), heads, rows, WIDE), bf16),
        pltpu.VMEM((heads, rows, WIDE), bf16),
        pltpu.VMEM(pieces, bf16),
        pltpu.VMEM(pieces, bf16),
        pltpu.VMEM(pieces, bf16),
        pltpu.VMEM((8, rows), f32),
        pltpu.VMEM((ntp - 1, 8, rows), f32),
        pltpu.VMEM(vec.shape, f32),
        pltpu.VMEM((nseq - 1,) + vec.shape, f32),
        pltpu.VMEM(vec.shape, f32),
        pltpu.VMEM((ntp - 1,) + vec.shape, f32),
        pltpu.VMEM((heads, share, band, columns[3]), bf16),
        pltpu.VMEM((heads, share, band, columns[4]), bf16),
        *lands,
    ]
    dma = lambda *shape: pltpu.SemaphoreType.DMA(tuple(max(size, 1) for size in shape))
    sems = (
        [dma(CHUNKS, heads - 1)] * 2 + [dma(share - 1)] * 2 + [dma(CHUNKS, heads - 1)] * 2
        + [dma(CHUNKS, ntp)] * 4 + [dma(ntp - 1)] * 2 + [dma(nseq - 1)] * 2 + [dma(ntp - 1)] * 2
        + [dma(5, share - 1)] * 2 + [dma(5, heads - 1)] * 2
    )
    operands = (dq, dkv, h1, x_parts, stats, gain, wq, wkv, da, *grads, vec)
    return pl.pallas_call(
        functools.partial(tail_kernel, dims),
        out_shape=outs,
        in_specs=[pl.BlockSpec(memory_space=pltpu.VMEM)] * len(operands),
        out_specs=[pl.BlockSpec(memory_space=pltpu.VMEM)] * len(outs),
        scratch_shapes=scratch + sems,
        name="tail",
        compiler_params=pltpu.CompilerParams(
            collective_id=3, has_side_effects=True, vmem_limit_bytes=60 << 20
        ),
    )(*operands)


def rows_product(left, right):
    return lax.dot_general(left, right, TN, preferred_element_type=jnp.float32)


def cols_product(left, right):
    return lax.dot_general(left, right, NT, preferred_element_type=jnp.float32)


def spread_heads(weight, heads, upper, axis):
    shape = weight.shape[:axis] + (heads, HEAD_DIM) + weight.shape[axis + 1 :]
    weight = weight.reshape(shape)
    pads = [(0, 0)] * len(shape)
    pads[axis + 1] = (HEAD_DIM, 0) if upper else (0, HEAD_DIM)
    weight = jnp.pad(weight, pads)
    return weight.reshape(shape[:axis] + (heads * WIDE,) + shape[axis + 2 :])


def pair_heads(left, right, heads):
    lead = left.shape[:-1]
    both = jnp.concatenate(
        [left.reshape(lead + (heads, HEAD_DIM)), right.reshape(lead + (heads, HEAD_DIM))], axis=-1
    )
    return both.reshape(lead + (heads * WIDE,))


def on_device(
    hidden_in,
    norm_gain,
    norm_shift,
    query_weight,
    query_bias,
    key_weight,
    value_weight,
    value_bias,
    output_weight,
    output_bias,
    feed_gain,
    feed_shift,
    inner_weight,
    inner_bias,
    outer_weight,
    outer_bias,
    doc_blocks,
    doc_padding,
    random_picks,
    cotangent,
):
    f32, bf16 = jnp.float32, jnp.bfloat16
    nrows, block_len, part_width = hidden_in.shape
    rows = nrows * block_len
    nseq, ntp = lax.axis_size("seq"), lax.axis_size("tp")
    seq_index, tp_index = lax.axis_index("seq"), lax.axis_index("tp")
    local_width = query_weight.shape[1]
    heads = local_width // HEAD_DIM
    share = nseq // heads
    nquery = nrows * heads
    nblocks = nrows * nseq
    tokens_part = rows // ntp
    across = [[h * share + r for h in range(heads)] for r in range(share)]
    within = [[h * share + r for r in range(share)] for h in range(heads)]

    def swap_heads(value):
        width = value.shape[1] // heads
        value = value.reshape(rows, heads, width).swapaxes(0, 1)
        value = lax.all_to_all(value, "seq", 0, 0, axis_index_groups=across, tiled=True)
        return value.reshape(heads * rows, width)

    def swap_back(value):
        width = value.shape[1]
        value = lax.all_to_all(
            value.reshape(heads, rows, width), "seq", 0, 0, axis_index_groups=across, tiled=True
        )
        return value.swapaxes(0, 1).reshape(rows, heads * width)

    tables = attention_tables(
        doc_blocks, doc_padding, random_picks, nrows, nseq, heads, seq_index % share
    )
    x_parts = lax.all_gather(hidden_in.reshape(rows, part_width), "tp", axis=0)
    x_full = x_parts.swapaxes(0, 1).reshape(rows, ntp * part_width).astype(f32)
    mean1 = jnp.mean(x_full, axis=-1, keepdims=True)
    centered = x_full - mean1
    scale1 = lax.rsqrt(jnp.mean(centered * centered, axis=-1, keepdims=True) + 1e-05)
    h1 = (centered * scale1 * norm_gain + norm_shift).astype(bf16)
    q_wide = (
        (
            jnp.dot(h1, spread_heads(query_weight, heads, False, 1), preferred_element_type=f32)
            + spread_heads(query_bias, heads, False, 0)
        )
        * 0.125
    ).astype(bf16)
    kv_bias = pair_heads(jnp.zeros_like(value_bias), value_bias, heads)
    kv = (
        jnp.dot(h1, pair_heads(key_weight, value_weight, heads), preferred_element_type=f32) + kv_bias
    ).astype(bf16)
    q_head = swap_heads(q_wide)
    kv_head = lax.all_gather(
        swap_heads(kv), "seq", axis=0, axis_index_groups=within, tiled=True
    )
    near_table, long_table, block_table = tables
    res = local_call(
        functools.partial(forward_kernel, nquery, nblocks, 2),
        "attention_forward",
        jax.ShapeDtypeStruct((nquery * BLK, WIDE), f32),
        3,
        2,
    )(near_table, long_table, block_table, q_head, kv_head)
    mixed = swap_back(res[:, HEAD_DIM:].astype(bf16))
    attn_part = jnp.dot(mixed, output_weight, preferred_element_type=f32).astype(bf16)
    attn = lax.psum_scatter(attn_part, "tp", scatter_dimension=0, tiled=True).astype(f32)
    token_start = tp_index * tokens_part
    x_part = lax.dynamic_slice_in_dim(x_full, token_start, tokens_part, 0)
    x1 = x_part + attn + output_bias
    h2_f, feed_pull = jax.vjp(layer_norm, x1, feed_gain, feed_shift)
    h2 = lax.all_gather(h2_f.astype(bf16), "tp", axis=0, tiled=True)
    pre = jnp.dot(h2, inner_weight, preferred_element_type=f32) + inner_bias
    act_f, gelu_pull = jax.vjp(gelu_tanh, pre)
    act = act_f.astype(bf16)
    ffn_part = jnp.dot(act, outer_weight, preferred_element_type=f32)
    own = lax.dynamic_slice_in_dim(ffn_part, token_start, tokens_part, 0) + x1
    ffn_part = lax.dynamic_update_slice_in_dim(ffn_part, own, token_start, 0).astype(bf16)
    result = lax.psum_scatter(ffn_part, "tp", scatter_dimension=1, tiled=True).astype(f32)
    bias_part = lax.dynamic_slice_in_dim(outer_bias, tp_index * part_width, part_width, 0)
    layer_out = (result + bias_part).astype(bf16).reshape(hidden_in.shape)

    cot = cotangent.reshape(rows, part_width)
    grad_out = lax.all_gather(cot, "tp", axis=1, tiled=True)
    grad_outer_bias_part = jnp.sum(cot.astype(f32), axis=0)
    grad_outer_weight = rows_product(grad_out, act)
    grad_act = cols_product(grad_out, outer_weight)
    grad_pre = gelu_pull(grad_act)[0].astype(bf16)
    grad_inner_bias = jnp.sum(grad_pre.astype(f32), axis=0)
    grad_inner_weight = rows_product(h2, grad_pre)
    grad_h2 = lax.psum_scatter(
        cols_product(grad_pre, inner_weight).astype(bf16), "tp", scatter_dimension=0, tiled=True
    ).astype(f32)
    grad_x1_norm, grad_feed_gain, grad_feed_shift = feed_pull(grad_h2)
    grad_out_part = lax.dynamic_slice_in_dim(grad_out, token_start, tokens_part, 0).astype(f32)
    grad_branch_part = (grad_out_part + grad_x1_norm).astype(bf16)
    grad_output_bias = jnp.sum(grad_branch_part.astype(f32), axis=0)
    grad_branch = lax.all_gather(grad_branch_part, "tp", axis=0, tiled=True)
    grad_output_weight = rows_product(grad_branch, mixed)
    do_wide = cols_product(grad_branch, spread_heads(output_weight, heads, True, 0)).astype(bf16)
    do_head = swap_heads(do_wide)
    dq_head, dkv_head = local_call(
        functools.partial(backward_kernel, nquery, nblocks, 2),
        "attention_backward",
        (
            jax.ShapeDtypeStruct((nquery * BLK, WIDE), bf16),
            jax.ShapeDtypeStruct((nblocks * BLK, WIDE), bf16),
        ),
        3,
        4,
        [pltpu.VMEM((nblocks * BLK, WIDE), f32)],
    )(near_table, long_table, block_table, q_head, do_head, res, kv_head)
    feature_start = tp_index * part_width
    per = part_width * ntp // WIDE
    spread = lambda item: item.reshape(-1, WIDE)
    outer_bias_sum = lax.dynamic_update_slice_in_dim(
        jnp.zeros((part_width * ntp,), f32), grad_outer_bias_part, feature_start, 0
    )
    vec = jnp.concatenate(
        [
            jnp.zeros((2 * per, WIDE), f32),
            spread(grad_output_bias),
            spread(grad_feed_gain),
            spread(grad_feed_shift),
            spread(outer_bias_sum),
            jnp.zeros((2 * heads, WIDE), f32),
            spread(grad_inner_bias),
        ]
    )
    ring = (heads, share, part_width * ntp // nseq)
    grads = [
        item.astype(bf16).reshape(ring + (-1,))
        for item in (grad_inner_weight, grad_outer_weight, grad_output_weight)
    ]
    tail = run_tail(
        (heads, share, nseq, ntp),
        dq_head.reshape(heads, rows, WIDE),
        dkv_head.reshape(share, heads, rows, WIDE),
        h1,
        x_parts,
        jnp.concatenate([mean1, scale1], axis=1),
        norm_gain[None, :],
        spread_heads(query_weight, heads, False, 1) * 0.125,
        pair_heads(key_weight, value_weight, heads),
        lax.dynamic_slice_in_dim(grad_branch, feature_start, part_width, 1),
        grads,
        vec,
    )
    grad_x, inner_part, outer_part, output_part, query_part, kv_part, vectors = tail
    split = kv_part.reshape(-1, heads, 2, HEAD_DIM)
    key_part, value_part = (split[:, :, index].reshape(-1, local_width) for index in range(2))
    wide = vectors[: 6 * per].reshape(6, -1)
    biases = vectors[6 * per : 6 * per + 2 * heads].reshape(2, heads, 2, HEAD_DIM)
    return (
        layer_out,
        grad_x.reshape(hidden_in.shape),
        wide[0],
        wide[1],
        query_part,
        0.125 * biases[0, :, 0].reshape(-1),
        key_part,
        value_part,
        biases[1, :, 1].reshape(-1),
        output_part.T,
        wide[2],
        wide[3],
        wide[4],
        inner_part,
        vectors[6 * per + 2 * heads :].reshape(-1),
        outer_part.T,
        wide[5],
    )


def solution(mesh):
    return jax.shard_map(
        on_device,
        mesh=mesh,
        in_specs=(
            P(None, "seq", "tp"),
            P(),
            P(),
            P(None, "tp"),
            P("tp"),
            P(None, "tp"),
            P(None, "tp"),
            P("tp"),
            P("tp", None),
            P(),
            P(),
            P(),
            P(None, "tp"),
            P("tp"),
            P("tp", None),
            P(),
            P(),
            P(),
            P(),
            P(None, "seq", "tp"),
        ),
        out_specs=(
            P(None, "seq", "tp"),
            P(None, "seq", "tp"),
            P(),
            P(),
            P("seq", "tp"),
            P("tp"),
            P("seq", "tp"),
            P("seq", "tp"),
            P("tp"),
            P("tp", "seq"),
            P(),
            P(),
            P(),
            P("seq", "tp"),
            P("tp"),
            P("tp", "seq"),
            P(),
        ),
        check_vma=False,
    )
```

```python
import functools
import math

import jax
import jax.numpy as jnp
from jax import lax
from jax.experimental import pallas as pl
from jax.experimental.pallas import tpu as pltpu
from jax.sharding import PartitionSpec as P

HEAD_DIM = 64
BLK = 64
GLOBAL = 2
SLOTS = 8
WIDE = 2 * HEAD_DIM
CHUNKS = 4
ROUNDS = 2
NEG = -1e30
NT = (((1,), (1,)), ((), ()))
TN = (((0,), (0,)), ((), ()))
MESH = pl.DeviceIdType.MESH
F32, BF16 = jnp.float32, jnp.bfloat16


def split_by(value, count):
    if count & (count - 1) == 0:
        return value >> (count.bit_length() - 1), value & (count - 1)
    return value // count, value % count


def remote(src, dst, send_sem, recv_sem, device):
    return pltpu.make_async_remote_copy(
        src_ref=src, dst_ref=dst, send_sem=send_sem, recv_sem=recv_sem,
        device_id=device, device_id_type=MESH,
    )


def greet(peers):
    barrier = pltpu.get_barrier_semaphore()
    for peer in peers:
        pl.semaphore_signal(barrier, inc=1, device_id=peer, device_id_type=MESH)
    pl.semaphore_wait(barrier, len(peers))


def add_up(*terms):
    total = terms[0].astype(F32)
    for term in terms[1:]:
        total = total + term.astype(F32)
    return total


def swap_halves(value):
    return pltpu.roll(value, HEAD_DIM, 1)


def low_half(value):
    return lax.broadcasted_iota(jnp.int32, value.shape, 1) < HEAD_DIM


def mix_pair(left, right):
    low = low_half(left)
    return (
        jnp.where(low, left, swap_halves(right)),
        jnp.where(low, swap_halves(left), right),
    )


def unpack_pair(left, right):
    even, odd = mix_pair(left.astype(F32), right.astype(F32))
    tiles = []
    for start in range(0, left.shape[0], BLK):
        tiles += [even[start : start + BLK], odd[start : start + BLK]]
    return jnp.concatenate(tiles, axis=0).astype(BF16)


def pack_pair(value):
    lefts, rights = [], []
    for start in range(0, value.shape[0], 2 * BLK):
        left, right = mix_pair(value[start : start + BLK], value[start + BLK : start + 2 * BLK])
        lefts.append(left)
        rights.append(right)
    return jnp.concatenate(lefts, axis=0).astype(BF16), jnp.concatenate(rights, axis=0).astype(BF16)


def dma(*shape):
    return pltpu.SemaphoreType.DMA(tuple(max(size, 1) for size in shape))


def vmem(*shape, dtype=BF16):
    return pltpu.VMEM(shape, dtype)


IN_VMEM = pl.BlockSpec(memory_space=pltpu.VMEM)
IN_SMEM = pl.BlockSpec(memory_space=pltpu.SMEM)
ANYWHERE = pl.BlockSpec(memory_space=pl.ANY)


class Place:
    def __init__(self, dims):
        self.heads, self.share, self.nseq, self.ntp = dims
        self.seq, self.tp = lax.axis_index("seq"), lax.axis_index("tp")
        self.head, self.part = self.seq // self.share, lax.rem(self.seq, self.share)

    def partner(self, step):
        other = lax.rem(self.part + step, self.share)
        return other, (self.head * self.share + other, self.tp)

    def across(self, step):
        other = lax.rem(self.head + step, self.heads)
        return other, (other * self.share + self.part, self.tp)

    def along(self, step):
        other = lax.rem(self.tp + step, self.ntp)
        return other, (self.seq, other)

    def apart(self, step):
        far, near = step // self.heads, step % self.heads
        head = lax.rem(self.head + near, self.heads)
        tp = lax.rem(self.tp + far, self.ntp)
        return head, tp, (head * self.share + self.part, tp)


def fill_table(place, docs_ref, pads_ref, picks_ref, table_ref, nrows):
    nblocks = table_ref.shape[1]
    block = lax.broadcasted_iota(jnp.int32, (1, nblocks), 1)

    def doc_step(doc, state):
        start, first, last, pad = state
        stop = start + docs_ref[doc]
        inside = (block >= start) & (block < stop)
        first = jnp.where(inside, start, first)
        last = jnp.where(inside, stop - 1, last)
        pad = jnp.where(inside, pads_ref[doc], pad)
        return stop, first, last, pad

    zero = jnp.zeros((1, nblocks), jnp.int32)
    _, first, last, pad = lax.fori_loop(
        0, docs_ref.shape[0], doc_step, (jnp.int32(0), zero, zero, zero)
    )
    length = last - first + 1
    picks = []
    for index in range(picks_ref.shape[0]):
        pick = picks_ref[index : index + 1, :]
        whole = (pick.astype(F32) / length.astype(F32)).astype(jnp.int32)
        left = pick - whole * length
        left = jnp.where(left < 0, left + length, left)
        left = jnp.where(left >= length, left - length, left)
        picks.append(first + left)
    glob = block - first < GLOBAL
    is_long = glob & (last - first >= SLOTS)
    never = block < 0
    p0, p1, p2 = picks
    fresh = lambda pick: (pick >= first + GLOBAL) & ((pick > block + 1) | (pick < block - 1))
    near = [
        (block - 1, ~never),
        (block, ~never),
        (block + 1, block < last),
        (first, ~never),
        (first + 1, block - 1 > first + 1),
        (p0, fresh(p0)),
        (p1, fresh(p1) & (p1 != p0)),
        (p2, fresh(p2) & (p2 != p0) & (p2 != p1)),
    ]
    for index, (other, use) in enumerate(near):
        whole = first + index
        use = (glob & (whole <= last) & ~is_long) | (~glob & use)
        other = jnp.where(use, jnp.where(glob, whole, other), block)
        live = jnp.where(use, jnp.where(other == last, BLK - pad, BLK), 0)
        table_ref[index : index + 1, :] = row_of(place, other, nrows) * WIDE + live
    table_ref[SLOTS : SLOTS + 1, :] = first
    table_ref[SLOTS + 1 : SLOTS + 2, :] = last
    table_ref[SLOTS + 2 : SLOTS + 3, :] = pad


def head_kernel(
    dims, nrows, docs_ref, pads_ref, picks_ref, x_ref, gain_ref, shift_ref,
    wq_ref, bq_ref, wk_ref, wv_ref, bv_ref,
    q_out, kv_out, h1_out, xs_out, xt_out, stat_out, table_out,
    xs, h1, qbuf, kvbuf, right_s, right_r, left_s, left_r, q_s, q_r, kv_s, kv_r, on_s, on_r, local,
):
    place = Place(dims)
    heads, share, nseq, ntp = dims
    head, part, seq, tp = place.head, place.part, place.seq, place.tp
    rows, width = x_ref.shape
    features = width * ntp
    chunk_rows = rows // CHUNKS

    def chunk_of(chunk):
        return pl.ds(chunk * chunk_rows, chunk_rows)

    def rightward(chunk, index):
        spot = xs.at[index, chunk_of(chunk)]
        return remote(
            spot, spot, right_s.at[chunk, index], right_r.at[chunk, index], (seq, tp + 1)
        )

    def leftward(chunk, index):
        spot = xs.at[index, chunk_of(chunk)]
        return remote(spot, spot, left_s.at[chunk, index], left_r.at[chunk, index], (seq, tp - 1))

    def q_copy(chunk, step):
        other, device = place.across(step)
        return remote(
            qbuf.at[other, chunk_of(chunk)], q_out.at[head, chunk_of(chunk)],
            q_s.at[chunk, step - 1], q_r.at[chunk, step - 1], device,
        )

    def kv_copy(chunk, step):
        other, device = place.across(step)
        return remote(
            kvbuf.at[other, chunk_of(chunk)], kv_out.at[part, head, chunk_of(chunk)],
            kv_s.at[chunk, step - 1], kv_r.at[chunk, step - 1], device,
        )

    def kv_on(chunk, hop, step):
        owner = lax.rem(head + heads - hop, heads)
        spot = kv_out.at[part, owner, chunk_of(chunk)]
        source = kvbuf.at[head, chunk_of(chunk)] if hop == 0 else spot
        return remote(
            source, spot, on_s.at[chunk, hop, step - 1], on_r.at[chunk, hop, step - 1],
            place.partner(step)[1],
        )

    def own_send(chunk):
        @pl.when(tp < ntp - 1)
        def _():
            rightward(chunk, tp).start()

        @pl.when(tp > 0)
        def _():
            leftward(chunk, tp).start()

    def pass_on(chunk):
        for hop in range(1, ntp):
            below, above = tp - hop, tp + hop

            @pl.when(below >= 0)
            def _():
                rightward(chunk, below).wait_recv()

                @pl.when(tp < ntp - 1)
                def _():
                    rightward(chunk, below).start()

            @pl.when(above < ntp)
            def _():
                leftward(chunk, above).wait_recv()

                @pl.when(tp > 0)
                def _():
                    leftward(chunk, above).start()

    def compute(chunk):
        here = chunk_of(chunk)
        x = jnp.concatenate([xs[index, here] for index in range(ntp)], axis=1).astype(F32)
        mean = jnp.sum(x, axis=1, keepdims=True) * (1.0 / features)
        centered = x - mean
        spread = jnp.sum(centered * centered, axis=1, keepdims=True) * (1.0 / features)
        scale = lax.rsqrt(spread + 1e-05)
        normed = (centered * scale * gain_ref[...] + shift_ref[...]).astype(BF16)
        h1[here] = normed
        stat_out[here, 0:1] = mean
        stat_out[here, 1:2] = scale
        q = (jnp.dot(normed, wq_ref[...], preferred_element_type=F32) + bq_ref[...]) * 0.125
        k = jnp.dot(normed, wk_ref[...], preferred_element_type=F32)
        v = jnp.dot(normed, wv_ref[...], preferred_element_type=F32) + bv_ref[...]
        for index in range(0, heads, 2):
            lanes = slice(index * HEAD_DIM, (index + 2) * HEAD_DIM)
            kv = mix_pair(k[:, lanes], v[:, lanes])
            low = low_half(q[:, lanes])
            qs = (q[:, lanes], swap_halves(q[:, lanes]))
            for off in range(2):
                kvbuf[index + off, here] = kv[off].astype(BF16)
                qbuf[index + off, here] = jnp.where(low, qs[off], 0.0).astype(BF16)

    def hand_on(chunk):
        for hop in range(heads):
            if hop:
                kv_copy(chunk, hop).wait_recv()
            for step in range(1, share):
                kv_on(chunk, hop, step).start()

    xs[tp] = x_ref[...]
    greet(
        [place.partner(step)[1] for step in range(1, share)]
        + [place.across(step)[1] for step in range(1, heads)]
        + [place.along(step)[1] for step in range(1, ntp)]
    )
    own_send(0)
    own_send(1)
    fill_table(place, docs_ref, pads_ref, picks_ref, table_out, nrows)
    for chunk in range(CHUNKS):
        if 0 < chunk < CHUNKS - 1:
            own_send(chunk + 1)
        pass_on(chunk)
        compute(chunk)
        for step in range(1, heads):
            kv_copy(chunk, step).start()
        for step in range(1, heads):
            q_copy(chunk, step).start()
        if chunk > 0:
            hand_on(chunk - 1)
    pairs = [
        (qbuf.at[head], q_out.at[head]),
        (kvbuf.at[head], kv_out.at[part, head]),
        (h1, h1_out),
        (xs, xs_out),
    ]
    copies = [
        pltpu.make_async_copy(source, target, local.at[index])
        for index, (source, target) in enumerate(pairs)
    ]
    for copy in copies:
        copy.start()
    mine = pl.ds(pl.multiple_of(tp * (rows // ntp), rows // ntp), rows // ntp)
    xt_out[...] = xs[:, mine]
    hand_on(CHUNKS - 1)
    for copy in copies:
        copy.wait()
    for chunk in range(CHUNKS):
        for step in range(1, heads):
            q_copy(chunk, step).wait_recv()
        for hop in range(heads):
            for step in range(1, share):
                kv_on(chunk, hop, step).wait_recv()
    for chunk in range(CHUNKS):
        for step in range(1, heads):
            q_copy(chunk, step).wait_send()
            kv_copy(chunk, step).wait_send()
        for hop in range(heads):
            for step in range(1, share):
                kv_on(chunk, hop, step).wait_send()
        for index in range(ntp):
            @pl.when((tp >= index) & (tp < ntp - 1))
            def _():
                rightward(chunk, index).wait_send()

            @pl.when((tp <= index) & (tp > 0))
            def _():
                leftward(chunk, index).wait_send()


def run_head(dims, nrows, docs, pads, picks, x, *params):
    heads, share, nseq, ntp = dims
    rows, width = x.shape
    nblocks = picks.shape[1]
    sds = jax.ShapeDtypeStruct
    outs = [
        sds((heads, rows, WIDE), BF16),
        sds((share, heads, rows, WIDE), BF16),
        sds((rows, width * ntp), BF16),
        sds((ntp, rows, width), BF16),
        sds((ntp, rows // ntp, width), BF16),
        sds((rows, 2), F32),
        sds((16, nblocks), jnp.int32),
    ]
    scratch = [
        vmem(ntp, rows, width),
        vmem(rows, width * ntp),
        vmem(heads, rows, WIDE),
        vmem(heads, rows, WIDE),
    ]
    sems = (
        [dma(CHUNKS, ntp)] * 4 + [dma(CHUNKS, heads - 1)] * 4
        + [dma(CHUNKS, heads, share - 1)] * 2 + [dma(4)]
    )
    return pl.pallas_call(
        functools.partial(head_kernel, dims, nrows),
        out_shape=outs,
        in_specs=[IN_SMEM, IN_SMEM] + [IN_VMEM] * (2 + len(params)),
        out_specs=[ANYWHERE] * 4 + [IN_VMEM] * 3,
        scratch_shapes=scratch + sems,
        name="head",
        compiler_params=pltpu.CompilerParams(
            collective_id=1, has_side_effects=True, vmem_limit_bytes=60 << 20
        ),
    )(docs, pads, picks, x, *params)


def block_of(place, query, nrows):
    source, row = split_by(query, nrows)
    return row * place.nseq + source * place.share + place.part


def row_of(place, block, nrows):
    row, holder = split_by(block, place.nseq)
    head, part = split_by(holder, place.share)
    return ((part * place.heads + head) * nrows + row) * BLK


def near_slots(table_ref, block):
    entries = [table_ref[index, block] for index in range(SLOTS)]
    slots = [pl.multiple_of(entry >> 7, BLK) for entry in entries]
    return slots, [entry & (WIDE - 1) for entry in entries]


def long_slots(place, table_ref, block, chunk, nrows):
    first, last = table_ref[SLOTS, block], table_ref[SLOTS + 1, block]
    final = BLK - table_ref[SLOTS + 2, block]
    slots, lives = [], []
    for index in range(SLOTS):
        wanted = first + chunk * SLOTS + index
        slots.append(pl.multiple_of(row_of(place, jnp.minimum(wanted, last), nrows), BLK))
        lives.append(jnp.where(wanted < last, BLK, jnp.where(wanted == last, final, 0)))
    return slots, lives


def for_long(place, table_ref, nquery, nrows, body):
    def step(query, carry):
        block = block_of(place, query, nrows)
        first, last = table_ref[SLOTS, block], table_ref[SLOTS + 1, block]

        @pl.when((block - first < GLOBAL) & (last - first >= SLOTS))
        def _():
            body(query, block, (last - first + SLOTS) >> 3)

        return carry

    lax.fori_loop(0, nquery, step, 0)


def bias_row(lives):
    lane = lax.broadcasted_iota(jnp.int32, (1, WIDE), 1)
    parts = []
    for index in range(0, SLOTS, 2):
        bound = jnp.where(lane < BLK, lives[index], lives[index + 1] + BLK)
        parts.append(jnp.where(lane < bound, 0.0, NEG))
    return jnp.concatenate(parts, axis=1)


def take(ref, slots):
    return jnp.concatenate([ref[pl.ds(slot, BLK), :] for slot in slots], axis=0)


def forward_kernel(dims, nrows, unroll, table_ref, q_ref, kv_ref, out_ref, res_ref):
    place = Place(dims)
    nquery = q_ref.shape[0] // BLK
    upper = lax.broadcasted_iota(jnp.int32, (BLK, WIDE), 1) >= HEAD_DIM

    def finish(query, top, total, accum):
        value = accum / total
        res_ref[pl.ds(query * BLK, BLK), :] = jnp.where(upper, value, top + jnp.log(total))
        return value

    def scores_of(query, slots, lives):
        kv = take(kv_ref, slots)
        scores = lax.dot_general(
            q_ref[pl.ds(query * BLK, BLK), :], kv, NT, preferred_element_type=F32
        )
        return kv, scores + bias_row(lives)

    def near_one(query):
        kv, scores = scores_of(query, *near_slots(table_ref, block_of(place, query, nrows)))
        top = jnp.max(scores, axis=1, keepdims=True)
        weights = jnp.exp(scores - top)
        total = jnp.sum(weights, axis=1, keepdims=True)
        accum = jnp.dot(weights.astype(BF16), kv, preferred_element_type=F32)
        return finish(query, top, total, accum)

    def near_step(index, carry):
        for offset in range(unroll):
            pair = index * unroll + offset
            even, odd = near_one(2 * pair), near_one(2 * pair + 1)
            out_ref[pl.ds(pair * BLK, BLK), :] = jnp.where(upper, odd, swap_halves(even)).astype(BF16)
        return carry

    lax.fori_loop(0, nquery // (2 * unroll), near_step, 0)

    def long_body(query, block, chunks):
        def chunk_step(chunk, state):
            top, total, accum = state
            kv, scores = scores_of(query, *long_slots(place, table_ref, block, chunk, nrows))
            new_top = jnp.maximum(top, jnp.max(scores, axis=1, keepdims=True))
            weights = jnp.exp(scores - new_top)
            decay = jnp.exp(top - new_top)
            total = total * decay + jnp.sum(weights, axis=1, keepdims=True)
            accum = accum * decay + jnp.dot(weights.astype(BF16), kv, preferred_element_type=F32)
            return new_top, total, accum

        start = (
            jnp.full((BLK, 1), NEG, F32),
            jnp.zeros((BLK, 1), F32),
            jnp.zeros((BLK, WIDE), F32),
        )
        value = finish(query, *lax.fori_loop(0, chunks, chunk_step, start))
        spot = pl.ds(pl.multiple_of((query >> 1) * BLK, BLK), BLK)
        is_odd = (query & 1) == 1
        moved = jnp.where(is_odd, value, swap_halves(value))
        out_ref[spot, :] = jnp.where(upper == is_odd, moved, out_ref[spot, :].astype(F32)).astype(BF16)

    for_long(place, table_ref, nquery, nrows, long_body)


def backward_kernel(
    dims, nrows, unroll, table_ref, q_ref, do_ref, res_ref, kv_ref, dq_ref, dkv_ref, sum_ref
):
    place = Place(dims)
    nquery = q_ref.shape[0] // BLK
    upper = lax.broadcasted_iota(jnp.int32, (BLK, WIDE), 1) >= HEAD_DIM
    sum_ref[...] = jnp.zeros_like(sum_ref)

    def load(query, packed, is_odd):
        moved = jnp.where(is_odd, packed, swap_halves(packed))
        grad = jnp.where(upper, moved, 0.0)
        rows = pl.ds(query * BLK, BLK)
        both = jnp.concatenate([q_ref[rows, :], grad.astype(BF16)], axis=0)
        res = res_ref[rows, :]
        delta = jnp.sum(res * grad, axis=1, keepdims=True)
        return both, res[:, :1], delta

    def terms(both, log_total, delta, slots, lives):
        kv = take(kv_ref, slots)
        pair = lax.dot_general(both, kv, NT, preferred_element_type=F32)
        probs = jnp.exp(pair[:BLK] + bias_row(lives) - log_total)
        grad_scores = (probs * (pair[BLK:] - delta)).astype(BF16)
        weights = jnp.concatenate([grad_scores, probs.astype(BF16)], axis=0)
        dkv = lax.dot_general(weights, both, TN, preferred_element_type=F32)
        dq = jnp.dot(grad_scores, kv, preferred_element_type=F32)
        return dq, dkv

    def scatter(slots, dkv):
        for index, slot in enumerate(slots):
            sum_ref[pl.ds(slot, BLK), :] += dkv[index * BLK : (index + 1) * BLK]

    def near_step(index, carry):
        done = []
        for offset in range(unroll):
            pair = index * unroll + offset
            packed = do_ref[pl.ds(pair * BLK, BLK), :].astype(F32)
            grads = []
            for is_odd in (False, True):
                query = 2 * pair + int(is_odd)
                slots, lives = near_slots(table_ref, block_of(place, query, nrows))
                dq, dkv = terms(*load(query, packed, is_odd), slots, lives)
                grads.append(dq)
                done.append((slots, dkv))
            dq_ref[pl.ds(pair * BLK, BLK), :] = jnp.where(
                upper, swap_halves(grads[1]), grads[0]
            ).astype(BF16)
        for slots, dkv in done:
            scatter(slots, dkv)
        return carry

    lax.fori_loop(0, nquery // (2 * unroll), near_step, 0)

    def long_body(query, block, chunks):
        is_odd = (query & 1) == 1
        spot = pl.ds(pl.multiple_of((query >> 1) * BLK, BLK), BLK)
        loaded = load(query, do_ref[spot, :].astype(F32), is_odd)

        def chunk_step(chunk, total):
            slots, lives = long_slots(place, table_ref, block, chunk, nrows)
            dq, dkv = terms(*loaded, slots, lives)
            scatter(slots, dkv)
            return total + dq

        total = lax.fori_loop(0, chunks, chunk_step, jnp.zeros((BLK, WIDE), F32))
        moved = jnp.where(is_odd, swap_halves(total), total)
        dq_ref[spot, :] = jnp.where(upper == is_odd, moved, dq_ref[spot, :].astype(F32)).astype(BF16)

    for_long(place, table_ref, nquery, nrows, long_body)
    dkv_ref[...] = sum_ref[...].astype(BF16)


def local_call(kernel, name, out_shape, nvmem, scratch=()):
    return pl.pallas_call(
        kernel,
        out_shape=out_shape,
        in_specs=[IN_SMEM] + [IN_VMEM] * nvmem,
        out_specs=jax.tree.map(lambda _: IN_VMEM, out_shape),
        scratch_shapes=list(scratch),
        name=name,
        cost_estimate=pl.CostEstimate(flops=30 << 30, bytes_accessed=8 << 20, transcendentals=0),
        compiler_params=pltpu.CompilerParams(vmem_limit_bytes=56 << 20),
    )


class GradScatter:
    def __init__(self, place, source, bufs, sems):
        self.place, self.source = place, source
        self.land, self.pair, self.far = bufs
        self.send1, self.recv1, self.send2, self.recv2 = sems

    @staticmethod
    def buffers(dims, band, cols):
        heads, share = dims[:2]
        return [
            vmem(max(share - 1, 1), heads, band, cols),
            vmem(heads, band, cols),
            vmem(max(heads - 1, 1), band, cols),
        ]

    @staticmethod
    def semaphores(dims, count):
        return [dma(count, dims[1] - 1)] * 2 + [dma(count, dims[0] - 1)] * 2

    def near(self, step):
        other, device = self.place.partner(step)
        return remote(
            self.source.at[:, other], self.land.at[step - 1],
            self.send1.at[step - 1], self.recv1.at[step - 1], device,
        )

    def across(self, step):
        other, device = self.place.across(step)
        return remote(
            self.pair.at[other], self.far.at[step - 1],
            self.send2.at[step - 1], self.recv2.at[step - 1], device,
        )

    def start_near(self):
        for step in range(1, self.place.share):
            self.near(step).start()

    def start_across(self):
        place = self.place
        for step in range(1, place.share):
            self.near(step).wait_recv()

        def body(head, carry):
            parts = [self.source[head, place.part]]
            parts += [self.land[step, head] for step in range(place.share - 1)]
            self.pair[head] = add_up(*parts).astype(BF16)
            return carry

        lax.fori_loop(0, place.heads, body, 0)
        for step in range(1, place.heads):
            self.across(step).start()

    def result(self):
        heads = self.place.heads
        for step in range(1, heads):
            self.across(step).wait_recv()
        return add_up(self.pair[self.place.head], *[self.far[step] for step in range(heads - 1)])

    def finish(self):
        for step in range(1, self.place.share):
            self.near(step).wait_send()
        for step in range(1, self.place.heads):
            self.across(step).wait_send()


def gelu_pair(value):
    root = math.sqrt(2.0 / math.pi)
    square = value * value
    curve = jnp.tanh(root * value * (1.0 + 0.044715 * square))
    half = 0.5 * (1.0 + curve)
    slope = half + 0.5 * value * (1.0 - curve * curve) * (root * (1.0 + 3 * 0.044715 * square))
    return value * half, slope


def rounds_of(tokens):
    return max(1, min(ROUNDS, tokens // (2 * BLK)))


def middle_kernel(
    dims,
    o_ref, xt_ref, g_ref, wo_ref, ob_ref, gain_ref, shift_ref, wi_ref, ib_ref, wu_ref,
    sum_out, do_out, da_out, mixed_out, vec_out, gi_out, gu_out,
    o_in, x1, xhat, scale, h2, act, dpre, outb, terms, from_left, from_right, do_buf, ib_sum, gi, gu,
    *rest,
):
    place = Place(dims)
    heads, share, nseq, ntp = dims
    head, part, seq, tp = place.head, place.part, place.seq, place.tp
    lands, sems = rest[:6], rest[6:]
    (o_s, o_r, hr_s, hr_r, hl_s, hl_r, tr_s, tr_r, tl_s, tl_r, do_s, do_r,
     g1_s, g1_r, g2_s, g2_r, local) = sems
    rows, width = g_ref.shape[1:]
    features = width * ntp
    tokens = rows // ntp
    rounds = rounds_of(tokens)
    span = tokens // rounds
    places = 2 * ntp - 1
    band = features // heads
    per = features // WIDE

    def packed_rows(index, count=tokens // 2):
        return pl.ds(pl.multiple_of(index * count, count), count)

    def span_of(index):
        return pl.ds(pl.multiple_of(index * span, span), span)

    def o_copy(step):
        to_head, to_tp, device = place.apart(step)
        return remote(
            o_ref.at[to_head, packed_rows(to_tp)], o_in.at[tp * heads + head],
            o_s.at[step], o_r.at[step], device,
        )

    def do_copy(index, step):
        to_head, to_tp, device = place.apart(step)
        count = span // 2
        return remote(
            do_buf.at[to_tp * heads + to_head, packed_rows(index, count)],
            do_out.at[head, packed_rows(tp * rounds + index, count)],
            do_s.at[index, step], do_r.at[index, step], device,
        )

    def h2_copy(index, owner, right):
        spot = h2.at[owner, span_of(index)]
        if right:
            return remote(spot, spot, hr_s.at[index, owner], hr_r.at[index, owner], (seq, tp + 1))
        return remote(spot, spot, hl_s.at[index, owner], hl_r.at[index, owner], (seq, tp - 1))

    def term_copy(index, owner, right):
        here = span_of(index)
        if right:
            return remote(
                terms.at[owner, here], from_left.at[owner, here],
                tr_s.at[index, owner], tr_r.at[index, owner], (seq, tp + 1),
            )
        return remote(
            terms.at[owner, here], from_right.at[owner, here],
            tl_s.at[index, owner], tl_r.at[index, owner], (seq, tp - 1),
        )

    scatters = [
        GradScatter(
            place, source, lands[3 * k : 3 * k + 3], (g1_s.at[k], g1_r.at[k], g2_s.at[k], g2_r.at[k])
        )
        for k, source in enumerate((gi, gu))
    ]

    greet(
        [place.partner(step)[1] for step in range(1, share)]
        + [place.apart(step)[2] for step in range(1, heads * ntp)]
    )
    for step in range(heads * ntp - 1, 0, -1):
        o_copy(step).start()
    o_in[tp * heads + head] = o_ref[head, packed_rows(tp)]
    ib_sum[...] = jnp.zeros_like(ib_sum)
    for step in range(1, heads * ntp):
        o_copy(step).wait_recv()

    for index in range(rounds):
        here = slice(index * span, (index + 1) * span)
        half = slice(index * span // 2, (index + 1) * span // 2)
        mixed = jnp.concatenate(
            [unpack_pair(o_in[i, half], o_in[i + 1, half]) for i in range(0, heads * ntp, 2)], axis=1
        )
        mixed_out[here] = mixed
        base = jnp.concatenate([xt_ref[i, here] for i in range(ntp)], axis=1).astype(F32)
        value = base + ob_ref[...] + jnp.dot(mixed, wo_ref[...], preferred_element_type=F32)
        x1[here] = value
        centered = value - jnp.sum(value, axis=1, keepdims=True) * (1.0 / features)
        spread = jnp.sum(centered * centered, axis=1, keepdims=True) * (1.0 / features)
        inverse = lax.rsqrt(spread + 1e-05)
        normed = centered * inverse
        xhat[here] = normed
        scale[here] = jnp.broadcast_to(inverse, (span, WIDE))
        h2[tp, here] = (normed * gain_ref[...] + shift_ref[...]).astype(BF16)

        @pl.when(tp < ntp - 1)
        def _():
            h2_copy(index, tp, True).start()

        @pl.when(tp > 0)
        def _():
            h2_copy(index, tp, False).start()

    def spot_of(position):
        hop = (position + 1) // 2
        owner = tp + jnp.where(position % 2 == 1, -hop, hop)
        return owner, (owner >= 0) & (owner < ntp)

    def feed(index, owner):
        @pl.when(owner < tp)
        def _():
            h2_copy(index, owner, True).wait_recv()

            @pl.when(tp < ntp - 1)
            def _():
                h2_copy(index, owner, True).start()

        @pl.when(owner > tp)
        def _():
            h2_copy(index, owner, False).wait_recv()

            @pl.when(tp > 0)
            def _():
                h2_copy(index, owner, False).start()

        here = span_of(index)
        wide = span_of(owner * rounds + index)
        pre = jnp.dot(h2[owner, here], wi_ref[...], preferred_element_type=F32) + ib_ref[...]
        value, slope = gelu_pair(pre)
        value = value.astype(BF16)
        act[wide] = value
        grad = jnp.concatenate([g_ref[i, wide] for i in range(ntp)], axis=1)
        back = lax.dot_general(grad, wu_ref[...], NT, preferred_element_type=F32) * slope
        back = back.astype(BF16)
        dpre[wide] = back
        ib_sum[0:1, :] += jnp.sum(back.astype(F32), axis=0, keepdims=True)
        terms[owner, here] = lax.dot_general(
            back, wi_ref[...], NT, preferred_element_type=F32
        ).astype(BF16)

        @pl.when((owner > tp) & (tp == 0))
        def _():
            term_copy(index, owner, True).start()

        @pl.when((owner < tp) & (tp == ntp - 1))
        def _():
            term_copy(index, owner, False).start()

        out = jnp.dot(value, wu_ref[...], preferred_element_type=F32)
        out = out + jnp.where(owner == tp, x1[here], 0.0)
        for i in range(ntp):
            outb[i, wide] = out[:, i * width : (i + 1) * width].astype(BF16)

    def relay(index, step):
        here = span_of(index)
        owner = step

        @pl.when((owner > tp) & (tp > 0))
        def _():
            term_copy(index, owner, True).wait_recv()
            terms[owner, here] = add_up(terms[owner, here], from_left[owner, here]).astype(BF16)
            term_copy(index, owner, True).start()

        other = ntp - 1 - step

        @pl.when((other < tp) & (tp < ntp - 1))
        def _():
            term_copy(index, other, False).wait_recv()
            terms[other, here] = add_up(terms[other, here], from_right[other, here]).astype(BF16)
            term_copy(index, other, False).start()

    def feed_step(count, carry):
        index, position = count // places, count % places
        owner, inside = spot_of(position)

        @pl.when(inside)
        def _():
            feed(index, owner)

        @pl.when((index > 0) & (position > 0) & (position % 2 == 0))
        def _():
            relay(index - 1, position // 2)

        return carry

    lax.fori_loop(0, rounds * places, feed_step, 0)
    save = pltpu.make_async_copy(outb, sum_out, local.at[0])
    save.start()

    def inner_grad(index):
        left = h2[:, :, index * band : (index + 1) * band].reshape(rows, band)
        value = lax.dot_general(left, dpre[...], TN, preferred_element_type=F32)
        gi[index] = value.astype(BF16).reshape(gi.shape[1:])

    def outer_grad(index):
        many = ntp // heads
        left = jnp.concatenate([g_ref[i] for i in range(index * many, (index + 1) * many)], axis=1)
        value = lax.dot_general(left, act[...], TN, preferred_element_type=F32)
        gu[index] = value.astype(BF16).reshape(gu.shape[1:])

    work = [functools.partial(inner_grad, index) for index in range(heads)]
    work += [functools.partial(outer_grad, index) for index in range(heads)]
    share_out = -(-len(work) // (ntp - 1))
    for position in range(ntp - 1):
        relay(rounds - 1, position + 1)
        for item in work[position * share_out : (position + 1) * share_out]:
            item()
        if (position + 1) * share_out >= heads > position * share_out:
            scatters[0].start_near()
        if (position + 1) * share_out >= 2 * heads > position * share_out:
            scatters[1].start_near()

    for index in range(rounds):
        here = slice(index * span, (index + 1) * span)
        half = slice(index * span // 2, (index + 1) * span // 2)
        wide = span_of(tp * rounds + index)

        @pl.when(tp > 0)
        def _():
            term_copy(index, tp, True).wait_recv()

        @pl.when(tp < ntp - 1)
        def _():
            term_copy(index, tp, False).wait_recv()

        grad = terms[tp, here].astype(F32)
        grad = grad + jnp.where(tp > 0, from_left[tp, here].astype(F32), 0.0)
        grad = grad + jnp.where(tp < ntp - 1, from_right[tp, here].astype(F32), 0.0)
        hat = xhat[here]
        inner = grad * gain_ref[...]
        mean0 = jnp.sum(inner, axis=1, keepdims=True) * (1.0 / features)
        mean1 = jnp.sum(inner * hat, axis=1, keepdims=True) * (1.0 / features)
        tail = scale[here, 0:1] * (inner - mean0 - hat * mean1)
        cot = jnp.concatenate([g_ref[i, wide] for i in range(ntp)], axis=1).astype(F32)
        branch = (cot + tail).astype(BF16)
        da_out[here] = branch
        do = lax.dot_general(branch, wo_ref[...], NT, preferred_element_type=F32)
        for i in range(0, heads * ntp, 2):
            pair = pack_pair(do[:, i * HEAD_DIM : (i + 2) * HEAD_DIM])
            do_buf[i, half] = pair[0]
            do_buf[i + 1, half] = pair[1]
        for step in range(heads * ntp - 1, 0, -1):
            do_copy(index, step).start()
        sums = (
            jnp.sum(branch.astype(F32), axis=0, keepdims=True),
            jnp.sum(grad * hat, axis=0, keepdims=True),
            jnp.sum(grad, axis=0, keepdims=True),
        )
        for kind, value in enumerate(sums):
            for sub in range(per):
                row = slice(kind * per + sub, kind * per + sub + 1)
                piece = value[:, sub * WIDE : (sub + 1) * WIDE]
                if index == 0:
                    vec_out[row, :] = piece
                else:
                    vec_out[row, :] += piece
    own = pltpu.make_async_copy(
        do_buf.at[tp * heads + head], do_out.at[head, packed_rows(tp)], local.at[1]
    )
    own.start()
    for scatter in scatters:
        scatter.start_across()
    cot = jnp.sum(g_ref[tp].astype(F32), axis=0, keepdims=True)
    for sub in range(per):
        owner, lane = divmod(sub * WIDE, width)
        vec_out[3 * per + sub : 3 * per + sub + 1, :] = jnp.where(
            tp == owner, cot[:, lane : lane + WIDE], 0.0
        )
    for sub in range(ib_sum.shape[1] // WIDE):
        row = 4 * per + sub
        vec_out[row : row + 1, :] = ib_sum[0:1, sub * WIDE : (sub + 1) * WIDE]
    gi_out[...] = scatters[0].result()
    gu_out[...] = scatters[1].result()
    save.wait()
    own.wait()
    for step in range(1, heads * ntp):
        for index in range(rounds):
            do_copy(index, step).wait_recv()
    for step in range(1, heads * ntp):
        o_copy(step).wait_send()
        for index in range(rounds):
            do_copy(index, step).wait_send()
    for index in range(rounds):
        for owner in range(ntp):
            @pl.when((tp >= owner) & (tp < ntp - 1))
            def _():
                h2_copy(index, owner, True).wait_send()

            @pl.when((tp <= owner) & (tp > 0))
            def _():
                h2_copy(index, owner, False).wait_send()

            @pl.when(tp < owner)
            def _():
                term_copy(index, owner, True).wait_send()

            @pl.when(tp > owner)
            def _():
                term_copy(index, owner, False).wait_send()

    for scatter in scatters:
        scatter.finish()


def run_middle(dims, o, xt, g, wo, ob, gain, shift, wi, ib, wu):
    heads, share, nseq, ntp = dims
    _, rows, width = g.shape
    features, hidden = width * ntp, wi.shape[1]
    tokens, band = rows // ntp, features // nseq
    per = features // WIDE
    rounds = rounds_of(tokens)
    sds = jax.ShapeDtypeStruct
    outs = [
        sds((ntp, rows, width), BF16),
        sds((heads, rows // 2, WIDE), BF16),
        sds((tokens, features), BF16),
        sds((tokens, features), BF16),
        sds((4 * per + hidden // WIDE, WIDE), F32),
        sds((band, hidden), F32),
        sds((band, hidden), F32),
    ]
    count = heads * ntp
    scratch = [
        vmem(count, tokens // 2, WIDE),
        vmem(tokens, features, dtype=F32),
        vmem(tokens, features, dtype=F32),
        vmem(tokens, WIDE, dtype=F32),
        vmem(ntp, tokens, features),
        vmem(rows, hidden),
        vmem(rows, hidden),
        vmem(ntp, rows, width),
        vmem(ntp, tokens, features),
        vmem(ntp, tokens, features),
        vmem(ntp, tokens, features),
        vmem(count, tokens // 2, WIDE),
        vmem(8, hidden, dtype=F32),
        vmem(heads, share, band, hidden),
        vmem(heads, share, band, hidden),
        *GradScatter.buffers(dims, band, hidden),
        *GradScatter.buffers(dims, band, hidden),
    ]
    sems = (
        [dma(count)] * 2 + [dma(rounds, ntp)] * 8 + [dma(rounds, count)] * 2
        + GradScatter.semaphores(dims, 2) + [dma(2)]
    )
    return pl.pallas_call(
        functools.partial(middle_kernel, dims),
        out_shape=outs,
        in_specs=[IN_VMEM] * 10,
        out_specs=[ANYWHERE] * 2 + [IN_VMEM] * 5,
        scratch_shapes=scratch + sems,
        name="middle",
        compiler_params=pltpu.CompilerParams(
            collective_id=2, has_side_effects=True, vmem_limit_bytes=63 << 20
        ),
    )(o, xt, g, wo, ob, gain, shift, wi, ib, wu)


def tail_kernel(
    dims,
    dq_ref, dkv_ref, h1_ref, x_ref, stat_ref, gain_ref, wq_ref, wk_ref, wv_ref,
    da_ref, mixed_ref, vec_ref,
    gx_ref, ow_ref, oq_ref, vout_ref,
    dq_in, dkv_in, dkv_land, dkv_sum, all3, da_in, pbuf, from_left, from_right,
    sums, sums_land, vbuf, vec_land, vsum, vec_far, gw, g3, wbuf, wfar,
    *rest,
):
    place = Place(dims)
    heads, share, nseq, ntp = dims
    head, part, seq, tp = place.head, place.part, place.seq, place.tp
    lands, sems = rest[:6], rest[6:]
    (dq_s, dq_r, kv1_s, kv1_r, kv2_s, kv2_r, right_s, right_r, left_s, left_r,
     da_s, da_r, st_s, st_r, v1_s, v1_r, v2_s, v2_r, w_s, w_r, g1_s, g1_r, g2_s, g2_r) = sems
    rows, features = h1_ref.shape
    width = features // ntp
    tokens = rows // ntp
    local_width = wq_ref.shape[1]
    chunk_rows = rows // CHUNKS
    band = features // heads
    per = features // WIDE

    def chunk_of(chunk):
        return pl.ds(chunk * chunk_rows, chunk_rows)

    def half_of(chunk):
        return pl.ds(chunk * chunk_rows // 2, chunk_rows // 2)

    def columns_of(index):
        return pl.ds(pl.multiple_of(index * width, width), width)

    def dq_copy(chunk, step):
        other, device = place.across(step)
        return remote(
            dq_ref.at[other, half_of(chunk)], dq_in.at[head, half_of(chunk)],
            dq_s.at[chunk, step - 1], dq_r.at[chunk, step - 1], device,
        )

    def dkv_near(step):
        other, device = place.partner(step)
        return remote(
            dkv_ref.at[other], dkv_land.at[step - 1], kv1_s.at[step - 1], kv1_r.at[step - 1], device
        )

    def dkv_copy(chunk, step):
        other, device = place.across(step)
        return remote(
            dkv_sum.at[other, chunk_of(chunk)], dkv_in.at[head, chunk_of(chunk)],
            kv2_s.at[chunk, step - 1], kv2_r.at[chunk, step - 1], device,
        )

    def da_copy(step):
        other, device = place.along(step)
        return remote(
            da_ref.at[:, columns_of(other)], da_in.at[tp], da_s.at[step - 1], da_r.at[step - 1], device
        )

    def rightward(chunk, index):
        return remote(
            pbuf.at[chunk, index], from_left.at[chunk, index],
            right_s.at[chunk, index], right_r.at[chunk, index], (seq, tp + 1),
        )

    def leftward(chunk, index):
        return remote(
            pbuf.at[chunk, index], from_right.at[chunk, index],
            left_s.at[chunk, index], left_r.at[chunk, index], (seq, tp - 1),
        )

    def sums_copy(step):
        return remote(
            sums, sums_land.at[step - 1], st_s.at[step - 1], st_r.at[step - 1], place.along(step)[1]
        )

    def vec_copy(step):
        return remote(
            vbuf, vec_land.at[step - 1], v1_s.at[step - 1], v1_r.at[step - 1],
            (lax.rem(seq + step, nseq), tp),
        )

    def vec_far_copy(step):
        return remote(
            vsum, vec_far.at[step - 1], v2_s.at[step - 1], v2_r.at[step - 1], place.along(step)[1]
        )

    def w_copy(step):
        other, device = place.along(step)
        return remote(wbuf.at[other], wfar.at[step - 1], w_s.at[step - 1], w_r.at[step - 1], device)

    scatters = [
        GradScatter(
            place, source, lands[3 * k : 3 * k + 3], (g1_s.at[k], g1_r.at[k], g2_s.at[k], g2_r.at[k])
        )
        for k, source in enumerate((gw, g3))
    ]

    greet(
        [(lax.rem(seq + step, nseq), tp) for step in range(1, nseq)]
        + [place.along(step)[1] for step in range(1, ntp)]
    )
    for step in range(1, share):
        dkv_near(step).start()
    for chunk in range(CHUNKS):
        for step in range(1, heads):
            dq_copy(chunk, step).start()
    dq_in[head] = dq_ref[head]
    for index in range(heads):
        value = lax.dot_general(
            da_ref[:, index * band : (index + 1) * band], mixed_ref[...], TN, preferred_element_type=F32
        )
        gw[index] = value.astype(BF16).reshape(gw.shape[1:])
    for step in range(1, share):
        dkv_near(step).wait_recv()
    scatters[0].start_near()
    for chunk in range(CHUNKS):
        for target in range(heads):
            where = (target, chunk_of(chunk))
            parts = [dkv_ref[(part,) + where]]
            parts += [dkv_land[(step,) + where] for step in range(share - 1)]
            dkv_sum[where] = add_up(*parts).astype(BF16)
        for step in range(1, heads):
            dkv_copy(chunk, step).start()
    dkv_in[head] = dkv_sum[head]
    vbuf[: 2 * per] = jnp.zeros((2 * per, WIDE), F32)
    vbuf[2 * per : 6 * per] = vec_ref[: 4 * per]
    narrow = 3 * local_width // WIDE
    vbuf[6 * per : 6 * per + narrow] = jnp.zeros((narrow, WIDE), F32)
    vbuf[6 * per + narrow :] = vec_ref[4 * per :]
    scatters[0].start_across()

    gain = gain_ref[...]
    lane = lax.broadcasted_iota(jnp.int32, (chunk_rows, WIDE), 1)

    def partial_step(chunk):
        here, half = chunk_of(chunk), half_of(chunk)
        for step in range(1, heads):
            dq_copy(chunk, step).wait_recv()
            dkv_copy(chunk, step).wait_recv()
        three = [[], [], []]
        for i in range(0, heads, 2):
            three[0].append(unpack_pair(dq_in[i, half], dq_in[i + 1, half]))
            k, v = mix_pair(dkv_in[i, here].astype(F32), dkv_in[i + 1, here].astype(F32))
            three[1].append(k.astype(BF16))
            three[2].append(v.astype(BF16))
        three = [jnp.concatenate(item, axis=1) for item in three]
        grad = 0.125 * lax.dot_general(three[0], wq_ref[...], NT, preferred_element_type=F32)
        grad = grad + lax.dot_general(three[1], wk_ref[...], NT, preferred_element_type=F32)
        grad = grad + lax.dot_general(three[2], wv_ref[...], NT, preferred_element_type=F32)
        row = 6 * per
        for kind, value in enumerate(three):
            all3[here, kind * local_width : (kind + 1) * local_width] = value
            column = jnp.sum(value.astype(F32), axis=0, keepdims=True)
            for start in range(0, local_width, WIDE):
                vbuf[row : row + 1, :] += column[:, start : start + WIDE]
                row += 1
        mean, scale = stat_ref[here, 0:1], stat_ref[here, 1:2]
        sum0 = jnp.zeros((chunk_rows, 1), F32)
        sum1 = jnp.zeros((chunk_rows, 1), F32)
        for index in range(ntp):
            cols = slice(index * width, (index + 1) * width)
            piece = grad[:, cols]
            xhat = (x_ref[index, here].astype(F32) - mean) * scale
            weighted = piece * gain[:, cols]
            sum0 = sum0 + jnp.sum(weighted, axis=1, keepdims=True)
            sum1 = sum1 + jnp.sum(weighted * xhat, axis=1, keepdims=True)
            col0 = jnp.sum(piece * xhat, axis=0, keepdims=True)
            col1 = jnp.sum(piece, axis=0, keepdims=True)
            for sub in range(width // WIDE):
                row = index * (width // WIDE) + sub
                lanes = slice(sub * WIDE, (sub + 1) * WIDE)
                vbuf[row : row + 1, :] += col0[:, lanes]
                vbuf[per + row : per + row + 1, :] += col1[:, lanes]
            pbuf[chunk, index] = piece.astype(BF16)
        both = jnp.where(lane == 0, sum0, jnp.where(lane == 1, sum1, 0.0))
        sums[:, here] = both.T[:8]

    def pass_on(chunk):
        for step in range(ntp - 1):
            far = ntp - 1 - step

            @pl.when(tp < far)
            def _():
                @pl.when(tp > 0)
                def _():
                    rightward(chunk, far).wait_recv()
                    pbuf[chunk, far] = add_up(pbuf[chunk, far], from_left[chunk, far]).astype(BF16)

                rightward(chunk, far).start()

            @pl.when(tp > step)
            def _():
                @pl.when(tp < ntp - 1)
                def _():
                    leftward(chunk, step).wait_recv()
                    pbuf[chunk, step] = add_up(pbuf[chunk, step], from_right[chunk, step]).astype(BF16)

                leftward(chunk, step).start()

    for chunk in range(CHUNKS):
        partial_step(chunk)
        if chunk > 0:
            pass_on(chunk - 1)
    for step in range(1, ntp):
        sums_copy(step).start()
    for step in range(1, nseq):
        vec_copy(step).start()
    for step in range(1, ntp):
        da_copy(step).start()
    da_in[tp] = da_ref[:, columns_of(tp)]

    def grad_step(index, carry):
        left = h1_ref[:, pl.ds(pl.multiple_of(index * band, band), band)]
        value = lax.dot_general(left, all3[...], TN, preferred_element_type=F32)
        g3[index] = value.astype(BF16).reshape(g3.shape[1:])
        return carry

    lax.fori_loop(0, heads, grad_step, 0)
    scatters[1].start_near()
    pass_on(CHUNKS - 1)
    for step in range(1, nseq):
        vec_copy(step).wait_recv()
    total = vbuf[...]
    for step in range(nseq - 1):
        total = total + vec_land[step]
    vsum[...] = total
    for step in range(1, ntp):
        vec_far_copy(step).start()
    scatters[1].start_across()
    value = scatters[0].result().astype(BF16)
    for index in range(ntp):
        wbuf[index] = value[:, index * local_width : (index + 1) * local_width]
    for step in range(1, ntp):
        w_copy(step).start()

    for step in range(1, ntp):
        sums_copy(step).wait_recv()
        da_copy(step).wait_recv()
    my_gain = gain_ref[:, columns_of(tp)]
    da_rows = da_in.shape[1]
    for chunk in range(CHUNKS):
        here = chunk_of(chunk)
        both = sums[:, here]
        for step in range(ntp - 1):
            both = both + sums_land[step, :, here]
        both = jnp.concatenate([both, jnp.zeros((WIDE - 8, chunk_rows), F32)], axis=0).T
        both = both * (1.0 / features)

        @pl.when(tp > 0)
        def _():
            rightward(chunk, tp).wait_recv()

        @pl.when(tp < ntp - 1)
        def _():
            leftward(chunk, tp).wait_recv()

        grad = pbuf[chunk, tp].astype(F32)
        grad = grad + jnp.where(tp > 0, from_left[chunk, tp].astype(F32), 0.0)
        grad = grad + jnp.where(tp < ntp - 1, from_right[chunk, tp].astype(F32), 0.0)
        mean, scale = stat_ref[here, 0:1], stat_ref[here, 1:2]
        xhat = (x_ref[tp, here].astype(F32) - mean) * scale
        inner = grad * my_gain - both[:, 0:1] - xhat * both[:, 1:2]
        many = chunk_rows // da_rows
        branch = da_in[chunk * many : (chunk + 1) * many].reshape(chunk_rows, width)
        gx_ref[here] = branch.astype(F32) + scale * inner
    oq_ref[...] = scatters[1].result()
    for step in range(1, ntp):
        vec_far_copy(step).wait_recv()
        w_copy(step).wait_recv()
    vout_ref[...] = vsum[...]
    for step in range(ntp - 1):
        vout_ref[: 6 * per] += vec_far[step, : 6 * per]
    ow_ref[...] = add_up(wbuf[tp], *[wfar[step] for step in range(ntp - 1)])

    for step in range(1, share):
        dkv_near(step).wait_send()
    for chunk in range(CHUNKS):
        for step in range(1, heads):
            dq_copy(chunk, step).wait_send()
            dkv_copy(chunk, step).wait_send()
        for index in range(ntp):
            @pl.when(tp < index)
            def _():
                rightward(chunk, index).wait_send()

            @pl.when(tp > index)
            def _():
                leftward(chunk, index).wait_send()

    for step in range(1, ntp):
        sums_copy(step).wait_send()
        da_copy(step).wait_send()
        vec_far_copy(step).wait_send()
        w_copy(step).wait_send()
    for step in range(1, nseq):
        vec_copy(step).wait_send()
    for scatter in scatters:
        scatter.finish()


def run_tail(dims, dq, dkv, h1, x_parts, stats, gain, wq, wk, wv, da, mixed, vec):
    heads, share, nseq, ntp = dims
    rows, features = h1.shape
    width, tokens = features // ntp, rows // ntp
    band = features // nseq
    local_width = wq.shape[1]
    per = features // WIDE
    sds = jax.ShapeDtypeStruct
    nvec = vec.shape[0] + 2 * per + 3 * local_width // WIDE
    outs = [
        sds((rows, width), F32),
        sds((band, local_width), F32),
        sds((band, 3 * local_width), F32),
        sds((nvec, WIDE), F32),
    ]
    pieces = (CHUNKS, ntp, rows // CHUNKS, width)
    scratch = [
        vmem(heads, rows // 2, WIDE),
        vmem(heads, rows, WIDE),
        vmem(max(share - 1, 1), heads, rows, WIDE),
        vmem(heads, rows, WIDE),
        vmem(rows, 3 * local_width),
        vmem(ntp, tokens, width),
        vmem(*pieces),
        vmem(*pieces),
        vmem(*pieces),
        vmem(8, rows, dtype=F32),
        vmem(ntp - 1, 8, rows, dtype=F32),
        vmem(nvec, WIDE, dtype=F32),
        vmem(nseq - 1, nvec, WIDE, dtype=F32),
        vmem(nvec, WIDE, dtype=F32),
        vmem(ntp - 1, nvec, WIDE, dtype=F32),
        vmem(heads, share, band, features),
        vmem(heads, share, band, 3 * local_width),
        vmem(ntp, band, local_width),
        vmem(ntp - 1, band, local_width),
        *GradScatter.buffers(dims, band, features),
        *GradScatter.buffers(dims, band, 3 * local_width),
    ]
    sems = (
        [dma(CHUNKS, heads - 1)] * 2 + [dma(share - 1)] * 2 + [dma(CHUNKS, heads - 1)] * 2
        + [dma(CHUNKS, ntp)] * 4 + [dma(ntp - 1)] * 4 + [dma(nseq - 1)] * 2 + [dma(ntp - 1)] * 4
        + GradScatter.semaphores(dims, 2)
    )
    return pl.pallas_call(
        functools.partial(tail_kernel, dims),
        out_shape=outs,
        in_specs=[IN_VMEM] * 12,
        out_specs=[IN_VMEM] * len(outs),
        scratch_shapes=scratch + sems,
        name="tail",
        compiler_params=pltpu.CompilerParams(
            collective_id=3, has_side_effects=True, vmem_limit_bytes=60 << 20
        ),
    )(dq, dkv, h1, x_parts, stats, gain, wq, wk, wv, da, mixed, vec)


def on_device(
    hidden_in,
    norm_gain,
    norm_shift,
    query_weight,
    query_bias,
    key_weight,
    value_weight,
    value_bias,
    output_weight,
    output_bias,
    feed_gain,
    feed_shift,
    inner_weight,
    inner_bias,
    outer_weight,
    outer_bias,
    doc_blocks,
    doc_padding,
    random_picks,
    cotangent,
):
    nrows, block_len, width = hidden_in.shape
    rows = nrows * block_len
    nseq, ntp = lax.axis_size("seq"), lax.axis_size("tp")
    tp = lax.axis_index("tp")
    local_width = query_weight.shape[1]
    heads = local_width // HEAD_DIM
    share = nseq // heads
    dims = (heads, share, nseq, ntp)
    features = width * ntp
    per = features // WIDE
    g_parts = lax.all_gather(cotangent.reshape(rows, width), "tp", axis=0)
    output_full = lax.all_gather(output_weight, "tp", axis=0, tiled=True)
    q, kv, h1, x_parts, x_mine, stats, table = run_head(
        dims, nrows, doc_blocks, doc_padding, random_picks.T, hidden_in.reshape(rows, width),
        norm_gain[None, :], norm_shift[None, :], query_weight, query_bias[None, :],
        key_weight, value_weight, value_bias[None, :],
    )
    q = q.reshape(heads * rows, WIDE)
    kv = kv.reshape(nseq * rows, WIDE)
    sds = jax.ShapeDtypeStruct
    packed, res = local_call(
        functools.partial(forward_kernel, dims, nrows, 1),
        "attention_forward",
        (sds((heads * rows // 2, WIDE), BF16), sds((heads * rows, WIDE), F32)),
        2,
    )(table, q, kv)
    out_sum, do, da, mixed, vec, inner_part, outer_part = run_middle(
        dims, packed.reshape(heads, rows // 2, WIDE), x_mine, g_parts, output_full,
        output_bias[None, :], feed_gain[None, :], feed_shift[None, :],
        inner_weight, inner_bias[None, :], outer_weight,
    )
    result = lax.psum_scatter(out_sum, "tp", scatter_dimension=0)
    dq, dkv = local_call(
        functools.partial(backward_kernel, dims, nrows, 1),
        "attention_backward",
        (sds((heads * rows // 2, WIDE), BF16), sds((nseq * rows, WIDE), BF16)),
        4,
        [pltpu.VMEM((nseq * rows, WIDE), F32)],
    )(table, q, do.reshape(heads * rows // 2, WIDE), res, kv)
    grad_x, output_part, qkv_part, vectors = run_tail(
        dims, dq.reshape(heads, rows // 2, WIDE), dkv.reshape(share, heads, rows, WIDE), h1, x_parts,
        stats, norm_gain[None, :], query_weight, key_weight, value_weight, da, mixed, vec,
    )
    my_bias = lax.dynamic_slice_in_dim(outer_bias, tp * width, width, 0)
    layer_out = (result.astype(F32) + my_bias).astype(BF16).reshape(hidden_in.shape)
    wide = vectors[: 6 * per].reshape(6, features)
    narrow = vectors[6 * per :].reshape(-1)
    return (
        layer_out,
        grad_x.reshape(hidden_in.shape),
        wide[0],
        wide[1],
        0.125 * qkv_part[:, :local_width],
        0.125 * narrow[:local_width],
        qkv_part[:, local_width : 2 * local_width],
        qkv_part[:, 2 * local_width :],
        narrow[2 * local_width : 3 * local_width],
        output_part.T,
        wide[2],
        wide[3],
        wide[4],
        inner_part,
        narrow[3 * local_width :],
        outer_part.T,
        wide[5],
    )


def solution(mesh):
    return jax.shard_map(
        on_device,
        mesh=mesh,
        in_specs=(
            P(None, "seq", "tp"),
            P(),
            P(),
            P(None, "tp"),
            P("tp"),
            P(None, "tp"),
            P(None, "tp"),
            P("tp"),
            P("tp", None),
            P(),
            P(),
            P(),
            P(None, "tp"),
            P("tp"),
            P("tp", None),
            P(),
            P(),
            P(),
            P(),
            P(None, "seq", "tp"),
        ),
        out_specs=(
            P(None, "seq", "tp"),
            P(None, "seq", "tp"),
            P(),
            P(),
            P("seq", "tp"),
            P("tp"),
            P("seq", "tp"),
            P("seq", "tp"),
            P("tp"),
            P("tp", "seq"),
            P(),
            P(),
            P(),
            P("seq", "tp"),
            P("tp"),
            P("tp", "seq"),
            P(),
        ),
        check_vma=False,
    )
```

```python
import functools
import math

import jax
import jax.numpy as jnp
from jax import lax
from jax.experimental import pallas as pl
from jax.experimental.pallas import tpu as pltpu
from jax.sharding import PartitionSpec as P

HEAD_DIM = 64
BLK = 64
GLOBAL = 2
SLOTS = 8
WIDE = 2 * HEAD_DIM
CHUNKS = 4
COT_CHUNKS = 1
ROUNDS = 2
NEG = -1e30
NT = (((1,), (1,)), ((), ()))
TN = (((0,), (0,)), ((), ()))
MESH = pl.DeviceIdType.MESH
F32, BF16 = jnp.float32, jnp.bfloat16


def split_by(value, count):
    if count & (count - 1) == 0:
        return value >> (count.bit_length() - 1), value & (count - 1)
    return value // count, value % count


def remote(src, dst, send_sem, recv_sem, device):
    return pltpu.make_async_remote_copy(
        src_ref=src, dst_ref=dst, send_sem=send_sem, recv_sem=recv_sem,
        device_id=device, device_id_type=MESH,
    )


def greet(peers):
    barrier = pltpu.get_barrier_semaphore()
    for peer in peers:
        pl.semaphore_signal(barrier, inc=1, device_id=peer, device_id_type=MESH)
    pl.semaphore_wait(barrier, len(peers))


def add_up(*terms):
    total = terms[0].astype(F32)
    for term in terms[1:]:
        total = total + term.astype(F32)
    return total


def swap_halves(value):
    return pltpu.roll(value, HEAD_DIM, 1)


def low_half(value):
    return lax.broadcasted_iota(jnp.int32, value.shape, 1) < HEAD_DIM


def mix_pair(left, right):
    low = low_half(left)
    return (
        jnp.where(low, left, swap_halves(right)),
        jnp.where(low, swap_halves(left), right),
    )


def unpack_pair(left, right):
    even, odd = mix_pair(left.astype(F32), right.astype(F32))
    tiles = []
    for start in range(0, left.shape[0], BLK):
        tiles += [even[start : start + BLK], odd[start : start + BLK]]
    return jnp.concatenate(tiles, axis=0).astype(BF16)


def pack_pair(value):
    lefts, rights = [], []
    for start in range(0, value.shape[0], 2 * BLK):
        left, right = mix_pair(value[start : start + BLK], value[start + BLK : start + 2 * BLK])
        lefts.append(left)
        rights.append(right)
    return jnp.concatenate(lefts, axis=0).astype(BF16), jnp.concatenate(rights, axis=0).astype(BF16)


def dma(*shape):
    return pltpu.SemaphoreType.DMA(tuple(max(size, 1) for size in shape))


def vmem(*shape, dtype=BF16):
    return pltpu.VMEM(shape, dtype)


IN_VMEM = pl.BlockSpec(memory_space=pltpu.VMEM)
IN_SMEM = pl.BlockSpec(memory_space=pltpu.SMEM)
ANYWHERE = pl.BlockSpec(memory_space=pl.ANY)


class Place:
    def __init__(self, dims):
        self.heads, self.share, self.nseq, self.ntp = dims
        self.seq, self.tp = lax.axis_index("seq"), lax.axis_index("tp")
        self.head, self.part = self.seq // self.share, lax.rem(self.seq, self.share)

    def partner(self, step):
        other = lax.rem(self.part + step, self.share)
        return other, (self.head * self.share + other, self.tp)

    def across(self, step):
        other = lax.rem(self.head + step, self.heads)
        return other, (other * self.share + self.part, self.tp)

    def along(self, step):
        other = lax.rem(self.tp + step, self.ntp)
        return other, (self.seq, other)

    def apart(self, step):
        far, near = step // self.heads, step % self.heads
        head = lax.rem(self.head + near, self.heads)
        tp = lax.rem(self.tp + far, self.ntp)
        return head, tp, (head * self.share + self.part, tp)


def fill_table(place, docs_ref, pads_ref, picks_ref, table_ref, nrows):
    nblocks = table_ref.shape[1]
    block = lax.broadcasted_iota(jnp.int32, (1, nblocks), 1)

    def doc_step(doc, state):
        start, first, last, pad = state
        stop = start + docs_ref[doc]
        inside = (block >= start) & (block < stop)
        first = jnp.where(inside, start, first)
        last = jnp.where(inside, stop - 1, last)
        pad = jnp.where(inside, pads_ref[doc], pad)
        return stop, first, last, pad

    zero = jnp.zeros((1, nblocks), jnp.int32)
    _, first, last, pad = lax.fori_loop(
        0, docs_ref.shape[0], doc_step, (jnp.int32(0), zero, zero, zero)
    )
    length = last - first + 1
    picks = []
    for index in range(picks_ref.shape[0]):
        pick = picks_ref[index : index + 1, :]
        whole = (pick.astype(F32) / length.astype(F32)).astype(jnp.int32)
        left = pick - whole * length
        left = jnp.where(left < 0, left + length, left)
        left = jnp.where(left >= length, left - length, left)
        picks.append(first + left)
    glob = block - first < GLOBAL
    is_long = glob & (last - first >= SLOTS)
    never = block < 0
    p0, p1, p2 = picks
    fresh = lambda pick: (pick >= first + GLOBAL) & ((pick > block + 1) | (pick < block - 1))
    near = [
        (block - 1, ~never),
        (block, ~never),
        (block + 1, block < last),
        (first, ~never),
        (first + 1, block - 1 > first + 1),
        (p0, fresh(p0)),
        (p1, fresh(p1) & (p1 != p0)),
        (p2, fresh(p2) & (p2 != p0) & (p2 != p1)),
    ]
    for index, (other, use) in enumerate(near):
        whole = first + index
        use = (glob & (whole <= last) & ~is_long) | (~glob & use)
        other = jnp.where(use, jnp.where(glob, whole, other), block)
        live = jnp.where(use, jnp.where(other == last, BLK - pad, BLK), 0)
        table_ref[index : index + 1, :] = row_of(place, other, nrows) * WIDE + live
    table_ref[SLOTS : SLOTS + 1, :] = first
    table_ref[SLOTS + 1 : SLOTS + 2, :] = last
    table_ref[SLOTS + 2 : SLOTS + 3, :] = pad


def head_kernel(
    dims, nrows, docs_ref, pads_ref, picks_ref, x_ref, gain_ref, shift_ref,
    wq_ref, bq_ref, wk_ref, wv_ref, bv_ref, cot_ref, wo_ref,
    q_out, kv_out, h1_out, xs_out, g_out, rest_out, wo_out, xt_out, stat_out, table_out,
    xs, h1, qbuf, kvbuf, right_s, right_r, left_s, left_r, q_s, q_r, kv_s, kv_r, on_s, on_r,
    wz_s, wz_r, wa_s, wa_r, wp_s, wp_r, local,
):
    place = Place(dims)
    heads, share, nseq, ntp = dims
    head, part, seq, tp = place.head, place.part, place.seq, place.tp
    rows, width = x_ref.shape
    features = width * ntp
    chunk_rows = rows // CHUNKS

    def chunk_of(chunk):
        return pl.ds(chunk * chunk_rows, chunk_rows)

    def traveller(chunk, index):
        if chunk < CHUNKS:
            return xs.at[index, chunk_of(chunk)]
        return g_out.at[index, chunk_of(chunk - CHUNKS)]

    def rightward(chunk, index):
        spot = traveller(chunk, index)
        return remote(
            spot, spot, right_s.at[chunk, index], right_r.at[chunk, index], (seq, tp + 1)
        )

    def leftward(chunk, index):
        spot = traveller(chunk, index)
        return remote(spot, spot, left_s.at[chunk, index], left_r.at[chunk, index], (seq, tp - 1))

    def q_copy(chunk, step):
        other, device = place.across(step)
        return remote(
            qbuf.at[other, chunk_of(chunk)], q_out.at[head, chunk_of(chunk)],
            q_s.at[chunk, step - 1], q_r.at[chunk, step - 1], device,
        )

    def kv_copy(chunk, step):
        other, device = place.across(step)
        return remote(
            kvbuf.at[other, chunk_of(chunk)], kv_out.at[part, head, chunk_of(chunk)],
            kv_s.at[chunk, step - 1], kv_r.at[chunk, step - 1], device,
        )

    def kv_on(chunk, hop, step):
        owner = lax.rem(head + heads - hop, heads)
        spot = kv_out.at[part, owner, chunk_of(chunk)]
        source = kvbuf.at[head, chunk_of(chunk)] if hop == 0 else spot
        return remote(
            source, spot, on_s.at[chunk, hop, step - 1], on_r.at[chunk, hop, step - 1],
            place.partner(step)[1],
        )

    def own_send(chunk):
        @pl.when(tp < ntp - 1)
        def _():
            rightward(chunk, tp).start()

        @pl.when(tp > 0)
        def _():
            leftward(chunk, tp).start()

    def pass_on(chunk):
        for hop in range(1, ntp):
            below, above = tp - hop, tp + hop

            @pl.when(below >= 0)
            def _():
                rightward(chunk, below).wait_recv()

                @pl.when(tp < ntp - 1)
                def _():
                    rightward(chunk, below).start()

            @pl.when(above < ntp)
            def _():
                leftward(chunk, above).wait_recv()

                @pl.when(tp > 0)
                def _():
                    leftward(chunk, above).start()

    def compute(chunk):
        here = chunk_of(chunk)
        x = jnp.concatenate([xs[index, here] for index in range(ntp)], axis=1).astype(F32)
        mean = jnp.sum(x, axis=1, keepdims=True) * (1.0 / features)
        centered = x - mean
        spread = jnp.sum(centered * centered, axis=1, keepdims=True) * (1.0 / features)
        scale = lax.rsqrt(spread + 1e-05)
        normed = (centered * scale * gain_ref[...] + shift_ref[...]).astype(BF16)
        h1[here] = normed
        stat_out[here, 0:1] = mean
        stat_out[here, 1:2] = scale
        q = (jnp.dot(normed, wq_ref[...], preferred_element_type=F32) + bq_ref[...]) * 0.125
        k = jnp.dot(normed, wk_ref[...], preferred_element_type=F32)
        v = jnp.dot(normed, wv_ref[...], preferred_element_type=F32) + bv_ref[...]
        for index in range(0, heads, 2):
            lanes = slice(index * HEAD_DIM, (index + 2) * HEAD_DIM)
            kv = mix_pair(k[:, lanes], v[:, lanes])
            low = low_half(q[:, lanes])
            qs = (q[:, lanes], swap_halves(q[:, lanes]))
            for off in range(2):
                kvbuf[index + off, here] = kv[off].astype(BF16)
                qbuf[index + off, here] = jnp.where(low, qs[off], 0.0).astype(BF16)

    def hand_on(chunk):
        for hop in range(heads):
            if hop:
                kv_copy(chunk, hop).wait_recv()
            for step in range(1, share):
                kv_on(chunk, hop, step).start()

    slice_rows = wo_out.shape[3]
    half = lax.rem(part, 2)

    def wo_along(step):
        start = pl.multiple_of((head * 2 + half) * slice_rows, slice_rows)
        return remote(
            wo_ref.at[pl.ds(start, slice_rows)], wo_out.at[tp, head, half],
            wz_s.at[step - 1], wz_r.at[step - 1], place.along(step)[1],
        )

    def wo_across(step):
        spot = wo_out.at[:, head, half]
        return remote(spot, spot, wa_s.at[step - 1], wa_r.at[step - 1], place.across(step)[1])

    def wo_swap():
        spot = wo_out.at[:, :, half]
        return remote(spot, spot, wp_s.at[0], wp_r.at[0], (seq + 1 - 2 * half, tp))

    xs[tp] = x_ref[...]
    own_rows = pl.ds(pl.multiple_of((head * 2 + half) * slice_rows, slice_rows), slice_rows)
    early = [
        pltpu.make_async_copy(wo_ref.at[own_rows], wo_out.at[tp, head, half], local.at[5]),
        pltpu.make_async_copy(cot_ref.at[pl.ds(0, g_out.shape[1])], g_out.at[tp], local.at[6]),
    ]
    for copy in early:
        copy.start()
    greet(
        [place.partner(step)[1] for step in range(1, share)]
        + [place.across(step)[1] for step in range(1, heads)]
        + [place.along(step)[1] for step in range(1, ntp)]
    )
    for step in range(1, ntp):
        wo_along(step).start()
    own_send(0)
    own_send(1)
    fill_table(place, docs_ref, pads_ref, picks_ref, table_out, nrows)
    for copy in early:
        copy.wait()
    for step in range(1, ntp):
        wo_along(step).wait_recv()
    for step in range(1, heads):
        wo_across(step).start()
    for chunk in range(CHUNKS):
        if chunk > 0:
            own_send(chunk + 1)
        pass_on(chunk)
        compute(chunk)
        for step in range(1, heads):
            kv_copy(chunk, step).start()
        for step in range(1, heads):
            q_copy(chunk, step).start()
        if chunk > 0:
            hand_on(chunk - 1)
        if chunk == 2:
            for step in range(1, heads):
                wo_across(step).wait_recv()
            wo_swap().start()
    pairs = [
        (qbuf.at[head], q_out.at[head]),
        (kvbuf.at[head], kv_out.at[part, head]),
        (h1, h1_out),
        (xs, xs_out),
        (cot_ref.at[pl.ds(g_out.shape[1], rest_out.shape[0])], rest_out),
    ]
    copies = [
        pltpu.make_async_copy(source, target, local.at[index])
        for index, (source, target) in enumerate(pairs)
    ]
    for copy in copies:
        copy.start()
    mine = pl.ds(pl.multiple_of(tp * (rows // ntp), rows // ntp), rows // ntp)
    xt_out[...] = xs[:, mine]
    hand_on(CHUNKS - 1)
    for chunk in range(CHUNKS, CHUNKS + COT_CHUNKS):
        if chunk + 1 < CHUNKS + COT_CHUNKS:
            own_send(chunk + 1)
        pass_on(chunk)
    wo_swap().wait()
    for step in range(1, ntp):
        wo_along(step).wait_send()
    for step in range(1, heads):
        wo_across(step).wait_send()
    for copy in copies:
        copy.wait()
    for chunk in range(CHUNKS):
        for step in range(1, heads):
            q_copy(chunk, step).wait_recv()
        for hop in range(heads):
            for step in range(1, share):
                kv_on(chunk, hop, step).wait_recv()
    for chunk in range(CHUNKS):
        for step in range(1, heads):
            q_copy(chunk, step).wait_send()
            kv_copy(chunk, step).wait_send()
        for hop in range(heads):
            for step in range(1, share):
                kv_on(chunk, hop, step).wait_send()
    for chunk in range(CHUNKS + COT_CHUNKS):
        for index in range(ntp):
            @pl.when((tp >= index) & (tp < ntp - 1))
            def _():
                rightward(chunk, index).wait_send()

            @pl.when((tp <= index) & (tp > 0))
            def _():
                leftward(chunk, index).wait_send()


def run_head(dims, nrows, docs, pads, picks, x, *params):
    heads, share, nseq, ntp = dims
    rows, width = x.shape
    nblocks = picks.shape[1]
    first = rows // CHUNKS * COT_CHUNKS
    sds = jax.ShapeDtypeStruct
    outs = [
        sds((heads, rows, WIDE), BF16),
        sds((share, heads, rows, WIDE), BF16),
        sds((rows, width * ntp), BF16),
        sds((ntp, rows, width), BF16),
        sds((ntp, first, width), BF16),
        sds((rows - first, width), BF16),
        sds((ntp, heads, 2, params[-1].shape[0] // (2 * heads), params[-1].shape[1]), BF16),
        sds((ntp, rows // ntp, width), BF16),
        sds((rows, 2), F32),
        sds((16, nblocks), jnp.int32),
    ]
    scratch = [
        vmem(ntp, rows, width),
        vmem(rows, width * ntp),
        vmem(heads, rows, WIDE),
        vmem(heads, rows, WIDE),
    ]
    sems = (
        [dma(CHUNKS + COT_CHUNKS, ntp)] * 4 + [dma(CHUNKS, heads - 1)] * 4
        + [dma(CHUNKS, heads, share - 1)] * 2 + [dma(ntp - 1)] * 2 + [dma(heads - 1)] * 2
        + [dma(1)] * 2 + [dma(7)]
    )
    return pl.pallas_call(
        functools.partial(head_kernel, dims, nrows),
        out_shape=outs,
        in_specs=[IN_SMEM, IN_SMEM] + [IN_VMEM] * len(params) + [ANYWHERE] * 2,
        out_specs=[ANYWHERE] * 7 + [IN_VMEM] * 3,
        scratch_shapes=scratch + sems,
        name="head",
        compiler_params=pltpu.CompilerParams(
            collective_id=1, has_side_effects=True, vmem_limit_bytes=60 << 20
        ),
    )(docs, pads, picks, x, *params)


def block_of(place, query, nrows):
    source, row = split_by(query, nrows)
    return row * place.nseq + source * place.share + place.part


def row_of(place, block, nrows):
    row, holder = split_by(block, place.nseq)
    head, part = split_by(holder, place.share)
    return ((part * place.heads + head) * nrows + row) * BLK


def near_slots(table_ref, block):
    entries = [table_ref[index, block] for index in range(SLOTS)]
    slots = [pl.multiple_of(entry >> 7, BLK) for entry in entries]
    return slots, [entry & (WIDE - 1) for entry in entries]


def long_slots(place, table_ref, block, chunk, nrows):
    first, last = table_ref[SLOTS, block], table_ref[SLOTS + 1, block]
    final = BLK - table_ref[SLOTS + 2, block]
    slots, lives = [], []
    for index in range(SLOTS):
        wanted = first + chunk * SLOTS + index
        slots.append(pl.multiple_of(row_of(place, jnp.minimum(wanted, last), nrows), BLK))
        lives.append(jnp.where(wanted < last, BLK, jnp.where(wanted == last, final, 0)))
    return slots, lives


def for_long(place, table_ref, nquery, nrows, body):
    def step(query, carry):
        block = block_of(place, query, nrows)
        first, last = table_ref[SLOTS, block], table_ref[SLOTS + 1, block]

        @pl.when((block - first < GLOBAL) & (last - first >= SLOTS))
        def _():
            body(query, block, (last - first + SLOTS) >> 3)

        return carry

    lax.fori_loop(0, nquery, step, 0)


def bias_row(lives):
    lane = lax.broadcasted_iota(jnp.int32, (1, WIDE), 1)
    parts = []
    for index in range(0, SLOTS, 2):
        bound = jnp.where(lane < BLK, lives[index], lives[index + 1] + BLK)
        parts.append(jnp.where(lane < bound, 0.0, NEG))
    return jnp.concatenate(parts, axis=1)


def take(ref, slots):
    return jnp.concatenate([ref[pl.ds(slot, BLK), :] for slot in slots], axis=0)


def forward_kernel(dims, nrows, unroll, table_ref, q_ref, kv_ref, out_ref, res_ref):
    place = Place(dims)
    nquery = q_ref.shape[0] // BLK
    upper = lax.broadcasted_iota(jnp.int32, (BLK, WIDE), 1) >= HEAD_DIM

    def finish(query, top, total, accum):
        value = accum / total
        res_ref[pl.ds(query * BLK, BLK), :] = jnp.where(upper, value, top + jnp.log(total))
        return value

    def scores_of(query, slots, lives):
        kv = take(kv_ref, slots)
        scores = lax.dot_general(
            q_ref[pl.ds(query * BLK, BLK), :], kv, NT, preferred_element_type=F32
        )
        return kv, scores + bias_row(lives)

    def near_one(query):
        kv, scores = scores_of(query, *near_slots(table_ref, block_of(place, query, nrows)))
        top = jnp.max(scores, axis=1, keepdims=True)
        weights = jnp.exp(scores - top)
        total = jnp.sum(weights, axis=1, keepdims=True)
        accum = jnp.dot(weights.astype(BF16), kv, preferred_element_type=F32)
        return finish(query, top, total, accum)

    def near_step(index, carry):
        for offset in range(unroll):
            pair = index * unroll + offset
            even, odd = near_one(2 * pair), near_one(2 * pair + 1)
            out_ref[pl.ds(pair * BLK, BLK), :] = jnp.where(upper, odd, swap_halves(even)).astype(BF16)
        return carry

    lax.fori_loop(0, nquery // (2 * unroll), near_step, 0)

    def long_body(query, block, chunks):
        def chunk_step(chunk, state):
            top, total, accum = state
            kv, scores = scores_of(query, *long_slots(place, table_ref, block, chunk, nrows))
            new_top = jnp.maximum(top, jnp.max(scores, axis=1, keepdims=True))
            weights = jnp.exp(scores - new_top)
            decay = jnp.exp(top - new_top)
            total = total * decay + jnp.sum(weights, axis=1, keepdims=True)
            accum = accum * decay + jnp.dot(weights.astype(BF16), kv, preferred_element_type=F32)
            return new_top, total, accum

        start = (
            jnp.full((BLK, 1), NEG, F32),
            jnp.zeros((BLK, 1), F32),
            jnp.zeros((BLK, WIDE), F32),
        )
        value = finish(query, *lax.fori_loop(0, chunks, chunk_step, start))
        spot = pl.ds(pl.multiple_of((query >> 1) * BLK, BLK), BLK)
        is_odd = (query & 1) == 1
        moved = jnp.where(is_odd, value, swap_halves(value))
        out_ref[spot, :] = jnp.where(upper == is_odd, moved, out_ref[spot, :].astype(F32)).astype(BF16)

    for_long(place, table_ref, nquery, nrows, long_body)


def backward_kernel(
    dims, nrows, unroll, table_ref, q_ref, do_ref, res_ref, kv_ref, dq_ref, dkv_ref, sum_ref
):
    place = Place(dims)
    nquery = q_ref.shape[0] // BLK
    upper = lax.broadcasted_iota(jnp.int32, (BLK, WIDE), 1) >= HEAD_DIM
    sum_ref[...] = jnp.zeros_like(sum_ref)

    def load(query, packed, is_odd):
        moved = jnp.where(is_odd, packed, swap_halves(packed))
        grad = jnp.where(upper, moved, 0.0)
        rows = pl.ds(query * BLK, BLK)
        both = jnp.concatenate([q_ref[rows, :], grad.astype(BF16)], axis=0)
        res = res_ref[rows, :]
        delta = jnp.sum(res * grad, axis=1, keepdims=True)
        return both, res[:, :1], delta

    def terms(both, log_total, delta, slots, lives):
        kv = take(kv_ref, slots)
        pair = lax.dot_general(both, kv, NT, preferred_element_type=F32)
        probs = jnp.exp(pair[:BLK] + bias_row(lives) - log_total)
        grad_scores = (probs * (pair[BLK:] - delta)).astype(BF16)
        weights = jnp.concatenate([grad_scores, probs.astype(BF16)], axis=0)
        dkv = lax.dot_general(weights, both, TN, preferred_element_type=F32)
        dq = jnp.dot(grad_scores, kv, preferred_element_type=F32)
        return dq, dkv

    def scatter(slots, dkv):
        for index, slot in enumerate(slots):
            sum_ref[pl.ds(slot, BLK), :] += dkv[index * BLK : (index + 1) * BLK]

    def near_step(index, carry):
        done = []
        for offset in range(unroll):
            pair = index * unroll + offset
            packed = do_ref[pl.ds(pair * BLK, BLK), :].astype(F32)
            grads = []
            for is_odd in (False, True):
                query = 2 * pair + int(is_odd)
                slots, lives = near_slots(table_ref, block_of(place, query, nrows))
                dq, dkv = terms(*load(query, packed, is_odd), slots, lives)
                grads.append(dq)
                done.append((slots, dkv))
            dq_ref[pl.ds(pair * BLK, BLK), :] = jnp.where(
                upper, swap_halves(grads[1]), grads[0]
            ).astype(BF16)
        for slots, dkv in done:
            scatter(slots, dkv)
        return carry

    lax.fori_loop(0, nquery // (2 * unroll), near_step, 0)

    def long_body(query, block, chunks):
        is_odd = (query & 1) == 1
        spot = pl.ds(pl.multiple_of((query >> 1) * BLK, BLK), BLK)
        loaded = load(query, do_ref[spot, :].astype(F32), is_odd)

        def chunk_step(chunk, total):
            slots, lives = long_slots(place, table_ref, block, chunk, nrows)
            dq, dkv = terms(*loaded, slots, lives)
            scatter(slots, dkv)
            return total + dq

        total = lax.fori_loop(0, chunks, chunk_step, jnp.zeros((BLK, WIDE), F32))
        moved = jnp.where(is_odd, swap_halves(total), total)
        dq_ref[spot, :] = jnp.where(upper == is_odd, moved, dq_ref[spot, :].astype(F32)).astype(BF16)

    for_long(place, table_ref, nquery, nrows, long_body)
    dkv_ref[...] = sum_ref[...].astype(BF16)


def local_call(kernel, name, out_shape, nvmem, scratch=()):
    return pl.pallas_call(
        kernel,
        out_shape=out_shape,
        in_specs=[IN_SMEM] + [IN_VMEM] * nvmem,
        out_specs=jax.tree.map(lambda _: IN_VMEM, out_shape),
        scratch_shapes=list(scratch),
        name=name,
        cost_estimate=pl.CostEstimate(flops=30 << 30, bytes_accessed=8 << 20, transcendentals=0),
        compiler_params=pltpu.CompilerParams(vmem_limit_bytes=56 << 20),
    )


class GradScatter:
    def __init__(self, place, source, bufs, sems):
        self.place, self.source = place, source
        self.land, self.pair, self.far = bufs
        self.send1, self.recv1, self.send2, self.recv2 = sems

    @staticmethod
    def buffers(dims, band, cols):
        heads, share = dims[:2]
        return [
            vmem(max(share - 1, 1), heads, band, cols),
            vmem(heads, band, cols),
            vmem(max(heads - 1, 1), band, cols),
        ]

    @staticmethod
    def semaphores(dims, count):
        return [dma(count, dims[1] - 1)] * 2 + [dma(count, dims[0] - 1)] * 2

    def near(self, step):
        other, device = self.place.partner(step)
        return remote(
            self.source.at[:, other], self.land.at[step - 1],
            self.send1.at[step - 1], self.recv1.at[step - 1], device,
        )

    def across(self, step):
        other, device = self.place.across(step)
        return remote(
            self.pair.at[other], self.far.at[step - 1],
            self.send2.at[step - 1], self.recv2.at[step - 1], device,
        )

    def start_near(self):
        for step in range(1, self.place.share):
            self.near(step).start()

    def start_across(self):
        place = self.place
        for step in range(1, place.share):
            self.near(step).wait_recv()

        def body(head, carry):
            parts = [self.source[head, place.part]]
            parts += [self.land[step, head] for step in range(place.share - 1)]
            self.pair[head] = add_up(*parts).astype(BF16)
            return carry

        lax.fori_loop(0, place.heads, body, 0)
        for step in range(1, place.heads):
            self.across(step).start()

    def result(self):
        heads = self.place.heads
        for step in range(1, heads):
            self.across(step).wait_recv()
        return add_up(self.pair[self.place.head], *[self.far[step] for step in range(heads - 1)])

    def finish(self):
        for step in range(1, self.place.share):
            self.near(step).wait_send()
        for step in range(1, self.place.heads):
            self.across(step).wait_send()


def gelu_pair(value):
    root = math.sqrt(2.0 / math.pi)
    square = value * value
    curve = jnp.tanh(root * value * (1.0 + 0.044715 * square))
    half = 0.5 * (1.0 + curve)
    slope = half + 0.5 * value * (1.0 - curve * curve) * (root * (1.0 + 3 * 0.044715 * square))
    return value * half, slope


def middle_kernel(
    dims,
    o_ref, g0_hbm, g1_hbm, wo_hbm, wi_hbm, wu_hbm, xt_ref, ob_ref, gain_ref, shift_ref, ib_ref,
    sum_out, do_out, da_out, mixed_out, vec_out, gi_out, gu_out,
    g_ref, wo_ref, wi_ref, wu_ref, o_in, x1, xhat, scale, h2, act, dpre, outb, terms, from_left, from_right, do_buf, ib_sum, gi, gu,
    *rest,
):
    place = Place(dims)
    heads, share, nseq, ntp = dims
    head, part, seq, tp = place.head, place.part, place.seq, place.tp
    lands, sems = rest[:6], rest[6:]
    (o_s, o_r, hr_s, hr_r, hl_s, hl_r, tr_s, tr_r, tl_s, tl_r, do_s, do_r,
     g1_s, g1_r, g2_s, g2_r, local) = sems
    rows, width = g_ref.shape[1:]
    features = width * ntp
    tokens = rows // ntp
    rounds = ROUNDS
    span = tokens // rounds
    pieces = tokens // (2 * BLK)
    places = 2 * ntp - 1
    band = features // heads
    per = features // WIDE

    def packed_rows(index, count=tokens // 2):
        return pl.ds(pl.multiple_of(index * count, count), count)

    def span_of(index):
        return pl.ds(pl.multiple_of(index * span, span), span)

    def o_copy(step):
        to_head, to_tp, device = place.apart(step)
        return remote(
            o_ref.at[to_head, packed_rows(to_tp)], o_in.at[tp * heads + head],
            o_s.at[step], o_r.at[step], device,
        )

    def do_copy(index, step):
        to_head, to_tp, device = place.apart(step)
        return remote(
            do_buf.at[to_tp * heads + to_head, packed_rows(index, BLK)],
            do_out.at[head, packed_rows(tp * pieces + index, BLK)],
            do_s.at[index, step], do_r.at[index, step], device,
        )

    def h2_copy(index, owner, right):
        spot = h2.at[owner, span_of(index)]
        if right:
            return remote(spot, spot, hr_s.at[index, owner], hr_r.at[index, owner], (seq, tp + 1))
        return remote(spot, spot, hl_s.at[index, owner], hl_r.at[index, owner], (seq, tp - 1))

    def term_copy(index, owner, right):
        here = span_of(index)
        if right:
            return remote(
                terms.at[owner, here], from_left.at[owner, here],
                tr_s.at[index, owner], tr_r.at[index, owner], (seq, tp + 1),
            )
        return remote(
            terms.at[owner, here], from_right.at[owner, here],
            tl_s.at[index, owner], tl_r.at[index, owner], (seq, tp - 1),
        )

    scatters = [
        GradScatter(
            place, source, lands[3 * k : 3 * k + 3], (g1_s.at[k], g1_r.at[k], g2_s.at[k], g2_r.at[k])
        )
        for k, source in enumerate((gi, gu))
    ]

    first_rows = g0_hbm.shape[1]
    loads = [
        pltpu.make_async_copy(o_ref.at[head, packed_rows(tp)], o_in.at[tp * heads + head], local.at[2]),
        pltpu.make_async_copy(wo_hbm, wo_ref, local.at[3]),
        pltpu.make_async_copy(wi_hbm, wi_ref, local.at[4]),
        pltpu.make_async_copy(wu_hbm, wu_ref, local.at[5]),
        pltpu.make_async_copy(g0_hbm, g_ref.at[:, pl.ds(0, first_rows)], local.at[6]),
        pltpu.make_async_copy(
            g1_hbm, g_ref.at[:, pl.ds(first_rows, rows - first_rows)], local.at[7]
        ),
    ]
    for load in loads:
        load.start()
    greet(
        [place.partner(step)[1] for step in range(1, share)]
        + [place.apart(step)[2] for step in range(1, heads * ntp)]
    )
    for step in range(heads * ntp - 1, 0, -1):
        o_copy(step).start()
    ib_sum[...] = jnp.zeros_like(ib_sum)
    for load in loads:
        load.wait()
    for step in range(1, heads * ntp):
        o_copy(step).wait_recv()

    for index in range(pieces):
        here = slice(index * 2 * BLK, (index + 1) * 2 * BLK)
        half = slice(index * BLK, (index + 1) * BLK)
        mixed = jnp.concatenate(
            [unpack_pair(o_in[i, half], o_in[i + 1, half]) for i in range(0, heads * ntp, 2)], axis=1
        )
        mixed_out[here] = mixed
        base = jnp.concatenate([xt_ref[i, here] for i in range(ntp)], axis=1).astype(F32)
        value = base + ob_ref[...] + jnp.dot(mixed, wo_ref[...].reshape(features, features), preferred_element_type=F32)
        x1[here] = value
        centered = value - jnp.sum(value, axis=1, keepdims=True) * (1.0 / features)
        spread = jnp.sum(centered * centered, axis=1, keepdims=True) * (1.0 / features)
        inverse = lax.rsqrt(spread + 1e-05)
        normed = centered * inverse
        xhat[here] = normed
        scale[here] = jnp.broadcast_to(inverse, (2 * BLK, WIDE))
        h2[tp, here] = (normed * gain_ref[...] + shift_ref[...]).astype(BF16)
        for part_index in range(index * rounds // pieces, (index + 1) * rounds // pieces):

            @pl.when(tp < ntp - 1)
            def _():
                h2_copy(part_index, tp, True).start()

            @pl.when(tp > 0)
            def _():
                h2_copy(part_index, tp, False).start()

    def spot_of(position):
        hop = (position + 1) // 2
        owner = tp + jnp.where(position % 2 == 1, -hop, hop)
        return owner, (owner >= 0) & (owner < ntp)

    def feed(index, owner):
        @pl.when(owner < tp)
        def _():
            h2_copy(index, owner, True).wait_recv()

            @pl.when(tp < ntp - 1)
            def _():
                h2_copy(index, owner, True).start()

        @pl.when(owner > tp)
        def _():
            h2_copy(index, owner, False).wait_recv()

            @pl.when(tp > 0)
            def _():
                h2_copy(index, owner, False).start()

        here = span_of(index)
        wide = span_of(owner * rounds + index)
        pre = jnp.dot(h2[owner, here], wi_ref[...], preferred_element_type=F32) + ib_ref[...]
        value, slope = gelu_pair(pre)
        value = value.astype(BF16)
        act[wide] = value
        grad = jnp.concatenate([g_ref[i, wide] for i in range(ntp)], axis=1)
        back = lax.dot_general(grad, wu_ref[...], NT, preferred_element_type=F32) * slope
        back = back.astype(BF16)
        dpre[wide] = back
        ib_sum[0:1, :] += jnp.sum(back.astype(F32), axis=0, keepdims=True)
        terms[owner, here] = lax.dot_general(
            back, wi_ref[...], NT, preferred_element_type=F32
        ).astype(BF16)

        @pl.when((owner > tp) & (tp == 0))
        def _():
            term_copy(index, owner, True).start()

        @pl.when((owner < tp) & (tp == ntp - 1))
        def _():
            term_copy(index, owner, False).start()

        out = jnp.dot(value, wu_ref[...], preferred_element_type=F32)
        out = out + jnp.where(owner == tp, x1[here], 0.0)
        for i in range(ntp):
            outb[i, wide] = out[:, i * width : (i + 1) * width].astype(BF16)

    def relay_right(index):
        here = span_of(index)
        for owner in range(1, ntp):

            @pl.when((owner > tp) & (tp > 0))
            def _():
                term_copy(index, owner, True).wait_recv()
                terms[owner, here] = add_up(terms[owner, here], from_left[owner, here]).astype(BF16)
                term_copy(index, owner, True).start()

    def relay_left(index):
        here = span_of(index)
        for owner in range(ntp - 2, -1, -1):

            @pl.when((owner < tp) & (tp < ntp - 1))
            def _():
                term_copy(index, owner, False).wait_recv()
                terms[owner, here] = add_up(terms[owner, here], from_right[owner, here]).astype(BF16)
                term_copy(index, owner, False).start()

    def relay(index, first):
        @pl.when((tp < ntp // 2) == first)
        def _():
            relay_right(index)

        @pl.when((tp < ntp // 2) != first)
        def _():
            relay_left(index)

    def feed_step(count, carry):
        index, position = count // places, count % places
        owner, inside = spot_of(position)

        @pl.when(inside)
        def _():
            feed(index, owner)

        @pl.when((index > 0) & (position == 2))
        def _():
            relay(index - 1, True)

        @pl.when((index > 0) & (position == places - 1))
        def _():
            relay(index - 1, False)

        return carry

    lax.fori_loop(0, rounds * places, feed_step, 0)
    save = pltpu.make_async_copy(outb, sum_out, local.at[0])
    save.start()

    def inner_grad(index):
        left = h2[:, :, index * band : (index + 1) * band].reshape(rows, band)
        value = lax.dot_general(left, dpre[...], TN, preferred_element_type=F32)
        gi[index] = value.astype(BF16).reshape(gi.shape[1:])

    def outer_grad(index):
        many = ntp // heads
        left = jnp.concatenate([g_ref[i] for i in range(index * many, (index + 1) * many)], axis=1)
        value = lax.dot_general(left, act[...], TN, preferred_element_type=F32)
        gu[index] = value.astype(BF16).reshape(gu.shape[1:])

    work = [functools.partial(inner_grad, index) for index in range(heads)]
    work += [functools.partial(outer_grad, index) for index in range(heads)]
    share_out = -(-len(work) // 2)
    for position in range(2):
        relay(rounds - 1, position == 0)
        for item in work[position * share_out : (position + 1) * share_out]:
            item()
        if (position + 1) * share_out >= heads > position * share_out:
            scatters[0].start_near()
        if (position + 1) * share_out >= 2 * heads > position * share_out:
            scatters[1].start_near()

    for index in range(pieces):
        here = slice(index * 2 * BLK, (index + 1) * 2 * BLK)
        half = slice(index * BLK, (index + 1) * BLK)
        wide = pl.ds(pl.multiple_of(tp * tokens + index * 2 * BLK, 2 * BLK), 2 * BLK)
        for part_index in range(index * rounds // pieces, (index + 1) * rounds // pieces):

            @pl.when(tp > 0)
            def _():
                term_copy(part_index, tp, True).wait_recv()

            @pl.when(tp < ntp - 1)
            def _():
                term_copy(part_index, tp, False).wait_recv()

        grad = terms[tp, here].astype(F32)
        grad = grad + jnp.where(tp > 0, from_left[tp, here].astype(F32), 0.0)
        grad = grad + jnp.where(tp < ntp - 1, from_right[tp, here].astype(F32), 0.0)
        hat = xhat[here]
        inner = grad * gain_ref[...]
        mean0 = jnp.sum(inner, axis=1, keepdims=True) * (1.0 / features)
        mean1 = jnp.sum(inner * hat, axis=1, keepdims=True) * (1.0 / features)
        tail = scale[here, 0:1] * (inner - mean0 - hat * mean1)
        cot = jnp.concatenate([g_ref[i, wide] for i in range(ntp)], axis=1).astype(F32)
        branch = (cot + tail).astype(BF16)
        da_out[here] = branch
        do = lax.dot_general(
            branch, wo_ref[...].reshape(features, features), NT, preferred_element_type=F32
        )
        for i in range(0, heads * ntp, 2):
            pair = pack_pair(do[:, i * HEAD_DIM : (i + 2) * HEAD_DIM])
            do_buf[i, half] = pair[0]
            do_buf[i + 1, half] = pair[1]
        for step in range(heads * ntp - 1, 0, -1):
            do_copy(index, step).start()
        sums = (
            jnp.sum(branch.astype(F32), axis=0, keepdims=True),
            jnp.sum(grad * hat, axis=0, keepdims=True),
            jnp.sum(grad, axis=0, keepdims=True),
        )
        for kind, value in enumerate(sums):
            for sub in range(per):
                row = slice(kind * per + sub, kind * per + sub + 1)
                piece = value[:, sub * WIDE : (sub + 1) * WIDE]
                if index == 0:
                    vec_out[row, :] = piece
                else:
                    vec_out[row, :] += piece
    own = pltpu.make_async_copy(
        do_buf.at[tp * heads + head], do_out.at[head, packed_rows(tp)], local.at[1]
    )
    own.start()
    for scatter in scatters:
        scatter.start_across()
    cot = jnp.sum(g_ref[tp].astype(F32), axis=0, keepdims=True)
    for sub in range(per):
        owner, lane = divmod(sub * WIDE, width)
        vec_out[3 * per + sub : 3 * per + sub + 1, :] = jnp.where(
            tp == owner, cot[:, lane : lane + WIDE], 0.0
        )
    for sub in range(ib_sum.shape[1] // WIDE):
        row = 4 * per + sub
        vec_out[row : row + 1, :] = ib_sum[0:1, sub * WIDE : (sub + 1) * WIDE]
    gi_out[...] = scatters[0].result()
    gu_out[...] = scatters[1].result()
    save.wait()
    own.wait()
    for step in range(1, heads * ntp):
        for index in range(pieces):
            do_copy(index, step).wait_recv()
    for step in range(1, heads * ntp):
        o_copy(step).wait_send()
        for index in range(pieces):
            do_copy(index, step).wait_send()
    for index in range(rounds):
        for owner in range(ntp):
            @pl.when((tp >= owner) & (tp < ntp - 1))
            def _():
                h2_copy(index, owner, True).wait_send()

            @pl.when((tp <= owner) & (tp > 0))
            def _():
                h2_copy(index, owner, False).wait_send()

            @pl.when(tp < owner)
            def _():
                term_copy(index, owner, True).wait_send()

            @pl.when(tp > owner)
            def _():
                term_copy(index, owner, False).wait_send()

    for scatter in scatters:
        scatter.finish()


def run_middle(dims, o, g0, g1, wo, wi, wu, xt, ob, gain, shift, ib):
    heads, share, nseq, ntp = dims
    rows, width = g0.shape[1] + g1.shape[1], g0.shape[2]
    features, hidden = width * ntp, wi.shape[1]
    tokens, band = rows // ntp, features // nseq
    per = features // WIDE
    rounds, pieces = ROUNDS, tokens // (2 * BLK)
    sds = jax.ShapeDtypeStruct
    outs = [
        sds((ntp, rows, width), BF16),
        sds((heads, rows // 2, WIDE), BF16),
        sds((tokens, features), BF16),
        sds((tokens, features), BF16),
        sds((4 * per + hidden // WIDE, WIDE), F32),
        sds((band, hidden), F32),
        sds((band, hidden), F32),
    ]
    count = heads * ntp
    scratch = [
        vmem(ntp, rows, width),
        vmem(*wo.shape),
        vmem(*wi.shape),
        vmem(*wu.shape),
        vmem(count, tokens // 2, WIDE),
        vmem(tokens, features, dtype=F32),
        vmem(tokens, features, dtype=F32),
        vmem(tokens, WIDE, dtype=F32),
        vmem(ntp, tokens, features),
        vmem(rows, hidden),
        vmem(rows, hidden),
        vmem(ntp, rows, width),
        vmem(ntp, tokens, features),
        vmem(ntp, tokens, features),
        vmem(ntp, tokens, features),
        vmem(count, tokens // 2, WIDE),
        vmem(8, hidden, dtype=F32),
        vmem(heads, share, band, hidden),
        vmem(heads, share, band, hidden),
        *GradScatter.buffers(dims, band, hidden),
        *GradScatter.buffers(dims, band, hidden),
    ]
    sems = (
        [dma(count)] * 2 + [dma(rounds, ntp)] * 8 + [dma(pieces, count)] * 2
        + GradScatter.semaphores(dims, 2) + [dma(8)]
    )
    return pl.pallas_call(
        functools.partial(middle_kernel, dims),
        out_shape=outs,
        in_specs=[ANYWHERE] * 6 + [IN_VMEM] * 5,
        out_specs=[ANYWHERE] * 2 + [IN_VMEM] * 5,
        scratch_shapes=scratch + sems,
        name="middle",
        compiler_params=pltpu.CompilerParams(
            collective_id=2, has_side_effects=True, vmem_limit_bytes=63 << 20
        ),
    )(o, g0, g1, wo, wi, wu, xt, ob, gain, shift, ib)


def tail_kernel(
    dims,
    dq_ref, dkv_hbm, h1_hbm, x_hbm, da_ref, mixed_ref, stat_ref, gain_ref, wq_ref, wk_ref, wv_ref, vec_ref,
    gx_ref, ow_ref, oq_ref, ok_ref, ov_ref, vout_ref,
    dkv_own, h1_ref, x_ref, dq_in, dkv_in, dkv_land, dkv_sum, all3, da_in, pbuf, from_left, from_right,
    sums, sums_land, vbuf, vec_land, vsum, vec_far, gw, g3, wbuf, wfar,
    *rest,
):
    place = Place(dims)
    heads, share, nseq, ntp = dims
    head, part, seq, tp = place.head, place.part, place.seq, place.tp
    lands, sems = rest[:6], rest[6:]
    (dq_s, dq_r, kv1_s, kv1_r, kv2_s, kv2_r, right_s, right_r, left_s, left_r,
     da_s, da_r, st_s, st_r, v1_s, v1_r, v2_s, v2_r, w_s, w_r, g1_s, g1_r, g2_s, g2_r, load_s) = sems
    rows, features = h1_ref.shape
    width = features // ntp
    tokens = rows // ntp
    local_width = wq_ref.shape[1]
    chunk_rows = rows // CHUNKS
    band = features // heads
    per = features // WIDE

    def chunk_of(chunk):
        return pl.ds(chunk * chunk_rows, chunk_rows)

    def half_of(chunk):
        return pl.ds(chunk * chunk_rows // 2, chunk_rows // 2)

    def columns_of(index):
        return pl.ds(pl.multiple_of(index * width, width), width)

    def dq_copy(chunk, step):
        other, device = place.across(step)
        return remote(
            dq_ref.at[other, half_of(chunk)], dq_in.at[head, half_of(chunk)],
            dq_s.at[chunk, step - 1], dq_r.at[chunk, step - 1], device,
        )

    def dkv_near(chunk, step):
        other, device = place.partner(step)
        here = chunk_of(chunk)
        return remote(
            dkv_hbm.at[other, :, here], dkv_land.at[step - 1, :, here],
            kv1_s.at[chunk, step - 1], kv1_r.at[chunk, step - 1], device,
        )

    def dkv_copy(chunk, step):
        other, device = place.across(step)
        return remote(
            dkv_sum.at[other, chunk_of(chunk)], dkv_in.at[head, chunk_of(chunk)],
            kv2_s.at[chunk, step - 1], kv2_r.at[chunk, step - 1], device,
        )

    def da_copy(step):
        other, device = place.along(step)
        return remote(
            da_ref.at[:, columns_of(other)], da_in.at[tp], da_s.at[step - 1], da_r.at[step - 1], device
        )

    def rightward(chunk, index):
        return remote(
            pbuf.at[chunk, index], from_left.at[chunk, index],
            right_s.at[chunk, index], right_r.at[chunk, index], (seq, tp + 1),
        )

    def leftward(chunk, index):
        return remote(
            pbuf.at[chunk, index], from_right.at[chunk, index],
            left_s.at[chunk, index], left_r.at[chunk, index], (seq, tp - 1),
        )

    def sums_copy(step):
        return remote(
            sums, sums_land.at[step - 1], st_s.at[step - 1], st_r.at[step - 1], place.along(step)[1]
        )

    def vec_copy(step):
        return remote(
            vbuf, vec_land.at[step - 1], v1_s.at[step - 1], v1_r.at[step - 1],
            (lax.rem(seq + step, nseq), tp),
        )

    def vec_far_copy(step):
        return remote(
            vsum, vec_far.at[step - 1], v2_s.at[step - 1], v2_r.at[step - 1], place.along(step)[1]
        )

    def w_copy(step):
        other, device = place.along(step)
        return remote(wbuf.at[other], wfar.at[step - 1], w_s.at[step - 1], w_r.at[step - 1], device)

    scatters = [
        GradScatter(
            place, source, lands[3 * k : 3 * k + 3], (g1_s.at[k], g1_r.at[k], g2_s.at[k], g2_r.at[k])
        )
        for k, source in enumerate((gw, g3))
    ]

    loads = [
        pltpu.make_async_copy(dkv_hbm.at[part], dkv_own, load_s.at[0]),
        pltpu.make_async_copy(dq_ref.at[head], dq_in.at[head], load_s.at[1]),
        pltpu.make_async_copy(x_hbm, x_ref, load_s.at[2]),
        pltpu.make_async_copy(h1_hbm, h1_ref, load_s.at[3]),
    ]
    for load in loads:
        load.start()
    greet(
        [(lax.rem(seq + step, nseq), tp) for step in range(1, nseq)]
        + [place.along(step)[1] for step in range(1, ntp)]
    )
    for chunk in range(CHUNKS):
        for step in range(1, share):
            dkv_near(chunk, step).start()
    for step in range(1, ntp):
        da_copy(step).start()
    da_in[tp] = da_ref[:, columns_of(tp)]
    vbuf[: 2 * per] = jnp.zeros((2 * per, WIDE), F32)
    vbuf[2 * per : 6 * per] = vec_ref[: 4 * per]
    narrow = 3 * local_width // WIDE
    vbuf[6 * per : 6 * per + narrow] = jnp.zeros((narrow, WIDE), F32)
    vbuf[6 * per + narrow :] = vec_ref[4 * per :]
    loads[0].wait()
    for chunk in range(CHUNKS):
        for step in range(1, heads):
            dq_copy(chunk, step).start()
        for step in range(1, share):
            dkv_near(chunk, step).wait_recv()
        for target in range(heads):
            where = (target, chunk_of(chunk))
            parts = [dkv_own[where]] + [dkv_land[(step,) + where] for step in range(share - 1)]
            dkv_sum[where] = add_up(*parts).astype(BF16)
        for step in range(1, heads):
            dkv_copy(chunk, step).start()
    dkv_in[head] = dkv_sum[head]
    for load in loads[1:]:
        load.wait()

    def output_grad(index):
        value = lax.dot_general(
            da_ref[:, index * band : (index + 1) * band], mixed_ref[...], TN, preferred_element_type=F32
        )
        gw[index] = value.astype(BF16).reshape(gw.shape[1:])

    gain = gain_ref[...]
    lane = lax.broadcasted_iota(jnp.int32, (chunk_rows, WIDE), 1)

    def partial_step(chunk):
        here, half = chunk_of(chunk), half_of(chunk)
        for step in range(1, heads):
            dq_copy(chunk, step).wait_recv()
            dkv_copy(chunk, step).wait_recv()
        three = [[], [], []]
        for i in range(0, heads, 2):
            three[0].append(unpack_pair(dq_in[i, half], dq_in[i + 1, half]))
            k, v = mix_pair(dkv_in[i, here].astype(F32), dkv_in[i + 1, here].astype(F32))
            three[1].append(k.astype(BF16))
            three[2].append(v.astype(BF16))
        three = [jnp.concatenate(item, axis=1) for item in three]
        grad = 0.125 * lax.dot_general(three[0], wq_ref[...], NT, preferred_element_type=F32)
        grad = grad + lax.dot_general(three[1], wk_ref[...], NT, preferred_element_type=F32)
        grad = grad + lax.dot_general(three[2], wv_ref[...], NT, preferred_element_type=F32)
        row = 6 * per
        for kind, value in enumerate(three):
            all3[here, kind * local_width : (kind + 1) * local_width] = value
            column = jnp.sum(value.astype(F32), axis=0, keepdims=True)
            for start in range(0, local_width, WIDE):
                vbuf[row : row + 1, :] += column[:, start : start + WIDE]
                row += 1
        mean, scale = stat_ref[here, 0:1], stat_ref[here, 1:2]
        sum0 = jnp.zeros((chunk_rows, 1), F32)
        sum1 = jnp.zeros((chunk_rows, 1), F32)
        for index in range(ntp):
            cols = slice(index * width, (index + 1) * width)
            piece = grad[:, cols]
            xhat = (x_ref[index, here].astype(F32) - mean) * scale
            weighted = piece * gain[:, cols]
            sum0 = sum0 + jnp.sum(weighted, axis=1, keepdims=True)
            sum1 = sum1 + jnp.sum(weighted * xhat, axis=1, keepdims=True)
            col0 = jnp.sum(piece * xhat, axis=0, keepdims=True)
            col1 = jnp.sum(piece, axis=0, keepdims=True)
            for sub in range(width // WIDE):
                row = index * (width // WIDE) + sub
                lanes = slice(sub * WIDE, (sub + 1) * WIDE)
                vbuf[row : row + 1, :] += col0[:, lanes]
                vbuf[per + row : per + row + 1, :] += col1[:, lanes]
            pbuf[chunk, index] = piece.astype(BF16)
        both = jnp.where(lane == 0, sum0, jnp.where(lane == 1, sum1, 0.0))
        sums[:, here] = both.T[:8]

    def set_off(chunk):
        for step in range(ntp - 1):
            far = ntp - 1 - step

            @pl.when(tp == 0)
            def _():
                rightward(chunk, far).start()

            @pl.when(tp == ntp - 1)
            def _():
                leftward(chunk, step).start()

    def relay_right(chunk):
        for step in range(ntp - 1):
            far = ntp - 1 - step

            @pl.when((tp < far) & (tp > 0))
            def _():
                rightward(chunk, far).wait_recv()
                pbuf[chunk, far] = add_up(pbuf[chunk, far], from_left[chunk, far]).astype(BF16)
                rightward(chunk, far).start()

    def relay_left(chunk):
        for step in range(ntp - 1):

            @pl.when((tp > step) & (tp < ntp - 1))
            def _():
                leftward(chunk, step).wait_recv()
                pbuf[chunk, step] = add_up(pbuf[chunk, step], from_right[chunk, step]).astype(BF16)
                leftward(chunk, step).start()

    def relay(chunk):
        @pl.when(tp < ntp // 2)
        def _():
            relay_right(chunk)
            relay_left(chunk)

        @pl.when(tp >= ntp // 2)
        def _():
            relay_left(chunk)
            relay_right(chunk)

    def grad_step(index, carry):
        left = h1_ref[:, pl.ds(pl.multiple_of(index * band, band), band)]
        value = lax.dot_general(left, all3[...], TN, preferred_element_type=F32)
        g3[index] = value.astype(BF16).reshape(g3.shape[1:])
        return carry

    for chunk in range(CHUNKS):
        partial_step(chunk)
        set_off(chunk)
        if chunk == 0:
            for index in range(heads):
                output_grad(index)
            scatters[0].start_near()
        if chunk > 1:
            relay(chunk - 2)
    for step in range(1, ntp):
        sums_copy(step).start()
    for step in range(1, nseq):
        vec_copy(step).start()
    scatters[0].start_across()
    lax.fori_loop(0, heads, grad_step, 0)
    scatters[1].start_near()
    relay(CHUNKS - 2)
    scatters[1].start_across()
    for step in range(1, nseq):
        vec_copy(step).wait_recv()
    total = vbuf[...]
    for step in range(nseq - 1):
        total = total + vec_land[step]
    vsum[...] = total
    for step in range(1, ntp):
        vec_far_copy(step).start()
    value = scatters[0].result().astype(BF16)
    for index in range(ntp):
        wbuf[index] = value[:, index * local_width : (index + 1) * local_width]
    for step in range(1, ntp):
        w_copy(step).start()
    relay(CHUNKS - 1)

    for step in range(1, ntp):
        sums_copy(step).wait_recv()
        da_copy(step).wait_recv()
    my_gain = gain_ref[:, columns_of(tp)]
    da_rows = da_in.shape[1]
    for chunk in range(CHUNKS):
        here = chunk_of(chunk)
        both = sums[:, here]
        for step in range(ntp - 1):
            both = both + sums_land[step, :, here]
        both = jnp.concatenate([both, jnp.zeros((WIDE - 8, chunk_rows), F32)], axis=0).T
        both = both * (1.0 / features)

        @pl.when(tp > 0)
        def _():
            rightward(chunk, tp).wait_recv()

        @pl.when(tp < ntp - 1)
        def _():
            leftward(chunk, tp).wait_recv()

        grad = pbuf[chunk, tp].astype(F32)
        grad = grad + jnp.where(tp > 0, from_left[chunk, tp].astype(F32), 0.0)
        grad = grad + jnp.where(tp < ntp - 1, from_right[chunk, tp].astype(F32), 0.0)
        mean, scale = stat_ref[here, 0:1], stat_ref[here, 1:2]
        xhat = (x_ref[tp, here].astype(F32) - mean) * scale
        inner = grad * my_gain - both[:, 0:1] - xhat * both[:, 1:2]
        many = chunk_rows // da_rows
        branch = da_in[chunk * many : (chunk + 1) * many].reshape(chunk_rows, width)
        gx_ref[here] = branch.astype(F32) + scale * inner
    value = scatters[1].result()
    oq_ref[...] = 0.125 * value[:, :local_width]
    ok_ref[...] = value[:, local_width : 2 * local_width]
    ov_ref[...] = value[:, 2 * local_width :]
    for step in range(1, ntp):
        vec_far_copy(step).wait_recv()
        w_copy(step).wait_recv()
    vout_ref[...] = vsum[...]
    for step in range(ntp - 1):
        vout_ref[: 6 * per] += vec_far[step, : 6 * per]
    ow_ref[...] = add_up(wbuf[tp], *[wfar[step] for step in range(ntp - 1)])

    for chunk in range(CHUNKS):
        for step in range(1, share):
            dkv_near(chunk, step).wait_send()
        for step in range(1, heads):
            dq_copy(chunk, step).wait_send()
            dkv_copy(chunk, step).wait_send()
        for index in range(ntp):
            @pl.when(tp < index)
            def _():
                rightward(chunk, index).wait_send()

            @pl.when(tp > index)
            def _():
                leftward(chunk, index).wait_send()

    for step in range(1, ntp):
        sums_copy(step).wait_send()
        da_copy(step).wait_send()
        vec_far_copy(step).wait_send()
        w_copy(step).wait_send()
    for step in range(1, nseq):
        vec_copy(step).wait_send()
    for scatter in scatters:
        scatter.finish()


def run_tail(dims, dq, dkv, h1, x_parts, da, mixed, stats, gain, wq, wk, wv, vec):
    heads, share, nseq, ntp = dims
    rows, features = h1.shape
    width, tokens = features // ntp, rows // ntp
    band = features // nseq
    local_width = wq.shape[1]
    per = features // WIDE
    sds = jax.ShapeDtypeStruct
    nvec = vec.shape[0] + 2 * per + 3 * local_width // WIDE
    outs = [
        sds((rows, width), F32),
        sds((band, local_width), F32),
        sds((band, local_width), F32),
        sds((band, local_width), F32),
        sds((band, local_width), F32),
        sds((nvec, WIDE), F32),
    ]
    pieces = (CHUNKS, ntp, rows // CHUNKS, width)
    scratch = [
        vmem(heads, rows, WIDE),
        vmem(rows, features),
        vmem(ntp, rows, width),
        vmem(heads, rows // 2, WIDE),
        vmem(heads, rows, WIDE),
        vmem(max(share - 1, 1), heads, rows, WIDE),
        vmem(heads, rows, WIDE),
        vmem(rows, 3 * local_width),
        vmem(ntp, tokens, width),
        vmem(*pieces),
        vmem(*pieces),
        vmem(*pieces),
        vmem(8, rows, dtype=F32),
        vmem(ntp - 1, 8, rows, dtype=F32),
        vmem(nvec, WIDE, dtype=F32),
        vmem(nseq - 1, nvec, WIDE, dtype=F32),
        vmem(nvec, WIDE, dtype=F32),
        vmem(ntp - 1, nvec, WIDE, dtype=F32),
        vmem(heads, share, band, features),
        vmem(heads, share, band, 3 * local_width),
        vmem(ntp, band, local_width),
        vmem(ntp - 1, band, local_width),
        *GradScatter.buffers(dims, band, features),
        *GradScatter.buffers(dims, band, 3 * local_width),
    ]
    sems = (
        [dma(CHUNKS, heads - 1)] * 2 + [dma(CHUNKS, share - 1)] * 2 + [dma(CHUNKS, heads - 1)] * 2
        + [dma(CHUNKS, ntp)] * 4 + [dma(ntp - 1)] * 4 + [dma(nseq - 1)] * 2 + [dma(ntp - 1)] * 4
        + GradScatter.semaphores(dims, 2) + [dma(4)]
    )
    return pl.pallas_call(
        functools.partial(tail_kernel, dims),
        out_shape=outs,
        in_specs=[ANYWHERE] * 4 + [IN_VMEM] * 8,
        out_specs=[IN_VMEM] * len(outs),
        scratch_shapes=scratch + sems,
        name="tail",
        compiler_params=pltpu.CompilerParams(
            collective_id=3, has_side_effects=True, vmem_limit_bytes=60 << 20
        ),
    )(dq, dkv, h1, x_parts, da, mixed, stats, gain, wq, wk, wv, vec)


def on_device(
    hidden_in,
    norm_gain,
    norm_shift,
    query_weight,
    query_bias,
    key_weight,
    value_weight,
    value_bias,
    output_weight,
    output_bias,
    feed_gain,
    feed_shift,
    inner_weight,
    inner_bias,
    outer_weight,
    outer_bias,
    doc_blocks,
    doc_padding,
    random_picks,
    cotangent,
):
    nrows, block_len, width = hidden_in.shape
    rows = nrows * block_len
    nseq, ntp = lax.axis_size("seq"), lax.axis_size("tp")
    tp = lax.axis_index("tp")
    local_width = query_weight.shape[1]
    heads = local_width // HEAD_DIM
    share = nseq // heads
    dims = (heads, share, nseq, ntp)
    features = width * ntp
    per = features // WIDE
    cot = cotangent.reshape(rows, width)
    q, kv, h1, x_parts, g_first, rest, output_full, x_mine, stats, table = run_head(
        dims, nrows, doc_blocks, doc_padding, random_picks.T, hidden_in.reshape(rows, width),
        norm_gain[None, :], norm_shift[None, :], query_weight, query_bias[None, :],
        key_weight, value_weight, value_bias[None, :], cot, output_weight,
    )
    g_rest = lax.all_gather(rest, "tp", axis=0)
    q = q.reshape(heads * rows, WIDE)
    kv = kv.reshape(nseq * rows, WIDE)
    sds = jax.ShapeDtypeStruct
    packed, res = local_call(
        functools.partial(forward_kernel, dims, nrows, 1),
        "attention_forward",
        (sds((heads * rows // 2, WIDE), BF16), sds((heads * rows, WIDE), F32)),
        2,
    )(table, q, kv)
    out_sum, do, da, mixed, vec, inner_part, outer_part = run_middle(
        dims, packed.reshape(heads, rows // 2, WIDE), g_first, g_rest, output_full,
        inner_weight, outer_weight, x_mine, output_bias[None, :], feed_gain[None, :],
        feed_shift[None, :], inner_bias[None, :],
    )
    result = lax.psum_scatter(out_sum, "tp", scatter_dimension=0)
    dq, dkv = local_call(
        functools.partial(backward_kernel, dims, nrows, 1),
        "attention_backward",
        (sds((heads * rows // 2, WIDE), BF16), sds((nseq * rows, WIDE), BF16)),
        4,
        [pltpu.VMEM((nseq * rows, WIDE), F32)],
    )(table, q, do.reshape(heads * rows // 2, WIDE), res, kv)
    grad_x, output_part, query_part, key_part, value_part, vectors = run_tail(
        dims, dq.reshape(heads, rows // 2, WIDE), dkv.reshape(share, heads, rows, WIDE), h1, x_parts,
        da, mixed, stats, norm_gain[None, :], query_weight, key_weight, value_weight, vec,
    )
    my_bias = lax.dynamic_slice_in_dim(outer_bias, tp * width, width, 0)
    layer_out = (result.astype(F32) + my_bias).astype(BF16).reshape(hidden_in.shape)
    wide = vectors[: 6 * per].reshape(6, features)
    narrow = vectors[6 * per :].reshape(-1)
    return (
        layer_out,
        grad_x.reshape(hidden_in.shape),
        wide[0],
        wide[1],
        query_part,
        0.125 * narrow[:local_width],
        key_part,
        value_part,
        narrow[2 * local_width : 3 * local_width],
        output_part.T,
        wide[2],
        wide[3],
        wide[4],
        inner_part,
        narrow[3 * local_width :],
        outer_part.T,
        wide[5],
    )


def solution(mesh):
    return jax.shard_map(
        on_device,
        mesh=mesh,
        in_specs=(
            P(None, "seq", "tp"),
            P(),
            P(),
            P(None, "tp"),
            P("tp"),
            P(None, "tp"),
            P(None, "tp"),
            P("tp"),
            P("tp", None),
            P(),
            P(),
            P(),
            P(None, "tp"),
            P("tp"),
            P("tp", None),
            P(),
            P(),
            P(),
            P(),
            P(None, "seq", "tp"),
        ),
        out_specs=(
            P(None, "seq", "tp"),
            P(None, "seq", "tp"),
            P(),
            P(),
            P("seq", "tp"),
            P("tp"),
            P("seq", "tp"),
            P("seq", "tp"),
            P("tp"),
            P("tp", "seq"),
            P(),
            P(),
            P(),
            P("seq", "tp"),
            P("tp"),
            P("tp", "seq"),
            P(),
        ),
        check_vma=False,
    )
```

```python
import functools
import math

import jax
import jax.numpy as jnp
from jax import lax
from jax.experimental import pallas as pl
from jax.experimental.pallas import tpu as pltpu
from jax.sharding import PartitionSpec as P

HEAD_DIM = 64
BLK = 64
GLOBAL = 2
SLOTS = 8
WIDE = 2 * HEAD_DIM
CHUNKS = 4
COT_CHUNKS = 1
ROUNDS = 2
NEG = -1e30
NT = (((1,), (1,)), ((), ()))
TN = (((0,), (0,)), ((), ()))
MESH = pl.DeviceIdType.MESH
F32, BF16 = jnp.float32, jnp.bfloat16


def split_by(value, count):
    if count & (count - 1) == 0:
        return value >> (count.bit_length() - 1), value & (count - 1)
    return value // count, value % count


def remote(src, dst, send_sem, recv_sem, device):
    return pltpu.make_async_remote_copy(
        src_ref=src, dst_ref=dst, send_sem=send_sem, recv_sem=recv_sem,
        device_id=device, device_id_type=MESH,
    )


def greet(peers):
    barrier = pltpu.get_barrier_semaphore()
    for peer in peers:
        pl.semaphore_signal(barrier, inc=1, device_id=peer, device_id_type=MESH)
    pl.semaphore_wait(barrier, len(peers))


def add_up(*terms):
    total = terms[0].astype(F32)
    for term in terms[1:]:
        total = total + term.astype(F32)
    return total


def swap_halves(value):
    return pltpu.roll(value, HEAD_DIM, 1)


def low_half(value):
    return lax.broadcasted_iota(jnp.int32, value.shape, 1) < HEAD_DIM


def mix_pair(left, right):
    low = low_half(left)
    return (
        jnp.where(low, left, swap_halves(right)),
        jnp.where(low, swap_halves(left), right),
    )


def unpack_pair(left, right):
    even, odd = mix_pair(left.astype(F32), right.astype(F32))
    tiles = []
    for start in range(0, left.shape[0], BLK):
        tiles += [even[start : start + BLK], odd[start : start + BLK]]
    return jnp.concatenate(tiles, axis=0).astype(BF16)


def pack_pair(value):
    lefts, rights = [], []
    for start in range(0, value.shape[0], 2 * BLK):
        left, right = mix_pair(value[start : start + BLK], value[start + BLK : start + 2 * BLK])
        lefts.append(left)
        rights.append(right)
    return jnp.concatenate(lefts, axis=0).astype(BF16), jnp.concatenate(rights, axis=0).astype(BF16)


def dma(*shape):
    return pltpu.SemaphoreType.DMA(tuple(max(size, 1) for size in shape))


def vmem(*shape, dtype=BF16):
    return pltpu.VMEM(shape, dtype)


IN_VMEM = pl.BlockSpec(memory_space=pltpu.VMEM)
IN_SMEM = pl.BlockSpec(memory_space=pltpu.SMEM)
ANYWHERE = pl.BlockSpec(memory_space=pl.ANY)


class Place:
    def __init__(self, dims):
        self.heads, self.share, self.nseq, self.ntp = dims
        self.seq, self.tp = lax.axis_index("seq"), lax.axis_index("tp")
        self.head, self.part = self.seq // self.share, lax.rem(self.seq, self.share)

    def partner(self, step):
        other = lax.rem(self.part + step, self.share)
        return other, (self.head * self.share + other, self.tp)

    def across(self, step):
        other = lax.rem(self.head + step, self.heads)
        return other, (other * self.share + self.part, self.tp)

    def along(self, step):
        other = lax.rem(self.tp + step, self.ntp)
        return other, (self.seq, other)

    def apart(self, step):
        far, near = step // self.heads, step % self.heads
        head = lax.rem(self.head + near, self.heads)
        tp = lax.rem(self.tp + far, self.ntp)
        return head, tp, (head * self.share + self.part, tp)


def fill_table(place, docs_ref, pads_ref, picks_ref, table_ref, nrows):
    nblocks = table_ref.shape[1]
    block = lax.broadcasted_iota(jnp.int32, (1, nblocks), 1)

    def doc_step(doc, state):
        start, first, last, pad = state
        stop = start + docs_ref[doc]
        inside = (block >= start) & (block < stop)
        first = jnp.where(inside, start, first)
        last = jnp.where(inside, stop - 1, last)
        pad = jnp.where(inside, pads_ref[doc], pad)
        return stop, first, last, pad

    zero = jnp.zeros((1, nblocks), jnp.int32)
    _, first, last, pad = lax.fori_loop(
        0, docs_ref.shape[0], doc_step, (jnp.int32(0), zero, zero, zero)
    )
    length = last - first + 1
    picks = []
    for index in range(picks_ref.shape[0]):
        pick = picks_ref[index : index + 1, :]
        whole = (pick.astype(F32) / length.astype(F32)).astype(jnp.int32)
        left = pick - whole * length
        left = jnp.where(left < 0, left + length, left)
        left = jnp.where(left >= length, left - length, left)
        picks.append(first + left)
    glob = block - first < GLOBAL
    is_long = glob & (last - first >= SLOTS)
    never = block < 0
    p0, p1, p2 = picks
    fresh = lambda pick: (pick >= first + GLOBAL) & ((pick > block + 1) | (pick < block - 1))
    near = [
        (block - 1, ~never),
        (block, ~never),
        (block + 1, block < last),
        (first, ~never),
        (first + 1, block - 1 > first + 1),
        (p0, fresh(p0)),
        (p1, fresh(p1) & (p1 != p0)),
        (p2, fresh(p2) & (p2 != p0) & (p2 != p1)),
    ]
    for index, (other, use) in enumerate(near):
        whole = first + index
        use = (glob & (whole <= last) & ~is_long) | (~glob & use)
        other = jnp.where(use, jnp.where(glob, whole, other), block)
        live = jnp.where(use, jnp.where(other == last, BLK - pad, BLK), 0)
        table_ref[index : index + 1, :] = row_of(place, other, nrows) * WIDE + live
    table_ref[SLOTS : SLOTS + 1, :] = first
    table_ref[SLOTS + 1 : SLOTS + 2, :] = last
    table_ref[SLOTS + 2 : SLOTS + 3, :] = pad


def head_kernel(
    dims, nrows, docs_ref, pads_ref, picks_ref, x_ref, gain_ref, shift_ref,
    wq_ref, bq_ref, wk_ref, wv_ref, bv_ref, cot_ref, wo_ref,
    q_out, kv_out, h1_out, xs_out, g_out, rest_out, wo_out, xt_out, stat_out, table_out,
    xs, h1, qbuf, kvbuf, right_s, right_r, left_s, left_r, q_s, q_r, kv_s, kv_r, on_s, on_r,
    wz_s, wz_r, wa_s, wa_r, wp_s, wp_r, local,
):
    place = Place(dims)
    heads, share, nseq, ntp = dims
    head, part, seq, tp = place.head, place.part, place.seq, place.tp
    rows, width = x_ref.shape
    features = width * ntp
    chunk_rows = rows // CHUNKS

    def chunk_of(chunk):
        return pl.ds(chunk * chunk_rows, chunk_rows)

    def traveller(chunk, index):
        if chunk < CHUNKS:
            return xs.at[index, chunk_of(chunk)]
        return g_out.at[index, chunk_of(chunk - CHUNKS)]

    def rightward(chunk, index):
        spot = traveller(chunk, index)
        return remote(
            spot, spot, right_s.at[chunk, index], right_r.at[chunk, index], (seq, tp + 1)
        )

    def leftward(chunk, index):
        spot = traveller(chunk, index)
        return remote(spot, spot, left_s.at[chunk, index], left_r.at[chunk, index], (seq, tp - 1))

    def q_copy(chunk, step):
        other, device = place.across(step)
        return remote(
            qbuf.at[other, chunk_of(chunk)], q_out.at[head, chunk_of(chunk)],
            q_s.at[chunk, step - 1], q_r.at[chunk, step - 1], device,
        )

    def kv_copy(chunk, step):
        other, device = place.across(step)
        return remote(
            kvbuf.at[other, chunk_of(chunk)], kv_out.at[part, head, chunk_of(chunk)],
            kv_s.at[chunk, step - 1], kv_r.at[chunk, step - 1], device,
        )

    def kv_on(chunk, hop, step):
        owner = lax.rem(head + heads - hop, heads)
        spot = kv_out.at[part, owner, chunk_of(chunk)]
        source = kvbuf.at[head, chunk_of(chunk)] if hop == 0 else spot
        return remote(
            source, spot, on_s.at[chunk, hop, step - 1], on_r.at[chunk, hop, step - 1],
            place.partner(step)[1],
        )

    def own_send(chunk):
        @pl.when(tp < ntp - 1)
        def _():
            rightward(chunk, tp).start()

        @pl.when(tp > 0)
        def _():
            leftward(chunk, tp).start()

    def pass_on(chunk):
        for hop in range(1, ntp):
            below, above = tp - hop, tp + hop

            @pl.when(below >= 0)
            def _():
                rightward(chunk, below).wait_recv()

                @pl.when(tp < ntp - 1)
                def _():
                    rightward(chunk, below).start()

            @pl.when(above < ntp)
            def _():
                leftward(chunk, above).wait_recv()

                @pl.when(tp > 0)
                def _():
                    leftward(chunk, above).start()

    def compute(chunk):
        here = chunk_of(chunk)
        x = jnp.concatenate([xs[index, here] for index in range(ntp)], axis=1).astype(F32)
        mean = jnp.sum(x, axis=1, keepdims=True) * (1.0 / features)
        centered = x - mean
        spread = jnp.sum(centered * centered, axis=1, keepdims=True) * (1.0 / features)
        scale = lax.rsqrt(spread + 1e-05)
        normed = (centered * scale * gain_ref[...] + shift_ref[...]).astype(BF16)
        h1[here] = normed
        stat_out[here, 0:1] = mean
        stat_out[here, 1:2] = scale
        q = (jnp.dot(normed, wq_ref[...], preferred_element_type=F32) + bq_ref[...]) * 0.125
        k = jnp.dot(normed, wk_ref[...], preferred_element_type=F32)
        v = jnp.dot(normed, wv_ref[...], preferred_element_type=F32) + bv_ref[...]
        for index in range(0, heads, 2):
            lanes = slice(index * HEAD_DIM, (index + 2) * HEAD_DIM)
            kv = mix_pair(k[:, lanes], v[:, lanes])
            low = low_half(q[:, lanes])
            qs = (q[:, lanes], swap_halves(q[:, lanes]))
            for off in range(2):
                kvbuf[index + off, here] = kv[off].astype(BF16)
                qbuf[index + off, here] = jnp.where(low, qs[off], 0.0).astype(BF16)

    def hand_on(chunk):
        for hop in range(heads):
            if hop:
                kv_copy(chunk, hop).wait_recv()
            for step in range(1, share):
                kv_on(chunk, hop, step).start()

    slice_rows = wo_out.shape[3]
    half = lax.rem(part, 2)

    def wo_along(step):
        start = pl.multiple_of((head * 2 + half) * slice_rows, slice_rows)
        return remote(
            wo_ref.at[pl.ds(start, slice_rows)], wo_out.at[tp, head, half],
            wz_s.at[step - 1], wz_r.at[step - 1], place.along(step)[1],
        )

    def wo_across(step):
        spot = wo_out.at[:, head, half]
        return remote(spot, spot, wa_s.at[step - 1], wa_r.at[step - 1], place.across(step)[1])

    def wo_swap():
        spot = wo_out.at[:, :, half]
        return remote(spot, spot, wp_s.at[0], wp_r.at[0], (seq + 1 - 2 * half, tp))

    xs[tp] = x_ref[...]
    own_rows = pl.ds(pl.multiple_of((head * 2 + half) * slice_rows, slice_rows), slice_rows)
    early = [
        pltpu.make_async_copy(wo_ref.at[own_rows], wo_out.at[tp, head, half], local.at[5]),
        pltpu.make_async_copy(cot_ref.at[pl.ds(0, g_out.shape[1])], g_out.at[tp], local.at[6]),
    ]
    for copy in early:
        copy.start()
    greet(
        [place.partner(step)[1] for step in range(1, share)]
        + [place.across(step)[1] for step in range(1, heads)]
        + [place.along(step)[1] for step in range(1, ntp)]
    )
    for step in range(1, ntp):
        wo_along(step).start()
    own_send(0)
    own_send(1)
    fill_table(place, docs_ref, pads_ref, picks_ref, table_out, nrows)
    for copy in early:
        copy.wait()
    for step in range(1, ntp):
        wo_along(step).wait_recv()
    for step in range(1, heads):
        wo_across(step).start()
    for chunk in range(CHUNKS):
        if chunk > 0:
            own_send(chunk + 1)
        pass_on(chunk)
        compute(chunk)
        for step in range(1, heads):
            kv_copy(chunk, step).start()
        for step in range(1, heads):
            q_copy(chunk, step).start()
        if chunk > 0:
            hand_on(chunk - 1)
        if chunk == 2:
            for step in range(1, heads):
                wo_across(step).wait_recv()
            wo_swap().start()
    pairs = [
        (qbuf.at[head], q_out.at[head]),
        (kvbuf.at[head], kv_out.at[part, head]),
        (h1, h1_out),
        (xs, xs_out),
        (cot_ref.at[pl.ds(g_out.shape[1], rest_out.shape[0])], rest_out),
    ]
    copies = [
        pltpu.make_async_copy(source, target, local.at[index])
        for index, (source, target) in enumerate(pairs)
    ]
    for copy in copies:
        copy.start()
    mine = pl.ds(pl.multiple_of(tp * (rows // ntp), rows // ntp), rows // ntp)
    xt_out[...] = xs[:, mine]
    hand_on(CHUNKS - 1)
    for chunk in range(CHUNKS, CHUNKS + COT_CHUNKS):
        if chunk + 1 < CHUNKS + COT_CHUNKS:
            own_send(chunk + 1)
        pass_on(chunk)
    wo_swap().wait()
    for step in range(1, ntp):
        wo_along(step).wait_send()
    for step in range(1, heads):
        wo_across(step).wait_send()
    for copy in copies:
        copy.wait()
    for chunk in range(CHUNKS):
        for step in range(1, heads):
            q_copy(chunk, step).wait_recv()
        for hop in range(heads):
            for step in range(1, share):
                kv_on(chunk, hop, step).wait_recv()
    for chunk in range(CHUNKS):
        for step in range(1, heads):
            q_copy(chunk, step).wait_send()
            kv_copy(chunk, step).wait_send()
        for hop in range(heads):
            for step in range(1, share):
                kv_on(chunk, hop, step).wait_send()
    for chunk in range(CHUNKS + COT_CHUNKS):
        for index in range(ntp):
            @pl.when((tp >= index) & (tp < ntp - 1))
            def _():
                rightward(chunk, index).wait_send()

            @pl.when((tp <= index) & (tp > 0))
            def _():
                leftward(chunk, index).wait_send()


def run_head(dims, nrows, docs, pads, picks, x, *params):
    heads, share, nseq, ntp = dims
    rows, width = x.shape
    nblocks = picks.shape[1]
    first = rows // CHUNKS * COT_CHUNKS
    sds = jax.ShapeDtypeStruct
    outs = [
        sds((heads, rows, WIDE), BF16),
        sds((share, heads, rows, WIDE), BF16),
        sds((rows, width * ntp), BF16),
        sds((ntp, rows, width), BF16),
        sds((ntp, first, width), BF16),
        sds((rows - first, width), BF16),
        sds((ntp, heads, 2, params[-1].shape[0] // (2 * heads), params[-1].shape[1]), BF16),
        sds((ntp, rows // ntp, width), BF16),
        sds((rows, 2), F32),
        sds((16, nblocks), jnp.int32),
    ]
    scratch = [
        vmem(ntp, rows, width),
        vmem(rows, width * ntp),
        vmem(heads, rows, WIDE),
        vmem(heads, rows, WIDE),
    ]
    sems = (
        [dma(CHUNKS + COT_CHUNKS, ntp)] * 4 + [dma(CHUNKS, heads - 1)] * 4
        + [dma(CHUNKS, heads, share - 1)] * 2 + [dma(ntp - 1)] * 2 + [dma(heads - 1)] * 2
        + [dma(1)] * 2 + [dma(7)]
    )
    return pl.pallas_call(
        functools.partial(head_kernel, dims, nrows),
        out_shape=outs,
        in_specs=[IN_SMEM, IN_SMEM] + [IN_VMEM] * len(params) + [ANYWHERE] * 2,
        out_specs=[ANYWHERE] * 7 + [IN_VMEM] * 3,
        scratch_shapes=scratch + sems,
        name="head",
        cost_estimate=pl.CostEstimate(flops=60 << 30, bytes_accessed=8 << 20, transcendentals=0),
        compiler_params=pltpu.CompilerParams(
            collective_id=1, has_side_effects=True, vmem_limit_bytes=60 << 20
        ),
    )(docs, pads, picks, x, *params)


def block_of(place, query, nrows):
    source, row = split_by(query, nrows)
    return row * place.nseq + source * place.share + place.part


def row_of(place, block, nrows):
    row, holder = split_by(block, place.nseq)
    head, part = split_by(holder, place.share)
    return ((part * place.heads + head) * nrows + row) * BLK


def near_slots(table_ref, block):
    entries = [table_ref[index, block] for index in range(SLOTS)]
    slots = [pl.multiple_of(entry >> 7, BLK) for entry in entries]
    return slots, [entry & (WIDE - 1) for entry in entries]


def long_slots(place, table_ref, block, chunk, nrows):
    first, last = table_ref[SLOTS, block], table_ref[SLOTS + 1, block]
    final = BLK - table_ref[SLOTS + 2, block]
    slots, lives = [], []
    for index in range(SLOTS):
        wanted = first + chunk * SLOTS + index
        slots.append(pl.multiple_of(row_of(place, jnp.minimum(wanted, last), nrows), BLK))
        lives.append(jnp.where(wanted < last, BLK, jnp.where(wanted == last, final, 0)))
    return slots, lives


def for_long(place, table_ref, nquery, nrows, body):
    def step(query, carry):
        block = block_of(place, query, nrows)
        first, last = table_ref[SLOTS, block], table_ref[SLOTS + 1, block]

        @pl.when((block - first < GLOBAL) & (last - first >= SLOTS))
        def _():
            body(query, block, (last - first + SLOTS) >> 3)

        return carry

    lax.fori_loop(0, nquery, step, 0)


def bias_row(lives):
    lane = lax.broadcasted_iota(jnp.int32, (1, WIDE), 1)
    parts = []
    for index in range(0, SLOTS, 2):
        bound = jnp.where(lane < BLK, lives[index], lives[index + 1] + BLK)
        parts.append(jnp.where(lane < bound, 0.0, NEG))
    return jnp.concatenate(parts, axis=1)


def take(ref, slots):
    return jnp.concatenate([ref[pl.ds(slot, BLK), :] for slot in slots], axis=0)


def forward_kernel(dims, nrows, unroll, table_ref, q_ref, kv_ref, out_ref, res_ref):
    place = Place(dims)
    nquery = q_ref.shape[0] // BLK
    upper = lax.broadcasted_iota(jnp.int32, (BLK, WIDE), 1) >= HEAD_DIM

    def finish(query, top, total, accum):
        value = accum / total
        res_ref[pl.ds(query * BLK, BLK), :] = jnp.where(upper, value, top + jnp.log(total))
        return value

    def scores_of(query, slots, lives):
        kv = take(kv_ref, slots)
        scores = lax.dot_general(
            q_ref[pl.ds(query * BLK, BLK), :], kv, NT, preferred_element_type=F32
        )
        return kv, scores + bias_row(lives)

    def near_one(query):
        kv, scores = scores_of(query, *near_slots(table_ref, block_of(place, query, nrows)))
        top = jnp.max(scores, axis=1, keepdims=True)
        weights = jnp.exp(scores - top)
        total = jnp.sum(weights, axis=1, keepdims=True)
        accum = jnp.dot(weights.astype(BF16), kv, preferred_element_type=F32)
        return finish(query, top, total, accum)

    def near_step(index, carry):
        for offset in range(unroll):
            pair = index * unroll + offset
            even, odd = near_one(2 * pair), near_one(2 * pair + 1)
            out_ref[pl.ds(pair * BLK, BLK), :] = jnp.where(upper, odd, swap_halves(even)).astype(BF16)
        return carry

    lax.fori_loop(0, nquery // (2 * unroll), near_step, 0)

    def long_body(query, block, chunks):
        def chunk_step(chunk, state):
            top, total, accum = state
            kv, scores = scores_of(query, *long_slots(place, table_ref, block, chunk, nrows))
            new_top = jnp.maximum(top, jnp.max(scores, axis=1, keepdims=True))
            weights = jnp.exp(scores - new_top)
            decay = jnp.exp(top - new_top)
            total = total * decay + jnp.sum(weights, axis=1, keepdims=True)
            accum = accum * decay + jnp.dot(weights.astype(BF16), kv, preferred_element_type=F32)
            return new_top, total, accum

        start = (
            jnp.full((BLK, 1), NEG, F32),
            jnp.zeros((BLK, 1), F32),
            jnp.zeros((BLK, WIDE), F32),
        )
        value = finish(query, *lax.fori_loop(0, chunks, chunk_step, start))
        spot = pl.ds(pl.multiple_of((query >> 1) * BLK, BLK), BLK)
        is_odd = (query & 1) == 1
        moved = jnp.where(is_odd, value, swap_halves(value))
        out_ref[spot, :] = jnp.where(upper == is_odd, moved, out_ref[spot, :].astype(F32)).astype(BF16)

    for_long(place, table_ref, nquery, nrows, long_body)


def backward_kernel(
    dims, nrows, unroll, table_ref, q_ref, do_ref, res_ref, kv_ref, dq_ref, dkv_ref, sum_ref
):
    place = Place(dims)
    nquery = q_ref.shape[0] // BLK
    upper = lax.broadcasted_iota(jnp.int32, (BLK, WIDE), 1) >= HEAD_DIM
    sum_ref[...] = jnp.zeros_like(sum_ref)

    def load(query, packed, is_odd):
        moved = jnp.where(is_odd, packed, swap_halves(packed))
        grad = jnp.where(upper, moved, 0.0)
        rows = pl.ds(query * BLK, BLK)
        both = jnp.concatenate([q_ref[rows, :], grad.astype(BF16)], axis=0)
        res = res_ref[rows, :]
        delta = jnp.sum(res * grad, axis=1, keepdims=True)
        return both, res[:, :1], delta

    def terms(both, log_total, delta, slots, lives):
        kv = take(kv_ref, slots)
        pair = lax.dot_general(both, kv, NT, preferred_element_type=F32)
        probs = jnp.exp(pair[:BLK] + bias_row(lives) - log_total)
        grad_scores = (probs * (pair[BLK:] - delta)).astype(BF16)
        weights = jnp.concatenate([grad_scores, probs.astype(BF16)], axis=0)
        dkv = lax.dot_general(weights, both, TN, preferred_element_type=F32)
        dq = jnp.dot(grad_scores, kv, preferred_element_type=F32)
        return dq, dkv

    def scatter(slots, dkv):
        for index, slot in enumerate(slots):
            sum_ref[pl.ds(slot, BLK), :] += dkv[index * BLK : (index + 1) * BLK]

    def near_step(index, carry):
        done = []
        for offset in range(unroll):
            pair = index * unroll + offset
            packed = do_ref[pl.ds(pair * BLK, BLK), :].astype(F32)
            grads = []
            for is_odd in (False, True):
                query = 2 * pair + int(is_odd)
                slots, lives = near_slots(table_ref, block_of(place, query, nrows))
                dq, dkv = terms(*load(query, packed, is_odd), slots, lives)
                grads.append(dq)
                done.append((slots, dkv))
            dq_ref[pl.ds(pair * BLK, BLK), :] = jnp.where(
                upper, swap_halves(grads[1]), grads[0]
            ).astype(BF16)
        for slots, dkv in done:
            scatter(slots, dkv)
        return carry

    lax.fori_loop(0, nquery // (2 * unroll), near_step, 0)

    def long_body(query, block, chunks):
        is_odd = (query & 1) == 1
        spot = pl.ds(pl.multiple_of((query >> 1) * BLK, BLK), BLK)
        loaded = load(query, do_ref[spot, :].astype(F32), is_odd)

        def chunk_step(chunk, total):
            slots, lives = long_slots(place, table_ref, block, chunk, nrows)
            dq, dkv = terms(*loaded, slots, lives)
            scatter(slots, dkv)
            return total + dq

        total = lax.fori_loop(0, chunks, chunk_step, jnp.zeros((BLK, WIDE), F32))
        moved = jnp.where(is_odd, swap_halves(total), total)
        dq_ref[spot, :] = jnp.where(upper == is_odd, moved, dq_ref[spot, :].astype(F32)).astype(BF16)

    for_long(place, table_ref, nquery, nrows, long_body)
    dkv_ref[...] = sum_ref[...].astype(BF16)


def local_call(kernel, name, out_shape, nvmem, scratch=()):
    return pl.pallas_call(
        kernel,
        out_shape=out_shape,
        in_specs=[IN_SMEM] + [IN_VMEM] * nvmem,
        out_specs=jax.tree.map(lambda _: IN_VMEM, out_shape),
        scratch_shapes=list(scratch),
        name=name,
        cost_estimate=pl.CostEstimate(flops=30 << 30, bytes_accessed=8 << 20, transcendentals=0),
        compiler_params=pltpu.CompilerParams(vmem_limit_bytes=56 << 20),
    )


class GradScatter:
    def __init__(self, place, source, bufs, sems):
        self.place, self.source = place, source
        self.land, self.pair, self.far = bufs
        self.send1, self.recv1, self.send2, self.recv2 = sems

    @staticmethod
    def buffers(dims, band, cols):
        heads, share = dims[:2]
        return [
            vmem(max(share - 1, 1), heads, band, cols),
            vmem(heads, band, cols),
            vmem(max(heads - 1, 1), band, cols),
        ]

    @staticmethod
    def semaphores(dims, count):
        return [dma(count, dims[1] - 1)] * 2 + [dma(count, dims[0] - 1)] * 2

    def near(self, step):
        other, device = self.place.partner(step)
        return remote(
            self.source.at[:, other], self.land.at[step - 1],
            self.send1.at[step - 1], self.recv1.at[step - 1], device,
        )

    def across(self, step):
        other, device = self.place.across(step)
        return remote(
            self.pair.at[other], self.far.at[step - 1],
            self.send2.at[step - 1], self.recv2.at[step - 1], device,
        )

    def start_near(self):
        for step in range(1, self.place.share):
            self.near(step).start()

    def sum_near(self):
        place = self.place
        for step in range(1, place.share):
            self.near(step).wait_recv()

        def body(head, carry):
            parts = [self.source[head, place.part]]
            parts += [self.land[step, head] for step in range(place.share - 1)]
            self.pair[head] = add_up(*parts).astype(BF16)
            return carry

        lax.fori_loop(0, place.heads, body, 0)

    def start_across(self):
        self.sum_near()
        for step in range(1, self.place.heads):
            self.across(step).start()

    def result(self):
        heads = self.place.heads
        for step in range(1, heads):
            self.across(step).wait_recv()
        return add_up(self.pair[self.place.head], *[self.far[step] for step in range(heads - 1)])

    def finish_near(self):
        for step in range(1, self.place.share):
            self.near(step).wait_send()

    def finish(self):
        self.finish_near()
        for step in range(1, self.place.heads):
            self.across(step).wait_send()


def gelu_pair(value):
    root = math.sqrt(2.0 / math.pi)
    square = value * value
    curve = jnp.tanh(root * value * (1.0 + 0.044715 * square))
    half = 0.5 * (1.0 + curve)
    slope = half + 0.5 * value * (1.0 - curve * curve) * (root * (1.0 + 3 * 0.044715 * square))
    return value * half, slope


def middle_kernel(
    dims,
    o_ref, g0_hbm, g1_hbm, wo_hbm, wi_hbm, wu_hbm, xt_ref, ob_ref, gain_ref, shift_ref, ib_ref,
    sum_out, do_out, da_out, mixed_out, vec_out, gi_out, gu_out,
    g_ref, wo_ref, wi_ref, wu_ref, o_in, x1, xhat, scale, h2, act, dpre, outb, terms, from_left, from_right, do_buf, ib_sum, gi, gu, land_i, land_u, pair_i, pair_u, far_i, far_u,
    *rest,
):
    place = Place(dims)
    heads, share, nseq, ntp = dims
    head, part, seq, tp = place.head, place.part, place.seq, place.tp
    sems = rest
    (o_s, o_r, hr_s, hr_r, hl_s, hl_r, tr_s, tr_r, tl_s, tl_r, do_s, do_r,
     g1_s, g1_r, g2_s, g2_r, local) = sems
    rows, width = g_ref.shape[1:]
    features = width * ntp
    tokens = rows // ntp
    rounds = ROUNDS
    span = tokens // rounds
    pieces = tokens // (2 * BLK)
    places = 2 * ntp - 1
    band = features // heads
    per = features // WIDE

    def packed_rows(index, count=tokens // 2):
        return pl.ds(pl.multiple_of(index * count, count), count)

    def span_of(index):
        return pl.ds(pl.multiple_of(index * span, span), span)

    def o_copy(step):
        to_head, to_tp, device = place.apart(step)
        return remote(
            o_ref.at[to_head, packed_rows(to_tp)], o_in.at[tp * heads + head],
            o_s.at[step], o_r.at[step], device,
        )

    def do_copy(index, step):
        to_head, to_tp, device = place.apart(step)
        return remote(
            do_buf.at[to_tp * heads + to_head, packed_rows(index, BLK)],
            do_out.at[head, packed_rows(tp * pieces + index, BLK)],
            do_s.at[index, step], do_r.at[index, step], device,
        )

    def h2_copy(index, owner, right):
        spot = h2.at[owner, span_of(index)]
        if right:
            return remote(spot, spot, hr_s.at[index, owner], hr_r.at[index, owner], (seq, tp + 1))
        return remote(spot, spot, hl_s.at[index, owner], hl_r.at[index, owner], (seq, tp - 1))

    def term_copy(index, owner, right):
        here = span_of(index)
        if right:
            return remote(
                terms.at[owner, here], from_left.at[owner, here],
                tr_s.at[index, owner], tr_r.at[index, owner], (seq, tp + 1),
            )
        return remote(
            terms.at[owner, here], from_right.at[owner, here],
            tl_s.at[index, owner], tl_r.at[index, owner], (seq, tp - 1),
        )

    scatters = [
        GradScatter(place, source, bufs, (g1_s.at[k], g1_r.at[k], g2_s.at[k], g2_r.at[k]))
        for k, (source, bufs) in enumerate(
            ((gi, (land_i, pair_i, far_i)), (gu, (land_u, pair_u, far_u)))
        )
    ]

    first_rows = g0_hbm.shape[1]
    loads = [
        pltpu.make_async_copy(o_ref.at[head, packed_rows(tp)], o_in.at[tp * heads + head], local.at[2]),
        pltpu.make_async_copy(wo_hbm, wo_ref, local.at[3]),
        pltpu.make_async_copy(wi_hbm, wi_ref, local.at[4]),
        pltpu.make_async_copy(wu_hbm, wu_ref, local.at[5]),
        pltpu.make_async_copy(g0_hbm, g_ref.at[:, pl.ds(0, first_rows)], local.at[6]),
        pltpu.make_async_copy(
            g1_hbm, g_ref.at[:, pl.ds(first_rows, rows - first_rows)], local.at[7]
        ),
    ]
    for load in loads:
        load.start()
    greet(
        [place.partner(step)[1] for step in range(1, share)]
        + [place.apart(step)[2] for step in range(1, heads * ntp)]
    )
    for step in range(heads * ntp - 1, 0, -1):
        o_copy(step).start()
    ib_sum[...] = jnp.zeros_like(ib_sum)
    for load in loads:
        load.wait()
    for step in range(1, heads * ntp):
        o_copy(step).wait_recv()

    for index in range(pieces):
        here = slice(index * 2 * BLK, (index + 1) * 2 * BLK)
        half = slice(index * BLK, (index + 1) * BLK)
        mixed = jnp.concatenate(
            [unpack_pair(o_in[i, half], o_in[i + 1, half]) for i in range(0, heads * ntp, 2)], axis=1
        )
        mixed_out[here] = mixed
        base = jnp.concatenate([xt_ref[i, here] for i in range(ntp)], axis=1).astype(F32)
        value = base + ob_ref[...] + jnp.dot(mixed, wo_ref[...].reshape(features, features), preferred_element_type=F32)
        x1[here] = value
        centered = value - jnp.sum(value, axis=1, keepdims=True) * (1.0 / features)
        spread = jnp.sum(centered * centered, axis=1, keepdims=True) * (1.0 / features)
        inverse = lax.rsqrt(spread + 1e-05)
        normed = centered * inverse
        xhat[here] = normed
        scale[here] = jnp.broadcast_to(inverse, (2 * BLK, WIDE))
        h2[tp, here] = (normed * gain_ref[...] + shift_ref[...]).astype(BF16)
        for part_index in range(index * rounds // pieces, (index + 1) * rounds // pieces):

            @pl.when(tp < ntp - 1)
            def _():
                h2_copy(part_index, tp, True).start()

            @pl.when(tp > 0)
            def _():
                h2_copy(part_index, tp, False).start()

    def spot_of(position):
        hop = (position + 1) // 2
        owner = tp + jnp.where(position % 2 == 1, -hop, hop)
        return owner, (owner >= 0) & (owner < ntp)

    def feed(index, owner):
        @pl.when(owner < tp)
        def _():
            h2_copy(index, owner, True).wait_recv()

            @pl.when(tp < ntp - 1)
            def _():
                h2_copy(index, owner, True).start()

        @pl.when(owner > tp)
        def _():
            h2_copy(index, owner, False).wait_recv()

            @pl.when(tp > 0)
            def _():
                h2_copy(index, owner, False).start()

        here = span_of(index)
        wide = span_of(owner * rounds + index)
        pre = jnp.dot(h2[owner, here], wi_ref[...], preferred_element_type=F32) + ib_ref[...]
        value, slope = gelu_pair(pre)
        value = value.astype(BF16)
        act[wide] = value
        grad = jnp.concatenate([g_ref[i, wide] for i in range(ntp)], axis=1)
        back = lax.dot_general(grad, wu_ref[...], NT, preferred_element_type=F32) * slope
        back = back.astype(BF16)
        dpre[wide] = back
        ib_sum[0:1, :] += jnp.sum(back.astype(F32), axis=0, keepdims=True)
        terms[owner, here] = lax.dot_general(
            back, wi_ref[...], NT, preferred_element_type=F32
        ).astype(BF16)

        @pl.when((owner > tp) & (tp == 0))
        def _():
            term_copy(index, owner, True).start()

        @pl.when((owner < tp) & (tp == ntp - 1))
        def _():
            term_copy(index, owner, False).start()

        out = jnp.dot(value, wu_ref[...], preferred_element_type=F32)
        out = out + jnp.where(owner == tp, x1[here], 0.0)
        for i in range(ntp):
            outb[i, wide] = out[:, i * width : (i + 1) * width].astype(BF16)

    def relay_right(index):
        here = span_of(index)
        for owner in range(1, ntp):

            @pl.when((owner > tp) & (tp > 0))
            def _():
                term_copy(index, owner, True).wait_recv()
                terms[owner, here] = add_up(terms[owner, here], from_left[owner, here]).astype(BF16)
                term_copy(index, owner, True).start()

    def relay_left(index):
        here = span_of(index)
        for owner in range(ntp - 2, -1, -1):

            @pl.when((owner < tp) & (tp < ntp - 1))
            def _():
                term_copy(index, owner, False).wait_recv()
                terms[owner, here] = add_up(terms[owner, here], from_right[owner, here]).astype(BF16)
                term_copy(index, owner, False).start()

    def relay(index, first):
        @pl.when((tp < ntp // 2) == first)
        def _():
            relay_right(index)

        @pl.when((tp < ntp // 2) != first)
        def _():
            relay_left(index)

    def feed_step(count, carry):
        index, position = count // places, count % places
        owner, inside = spot_of(position)

        @pl.when(inside)
        def _():
            feed(index, owner)

        @pl.when((index > 0) & (position == 2))
        def _():
            relay(index - 1, True)

        @pl.when((index > 0) & (position == places - 1))
        def _():
            relay(index - 1, False)

        return carry

    lax.fori_loop(0, rounds * places, feed_step, 0)
    save = pltpu.make_async_copy(outb, sum_out, local.at[0])
    save.start()

    def inner_grad(index):
        left = h2[:, :, index * band : (index + 1) * band].reshape(rows, band)
        value = lax.dot_general(left, dpre[...], TN, preferred_element_type=F32)
        gi[index] = value.astype(BF16).reshape(gi.shape[1:])

    def outer_grad(index):
        many = ntp // heads
        left = jnp.concatenate([g_ref[i] for i in range(index * many, (index + 1) * many)], axis=1)
        value = lax.dot_general(left, act[...], TN, preferred_element_type=F32)
        gu[index] = value.astype(BF16).reshape(gu.shape[1:])

    work = [functools.partial(inner_grad, index) for index in range(heads)]
    work += [functools.partial(outer_grad, index) for index in range(heads)]
    def finish(index):
        here = slice(index * 2 * BLK, (index + 1) * 2 * BLK)
        half = slice(index * BLK, (index + 1) * BLK)
        wide = pl.ds(pl.multiple_of(tp * tokens + index * 2 * BLK, 2 * BLK), 2 * BLK)
        for part_index in range(index * rounds // pieces, (index + 1) * rounds // pieces):

            @pl.when(tp > 0)
            def _():
                term_copy(part_index, tp, True).wait_recv()

            @pl.when(tp < ntp - 1)
            def _():
                term_copy(part_index, tp, False).wait_recv()

        grad = terms[tp, here].astype(F32)
        grad = grad + jnp.where(tp > 0, from_left[tp, here].astype(F32), 0.0)
        grad = grad + jnp.where(tp < ntp - 1, from_right[tp, here].astype(F32), 0.0)
        hat = xhat[here]
        inner = grad * gain_ref[...]
        mean0 = jnp.sum(inner, axis=1, keepdims=True) * (1.0 / features)
        mean1 = jnp.sum(inner * hat, axis=1, keepdims=True) * (1.0 / features)
        tail = scale[here, 0:1] * (inner - mean0 - hat * mean1)
        cot = jnp.concatenate([g_ref[i, wide] for i in range(ntp)], axis=1).astype(F32)
        branch = (cot + tail).astype(BF16)
        da_out[here] = branch
        do = lax.dot_general(
            branch, wo_ref[...].reshape(features, features), NT, preferred_element_type=F32
        )
        for i in range(0, heads * ntp, 2):
            pair = pack_pair(do[:, i * HEAD_DIM : (i + 2) * HEAD_DIM])
            do_buf[i, half] = pair[0]
            do_buf[i + 1, half] = pair[1]
        for step in range(heads * ntp - 1, 0, -1):
            do_copy(index, step).start()
        sums = (
            jnp.sum(branch.astype(F32), axis=0, keepdims=True),
            jnp.sum(grad * hat, axis=0, keepdims=True),
            jnp.sum(grad, axis=0, keepdims=True),
        )
        for kind, value in enumerate(sums):
            for sub in range(per):
                row = slice(kind * per + sub, kind * per + sub + 1)
                piece = value[:, sub * WIDE : (sub + 1) * WIDE]
                if index == 0:
                    vec_out[row, :] = piece
                else:
                    vec_out[row, :] += piece
    early = pieces * (rounds - 1) // rounds
    for item in work[:heads]:
        item()
    scatters[0].start_near()
    for index in range(early):
        finish(index)
    relay(rounds - 1, True)
    scatters[0].start_across()
    for item in work[heads:]:
        item()
    scatters[1].start_near()
    relay(rounds - 1, False)
    for index in range(early, pieces):
        finish(index)
    own = pltpu.make_async_copy(
        do_buf.at[tp * heads + head], do_out.at[head, packed_rows(tp)], local.at[1]
    )
    own.start()
    scatters[1].start_across()
    cot = jnp.sum(g_ref[tp].astype(F32), axis=0, keepdims=True)
    for sub in range(per):
        owner, lane = divmod(sub * WIDE, width)
        vec_out[3 * per + sub : 3 * per + sub + 1, :] = jnp.where(
            tp == owner, cot[:, lane : lane + WIDE], 0.0
        )
    for sub in range(ib_sum.shape[1] // WIDE):
        row = 4 * per + sub
        vec_out[row : row + 1, :] = ib_sum[0:1, sub * WIDE : (sub + 1) * WIDE]
    gi_out[...] = scatters[0].result()
    gu_out[...] = scatters[1].result().T
    save.wait()
    own.wait()
    for step in range(1, heads * ntp):
        for index in range(pieces):
            do_copy(index, step).wait_recv()
    for step in range(1, heads * ntp):
        o_copy(step).wait_send()
        for index in range(pieces):
            do_copy(index, step).wait_send()
    for index in range(rounds):
        for owner in range(ntp):
            @pl.when((tp >= owner) & (tp < ntp - 1))
            def _():
                h2_copy(index, owner, True).wait_send()

            @pl.when((tp <= owner) & (tp > 0))
            def _():
                h2_copy(index, owner, False).wait_send()

            @pl.when(tp < owner)
            def _():
                term_copy(index, owner, True).wait_send()

            @pl.when(tp > owner)
            def _():
                term_copy(index, owner, False).wait_send()

    for scatter in scatters:
        scatter.finish()


def run_middle(dims, o, g0, g1, wo, wi, wu, xt, ob, gain, shift, ib):
    heads, share, nseq, ntp = dims
    rows, width = g0.shape[1] + g1.shape[1], g0.shape[2]
    features, hidden = width * ntp, wi.shape[1]
    tokens, band = rows // ntp, features // nseq
    per = features // WIDE
    rounds, pieces = ROUNDS, tokens // (2 * BLK)
    sds = jax.ShapeDtypeStruct
    outs = [
        sds((ntp, rows, width), BF16),
        sds((heads, rows // 2, WIDE), BF16),
        sds((tokens, features), BF16),
        sds((tokens, features), BF16),
        sds((4 * per + hidden // WIDE, WIDE), F32),
        sds((band, hidden), F32),
        sds((hidden, band), F32),
    ]
    count = heads * ntp
    scratch = [
        vmem(ntp, rows, width),
        vmem(*wo.shape),
        vmem(*wi.shape),
        vmem(*wu.shape),
        vmem(count, tokens // 2, WIDE),
        vmem(tokens, features, dtype=F32),
        vmem(tokens, features, dtype=F32),
        vmem(tokens, WIDE, dtype=F32),
        vmem(ntp, tokens, features),
        vmem(rows, hidden),
        vmem(rows, hidden),
        vmem(ntp, rows, width),
        vmem(ntp, tokens, features),
        vmem(ntp, tokens, features),
        vmem(ntp, tokens, features),
        vmem(count, tokens // 2, WIDE),
        vmem(8, hidden, dtype=F32),
        vmem(heads, share, band, hidden),
        vmem(heads, share, band, hidden),
        vmem(max(share - 1, 1), heads, band, hidden),
        vmem(max(share - 1, 1), heads, band, hidden),
        vmem(heads, band, hidden),
        vmem(heads, band, hidden),
        vmem(max(heads - 1, 1), band, hidden),
        vmem(max(heads - 1, 1), band, hidden),
    ]
    sems = (
        [dma(count)] * 2 + [dma(rounds, ntp)] * 8 + [dma(pieces, count)] * 2
        + GradScatter.semaphores(dims, 2) + [dma(8)]
    )
    return pl.pallas_call(
        functools.partial(middle_kernel, dims),
        out_shape=outs,
        in_specs=[ANYWHERE] * 6 + [IN_VMEM] * 5,
        out_specs=[ANYWHERE] * 2 + [IN_VMEM] * 5,
        scratch_shapes=scratch + sems,
        name="middle",
        cost_estimate=pl.CostEstimate(flops=110 << 30, bytes_accessed=8 << 20, transcendentals=0),
        compiler_params=pltpu.CompilerParams(
            collective_id=2, has_side_effects=True, vmem_limit_bytes=63 << 20
        ),
    )(o, g0, g1, wo, wi, wu, xt, ob, gain, shift, ib)


def tail_kernel(
    dims,
    dq_ref, dkv_hbm, h1_hbm, x_hbm, da_ref, mixed_ref, stat_ref, gain_ref, wq_ref, wk_ref, wv_ref, vec_ref,
    gx_ref, ow_ref, oq_ref, ok_ref, ov_ref, vout_ref,
    dkv_own, h1_ref, x_ref, dq_in, dkv_in, dkv_land, dkv_sum, all3, da_in, pbuf, from_left, from_right,
    sums, sums_land, vbuf, vec_land, vsum, vec_far, gw, g3, wbuf, wfar,
    *rest,
):
    place = Place(dims)
    heads, share, nseq, ntp = dims
    head, part, seq, tp = place.head, place.part, place.seq, place.tp
    lands, sems = rest[:6], rest[6:]
    (dq_s, dq_r, kv1_s, kv1_r, kv2_s, kv2_r, right_s, right_r, left_s, left_r,
     da_s, da_r, st_s, st_r, v1_s, v1_r, v2_s, v2_r, w_s, w_r, g1_s, g1_r, g2_s, g2_r, load_s) = sems
    rows, features = h1_ref.shape
    width = features // ntp
    tokens = rows // ntp
    local_width = wq_ref.shape[1]
    chunk_rows = rows // CHUNKS
    band = features // heads
    per = features // WIDE

    def chunk_of(chunk):
        return pl.ds(chunk * chunk_rows, chunk_rows)

    def half_of(chunk):
        return pl.ds(chunk * chunk_rows // 2, chunk_rows // 2)

    def columns_of(index):
        return pl.ds(pl.multiple_of(index * width, width), width)

    def dq_copy(chunk, step):
        other, device = place.across(step)
        return remote(
            dq_ref.at[other, half_of(chunk)], dq_in.at[head, half_of(chunk)],
            dq_s.at[chunk, step - 1], dq_r.at[chunk, step - 1], device,
        )

    def dkv_near(chunk, step):
        other, device = place.partner(step)
        here = chunk_of(chunk)
        return remote(
            dkv_hbm.at[other, :, here], dkv_land.at[step - 1, :, here],
            kv1_s.at[chunk, step - 1], kv1_r.at[chunk, step - 1], device,
        )

    def dkv_copy(chunk, step):
        other, device = place.across(step)
        return remote(
            dkv_sum.at[other, chunk_of(chunk)], dkv_in.at[head, chunk_of(chunk)],
            kv2_s.at[chunk, step - 1], kv2_r.at[chunk, step - 1], device,
        )

    def da_copy(step):
        other, device = place.along(step)
        return remote(
            da_ref.at[:, columns_of(other)], da_in.at[tp], da_s.at[step - 1], da_r.at[step - 1], device
        )

    def rightward(chunk, index):
        return remote(
            pbuf.at[chunk, index], from_left.at[chunk, index],
            right_s.at[chunk, index], right_r.at[chunk, index], (seq, tp + 1),
        )

    def leftward(chunk, index):
        return remote(
            pbuf.at[chunk, index], from_right.at[chunk, index],
            left_s.at[chunk, index], left_r.at[chunk, index], (seq, tp - 1),
        )

    def sums_copy(step):
        return remote(
            sums, sums_land.at[step - 1], st_s.at[step - 1], st_r.at[step - 1], place.along(step)[1]
        )

    def vec_copy(step):
        return remote(
            vbuf, vec_land.at[step - 1], v1_s.at[step - 1], v1_r.at[step - 1],
            (lax.rem(seq + step, nseq), tp),
        )

    def vec_far_copy(step):
        return remote(
            vsum, vec_far.at[step - 1], v2_s.at[step - 1], v2_r.at[step - 1], place.along(step)[1]
        )

    def w_copy(step):
        other, device = place.along(step)
        return remote(wbuf.at[other], wfar.at[step - 1], w_s.at[step - 1], w_r.at[step - 1], device)

    scatters = [
        GradScatter(
            place, source, lands[3 * k : 3 * k + 3], (g1_s.at[k], g1_r.at[k], g2_s.at[k], g2_r.at[k])
        )
        for k, source in enumerate((gw, g3))
    ]

    loads = [
        pltpu.make_async_copy(dkv_hbm.at[part], dkv_own, load_s.at[0]),
        pltpu.make_async_copy(dq_ref.at[head], dq_in.at[head], load_s.at[1]),
        pltpu.make_async_copy(x_hbm, x_ref, load_s.at[2]),
        pltpu.make_async_copy(h1_hbm, h1_ref, load_s.at[3]),
    ]
    for load in loads:
        load.start()
    greet(
        [(lax.rem(seq + step, nseq), tp) for step in range(1, nseq)]
        + [place.along(step)[1] for step in range(1, ntp)]
    )
    for chunk in range(CHUNKS):
        for step in range(1, share):
            dkv_near(chunk, step).start()
    for step in range(1, ntp):
        da_copy(step).start()
    da_in[tp] = da_ref[:, columns_of(tp)]
    vbuf[: 2 * per] = jnp.zeros((2 * per, WIDE), F32)
    vbuf[2 * per : 6 * per] = vec_ref[: 4 * per]
    narrow = 3 * local_width // WIDE
    vbuf[6 * per : 6 * per + narrow] = jnp.zeros((narrow, WIDE), F32)
    vbuf[6 * per + narrow :] = vec_ref[4 * per :]
    loads[0].wait()
    for chunk in range(CHUNKS):
        for step in range(1, heads):
            dq_copy(chunk, step).start()
        for step in range(1, share):
            dkv_near(chunk, step).wait_recv()
        for target in range(heads):
            where = (target, chunk_of(chunk))
            parts = [dkv_own[where]] + [dkv_land[(step,) + where] for step in range(share - 1)]
            dkv_sum[where] = add_up(*parts).astype(BF16)
        for step in range(1, heads):
            dkv_copy(chunk, step).start()
    dkv_in[head] = dkv_sum[head]
    for load in loads[1:]:
        load.wait()

    def output_grad(index):
        value = lax.dot_general(
            da_ref[:, index * band : (index + 1) * band], mixed_ref[...], TN, preferred_element_type=F32
        )
        gw[index] = value.astype(BF16).reshape(gw.shape[1:])

    gain = gain_ref[...]
    lane = lax.broadcasted_iota(jnp.int32, (chunk_rows, WIDE), 1)

    def partial_step(chunk):
        here, half = chunk_of(chunk), half_of(chunk)
        for step in range(1, heads):
            dq_copy(chunk, step).wait_recv()
            dkv_copy(chunk, step).wait_recv()
        three = [[], [], []]
        for i in range(0, heads, 2):
            three[0].append(unpack_pair(dq_in[i, half], dq_in[i + 1, half]))
            k, v = mix_pair(dkv_in[i, here].astype(F32), dkv_in[i + 1, here].astype(F32))
            three[1].append(k.astype(BF16))
            three[2].append(v.astype(BF16))
        three = [jnp.concatenate(item, axis=1) for item in three]
        grad = 0.125 * lax.dot_general(three[0], wq_ref[...], NT, preferred_element_type=F32)
        grad = grad + lax.dot_general(three[1], wk_ref[...], NT, preferred_element_type=F32)
        grad = grad + lax.dot_general(three[2], wv_ref[...], NT, preferred_element_type=F32)
        row = 6 * per
        for kind, value in enumerate(three):
            all3[here, kind * local_width : (kind + 1) * local_width] = value
            column = jnp.sum(value.astype(F32), axis=0, keepdims=True)
            for start in range(0, local_width, WIDE):
                vbuf[row : row + 1, :] += column[:, start : start + WIDE]
                row += 1
        mean, scale = stat_ref[here, 0:1], stat_ref[here, 1:2]
        sum0 = jnp.zeros((chunk_rows, 1), F32)
        sum1 = jnp.zeros((chunk_rows, 1), F32)
        for index in range(ntp):
            cols = slice(index * width, (index + 1) * width)
            piece = grad[:, cols]
            xhat = (x_ref[index, here].astype(F32) - mean) * scale
            weighted = piece * gain[:, cols]
            sum0 = sum0 + jnp.sum(weighted, axis=1, keepdims=True)
            sum1 = sum1 + jnp.sum(weighted * xhat, axis=1, keepdims=True)
            col0 = jnp.sum(piece * xhat, axis=0, keepdims=True)
            col1 = jnp.sum(piece, axis=0, keepdims=True)
            for sub in range(width // WIDE):
                row = index * (width // WIDE) + sub
                lanes = slice(sub * WIDE, (sub + 1) * WIDE)
                vbuf[row : row + 1, :] += col0[:, lanes]
                vbuf[per + row : per + row + 1, :] += col1[:, lanes]
            pbuf[chunk, index] = piece.astype(BF16)
        both = jnp.where(lane == 0, sum0, jnp.where(lane == 1, sum1, 0.0))
        sums[:, here] = both.T[:8]

    def set_off(chunk):
        for step in range(ntp - 1):
            far = ntp - 1 - step

            @pl.when(tp == 0)
            def _():
                rightward(chunk, far).start()

            @pl.when(tp == ntp - 1)
            def _():
                leftward(chunk, step).start()

    def relay_right(chunk):
        for step in range(ntp - 1):
            far = ntp - 1 - step

            @pl.when((tp < far) & (tp > 0))
            def _():
                rightward(chunk, far).wait_recv()
                pbuf[chunk, far] = add_up(pbuf[chunk, far], from_left[chunk, far]).astype(BF16)
                rightward(chunk, far).start()

    def relay_left(chunk):
        for step in range(ntp - 1):

            @pl.when((tp > step) & (tp < ntp - 1))
            def _():
                leftward(chunk, step).wait_recv()
                pbuf[chunk, step] = add_up(pbuf[chunk, step], from_right[chunk, step]).astype(BF16)
                leftward(chunk, step).start()

    def relay(chunk):
        @pl.when(tp < ntp // 2)
        def _():
            relay_right(chunk)
            relay_left(chunk)

        @pl.when(tp >= ntp // 2)
        def _():
            relay_left(chunk)
            relay_right(chunk)

    def projection_grad(index):
        left = h1_ref[:, pl.ds(index * band, band)]
        value = lax.dot_general(left, all3[...], TN, preferred_element_type=F32)
        g3[index] = value.astype(BF16).reshape(g3.shape[1:])

    for index in range(heads):
        output_grad(index)
    scatters[0].start_near()
    for chunk in range(CHUNKS):
        partial_step(chunk)
        set_off(chunk)
        if chunk == 0:
            scatters[0].start_across()
        if chunk > 1:
            relay(chunk - 2)
    for step in range(1, ntp):
        sums_copy(step).start()
    for step in range(1, nseq):
        vec_copy(step).start()
    for index in range(heads // 2):
        projection_grad(index)
    relay(CHUNKS - 2)
    for index in range(heads // 2, heads):
        projection_grad(index)
    scatters[1].start_near()
    for step in range(1, nseq):
        vec_copy(step).wait_recv()
    total = vbuf[...]
    for step in range(nseq - 1):
        total = total + vec_land[step]
    vsum[...] = total
    for step in range(1, ntp):
        vec_far_copy(step).start()
    scatters[1].start_across()
    relay(CHUNKS - 1)
    value = scatters[0].result().astype(BF16)
    for index in range(ntp):
        wbuf[index] = value[:, index * local_width : (index + 1) * local_width]
    for step in range(1, ntp):
        w_copy(step).start()

    for step in range(1, ntp):
        sums_copy(step).wait_recv()
        da_copy(step).wait_recv()
    my_gain = gain_ref[:, columns_of(tp)]
    da_rows = da_in.shape[1]
    for chunk in range(CHUNKS):
        here = chunk_of(chunk)
        both = sums[:, here]
        for step in range(ntp - 1):
            both = both + sums_land[step, :, here]
        both = jnp.concatenate([both, jnp.zeros((WIDE - 8, chunk_rows), F32)], axis=0).T
        both = both * (1.0 / features)

        @pl.when(tp > 0)
        def _():
            rightward(chunk, tp).wait_recv()

        @pl.when(tp < ntp - 1)
        def _():
            leftward(chunk, tp).wait_recv()

        grad = pbuf[chunk, tp].astype(F32)
        grad = grad + jnp.where(tp > 0, from_left[chunk, tp].astype(F32), 0.0)
        grad = grad + jnp.where(tp < ntp - 1, from_right[chunk, tp].astype(F32), 0.0)
        mean, scale = stat_ref[here, 0:1], stat_ref[here, 1:2]
        xhat = (x_ref[tp, here].astype(F32) - mean) * scale
        inner = grad * my_gain - both[:, 0:1] - xhat * both[:, 1:2]
        many = chunk_rows // da_rows
        branch = da_in[chunk * many : (chunk + 1) * many].reshape(chunk_rows, width)
        gx_ref[here] = branch.astype(F32) + scale * inner
    value = scatters[1].result()
    oq_ref[...] = 0.125 * value[:, :local_width]
    ok_ref[...] = value[:, local_width : 2 * local_width]
    ov_ref[...] = value[:, 2 * local_width :]
    for step in range(1, ntp):
        vec_far_copy(step).wait_recv()
        w_copy(step).wait_recv()
    vout_ref[...] = vsum[...]
    for step in range(ntp - 1):
        vout_ref[: 6 * per] += vec_far[step, : 6 * per]
    ow_ref[...] = add_up(wbuf[tp], *[wfar[step] for step in range(ntp - 1)]).T

    for chunk in range(CHUNKS):
        for step in range(1, share):
            dkv_near(chunk, step).wait_send()
        for step in range(1, heads):
            dq_copy(chunk, step).wait_send()
            dkv_copy(chunk, step).wait_send()
        for index in range(ntp):
            @pl.when(tp < index)
            def _():
                rightward(chunk, index).wait_send()

            @pl.when(tp > index)
            def _():
                leftward(chunk, index).wait_send()

    for step in range(1, ntp):
        sums_copy(step).wait_send()
        da_copy(step).wait_send()
        vec_far_copy(step).wait_send()
        w_copy(step).wait_send()
    for step in range(1, nseq):
        vec_copy(step).wait_send()
    for scatter in scatters:
        scatter.finish()


def run_tail(dims, dq, dkv, h1, x_parts, da, mixed, stats, gain, wq, wk, wv, vec):
    heads, share, nseq, ntp = dims
    rows, features = h1.shape
    width, tokens = features // ntp, rows // ntp
    band = features // nseq
    local_width = wq.shape[1]
    per = features // WIDE
    sds = jax.ShapeDtypeStruct
    nvec = vec.shape[0] + 2 * per + 3 * local_width // WIDE
    outs = [
        sds((rows, width), F32),
        sds((local_width, band), F32),
        sds((band, local_width), F32),
        sds((band, local_width), F32),
        sds((band, local_width), F32),
        sds((nvec, WIDE), F32),
    ]
    pieces = (CHUNKS, ntp, rows // CHUNKS, width)
    scratch = [
        vmem(heads, rows, WIDE),
        vmem(rows, features),
        vmem(ntp, rows, width),
        vmem(heads, rows // 2, WIDE),
        vmem(heads, rows, WIDE),
        vmem(max(share - 1, 1), heads, rows, WIDE),
        vmem(heads, rows, WIDE),
        vmem(rows, 3 * local_width),
        vmem(ntp, tokens, width),
        vmem(*pieces),
        vmem(*pieces),
        vmem(*pieces),
        vmem(8, rows, dtype=F32),
        vmem(ntp - 1, 8, rows, dtype=F32),
        vmem(nvec, WIDE, dtype=F32),
        vmem(nseq - 1, nvec, WIDE, dtype=F32),
        vmem(nvec, WIDE, dtype=F32),
        vmem(ntp - 1, nvec, WIDE, dtype=F32),
        vmem(heads, share, band, features),
        vmem(heads, share, band, 3 * local_width),
        vmem(ntp, band, local_width),
        vmem(ntp - 1, band, local_width),
        *GradScatter.buffers(dims, band, features),
        *GradScatter.buffers(dims, band, 3 * local_width),
    ]
    sems = (
        [dma(CHUNKS, heads - 1)] * 2 + [dma(CHUNKS, share - 1)] * 2 + [dma(CHUNKS, heads - 1)] * 2
        + [dma(CHUNKS, ntp)] * 4 + [dma(ntp - 1)] * 4 + [dma(nseq - 1)] * 2 + [dma(ntp - 1)] * 4
        + GradScatter.semaphores(dims, 2) + [dma(4)]
    )
    return pl.pallas_call(
        functools.partial(tail_kernel, dims),
        out_shape=outs,
        in_specs=[ANYWHERE] * 4 + [IN_VMEM] * 8,
        out_specs=[IN_VMEM] * len(outs),
        scratch_shapes=scratch + sems,
        name="tail",
        cost_estimate=pl.CostEstimate(flops=70 << 30, bytes_accessed=8 << 20, transcendentals=0),
        compiler_params=pltpu.CompilerParams(
            collective_id=3, has_side_effects=True, vmem_limit_bytes=60 << 20
        ),
    )(dq, dkv, h1, x_parts, da, mixed, stats, gain, wq, wk, wv, vec)


def on_device(
    hidden_in,
    norm_gain,
    norm_shift,
    query_weight,
    query_bias,
    key_weight,
    value_weight,
    value_bias,
    output_weight,
    output_bias,
    feed_gain,
    feed_shift,
    inner_weight,
    inner_bias,
    outer_weight,
    outer_bias,
    doc_blocks,
    doc_padding,
    random_picks,
    cotangent,
):
    nrows, block_len, width = hidden_in.shape
    rows = nrows * block_len
    nseq, ntp = lax.axis_size("seq"), lax.axis_size("tp")
    tp = lax.axis_index("tp")
    local_width = query_weight.shape[1]
    heads = local_width // HEAD_DIM
    share = nseq // heads
    dims = (heads, share, nseq, ntp)
    features = width * ntp
    per = features // WIDE
    cot = cotangent.reshape(rows, width)
    q, kv, h1, x_parts, g_first, rest, output_full, x_mine, stats, table = run_head(
        dims, nrows, doc_blocks, doc_padding, random_picks.T, hidden_in.reshape(rows, width),
        norm_gain[None, :], norm_shift[None, :], query_weight, query_bias[None, :],
        key_weight, value_weight, value_bias[None, :], cot, output_weight,
    )
    g_rest = lax.all_gather(rest, "tp", axis=0)
    q = q.reshape(heads * rows, WIDE)
    kv = kv.reshape(nseq * rows, WIDE)
    sds = jax.ShapeDtypeStruct
    packed, res = local_call(
        functools.partial(forward_kernel, dims, nrows, 4),
        "attention_forward",
        (sds((heads * rows // 2, WIDE), BF16), sds((heads * rows, WIDE), F32)),
        2,
    )(table, q, kv)
    out_sum, do, da, mixed, vec, inner_part, outer_part = run_middle(
        dims, packed.reshape(heads, rows // 2, WIDE), g_first, g_rest, output_full,
        inner_weight, outer_weight, x_mine, output_bias[None, :], feed_gain[None, :],
        feed_shift[None, :], inner_bias[None, :],
    )
    result = lax.psum_scatter(out_sum, "tp", scatter_dimension=0)
    dq, dkv = local_call(
        functools.partial(backward_kernel, dims, nrows, 4),
        "attention_backward",
        (sds((heads * rows // 2, WIDE), BF16), sds((nseq * rows, WIDE), BF16)),
        4,
        [pltpu.VMEM((nseq * rows, WIDE), F32)],
    )(table, q, do.reshape(heads * rows // 2, WIDE), res, kv)
    grad_x, output_part, query_part, key_part, value_part, vectors = run_tail(
        dims, dq.reshape(heads, rows // 2, WIDE), dkv.reshape(share, heads, rows, WIDE), h1,
        x_parts, da, mixed, stats, norm_gain[None, :], query_weight, key_weight, value_weight, vec,
    )
    my_bias = lax.dynamic_slice_in_dim(outer_bias, tp * width, width, 0)
    layer_out = (result.astype(F32) + my_bias).astype(BF16).reshape(hidden_in.shape)
    wide = vectors[: 6 * per].reshape(6, features)
    narrow = vectors[6 * per :].reshape(-1)
    return (
        layer_out,
        grad_x.reshape(hidden_in.shape),
        wide[0],
        wide[1],
        query_part,
        0.125 * narrow[:local_width],
        key_part,
        value_part,
        narrow[2 * local_width : 3 * local_width],
        output_part,
        wide[2],
        wide[3],
        wide[4],
        inner_part,
        narrow[3 * local_width :],
        outer_part,
        wide[5],
    )


def solution(mesh):
    return jax.shard_map(
        on_device,
        mesh=mesh,
        in_specs=(
            P(None, "seq", "tp"),
            P(),
            P(),
            P(None, "tp"),
            P("tp"),
            P(None, "tp"),
            P(None, "tp"),
            P("tp"),
            P("tp", None),
            P(),
            P(),
            P(),
            P(None, "tp"),
            P("tp"),
            P("tp", None),
            P(),
            P(),
            P(),
            P(),
            P(None, "seq", "tp"),
        ),
        out_specs=(
            P(None, "seq", "tp"),
            P(None, "seq", "tp"),
            P(),
            P(),
            P("seq", "tp"),
            P("tp"),
            P("seq", "tp"),
            P("seq", "tp"),
            P("tp"),
            P("tp", "seq"),
            P(),
            P(),
            P(),
            P("seq", "tp"),
            P("tp"),
            P("tp", "seq"),
            P(),
        ),
        check_vma=False,
    )
```

```python
import functools
import math

import jax
import jax.numpy as jnp
from jax import lax
from jax.experimental import pallas as pl
from jax.experimental.pallas import tpu as pltpu
from jax.sharding import PartitionSpec as P

HEAD_DIM = 64
BLK = 64
GLOBAL = 2
SLOTS = 8
WIDE = 2 * HEAD_DIM
CHUNKS = 4
COT_CHUNKS = 1
ROUNDS = 2
NEG = -1e30
NT = (((1,), (1,)), ((), ()))
TN = (((0,), (0,)), ((), ()))
MESH = pl.DeviceIdType.MESH
F32, BF16 = jnp.float32, jnp.bfloat16


def split_by(value, count):
    if count & (count - 1) == 0:
        return value >> (count.bit_length() - 1), value & (count - 1)
    return value // count, value % count


def remote(src, dst, send_sem, recv_sem, device):
    return pltpu.make_async_remote_copy(
        src_ref=src, dst_ref=dst, send_sem=send_sem, recv_sem=recv_sem,
        device_id=device, device_id_type=MESH,
    )


def greet(peers):
    barrier = pltpu.get_barrier_semaphore()
    for peer in peers:
        pl.semaphore_signal(barrier, inc=1, device_id=peer, device_id_type=MESH)
    pl.semaphore_wait(barrier, len(peers))


def add_up(*terms):
    total = terms[0].astype(F32)
    for term in terms[1:]:
        total = total + term.astype(F32)
    return total


def swap_halves(value):
    return pltpu.roll(value, HEAD_DIM, 1)


def low_half(value):
    return lax.broadcasted_iota(jnp.int32, value.shape, 1) < HEAD_DIM


def mix_pair(left, right):
    low = low_half(left)
    return (
        jnp.where(low, left, swap_halves(right)),
        jnp.where(low, swap_halves(left), right),
    )


def unpack_pair(left, right):
    even, odd = mix_pair(left.astype(F32), right.astype(F32))
    tiles = []
    for start in range(0, left.shape[0], BLK):
        tiles += [even[start : start + BLK], odd[start : start + BLK]]
    return jnp.concatenate(tiles, axis=0).astype(BF16)


def pack_pair(value):
    lefts, rights = [], []
    for start in range(0, value.shape[0], 2 * BLK):
        left, right = mix_pair(value[start : start + BLK], value[start + BLK : start + 2 * BLK])
        lefts.append(left)
        rights.append(right)
    return jnp.concatenate(lefts, axis=0).astype(BF16), jnp.concatenate(rights, axis=0).astype(BF16)


def dma(*shape):
    return pltpu.SemaphoreType.DMA(tuple(max(size, 1) for size in shape))


def vmem(*shape, dtype=BF16):
    return pltpu.VMEM(shape, dtype)


IN_VMEM = pl.BlockSpec(memory_space=pltpu.VMEM)
IN_SMEM = pl.BlockSpec(memory_space=pltpu.SMEM)
ANYWHERE = pl.BlockSpec(memory_space=pl.ANY)


class Place:
    def __init__(self, dims):
        self.heads, self.share, self.nseq, self.ntp = dims
        self.seq, self.tp = lax.axis_index("seq"), lax.axis_index("tp")
        self.head, self.part = self.seq // self.share, lax.rem(self.seq, self.share)

    def partner(self, step):
        other = lax.rem(self.part + step, self.share)
        return other, (self.head * self.share + other, self.tp)

    def across(self, step):
        other = lax.rem(self.head + step, self.heads)
        return other, (other * self.share + self.part, self.tp)

    def along(self, step):
        other = lax.rem(self.tp + step, self.ntp)
        return other, (self.seq, other)

    def apart(self, step):
        far, near = step // self.heads, step % self.heads
        head = lax.rem(self.head + near, self.heads)
        tp = lax.rem(self.tp + far, self.ntp)
        return head, tp, (head * self.share + self.part, tp)


def fill_table(place, docs_ref, pads_ref, picks_ref, table_ref, nrows):
    nblocks = table_ref.shape[1]
    block = lax.broadcasted_iota(jnp.int32, (1, nblocks), 1)

    def doc_step(doc, state):
        start, first, last, pad = state
        stop = start + docs_ref[doc]
        inside = (block >= start) & (block < stop)
        first = jnp.where(inside, start, first)
        last = jnp.where(inside, stop - 1, last)
        pad = jnp.where(inside, pads_ref[doc], pad)
        return stop, first, last, pad

    zero = jnp.zeros((1, nblocks), jnp.int32)
    _, first, last, pad = lax.fori_loop(
        0, docs_ref.shape[0], doc_step, (jnp.int32(0), zero, zero, zero)
    )
    length = last - first + 1
    picks = []
    for index in range(picks_ref.shape[0]):
        pick = picks_ref[index : index + 1, :]
        whole = (pick.astype(F32) / length.astype(F32)).astype(jnp.int32)
        left = pick - whole * length
        left = jnp.where(left < 0, left + length, left)
        left = jnp.where(left >= length, left - length, left)
        picks.append(first + left)
    glob = block - first < GLOBAL
    is_long = glob & (last - first >= SLOTS)
    never = block < 0
    p0, p1, p2 = picks
    fresh = lambda pick: (pick >= first + GLOBAL) & ((pick > block + 1) | (pick < block - 1))
    near = [
        (block - 1, ~never),
        (block, ~never),
        (block + 1, block < last),
        (first, ~never),
        (first + 1, block - 1 > first + 1),
        (p0, fresh(p0)),
        (p1, fresh(p1) & (p1 != p0)),
        (p2, fresh(p2) & (p2 != p0) & (p2 != p1)),
    ]
    for index, (other, use) in enumerate(near):
        whole = first + index
        use = (glob & (whole <= last) & ~is_long) | (~glob & use)
        other = jnp.where(use, jnp.where(glob, whole, other), block)
        live = jnp.where(use, jnp.where(other == last, BLK - pad, BLK), 0)
        table_ref[index : index + 1, :] = row_of(place, other, nrows) * WIDE + live
    table_ref[SLOTS : SLOTS + 1, :] = first
    table_ref[SLOTS + 1 : SLOTS + 2, :] = last
    table_ref[SLOTS + 2 : SLOTS + 3, :] = pad


def head_kernel(
    dims, nrows, docs_ref, pads_ref, picks_ref, x_ref, gain_ref, shift_ref,
    wq_ref, bq_ref, wk_ref, wv_ref, bv_ref, cot_ref, wo_ref,
    q_out, kv_out, h1_out, xs_out, g_out, rest_out, wo_out, xt_out, stat_out, table_out,
    xs, h1, qbuf, kvbuf, right_s, right_r, left_s, left_r, q_s, q_r, kv_s, kv_r, on_s, on_r,
    wz_s, wz_r, wa_s, wa_r, wp_s, wp_r, local,
):
    place = Place(dims)
    heads, share, nseq, ntp = dims
    head, part, seq, tp = place.head, place.part, place.seq, place.tp
    rows, width = x_ref.shape
    features = width * ntp
    chunk_rows = rows // CHUNKS

    def chunk_of(chunk):
        return pl.ds(chunk * chunk_rows, chunk_rows)

    def traveller(chunk, index):
        if chunk < CHUNKS:
            return xs.at[index, chunk_of(chunk)]
        return g_out.at[index, chunk_of(chunk - CHUNKS)]

    def rightward(chunk, index):
        spot = traveller(chunk, index)
        return remote(
            spot, spot, right_s.at[chunk, index], right_r.at[chunk, index], (seq, tp + 1)
        )

    def leftward(chunk, index):
        spot = traveller(chunk, index)
        return remote(spot, spot, left_s.at[chunk, index], left_r.at[chunk, index], (seq, tp - 1))

    def q_copy(chunk, step):
        other, device = place.across(step)
        return remote(
            qbuf.at[other, chunk_of(chunk)], q_out.at[head, chunk_of(chunk)],
            q_s.at[chunk, step - 1], q_r.at[chunk, step - 1], device,
        )

    def kv_copy(chunk, step):
        other, device = place.across(step)
        return remote(
            kvbuf.at[other, chunk_of(chunk)], kv_out.at[part, head, chunk_of(chunk)],
            kv_s.at[chunk, step - 1], kv_r.at[chunk, step - 1], device,
        )

    def kv_on(chunk, hop, step):
        owner = lax.rem(head + heads - hop, heads)
        spot = kv_out.at[part, owner, chunk_of(chunk)]
        source = kvbuf.at[head, chunk_of(chunk)] if hop == 0 else spot
        return remote(
            source, spot, on_s.at[chunk, hop, step - 1], on_r.at[chunk, hop, step - 1],
            place.partner(step)[1],
        )

    def own_send(chunk):
        @pl.when(tp < ntp - 1)
        def _():
            rightward(chunk, tp).start()

        @pl.when(tp > 0)
        def _():
            leftward(chunk, tp).start()

    def pass_on(chunk):
        for hop in range(1, ntp):
            below, above = tp - hop, tp + hop

            @pl.when(below >= 0)
            def _():
                rightward(chunk, below).wait_recv()

                @pl.when(tp < ntp - 1)
                def _():
                    rightward(chunk, below).start()

            @pl.when(above < ntp)
            def _():
                leftward(chunk, above).wait_recv()

                @pl.when(tp > 0)
                def _():
                    leftward(chunk, above).start()

    def compute(chunk):
        here = chunk_of(chunk)
        x = jnp.concatenate([xs[index, here] for index in range(ntp)], axis=1).astype(F32)
        mean = jnp.sum(x, axis=1, keepdims=True) * (1.0 / features)
        centered = x - mean
        spread = jnp.sum(centered * centered, axis=1, keepdims=True) * (1.0 / features)
        scale = lax.rsqrt(spread + 1e-05)
        normed = (centered * scale * gain_ref[...] + shift_ref[...]).astype(BF16)
        h1[here] = normed
        stat_out[here, 0:1] = mean
        stat_out[here, 1:2] = scale
        q = (jnp.dot(normed, wq_ref[...], preferred_element_type=F32) + bq_ref[...]) * 0.125
        k = jnp.dot(normed, wk_ref[...], preferred_element_type=F32)
        v = jnp.dot(normed, wv_ref[...], preferred_element_type=F32) + bv_ref[...]
        for index in range(0, heads, 2):
            lanes = slice(index * HEAD_DIM, (index + 2) * HEAD_DIM)
            kv = mix_pair(k[:, lanes], v[:, lanes])
            low = low_half(q[:, lanes])
            qs = (q[:, lanes], swap_halves(q[:, lanes]))
            for off in range(2):
                kvbuf[index + off, here] = kv[off].astype(BF16)
                qbuf[index + off, here] = jnp.where(low, qs[off], 0.0).astype(BF16)

    def hand_on(chunk):
        for hop in range(heads):
            if hop:
                kv_copy(chunk, hop).wait_recv()
            for step in range(1, share):
                kv_on(chunk, hop, step).start()

    slice_rows = wo_out.shape[3]
    half = lax.rem(part, 2)

    def wo_along(step):
        start = pl.multiple_of((head * 2 + half) * slice_rows, slice_rows)
        return remote(
            wo_ref.at[pl.ds(start, slice_rows)], wo_out.at[tp, head, half],
            wz_s.at[step - 1], wz_r.at[step - 1], place.along(step)[1],
        )

    def wo_across(step):
        spot = wo_out.at[:, head, half]
        return remote(spot, spot, wa_s.at[step - 1], wa_r.at[step - 1], place.across(step)[1])

    def wo_swap():
        spot = wo_out.at[:, :, half]
        return remote(spot, spot, wp_s.at[0], wp_r.at[0], (seq + 1 - 2 * half, tp))

    xs[tp] = x_ref[...]
    own_rows = pl.ds(pl.multiple_of((head * 2 + half) * slice_rows, slice_rows), slice_rows)
    early = [
        pltpu.make_async_copy(wo_ref.at[own_rows], wo_out.at[tp, head, half], local.at[5]),
        pltpu.make_async_copy(cot_ref.at[pl.ds(0, g_out.shape[1])], g_out.at[tp], local.at[6]),
    ]
    for copy in early:
        copy.start()
    copies = [
        pltpu.make_async_copy(
            cot_ref.at[pl.ds(g_out.shape[1], rest_out.shape[0])], rest_out, local.at[2]
        )
    ]
    copies[0].start()
    greet(
        [place.partner(step)[1] for step in range(1, share)]
        + [place.across(step)[1] for step in range(1, heads)]
        + [place.along(step)[1] for step in range(1, ntp)]
    )
    for step in range(1, ntp):
        wo_along(step).start()
    own_send(0)
    own_send(1)
    fill_table(place, docs_ref, pads_ref, picks_ref, table_out, nrows)
    for copy in early:
        copy.wait()
    for step in range(1, ntp):
        wo_along(step).wait_recv()
    for step in range(1, heads):
        wo_across(step).start()
    for chunk in range(CHUNKS):
        if chunk > 0:
            own_send(chunk + 1)
        pass_on(chunk)
        compute(chunk)
        here = chunk_of(chunk)
        for index, (source, target) in enumerate(
            [(h1.at[here], h1_out.at[here]), (xs.at[:, here], xs_out.at[:, here])]
        ):
            copies.append(pltpu.make_async_copy(source, target, local.at[7 + 2 * chunk + index]))
            copies[-1].start()
        for step in range(1, heads):
            kv_copy(chunk, step).start()
        for step in range(1, heads):
            q_copy(chunk, step).start()
        if chunk > 0:
            hand_on(chunk - 1)
        if chunk == 2:
            for step in range(1, heads):
                wo_across(step).wait_recv()
            wo_swap().start()
    for index, (source, target) in enumerate(
        [(qbuf.at[head], q_out.at[head]), (kvbuf.at[head], kv_out.at[part, head])]
    ):
        copies.append(pltpu.make_async_copy(source, target, local.at[index]))
        copies[-1].start()
    mine = pl.ds(pl.multiple_of(tp * (rows // ntp), rows // ntp), rows // ntp)
    xt_out[...] = xs[:, mine]
    hand_on(CHUNKS - 1)
    for chunk in range(CHUNKS, CHUNKS + COT_CHUNKS):
        if chunk + 1 < CHUNKS + COT_CHUNKS:
            own_send(chunk + 1)
        pass_on(chunk)
    wo_swap().wait()
    for step in range(1, ntp):
        wo_along(step).wait_send()
    for step in range(1, heads):
        wo_across(step).wait_send()
    for copy in copies:
        copy.wait()
    for chunk in range(CHUNKS):
        for step in range(1, heads):
            q_copy(chunk, step).wait_recv()
        for hop in range(heads):
            for step in range(1, share):
                kv_on(chunk, hop, step).wait_recv()
    for chunk in range(CHUNKS):
        for step in range(1, heads):
            q_copy(chunk, step).wait_send()
            kv_copy(chunk, step).wait_send()
        for hop in range(heads):
            for step in range(1, share):
                kv_on(chunk, hop, step).wait_send()
    for chunk in range(CHUNKS + COT_CHUNKS):
        for index in range(ntp):
            @pl.when((tp >= index) & (tp < ntp - 1))
            def _():
                rightward(chunk, index).wait_send()

            @pl.when((tp <= index) & (tp > 0))
            def _():
                leftward(chunk, index).wait_send()


def run_head(dims, nrows, docs, pads, picks, x, *params):
    heads, share, nseq, ntp = dims
    rows, width = x.shape
    nblocks = picks.shape[1]
    first = rows // CHUNKS * COT_CHUNKS
    sds = jax.ShapeDtypeStruct
    outs = [
        sds((heads, rows, WIDE), BF16),
        sds((share, heads, rows, WIDE), BF16),
        sds((rows, width * ntp), BF16),
        sds((ntp, rows, width), BF16),
        sds((ntp, first, width), BF16),
        sds((rows - first, width), BF16),
        sds((ntp, heads, 2, params[-1].shape[0] // (2 * heads), params[-1].shape[1]), BF16),
        sds((ntp, rows // ntp, width), BF16),
        sds((rows, 2), F32),
        sds((16, nblocks), jnp.int32),
    ]
    scratch = [
        vmem(ntp, rows, width),
        vmem(rows, width * ntp),
        vmem(heads, rows, WIDE),
        vmem(heads, rows, WIDE),
    ]
    sems = (
        [dma(CHUNKS + COT_CHUNKS, ntp)] * 4 + [dma(CHUNKS, heads - 1)] * 4
        + [dma(CHUNKS, heads, share - 1)] * 2 + [dma(ntp - 1)] * 2 + [dma(heads - 1)] * 2
        + [dma(1)] * 2 + [dma(7 + 2 * CHUNKS)]
    )
    return pl.pallas_call(
        functools.partial(head_kernel, dims, nrows),
        out_shape=outs,
        in_specs=[IN_SMEM, IN_SMEM] + [IN_VMEM] * (2 + len(params)),
        out_specs=[ANYWHERE] * 7 + [IN_VMEM] * 3,
        scratch_shapes=scratch + sems,
        name="head",
        cost_estimate=pl.CostEstimate(flops=60 << 30, bytes_accessed=8 << 20, transcendentals=0),
        compiler_params=pltpu.CompilerParams(
            collective_id=1, has_side_effects=True, vmem_limit_bytes=60 << 20
        ),
    )(docs, pads, picks, x, *params)


def block_of(place, query, nrows):
    source, row = split_by(query, nrows)
    return row * place.nseq + source * place.share + place.part


def row_of(place, block, nrows):
    row, holder = split_by(block, place.nseq)
    head, part = split_by(holder, place.share)
    return ((part * place.heads + head) * nrows + row) * BLK


def near_slots(table_ref, block):
    entries = [table_ref[index, block] for index in range(SLOTS)]
    slots = [pl.multiple_of(entry >> 7, BLK) for entry in entries]
    return slots, [entry & (WIDE - 1) for entry in entries]


def long_slots(place, table_ref, block, chunk, nrows):
    first, last = table_ref[SLOTS, block], table_ref[SLOTS + 1, block]
    final = BLK - table_ref[SLOTS + 2, block]
    slots, lives = [], []
    for index in range(SLOTS):
        wanted = first + chunk * SLOTS + index
        slots.append(pl.multiple_of(row_of(place, jnp.minimum(wanted, last), nrows), BLK))
        lives.append(jnp.where(wanted < last, BLK, jnp.where(wanted == last, final, 0)))
    return slots, lives


def for_long(place, table_ref, nquery, nrows, body):
    def step(query, carry):
        block = block_of(place, query, nrows)
        first, last = table_ref[SLOTS, block], table_ref[SLOTS + 1, block]

        @pl.when((block - first < GLOBAL) & (last - first >= SLOTS))
        def _():
            body(query, block, (last - first + SLOTS) >> 3)

        return carry

    lax.fori_loop(0, nquery, step, 0)


def bias_row(lives):
    lane = lax.broadcasted_iota(jnp.int32, (1, WIDE), 1)
    parts = []
    for index in range(0, SLOTS, 2):
        bound = jnp.where(lane < BLK, lives[index], lives[index + 1] + BLK)
        parts.append(jnp.where(lane < bound, 0.0, NEG))
    return jnp.concatenate(parts, axis=1)


def take(ref, slots):
    return jnp.concatenate([ref[pl.ds(slot, BLK), :] for slot in slots], axis=0)


def forward_kernel(dims, nrows, unroll, table_ref, q_ref, kv_ref, out_ref, res_ref):
    place = Place(dims)
    nquery = q_ref.shape[0] // BLK
    upper = lax.broadcasted_iota(jnp.int32, (BLK, WIDE), 1) >= HEAD_DIM

    def finish(query, top, total, accum):
        value = accum / total
        res_ref[pl.ds(query * BLK, BLK), :] = jnp.where(upper, value, top + jnp.log(total))
        return value

    def scores_of(query, slots, lives):
        kv = take(kv_ref, slots)
        scores = lax.dot_general(
            q_ref[pl.ds(query * BLK, BLK), :], kv, NT, preferred_element_type=F32
        )
        return kv, scores + bias_row(lives)

    def near_one(query):
        kv, scores = scores_of(query, *near_slots(table_ref, block_of(place, query, nrows)))
        top = jnp.max(scores, axis=1, keepdims=True)
        weights = jnp.exp(scores - top)
        total = jnp.sum(weights, axis=1, keepdims=True)
        accum = jnp.dot(weights.astype(BF16), kv, preferred_element_type=F32)
        return finish(query, top, total, accum)

    def near_step(index, carry):
        for offset in range(unroll):
            pair = index * unroll + offset
            even, odd = near_one(2 * pair), near_one(2 * pair + 1)
            out_ref[pl.ds(pair * BLK, BLK), :] = jnp.where(upper, odd, swap_halves(even)).astype(BF16)
        return carry

    lax.fori_loop(0, nquery // (2 * unroll), near_step, 0)

    def long_body(query, block, chunks):
        def chunk_step(chunk, state):
            top, total, accum = state
            kv, scores = scores_of(query, *long_slots(place, table_ref, block, chunk, nrows))
            new_top = jnp.maximum(top, jnp.max(scores, axis=1, keepdims=True))
            weights = jnp.exp(scores - new_top)
            decay = jnp.exp(top - new_top)
            total = total * decay + jnp.sum(weights, axis=1, keepdims=True)
            accum = accum * decay + jnp.dot(weights.astype(BF16), kv, preferred_element_type=F32)
            return new_top, total, accum

        start = (
            jnp.full((BLK, 1), NEG, F32),
            jnp.zeros((BLK, 1), F32),
            jnp.zeros((BLK, WIDE), F32),
        )
        value = finish(query, *lax.fori_loop(0, chunks, chunk_step, start))
        spot = pl.ds(pl.multiple_of((query >> 1) * BLK, BLK), BLK)
        is_odd = (query & 1) == 1
        moved = jnp.where(is_odd, value, swap_halves(value))
        out_ref[spot, :] = jnp.where(upper == is_odd, moved, out_ref[spot, :].astype(F32)).astype(BF16)

    for_long(place, table_ref, nquery, nrows, long_body)


def backward_kernel(
    dims, nrows, unroll, table_ref, q_ref, do_ref, res_ref, kv_ref, dq_ref, dkv_ref, sum_ref
):
    place = Place(dims)
    nquery = q_ref.shape[0] // BLK
    upper = lax.broadcasted_iota(jnp.int32, (BLK, WIDE), 1) >= HEAD_DIM
    sum_ref[...] = jnp.zeros_like(sum_ref)

    def load(query, packed, is_odd):
        moved = jnp.where(is_odd, packed, swap_halves(packed))
        grad = jnp.where(upper, moved, 0.0)
        rows = pl.ds(query * BLK, BLK)
        both = jnp.concatenate([q_ref[rows, :], grad.astype(BF16)], axis=0)
        res = res_ref[rows, :]
        delta = jnp.sum(res * grad, axis=1, keepdims=True)
        return both, res[:, :1], delta

    def terms(both, log_total, delta, slots, lives):
        kv = take(kv_ref, slots)
        pair = lax.dot_general(both, kv, NT, preferred_element_type=F32)
        probs = jnp.exp(pair[:BLK] + bias_row(lives) - log_total)
        grad_scores = (probs * (pair[BLK:] - delta)).astype(BF16)
        weights = jnp.concatenate([grad_scores, probs.astype(BF16)], axis=0)
        dkv = lax.dot_general(weights, both, TN, preferred_element_type=F32)
        dq = jnp.dot(grad_scores, kv, preferred_element_type=F32)
        return dq, dkv

    def scatter(slots, dkv):
        for index, slot in enumerate(slots):
            sum_ref[pl.ds(slot, BLK), :] += dkv[index * BLK : (index + 1) * BLK]

    def near_step(index, carry):
        done = []
        for offset in range(unroll):
            pair = index * unroll + offset
            packed = do_ref[pl.ds(pair * BLK, BLK), :].astype(F32)
            grads = []
            for is_odd in (False, True):
                query = 2 * pair + int(is_odd)
                slots, lives = near_slots(table_ref, block_of(place, query, nrows))
                dq, dkv = terms(*load(query, packed, is_odd), slots, lives)
                grads.append(dq)
                done.append((slots, dkv))
            dq_ref[pl.ds(pair * BLK, BLK), :] = jnp.where(
                upper, swap_halves(grads[1]), grads[0]
            ).astype(BF16)
        for slots, dkv in done:
            scatter(slots, dkv)
        return carry

    lax.fori_loop(0, nquery // (2 * unroll), near_step, 0)

    def long_body(query, block, chunks):
        is_odd = (query & 1) == 1
        spot = pl.ds(pl.multiple_of((query >> 1) * BLK, BLK), BLK)
        loaded = load(query, do_ref[spot, :].astype(F32), is_odd)

        def chunk_step(chunk, total):
            slots, lives = long_slots(place, table_ref, block, chunk, nrows)
            dq, dkv = terms(*loaded, slots, lives)
            scatter(slots, dkv)
            return total + dq

        total = lax.fori_loop(0, chunks, chunk_step, jnp.zeros((BLK, WIDE), F32))
        moved = jnp.where(is_odd, swap_halves(total), total)
        dq_ref[spot, :] = jnp.where(upper == is_odd, moved, dq_ref[spot, :].astype(F32)).astype(BF16)

    for_long(place, table_ref, nquery, nrows, long_body)
    dkv_ref[...] = sum_ref[...].astype(BF16)


def local_call(kernel, name, out_shape, nvmem, scratch=()):
    return pl.pallas_call(
        kernel,
        out_shape=out_shape,
        in_specs=[IN_SMEM] + [IN_VMEM] * nvmem,
        out_specs=jax.tree.map(lambda _: IN_VMEM, out_shape),
        scratch_shapes=list(scratch),
        name=name,
        cost_estimate=pl.CostEstimate(flops=30 << 30, bytes_accessed=8 << 20, transcendentals=0),
        compiler_params=pltpu.CompilerParams(vmem_limit_bytes=56 << 20),
    )


class GradScatter:
    def __init__(self, place, source, bufs, sems):
        self.place, self.source = place, source
        self.land, self.pair, self.far = bufs
        self.send1, self.recv1, self.send2, self.recv2 = sems

    @staticmethod
    def buffers(dims, band, cols):
        heads, share = dims[:2]
        return [
            vmem(max(share - 1, 1), heads, band, cols),
            vmem(heads, band, cols),
            vmem(max(heads - 1, 1), band, cols),
        ]

    @staticmethod
    def semaphores(dims, count):
        return [dma(count, dims[1] - 1)] * 2 + [dma(count, dims[0] - 1)] * 2

    def near(self, step):
        other, device = self.place.partner(step)
        return remote(
            self.source.at[:, other], self.land.at[step - 1],
            self.send1.at[step - 1], self.recv1.at[step - 1], device,
        )

    def across(self, step):
        other, device = self.place.across(step)
        return remote(
            self.pair.at[other], self.far.at[step - 1],
            self.send2.at[step - 1], self.recv2.at[step - 1], device,
        )

    def start_near(self):
        for step in range(1, self.place.share):
            self.near(step).start()

    def sum_near(self):
        place = self.place
        for step in range(1, place.share):
            self.near(step).wait_recv()

        def body(head, carry):
            parts = [self.source[head, place.part]]
            parts += [self.land[step, head] for step in range(place.share - 1)]
            self.pair[head] = add_up(*parts).astype(BF16)
            return carry

        lax.fori_loop(0, place.heads, body, 0)

    def start_across(self):
        self.sum_near()
        for step in range(1, self.place.heads):
            self.across(step).start()

    def result(self):
        heads = self.place.heads
        for step in range(1, heads):
            self.across(step).wait_recv()
        return add_up(self.pair[self.place.head], *[self.far[step] for step in range(heads - 1)])

    def finish_near(self):
        for step in range(1, self.place.share):
            self.near(step).wait_send()

    def finish(self):
        self.finish_near()
        for step in range(1, self.place.heads):
            self.across(step).wait_send()


def gelu_pair(value):
    root = math.sqrt(2.0 / math.pi)
    square = value * value
    curve = jnp.tanh(root * value * (1.0 + 0.044715 * square))
    half = 0.5 * (1.0 + curve)
    slope = half + 0.5 * value * (1.0 - curve * curve) * (root * (1.0 + 3 * 0.044715 * square))
    return value * half, slope


def middle_kernel(
    dims,
    o_ref, g0_hbm, g1_hbm, wo_hbm, wi_hbm, wu_hbm, xt_ref, ob_ref, gain_ref, shift_ref, ib_ref, ub_ref,
    sum_out, do_out, da_out, mixed_out, vec_out, gi_out, gu_out,
    g_ref, wo_ref, wi_ref, wu_ref, o_in, x1, xhat, scale, h2, act, dpre, outb, terms, from_left, from_right, do_buf, ib_sum, gi, gu, land_i, land_u, pair_i, pair_u, far_i, far_u,
    *rest,
):
    place = Place(dims)
    heads, share, nseq, ntp = dims
    head, part, seq, tp = place.head, place.part, place.seq, place.tp
    sems = rest
    (o_s, o_r, hr_s, hr_r, hl_s, hl_r, tr_s, tr_r, tl_s, tl_r, do_s, do_r,
     g1_s, g1_r, g2_s, g2_r, local) = sems
    rows, width = g_ref.shape[1:]
    features = width * ntp
    tokens = rows // ntp
    rounds = ROUNDS
    span = tokens // rounds
    pieces = tokens // (2 * BLK)
    places = 2 * ntp - 1
    band = features // heads
    per = features // WIDE

    def packed_rows(index, count=tokens // 2):
        return pl.ds(pl.multiple_of(index * count, count), count)

    def span_of(index):
        return pl.ds(pl.multiple_of(index * span, span), span)

    def o_copy(step):
        to_head, to_tp, device = place.apart(step)
        return remote(
            o_ref.at[to_head, packed_rows(to_tp)], o_in.at[tp * heads + head],
            o_s.at[step], o_r.at[step], device,
        )

    def do_copy(index, step):
        to_head, to_tp, device = place.apart(step)
        return remote(
            do_buf.at[to_tp * heads + to_head, packed_rows(index, BLK)],
            do_out.at[head, packed_rows(tp * pieces + index, BLK)],
            do_s.at[index, step], do_r.at[index, step], device,
        )

    def h2_copy(index, owner, right):
        spot = h2.at[owner, span_of(index)]
        if right:
            return remote(spot, spot, hr_s.at[index, owner], hr_r.at[index, owner], (seq, tp + 1))
        return remote(spot, spot, hl_s.at[index, owner], hl_r.at[index, owner], (seq, tp - 1))

    def term_copy(index, owner, right):
        here = span_of(index)
        if right:
            return remote(
                terms.at[owner, here], from_left.at[owner, here],
                tr_s.at[index, owner], tr_r.at[index, owner], (seq, tp + 1),
            )
        return remote(
            terms.at[owner, here], from_right.at[owner, here],
            tl_s.at[index, owner], tl_r.at[index, owner], (seq, tp - 1),
        )

    scatters = [
        GradScatter(place, source, bufs, (g1_s.at[k], g1_r.at[k], g2_s.at[k], g2_r.at[k]))
        for k, (source, bufs) in enumerate(
            ((gi, (land_i, pair_i, far_i)), (gu, (land_u, pair_u, far_u)))
        )
    ]

    first_rows = g0_hbm.shape[1]
    loads = [
        pltpu.make_async_copy(o_ref.at[head, packed_rows(tp)], o_in.at[tp * heads + head], local.at[2]),
        pltpu.make_async_copy(wo_hbm, wo_ref, local.at[3]),
        pltpu.make_async_copy(wi_hbm, wi_ref, local.at[4]),
        pltpu.make_async_copy(wu_hbm, wu_ref, local.at[5]),
        pltpu.make_async_copy(g0_hbm, g_ref.at[:, pl.ds(0, first_rows)], local.at[6]),
        pltpu.make_async_copy(
            g1_hbm, g_ref.at[:, pl.ds(first_rows, rows - first_rows)], local.at[7]
        ),
    ]
    for load in loads:
        load.start()
    greet(
        [place.partner(step)[1] for step in range(1, share)]
        + [place.apart(step)[2] for step in range(1, heads * ntp)]
    )
    for step in range(heads * ntp - 1, 0, -1):
        o_copy(step).start()
    ib_sum[...] = jnp.zeros_like(ib_sum)
    for load in loads:
        load.wait()
    for step in range(1, heads * ntp):
        o_copy(step).wait_recv()

    for index in range(pieces):
        here = slice(index * 2 * BLK, (index + 1) * 2 * BLK)
        half = slice(index * BLK, (index + 1) * BLK)
        mixed = jnp.concatenate(
            [unpack_pair(o_in[i, half], o_in[i + 1, half]) for i in range(0, heads * ntp, 2)], axis=1
        )
        mixed_out[here] = mixed
        base = jnp.concatenate([xt_ref[i, here] for i in range(ntp)], axis=1).astype(F32)
        value = base + ob_ref[...] + jnp.dot(mixed, wo_ref[...].reshape(features, features), preferred_element_type=F32)
        x1[here] = value
        centered = value - jnp.sum(value, axis=1, keepdims=True) * (1.0 / features)
        spread = jnp.sum(centered * centered, axis=1, keepdims=True) * (1.0 / features)
        inverse = lax.rsqrt(spread + 1e-05)
        normed = centered * inverse
        xhat[here] = normed
        scale[here] = jnp.broadcast_to(inverse, (2 * BLK, WIDE))
        h2[tp, here] = (normed * gain_ref[...] + shift_ref[...]).astype(BF16)
        for part_index in range(index * rounds // pieces, (index + 1) * rounds // pieces):

            @pl.when(tp < ntp - 1)
            def _():
                h2_copy(part_index, tp, True).start()

            @pl.when(tp > 0)
            def _():
                h2_copy(part_index, tp, False).start()

    def spot_of(position):
        hop = (position + 1) // 2
        owner = tp + jnp.where(position % 2 == 1, -hop, hop)
        return owner, (owner >= 0) & (owner < ntp)

    def feed(index, owner):
        @pl.when(owner < tp)
        def _():
            h2_copy(index, owner, True).wait_recv()

            @pl.when(tp < ntp - 1)
            def _():
                h2_copy(index, owner, True).start()

        @pl.when(owner > tp)
        def _():
            h2_copy(index, owner, False).wait_recv()

            @pl.when(tp > 0)
            def _():
                h2_copy(index, owner, False).start()

        here = span_of(index)
        wide = span_of(owner * rounds + index)
        pre = jnp.dot(h2[owner, here], wi_ref[...], preferred_element_type=F32) + ib_ref[...]
        value, slope = gelu_pair(pre)
        value = value.astype(BF16)
        act[wide] = value
        grad = jnp.concatenate([g_ref[i, wide] for i in range(ntp)], axis=1)
        back = lax.dot_general(grad, wu_ref[...], NT, preferred_element_type=F32) * slope
        back = back.astype(BF16)
        dpre[wide] = back
        ib_sum[0:1, :] += jnp.sum(back.astype(F32), axis=0, keepdims=True)
        terms[owner, here] = lax.dot_general(
            back, wi_ref[...], NT, preferred_element_type=F32
        ).astype(BF16)

        @pl.when((owner > tp) & (tp == 0))
        def _():
            term_copy(index, owner, True).start()

        @pl.when((owner < tp) & (tp == ntp - 1))
        def _():
            term_copy(index, owner, False).start()

        out = jnp.dot(value, wu_ref[...], preferred_element_type=F32)
        out = out + jnp.where(owner == tp, x1[here] + ub_ref[...], 0.0)
        for i in range(ntp):
            outb[i, wide] = out[:, i * width : (i + 1) * width].astype(BF16)

    def relay_right(index):
        here = span_of(index)
        for owner in range(1, ntp):

            @pl.when((owner > tp) & (tp > 0))
            def _():
                term_copy(index, owner, True).wait_recv()
                terms[owner, here] = add_up(terms[owner, here], from_left[owner, here]).astype(BF16)
                term_copy(index, owner, True).start()

    def relay_left(index):
        here = span_of(index)
        for owner in range(ntp - 2, -1, -1):

            @pl.when((owner < tp) & (tp < ntp - 1))
            def _():
                term_copy(index, owner, False).wait_recv()
                terms[owner, here] = add_up(terms[owner, here], from_right[owner, here]).astype(BF16)
                term_copy(index, owner, False).start()

    def relay(index, first):
        @pl.when((tp < ntp // 2) == first)
        def _():
            relay_right(index)

        @pl.when((tp < ntp // 2) != first)
        def _():
            relay_left(index)

    def feed_step(count, carry):
        index, position = count // places, count % places
        owner, inside = spot_of(position)

        @pl.when(inside)
        def _():
            feed(index, owner)

        @pl.when((index > 0) & (position == 2))
        def _():
            relay(index - 1, True)

        @pl.when((index > 0) & (position == places - 1))
        def _():
            relay(index - 1, False)

        return carry

    lax.fori_loop(0, rounds * places, feed_step, 0)
    save = pltpu.make_async_copy(outb, sum_out, local.at[0])
    save.start()

    def inner_grad(index):
        left = h2[:, :, index * band : (index + 1) * band].reshape(rows, band)
        value = lax.dot_general(left, dpre[...], TN, preferred_element_type=F32)
        gi[index] = value.astype(BF16).reshape(gi.shape[1:])

    def outer_grad(index):
        many = ntp // heads
        left = jnp.concatenate([g_ref[i] for i in range(index * many, (index + 1) * many)], axis=1)
        value = lax.dot_general(left, act[...], TN, preferred_element_type=F32)
        gu[index] = value.astype(BF16).reshape(gu.shape[1:])

    work = [functools.partial(inner_grad, index) for index in range(heads)]
    work += [functools.partial(outer_grad, index) for index in range(heads)]
    def finish(index):
        here = slice(index * 2 * BLK, (index + 1) * 2 * BLK)
        half = slice(index * BLK, (index + 1) * BLK)
        wide = pl.ds(pl.multiple_of(tp * tokens + index * 2 * BLK, 2 * BLK), 2 * BLK)
        for part_index in range(index * rounds // pieces, (index + 1) * rounds // pieces):

            @pl.when(tp > 0)
            def _():
                term_copy(part_index, tp, True).wait_recv()

            @pl.when(tp < ntp - 1)
            def _():
                term_copy(part_index, tp, False).wait_recv()

        grad = terms[tp, here].astype(F32)
        grad = grad + jnp.where(tp > 0, from_left[tp, here].astype(F32), 0.0)
        grad = grad + jnp.where(tp < ntp - 1, from_right[tp, here].astype(F32), 0.0)
        hat = xhat[here]
        inner = grad * gain_ref[...]
        mean0 = jnp.sum(inner, axis=1, keepdims=True) * (1.0 / features)
        mean1 = jnp.sum(inner * hat, axis=1, keepdims=True) * (1.0 / features)
        tail = scale[here, 0:1] * (inner - mean0 - hat * mean1)
        cot = jnp.concatenate([g_ref[i, wide] for i in range(ntp)], axis=1).astype(F32)
        branch = (cot + tail).astype(BF16)
        da_out[here] = branch
        do = lax.dot_general(
            branch, wo_ref[...].reshape(features, features), NT, preferred_element_type=F32
        )
        for i in range(0, heads * ntp, 2):
            pair = pack_pair(do[:, i * HEAD_DIM : (i + 2) * HEAD_DIM])
            do_buf[i, half] = pair[0]
            do_buf[i + 1, half] = pair[1]
        for step in range(heads * ntp - 1, 0, -1):
            do_copy(index, step).start()
        sums = (
            jnp.sum(branch.astype(F32), axis=0, keepdims=True),
            jnp.sum(grad * hat, axis=0, keepdims=True),
            jnp.sum(grad, axis=0, keepdims=True),
        )
        for kind, value in enumerate(sums):
            for sub in range(per):
                row = slice(kind * per + sub, kind * per + sub + 1)
                piece = value[:, sub * WIDE : (sub + 1) * WIDE]
                if index == 0:
                    vec_out[row, :] = piece
                else:
                    vec_out[row, :] += piece
    early = pieces * (rounds - 1) // rounds
    for item in work[:heads]:
        item()
    scatters[0].start_near()
    for index in range(early):
        finish(index)
    relay(rounds - 1, True)
    scatters[0].start_across()
    for item in work[heads:]:
        item()
    scatters[1].start_near()
    relay(rounds - 1, False)
    for index in range(early, pieces):
        finish(index)
    own = pltpu.make_async_copy(
        do_buf.at[tp * heads + head], do_out.at[head, packed_rows(tp)], local.at[1]
    )
    own.start()
    scatters[1].start_across()
    cot = jnp.sum(g_ref[tp].astype(F32), axis=0, keepdims=True)
    for sub in range(per):
        owner, lane = divmod(sub * WIDE, width)
        vec_out[3 * per + sub : 3 * per + sub + 1, :] = jnp.where(
            tp == owner, cot[:, lane : lane + WIDE], 0.0
        )
    for sub in range(ib_sum.shape[1] // WIDE):
        row = 4 * per + sub
        vec_out[row : row + 1, :] = ib_sum[0:1, sub * WIDE : (sub + 1) * WIDE]
    gi_out[...] = scatters[0].result()
    gu_out[...] = scatters[1].result().T
    save.wait()
    own.wait()
    for step in range(1, heads * ntp):
        for index in range(pieces):
            do_copy(index, step).wait_recv()
    for step in range(1, heads * ntp):
        o_copy(step).wait_send()
        for index in range(pieces):
            do_copy(index, step).wait_send()
    for index in range(rounds):
        for owner in range(ntp):
            @pl.when((tp >= owner) & (tp < ntp - 1))
            def _():
                h2_copy(index, owner, True).wait_send()

            @pl.when((tp <= owner) & (tp > 0))
            def _():
                h2_copy(index, owner, False).wait_send()

            @pl.when(tp < owner)
            def _():
                term_copy(index, owner, True).wait_send()

            @pl.when(tp > owner)
            def _():
                term_copy(index, owner, False).wait_send()

    for scatter in scatters:
        scatter.finish()


def run_middle(dims, o, g0, g1, wo, wi, wu, xt, ob, gain, shift, ib, ub):
    heads, share, nseq, ntp = dims
    rows, width = g0.shape[1] + g1.shape[1], g0.shape[2]
    features, hidden = width * ntp, wi.shape[1]
    tokens, band = rows // ntp, features // nseq
    per = features // WIDE
    rounds, pieces = ROUNDS, tokens // (2 * BLK)
    sds = jax.ShapeDtypeStruct
    outs = [
        sds((ntp, rows, width), BF16),
        sds((heads, rows // 2, WIDE), BF16),
        sds((tokens, features), BF16),
        sds((tokens, features), BF16),
        sds((4 * per + hidden // WIDE, WIDE), F32),
        sds((band, hidden), F32),
        sds((hidden, band), F32),
    ]
    count = heads * ntp
    scratch = [
        vmem(ntp, rows, width),
        vmem(*wo.shape),
        vmem(*wi.shape),
        vmem(*wu.shape),
        vmem(count, tokens // 2, WIDE),
        vmem(tokens, features, dtype=F32),
        vmem(tokens, features, dtype=F32),
        vmem(tokens, WIDE, dtype=F32),
        vmem(ntp, tokens, features),
        vmem(rows, hidden),
        vmem(rows, hidden),
        vmem(ntp, rows, width),
        vmem(ntp, tokens, features),
        vmem(ntp, tokens, features),
        vmem(ntp, tokens, features),
        vmem(count, tokens // 2, WIDE),
        vmem(8, hidden, dtype=F32),
        vmem(heads, share, band, hidden),
        vmem(heads, share, band, hidden),
        vmem(max(share - 1, 1), heads, band, hidden),
        vmem(max(share - 1, 1), heads, band, hidden),
        vmem(heads, band, hidden),
        vmem(heads, band, hidden),
        vmem(max(heads - 1, 1), band, hidden),
        vmem(max(heads - 1, 1), band, hidden),
    ]
    sems = (
        [dma(count)] * 2 + [dma(rounds, ntp)] * 8 + [dma(pieces, count)] * 2
        + GradScatter.semaphores(dims, 2) + [dma(8)]
    )
    return pl.pallas_call(
        functools.partial(middle_kernel, dims),
        out_shape=outs,
        in_specs=[ANYWHERE] * 6 + [IN_VMEM] * 6,
        out_specs=[ANYWHERE] * 2 + [IN_VMEM] * 5,
        scratch_shapes=scratch + sems,
        name="middle",
        cost_estimate=pl.CostEstimate(flops=110 << 30, bytes_accessed=8 << 20, transcendentals=0),
        compiler_params=pltpu.CompilerParams(
            collective_id=2, has_side_effects=True, vmem_limit_bytes=63 << 20
        ),
    )(o, g0, g1, wo, wi, wu, xt, ob, gain, shift, ib, ub)


def tail_kernel(
    dims,
    dq_ref, dkv_hbm, h1_hbm, x_hbm, da_ref, mixed_ref, stat_ref, gain_ref, wq_ref, wk_ref, wv_ref, vec_ref,
    gx_ref, ow_ref, oq_ref, ok_ref, ov_ref, vout_ref,
    dkv_own, h1_ref, x_ref, dq_in, dkv_in, dkv_land, dkv_sum, all3, pbuf, from_left, from_right,
    sums, sums_land, vbuf, vec_land, vsum, vec_far, gw, g3, wbuf, wfar,
    *rest,
):
    place = Place(dims)
    heads, share, nseq, ntp = dims
    head, part, seq, tp = place.head, place.part, place.seq, place.tp
    lands, sems = rest[:6], rest[6:]
    (dq_s, dq_r, kv1_s, kv1_r, kv2_s, kv2_r, right_s, right_r, left_s, left_r,
     st_s, st_r, v1_s, v1_r, v2_s, v2_r, w_s, w_r, g1_s, g1_r, g2_s, g2_r, load_s) = sems
    rows, features = h1_ref.shape
    width = features // ntp
    tokens = rows // ntp
    local_width = wq_ref.shape[1]
    chunk_rows = rows // CHUNKS
    band = features // heads
    per = features // WIDE

    def chunk_of(chunk):
        return pl.ds(chunk * chunk_rows, chunk_rows)

    def half_of(chunk):
        return pl.ds(chunk * chunk_rows // 2, chunk_rows // 2)

    def columns_of(index):
        return pl.ds(pl.multiple_of(index * width, width), width)

    def dq_copy(chunk, step):
        other, device = place.across(step)
        return remote(
            dq_ref.at[other, half_of(chunk)], dq_in.at[head, half_of(chunk)],
            dq_s.at[chunk, step - 1], dq_r.at[chunk, step - 1], device,
        )

    def dkv_near(chunk, step):
        other, device = place.partner(step)
        here = chunk_of(chunk)
        return remote(
            dkv_hbm.at[other, :, here], dkv_land.at[step - 1, :, here],
            kv1_s.at[chunk, step - 1], kv1_r.at[chunk, step - 1], device,
        )

    def dkv_copy(chunk, step):
        other, device = place.across(step)
        return remote(
            dkv_sum.at[other, chunk_of(chunk)], dkv_in.at[head, chunk_of(chunk)],
            kv2_s.at[chunk, step - 1], kv2_r.at[chunk, step - 1], device,
        )

    def rightward(chunk, index):
        return remote(
            pbuf.at[chunk, index], from_left.at[chunk, index],
            right_s.at[chunk, index], right_r.at[chunk, index], (seq, tp + 1),
        )

    def leftward(chunk, index):
        return remote(
            pbuf.at[chunk, index], from_right.at[chunk, index],
            left_s.at[chunk, index], left_r.at[chunk, index], (seq, tp - 1),
        )

    def sums_copy(step):
        return remote(
            sums, sums_land.at[step - 1], st_s.at[step - 1], st_r.at[step - 1], place.along(step)[1]
        )

    def vec_copy(step):
        return remote(
            vbuf, vec_land.at[step - 1], v1_s.at[step - 1], v1_r.at[step - 1],
            (lax.rem(seq + step, nseq), tp),
        )

    def vec_far_copy(step):
        return remote(
            vsum, vec_far.at[step - 1], v2_s.at[step - 1], v2_r.at[step - 1], place.along(step)[1]
        )

    def w_copy(step):
        other, device = place.along(step)
        return remote(wbuf.at[other], wfar.at[step - 1], w_s.at[step - 1], w_r.at[step - 1], device)

    scatters = [
        GradScatter(
            place, source, lands[3 * k : 3 * k + 3], (g1_s.at[k], g1_r.at[k], g2_s.at[k], g2_r.at[k])
        )
        for k, source in enumerate((gw, g3))
    ]

    loads = [
        pltpu.make_async_copy(dkv_hbm.at[part], dkv_own, load_s.at[0]),
        pltpu.make_async_copy(dq_ref.at[head], dq_in.at[head], load_s.at[1]),
        pltpu.make_async_copy(x_hbm, x_ref, load_s.at[2]),
        pltpu.make_async_copy(h1_hbm, h1_ref, load_s.at[3]),
    ]
    for load in loads:
        load.start()
    greet(
        [(lax.rem(seq + step, nseq), tp) for step in range(1, nseq)]
        + [place.along(step)[1] for step in range(1, ntp)]
    )
    for chunk in range(CHUNKS):
        for step in range(1, share):
            dkv_near(chunk, step).start()
    vbuf[: 2 * per] = jnp.zeros((2 * per, WIDE), F32)
    vbuf[2 * per : 6 * per] = vec_ref[: 4 * per]
    narrow = 3 * local_width // WIDE
    vbuf[6 * per : 6 * per + narrow] = jnp.zeros((narrow, WIDE), F32)
    vbuf[6 * per + narrow :] = vec_ref[4 * per :]
    loads[0].wait()
    for chunk in range(CHUNKS):
        for step in range(1, heads):
            dq_copy(chunk, step).start()
        for step in range(1, share):
            dkv_near(chunk, step).wait_recv()
        for target in range(heads):
            where = (target, chunk_of(chunk))
            parts = [dkv_own[where]] + [dkv_land[(step,) + where] for step in range(share - 1)]
            dkv_sum[where] = add_up(*parts).astype(BF16)
        for step in range(1, heads):
            dkv_copy(chunk, step).start()
    dkv_in[head] = dkv_sum[head]
    for load in loads[1:]:
        load.wait()

    def output_grad(index):
        value = lax.dot_general(
            da_ref[:, index * band : (index + 1) * band], mixed_ref[...], TN, preferred_element_type=F32
        )
        gw[index] = value.astype(BF16).reshape(gw.shape[1:])

    gain = gain_ref[...]
    lane = lax.broadcasted_iota(jnp.int32, (chunk_rows, WIDE), 1)

    def partial_step(chunk):
        here, half = chunk_of(chunk), half_of(chunk)
        for step in range(1, heads):
            dq_copy(chunk, step).wait_recv()
            dkv_copy(chunk, step).wait_recv()
        three = [[], [], []]
        for i in range(0, heads, 2):
            three[0].append(unpack_pair(dq_in[i, half], dq_in[i + 1, half]))
            k, v = mix_pair(dkv_in[i, here].astype(F32), dkv_in[i + 1, here].astype(F32))
            three[1].append(k.astype(BF16))
            three[2].append(v.astype(BF16))
        three = [jnp.concatenate(item, axis=1) for item in three]
        grad = 0.125 * lax.dot_general(three[0], wq_ref[...], NT, preferred_element_type=F32)
        grad = grad + lax.dot_general(three[1], wk_ref[...], NT, preferred_element_type=F32)
        grad = grad + lax.dot_general(three[2], wv_ref[...], NT, preferred_element_type=F32)
        row = 6 * per
        for kind, value in enumerate(three):
            all3[here, kind * local_width : (kind + 1) * local_width] = value
            column = jnp.sum(value.astype(F32), axis=0, keepdims=True)
            for start in range(0, local_width, WIDE):
                vbuf[row : row + 1, :] += column[:, start : start + WIDE]
                row += 1
        mean, scale = stat_ref[here, 0:1], stat_ref[here, 1:2]
        sum0 = jnp.zeros((chunk_rows, 1), F32)
        sum1 = jnp.zeros((chunk_rows, 1), F32)
        for index in range(ntp):
            cols = slice(index * width, (index + 1) * width)
            piece = grad[:, cols]
            xhat = (x_ref[index, here].astype(F32) - mean) * scale
            weighted = piece * gain[:, cols]
            sum0 = sum0 + jnp.sum(weighted, axis=1, keepdims=True)
            sum1 = sum1 + jnp.sum(weighted * xhat, axis=1, keepdims=True)
            col0 = jnp.sum(piece * xhat, axis=0, keepdims=True)
            col1 = jnp.sum(piece, axis=0, keepdims=True)
            for sub in range(width // WIDE):
                row = index * (width // WIDE) + sub
                lanes = slice(sub * WIDE, (sub + 1) * WIDE)
                vbuf[row : row + 1, :] += col0[:, lanes]
                vbuf[per + row : per + row + 1, :] += col1[:, lanes]
            pbuf[chunk, index] = piece.astype(BF16)
            for sub in range(max(chunk_rows // tokens, 1)):
                rows_here = slice(sub * tokens, sub * tokens + min(tokens, chunk_rows))

                @pl.when(tp == chunk * chunk_rows // tokens + sub)
                def _():
                    start = chunk * chunk_rows % tokens
                    carried = da_ref[start : start + min(tokens, chunk_rows), cols].astype(F32)
                    carried = carried / (scale[rows_here] * gain[:, cols])
                    pbuf[chunk, index, rows_here] = (piece[rows_here] + carried).astype(BF16)

        both = jnp.where(lane == 0, sum0, jnp.where(lane == 1, sum1, 0.0))
        sums[:, here] = both.T[:8]

    def set_off(chunk):
        for step in range(ntp - 1):
            far = ntp - 1 - step

            @pl.when(tp == 0)
            def _():
                rightward(chunk, far).start()

            @pl.when(tp == ntp - 1)
            def _():
                leftward(chunk, step).start()

    def relay_right(chunk):
        for step in range(ntp - 1):
            far = ntp - 1 - step

            @pl.when((tp < far) & (tp > 0))
            def _():
                rightward(chunk, far).wait_recv()
                pbuf[chunk, far] = add_up(pbuf[chunk, far], from_left[chunk, far]).astype(BF16)
                rightward(chunk, far).start()

    def relay_left(chunk):
        for step in range(ntp - 1):

            @pl.when((tp > step) & (tp < ntp - 1))
            def _():
                leftward(chunk, step).wait_recv()
                pbuf[chunk, step] = add_up(pbuf[chunk, step], from_right[chunk, step]).astype(BF16)
                leftward(chunk, step).start()

    def relay(chunk):
        @pl.when(tp < ntp // 2)
        def _():
            relay_right(chunk)
            relay_left(chunk)

        @pl.when(tp >= ntp // 2)
        def _():
            relay_left(chunk)
            relay_right(chunk)

    def projection_grad(index):
        left = h1_ref[:, pl.ds(index * band, band)]
        value = lax.dot_general(left, all3[...], TN, preferred_element_type=F32)
        g3[index] = value.astype(BF16).reshape(g3.shape[1:])

    for index in range(heads):
        output_grad(index)
    scatters[0].start_near()
    for chunk in range(CHUNKS):
        partial_step(chunk)
        set_off(chunk)
        if chunk == 0:
            scatters[0].start_across()
        if chunk > 1:
            relay(chunk - 2)
    for step in range(1, ntp):
        sums_copy(step).start()
    for step in range(1, nseq):
        vec_copy(step).start()
    for index in range(heads // 2):
        projection_grad(index)
    relay(CHUNKS - 2)
    for index in range(heads // 2, heads):
        projection_grad(index)
    scatters[1].start_near()
    for step in range(1, nseq):
        vec_copy(step).wait_recv()
    total = vbuf[...]
    for step in range(nseq - 1):
        total = total + vec_land[step]
    vsum[...] = total
    for step in range(1, ntp):
        vec_far_copy(step).start()
    scatters[1].start_across()
    relay(CHUNKS - 1)
    value = scatters[0].result().astype(BF16)
    for index in range(ntp):
        wbuf[index] = value[:, index * local_width : (index + 1) * local_width]
    for step in range(1, ntp):
        w_copy(step).start()

    for step in range(1, ntp):
        sums_copy(step).wait_recv()
    my_gain = gain_ref[:, columns_of(tp)]
    for chunk in range(CHUNKS):
        here = chunk_of(chunk)
        both = sums[:, here]
        for step in range(ntp - 1):
            both = both + sums_land[step, :, here]
        both = jnp.concatenate([both, jnp.zeros((WIDE - 8, chunk_rows), F32)], axis=0).T
        both = both * (1.0 / features)

        @pl.when(tp > 0)
        def _():
            rightward(chunk, tp).wait_recv()

        @pl.when(tp < ntp - 1)
        def _():
            leftward(chunk, tp).wait_recv()

        grad = pbuf[chunk, tp].astype(F32)
        grad = grad + jnp.where(tp > 0, from_left[chunk, tp].astype(F32), 0.0)
        grad = grad + jnp.where(tp < ntp - 1, from_right[chunk, tp].astype(F32), 0.0)
        mean, scale = stat_ref[here, 0:1], stat_ref[here, 1:2]
        xhat = (x_ref[tp, here].astype(F32) - mean) * scale
        gx_ref[here] = scale * (grad * my_gain - both[:, 0:1] - xhat * both[:, 1:2])
    value = scatters[1].result()
    oq_ref[...] = 0.125 * value[:, :local_width]
    ok_ref[...] = value[:, local_width : 2 * local_width]
    ov_ref[...] = value[:, 2 * local_width :]
    for step in range(1, ntp):
        vec_far_copy(step).wait_recv()
        w_copy(step).wait_recv()
    vout_ref[...] = vsum[...]
    for step in range(ntp - 1):
        vout_ref[: 6 * per] += vec_far[step, : 6 * per]
    ow_ref[...] = add_up(wbuf[tp], *[wfar[step] for step in range(ntp - 1)]).T

    for chunk in range(CHUNKS):
        for step in range(1, share):
            dkv_near(chunk, step).wait_send()
        for step in range(1, heads):
            dq_copy(chunk, step).wait_send()
            dkv_copy(chunk, step).wait_send()
        for index in range(ntp):
            @pl.when(tp < index)
            def _():
                rightward(chunk, index).wait_send()

            @pl.when(tp > index)
            def _():
                leftward(chunk, index).wait_send()

    for step in range(1, ntp):
        sums_copy(step).wait_send()
        vec_far_copy(step).wait_send()
        w_copy(step).wait_send()
    for step in range(1, nseq):
        vec_copy(step).wait_send()
    for scatter in scatters:
        scatter.finish()


def run_tail(dims, dq, dkv, h1, x_parts, da, mixed, stats, gain, wq, wk, wv, vec):
    heads, share, nseq, ntp = dims
    rows, features = h1.shape
    width, tokens = features // ntp, rows // ntp
    band = features // nseq
    local_width = wq.shape[1]
    per = features // WIDE
    sds = jax.ShapeDtypeStruct
    nvec = vec.shape[0] + 2 * per + 3 * local_width // WIDE
    outs = [
        sds((rows, width), F32),
        sds((local_width, band), F32),
        sds((band, local_width), F32),
        sds((band, local_width), F32),
        sds((band, local_width), F32),
        sds((nvec, WIDE), F32),
    ]
    pieces = (CHUNKS, ntp, rows // CHUNKS, width)
    scratch = [
        vmem(heads, rows, WIDE),
        vmem(rows, features),
        vmem(ntp, rows, width),
        vmem(heads, rows // 2, WIDE),
        vmem(heads, rows, WIDE),
        vmem(max(share - 1, 1), heads, rows, WIDE),
        vmem(heads, rows, WIDE),
        vmem(rows, 3 * local_width),
        vmem(*pieces),
        vmem(*pieces),
        vmem(*pieces),
        vmem(8, rows, dtype=F32),
        vmem(ntp - 1, 8, rows, dtype=F32),
        vmem(nvec, WIDE, dtype=F32),
        vmem(nseq - 1, nvec, WIDE, dtype=F32),
        vmem(nvec, WIDE, dtype=F32),
        vmem(ntp - 1, nvec, WIDE, dtype=F32),
        vmem(heads, share, band, features),
        vmem(heads, share, band, 3 * local_width),
        vmem(ntp, band, local_width),
        vmem(ntp - 1, band, local_width),
        *GradScatter.buffers(dims, band, features),
        *GradScatter.buffers(dims, band, 3 * local_width),
    ]
    sems = (
        [dma(CHUNKS, heads - 1)] * 2 + [dma(CHUNKS, share - 1)] * 2 + [dma(CHUNKS, heads - 1)] * 2
        + [dma(CHUNKS, ntp)] * 4 + [dma(ntp - 1)] * 2 + [dma(nseq - 1)] * 2 + [dma(ntp - 1)] * 4
        + GradScatter.semaphores(dims, 2) + [dma(4)]
    )
    return pl.pallas_call(
        functools.partial(tail_kernel, dims),
        out_shape=outs,
        in_specs=[ANYWHERE] * 4 + [IN_VMEM] * 8,
        out_specs=[IN_VMEM] * len(outs),
        scratch_shapes=scratch + sems,
        name="tail",
        cost_estimate=pl.CostEstimate(flops=70 << 30, bytes_accessed=8 << 20, transcendentals=0),
        compiler_params=pltpu.CompilerParams(
            collective_id=3, has_side_effects=True, vmem_limit_bytes=60 << 20
        ),
    )(dq, dkv, h1, x_parts, da, mixed, stats, gain, wq, wk, wv, vec)


def on_device(
    hidden_in,
    norm_gain,
    norm_shift,
    query_weight,
    query_bias,
    key_weight,
    value_weight,
    value_bias,
    output_weight,
    output_bias,
    feed_gain,
    feed_shift,
    inner_weight,
    inner_bias,
    outer_weight,
    outer_bias,
    doc_blocks,
    doc_padding,
    random_picks,
    cotangent,
):
    nrows, block_len, width = hidden_in.shape
    rows = nrows * block_len
    nseq, ntp = lax.axis_size("seq"), lax.axis_size("tp")
    local_width = query_weight.shape[1]
    heads = local_width // HEAD_DIM
    share = nseq // heads
    dims = (heads, share, nseq, ntp)
    features = width * ntp
    per = features // WIDE
    cot = cotangent.reshape(rows, width)
    q, kv, h1, x_parts, g_first, rest, output_full, x_mine, stats, table = run_head(
        dims, nrows, doc_blocks, doc_padding, random_picks.T, hidden_in.reshape(rows, width),
        norm_gain[None, :], norm_shift[None, :], query_weight, query_bias[None, :],
        key_weight, value_weight, value_bias[None, :], cot, output_weight,
    )
    g_rest = lax.all_gather(rest, "tp", axis=0)
    q = q.reshape(heads * rows, WIDE)
    kv = kv.reshape(nseq * rows, WIDE)
    sds = jax.ShapeDtypeStruct
    packed, res = local_call(
        functools.partial(forward_kernel, dims, nrows, 4),
        "attention_forward",
        (sds((heads * rows // 2, WIDE), BF16), sds((heads * rows, WIDE), F32)),
        2,
    )(table, q, kv)
    out_sum, do, da, mixed, vec, inner_part, outer_part = run_middle(
        dims, packed.reshape(heads, rows // 2, WIDE), g_first, g_rest, output_full,
        inner_weight, outer_weight, x_mine, output_bias[None, :], feed_gain[None, :],
        feed_shift[None, :], inner_bias[None, :], outer_bias[None, :],
    )
    result = lax.psum_scatter(out_sum, "tp", scatter_dimension=0)
    dq, dkv = local_call(
        functools.partial(backward_kernel, dims, nrows, 4),
        "attention_backward",
        (sds((heads * rows // 2, WIDE), BF16), sds((nseq * rows, WIDE), BF16)),
        4,
        [pltpu.VMEM((nseq * rows, WIDE), F32)],
    )(table, q, do.reshape(heads * rows // 2, WIDE), res, kv)
    grad_x, output_part, query_part, key_part, value_part, vectors = run_tail(
        dims, dq.reshape(heads, rows // 2, WIDE), dkv.reshape(share, heads, rows, WIDE), h1,
        x_parts, da, mixed, stats, norm_gain[None, :], query_weight, key_weight, value_weight, vec,
    )
    wide = vectors[: 6 * per].reshape(6, features)
    narrow = vectors[6 * per :].reshape(-1)
    return (
        result.reshape(hidden_in.shape),
        grad_x.reshape(hidden_in.shape),
        wide[0],
        wide[1],
        query_part,
        0.125 * narrow[:local_width],
        key_part,
        value_part,
        narrow[2 * local_width : 3 * local_width],
        output_part,
        wide[2],
        wide[3],
        wide[4],
        inner_part,
        narrow[3 * local_width :],
        outer_part,
        wide[5],
    )


def solution(mesh):
    return jax.shard_map(
        on_device,
        mesh=mesh,
        in_specs=(
            P(None, "seq", "tp"),
            P(),
            P(),
            P(None, "tp"),
            P("tp"),
            P(None, "tp"),
            P(None, "tp"),
            P("tp"),
            P("tp", None),
            P(),
            P(),
            P(),
            P(None, "tp"),
            P("tp"),
            P("tp", None),
            P(),
            P(),
            P(),
            P(),
            P(None, "seq", "tp"),
        ),
        out_specs=(
            P(None, "seq", "tp"),
            P(None, "seq", "tp"),
            P(),
            P(),
            P("seq", "tp"),
            P("tp"),
            P("seq", "tp"),
            P("seq", "tp"),
            P("tp"),
            P("tp", "seq"),
            P(),
            P(),
            P(),
            P("seq", "tp"),
            P("tp"),
            P("tp", "seq"),
            P(),
        ),
        check_vma=False,
    )
```

```python
import functools
import math

import jax
import jax.numpy as jnp
from jax import lax
from jax.experimental import pallas as pl
from jax.experimental.pallas import tpu as pltpu
from jax.sharding import PartitionSpec as P

HEAD_DIM = 64
BLK = 64
GLOBAL = 2
SLOTS = 8
WIDE = 2 * HEAD_DIM
CHUNKS = 4
COT_CHUNKS = 1
ROUNDS = 2
SPLIT = 2
NEG = -1e30
NT = (((1,), (1,)), ((), ()))
TN = (((0,), (0,)), ((), ()))
MESH = pl.DeviceIdType.MESH
F32, BF16 = jnp.float32, jnp.bfloat16


def split_by(value, count):
    if count & (count - 1) == 0:
        return value >> (count.bit_length() - 1), value & (count - 1)
    return value // count, value % count


def remote(src, dst, send_sem, recv_sem, device):
    return pltpu.make_async_remote_copy(
        src_ref=src, dst_ref=dst, send_sem=send_sem, recv_sem=recv_sem,
        device_id=device, device_id_type=MESH,
    )


def greet(peers):
    barrier = pltpu.get_barrier_semaphore()
    for peer in peers:
        pl.semaphore_signal(barrier, inc=1, device_id=peer, device_id_type=MESH)
    pl.semaphore_wait(barrier, len(peers))


def add_up(*terms):
    total = terms[0].astype(F32)
    for term in terms[1:]:
        total = total + term.astype(F32)
    return total


def swap_halves(value):
    return pltpu.roll(value, HEAD_DIM, 1)


def low_half(value):
    return lax.broadcasted_iota(jnp.int32, value.shape, 1) < HEAD_DIM


def mix_pair(left, right):
    low = low_half(left)
    return (
        jnp.where(low, left, swap_halves(right)),
        jnp.where(low, swap_halves(left), right),
    )


def unpack_pair(left, right):
    even, odd = mix_pair(left.astype(F32), right.astype(F32))
    tiles = []
    for start in range(0, left.shape[0], BLK):
        tiles += [even[start : start + BLK], odd[start : start + BLK]]
    return jnp.concatenate(tiles, axis=0).astype(BF16)


def pack_pair(value):
    lefts, rights = [], []
    for start in range(0, value.shape[0], 2 * BLK):
        left, right = mix_pair(value[start : start + BLK], value[start + BLK : start + 2 * BLK])
        lefts.append(left)
        rights.append(right)
    return jnp.concatenate(lefts, axis=0).astype(BF16), jnp.concatenate(rights, axis=0).astype(BF16)


def dma(*shape):
    return pltpu.SemaphoreType.DMA(tuple(max(size, 1) for size in shape))


def vmem(*shape, dtype=BF16):
    return pltpu.VMEM(shape, dtype)


IN_VMEM = pl.BlockSpec(memory_space=pltpu.VMEM)
IN_SMEM = pl.BlockSpec(memory_space=pltpu.SMEM)
ANYWHERE = pl.BlockSpec(memory_space=pl.ANY)


class Place:
    def __init__(self, dims):
        self.heads, self.share, self.nseq, self.ntp = dims
        self.seq, self.tp = lax.axis_index("seq"), lax.axis_index("tp")
        self.head, self.part = self.seq // self.share, lax.rem(self.seq, self.share)

    def partner(self, step):
        other = lax.rem(self.part + step, self.share)
        return other, (self.head * self.share + other, self.tp)

    def across(self, step):
        other = lax.rem(self.head + step, self.heads)
        return other, (other * self.share + self.part, self.tp)

    def along(self, step):
        other = lax.rem(self.tp + step, self.ntp)
        return other, (self.seq, other)

    def apart(self, step):
        far, near = step // self.heads, step % self.heads
        head = lax.rem(self.head + near, self.heads)
        tp = lax.rem(self.tp + far, self.ntp)
        return head, tp, (head * self.share + self.part, tp)


def fill_table(place, docs_ref, pads_ref, picks_ref, table_ref, nrows):
    nblocks = table_ref.shape[1]
    block = lax.broadcasted_iota(jnp.int32, (1, nblocks), 1)

    def doc_step(doc, state):
        start, first, last, pad = state
        stop = start + docs_ref[doc]
        inside = (block >= start) & (block < stop)
        first = jnp.where(inside, start, first)
        last = jnp.where(inside, stop - 1, last)
        pad = jnp.where(inside, pads_ref[doc], pad)
        return stop, first, last, pad

    zero = jnp.zeros((1, nblocks), jnp.int32)
    _, first, last, pad = lax.fori_loop(
        0, docs_ref.shape[0], doc_step, (jnp.int32(0), zero, zero, zero)
    )
    length = last - first + 1
    picks = []
    for index in range(picks_ref.shape[0]):
        pick = picks_ref[index : index + 1, :]
        whole = (pick.astype(F32) / length.astype(F32)).astype(jnp.int32)
        left = pick - whole * length
        left = jnp.where(left < 0, left + length, left)
        left = jnp.where(left >= length, left - length, left)
        picks.append(first + left)
    glob = block - first < GLOBAL
    is_long = glob & (last - first >= SLOTS)
    never = block < 0
    p0, p1, p2 = picks
    fresh = lambda pick: (pick >= first + GLOBAL) & ((pick > block + 1) | (pick < block - 1))
    near = [
        (block - 1, ~never),
        (block, ~never),
        (block + 1, block < last),
        (first, ~never),
        (first + 1, block - 1 > first + 1),
        (p0, fresh(p0)),
        (p1, fresh(p1) & (p1 != p0)),
        (p2, fresh(p2) & (p2 != p0) & (p2 != p1)),
    ]
    for index, (other, use) in enumerate(near):
        whole = first + index
        use = (glob & (whole <= last) & ~is_long) | (~glob & use)
        other = jnp.where(use, jnp.where(glob, whole, other), block)
        live = jnp.where(use, jnp.where(other == last, BLK - pad, BLK), 0)
        table_ref[index : index + 1, :] = row_of(place, other, nrows) * WIDE + live
    table_ref[SLOTS : SLOTS + 1, :] = first
    table_ref[SLOTS + 1 : SLOTS + 2, :] = last
    table_ref[SLOTS + 2 : SLOTS + 3, :] = pad


def head_kernel(
    dims, nrows, docs_ref, pads_ref, picks_ref, x_ref, gain_ref, shift_ref,
    wq_ref, bq_ref, wk_ref, wv_ref, bv_ref, cot_ref, wo_ref,
    q_out, kv_out, h1_out, xs_out, g_out, rest_out, wo_out, xt_out, stat_out, table_out,
    xs, h1, qbuf, kvbuf, right_s, right_r, left_s, left_r, q_s, q_r, kv_s, kv_r, on_s, on_r,
    wz_s, wz_r, wa_s, wa_r, wp_s, wp_r, local,
):
    place = Place(dims)
    heads, share, nseq, ntp = dims
    head, part, seq, tp = place.head, place.part, place.seq, place.tp
    rows, width = x_ref.shape
    features = width * ntp
    chunk_rows = rows // CHUNKS

    def chunk_of(chunk):
        return pl.ds(chunk * chunk_rows, chunk_rows)

    def traveller(chunk, index):
        if chunk < CHUNKS:
            return xs.at[index, chunk_of(chunk)]
        return g_out.at[index, chunk_of(chunk - CHUNKS)]

    def rightward(chunk, index):
        spot = traveller(chunk, index)
        return remote(
            spot, spot, right_s.at[chunk, index], right_r.at[chunk, index], (seq, tp + 1)
        )

    def leftward(chunk, index):
        spot = traveller(chunk, index)
        return remote(spot, spot, left_s.at[chunk, index], left_r.at[chunk, index], (seq, tp - 1))

    def q_copy(chunk, step):
        other, device = place.across(step)
        return remote(
            qbuf.at[other, chunk_of(chunk)], q_out.at[head, chunk_of(chunk)],
            q_s.at[chunk, step - 1], q_r.at[chunk, step - 1], device,
        )

    def kv_copy(chunk, step):
        other, device = place.across(step)
        return remote(
            kvbuf.at[other, chunk_of(chunk)], kv_out.at[part, head, chunk_of(chunk)],
            kv_s.at[chunk, step - 1], kv_r.at[chunk, step - 1], device,
        )

    def kv_on(chunk, hop, step):
        owner = lax.rem(head + heads - hop, heads)
        spot = kv_out.at[part, owner, chunk_of(chunk)]
        source = kvbuf.at[head, chunk_of(chunk)] if hop == 0 else spot
        return remote(
            source, spot, on_s.at[chunk, hop, step - 1], on_r.at[chunk, hop, step - 1],
            place.partner(step)[1],
        )

    def own_send(chunk):
        @pl.when(tp < ntp - 1)
        def _():
            rightward(chunk, tp).start()

        @pl.when(tp > 0)
        def _():
            leftward(chunk, tp).start()

    def pass_on(chunk):
        for hop in range(1, ntp):
            below, above = tp - hop, tp + hop

            @pl.when(below >= 0)
            def _():
                rightward(chunk, below).wait_recv()

                @pl.when(tp < ntp - 1)
                def _():
                    rightward(chunk, below).start()

            @pl.when(above < ntp)
            def _():
                leftward(chunk, above).wait_recv()

                @pl.when(tp > 0)
                def _():
                    leftward(chunk, above).start()

    def compute(chunk):
        here = chunk_of(chunk)
        x = jnp.concatenate([xs[index, here] for index in range(ntp)], axis=1).astype(F32)
        mean = jnp.sum(x, axis=1, keepdims=True) * (1.0 / features)
        centered = x - mean
        spread = jnp.sum(centered * centered, axis=1, keepdims=True) * (1.0 / features)
        scale = lax.rsqrt(spread + 1e-05)
        normed = (centered * scale * gain_ref[...] + shift_ref[...]).astype(BF16)
        h1[here] = normed
        stat_out[here, 0:1] = mean
        stat_out[here, 1:2] = scale
        q = (jnp.dot(normed, wq_ref[...], preferred_element_type=F32) + bq_ref[...]) * 0.125
        k = jnp.dot(normed, wk_ref[...], preferred_element_type=F32)
        v = jnp.dot(normed, wv_ref[...], preferred_element_type=F32) + bv_ref[...]
        for index in range(0, heads, 2):
            lanes = slice(index * HEAD_DIM, (index + 2) * HEAD_DIM)
            kv = mix_pair(k[:, lanes], v[:, lanes])
            low = low_half(q[:, lanes])
            qs = (q[:, lanes], swap_halves(q[:, lanes]))
            for off in range(2):
                kvbuf[index + off, here] = kv[off].astype(BF16)
                qbuf[index + off, here] = jnp.where(low, qs[off], 0.0).astype(BF16)

    def hand_on(chunk):
        for hop in range(heads):
            if hop:
                kv_copy(chunk, hop).wait_recv()
            for step in range(1, share):
                kv_on(chunk, hop, step).start()

    slice_rows = wo_out.shape[3]
    half = lax.rem(part, 2)

    def wo_along(step):
        start = pl.multiple_of((head * 2 + half) * slice_rows, slice_rows)
        return remote(
            wo_ref.at[pl.ds(start, slice_rows)], wo_out.at[tp, head, half],
            wz_s.at[step - 1], wz_r.at[step - 1], place.along(step)[1],
        )

    def wo_across(step):
        spot = wo_out.at[:, head, half]
        return remote(spot, spot, wa_s.at[step - 1], wa_r.at[step - 1], place.across(step)[1])

    def wo_swap():
        spot = wo_out.at[:, :, half]
        return remote(spot, spot, wp_s.at[0], wp_r.at[0], (seq + 1 - 2 * half, tp))

    xs[tp] = x_ref[...]
    own_rows = pl.ds(pl.multiple_of((head * 2 + half) * slice_rows, slice_rows), slice_rows)
    early = [
        pltpu.make_async_copy(wo_ref.at[own_rows], wo_out.at[tp, head, half], local.at[5]),
        pltpu.make_async_copy(cot_ref.at[pl.ds(0, g_out.shape[1])], g_out.at[tp], local.at[6]),
    ]
    for copy in early:
        copy.start()
    copies = [
        pltpu.make_async_copy(
            cot_ref.at[pl.ds(g_out.shape[1], rest_out.shape[0])], rest_out, local.at[2]
        )
    ]
    copies[0].start()
    greet(
        [place.partner(step)[1] for step in range(1, share)]
        + [place.across(step)[1] for step in range(1, heads)]
        + [place.along(step)[1] for step in range(1, ntp)]
    )
    for step in range(1, ntp):
        wo_along(step).start()
    own_send(0)
    own_send(1)
    fill_table(place, docs_ref, pads_ref, picks_ref, table_out, nrows)
    for copy in early:
        copy.wait()
    for step in range(1, ntp):
        wo_along(step).wait_recv()
    for step in range(1, heads):
        wo_across(step).start()
    for chunk in range(CHUNKS):
        if chunk > 0:
            own_send(chunk + 1)
        pass_on(chunk)
        compute(chunk)
        here = chunk_of(chunk)
        for index, (source, target) in enumerate(
            [(h1.at[here], h1_out.at[here]), (xs.at[:, here], xs_out.at[:, here])]
        ):
            copies.append(pltpu.make_async_copy(source, target, local.at[7 + 2 * chunk + index]))
            copies[-1].start()
        for step in range(1, heads):
            kv_copy(chunk, step).start()
        for step in range(1, heads):
            q_copy(chunk, step).start()
        if chunk > 0:
            hand_on(chunk - 1)
        if chunk == 2:
            for step in range(1, heads):
                wo_across(step).wait_recv()
            wo_swap().start()
    for index, (source, target) in enumerate(
        [(qbuf.at[head], q_out.at[head]), (kvbuf.at[head], kv_out.at[part, head])]
    ):
        copies.append(pltpu.make_async_copy(source, target, local.at[index]))
        copies[-1].start()
    mine = pl.ds(pl.multiple_of(tp * (rows // ntp), rows // ntp), rows // ntp)
    xt_out[...] = xs[:, mine]
    hand_on(CHUNKS - 1)
    for chunk in range(CHUNKS, CHUNKS + COT_CHUNKS):
        if chunk + 1 < CHUNKS + COT_CHUNKS:
            own_send(chunk + 1)
        pass_on(chunk)
    wo_swap().wait()
    for step in range(1, ntp):
        wo_along(step).wait_send()
    for step in range(1, heads):
        wo_across(step).wait_send()
    for copy in copies:
        copy.wait()
    for chunk in range(CHUNKS):
        for step in range(1, heads):
            q_copy(chunk, step).wait_recv()
        for hop in range(heads):
            for step in range(1, share):
                kv_on(chunk, hop, step).wait_recv()
    for chunk in range(CHUNKS):
        for step in range(1, heads):
            q_copy(chunk, step).wait_send()
            kv_copy(chunk, step).wait_send()
        for hop in range(heads):
            for step in range(1, share):
                kv_on(chunk, hop, step).wait_send()
    for chunk in range(CHUNKS + COT_CHUNKS):
        for index in range(ntp):
            @pl.when((tp >= index) & (tp < ntp - 1))
            def _():
                rightward(chunk, index).wait_send()

            @pl.when((tp <= index) & (tp > 0))
            def _():
                leftward(chunk, index).wait_send()


def run_head(dims, nrows, docs, pads, picks, x, *params):
    heads, share, nseq, ntp = dims
    rows, width = x.shape
    nblocks = picks.shape[1]
    first = rows // CHUNKS * COT_CHUNKS
    sds = jax.ShapeDtypeStruct
    outs = [
        sds((heads, rows, WIDE), BF16),
        sds((share, heads, rows, WIDE), BF16),
        sds((rows, width * ntp), BF16),
        sds((ntp, rows, width), BF16),
        sds((ntp, first, width), BF16),
        sds((rows - first, width), BF16),
        sds((ntp, heads, 2, params[-1].shape[0] // (2 * heads), params[-1].shape[1]), BF16),
        sds((ntp, rows // ntp, width), BF16),
        sds((rows, 2), F32),
        sds((16, nblocks), jnp.int32),
    ]
    scratch = [
        vmem(ntp, rows, width),
        vmem(rows, width * ntp),
        vmem(heads, rows, WIDE),
        vmem(heads, rows, WIDE),
    ]
    sems = (
        [dma(CHUNKS + COT_CHUNKS, ntp)] * 4 + [dma(CHUNKS, heads - 1)] * 4
        + [dma(CHUNKS, heads, share - 1)] * 2 + [dma(ntp - 1)] * 2 + [dma(heads - 1)] * 2
        + [dma(1)] * 2 + [dma(7 + 2 * CHUNKS)]
    )
    return pl.pallas_call(
        functools.partial(head_kernel, dims, nrows),
        out_shape=outs,
        in_specs=[IN_SMEM, IN_SMEM] + [IN_VMEM] * (2 + len(params)),
        out_specs=[ANYWHERE] * 7 + [IN_VMEM] * 3,
        scratch_shapes=scratch + sems,
        name="head",
        cost_estimate=pl.CostEstimate(flops=60 << 30, bytes_accessed=8 << 20, transcendentals=0),
        compiler_params=pltpu.CompilerParams(
            collective_id=1, has_side_effects=True, vmem_limit_bytes=60 << 20
        ),
    )(docs, pads, picks, x, *params)


def block_of(place, query, nrows):
    source, row = split_by(query, nrows)
    return row * place.nseq + source * place.share + place.part


def row_of(place, block, nrows):
    row, holder = split_by(block, place.nseq)
    head, part = split_by(holder, place.share)
    return ((part * place.heads + head) * nrows + row) * BLK


def near_slots(table_ref, block):
    entries = [table_ref[index, block] for index in range(SLOTS)]
    slots = [pl.multiple_of(entry >> 7, BLK) for entry in entries]
    return slots, [entry & (WIDE - 1) for entry in entries]


def long_slots(place, table_ref, block, chunk, nrows):
    first, last = table_ref[SLOTS, block], table_ref[SLOTS + 1, block]
    final = BLK - table_ref[SLOTS + 2, block]
    slots, lives = [], []
    for index in range(SLOTS):
        wanted = first + chunk * SLOTS + index
        slots.append(pl.multiple_of(row_of(place, jnp.minimum(wanted, last), nrows), BLK))
        lives.append(jnp.where(wanted < last, BLK, jnp.where(wanted == last, final, 0)))
    return slots, lives


def for_long(place, table_ref, nquery, nrows, body):
    def step(query, carry):
        block = block_of(place, query, nrows)
        first, last = table_ref[SLOTS, block], table_ref[SLOTS + 1, block]

        @pl.when((block - first < GLOBAL) & (last - first >= SLOTS))
        def _():
            body(query, block, (last - first + SLOTS) >> 3)

        return carry

    lax.fori_loop(0, nquery, step, 0)


def bias_row(lives):
    lane = lax.broadcasted_iota(jnp.int32, (1, WIDE), 1)
    parts = []
    for index in range(0, SLOTS, 2):
        bound = jnp.where(lane < BLK, lives[index], lives[index + 1] + BLK)
        parts.append(jnp.where(lane < bound, 0.0, NEG))
    return jnp.concatenate(parts, axis=1)


def take(ref, slots):
    return jnp.concatenate([ref[pl.ds(slot, BLK), :] for slot in slots], axis=0)


def forward_kernel(dims, nrows, unroll, table_ref, q_ref, kv_ref, out_ref, res_ref):
    place = Place(dims)
    nquery = q_ref.shape[0] // BLK
    upper = lax.broadcasted_iota(jnp.int32, (BLK, WIDE), 1) >= HEAD_DIM

    def finish(query, top, total, accum):
        value = accum / total
        res_ref[pl.ds(query * BLK, BLK), :] = jnp.where(upper, value, top + jnp.log(total))
        return value

    def scores_of(query, slots, lives):
        kv = take(kv_ref, slots)
        scores = lax.dot_general(
            q_ref[pl.ds(query * BLK, BLK), :], kv, NT, preferred_element_type=F32
        )
        return kv, scores + bias_row(lives)

    def near_one(query):
        kv, scores = scores_of(query, *near_slots(table_ref, block_of(place, query, nrows)))
        top = jnp.max(scores, axis=1, keepdims=True)
        weights = jnp.exp(scores - top)
        total = jnp.sum(weights, axis=1, keepdims=True)
        accum = jnp.dot(weights.astype(BF16), kv, preferred_element_type=F32)
        return finish(query, top, total, accum)

    def near_step(index, carry):
        for offset in range(unroll):
            pair = index * unroll + offset
            even, odd = near_one(2 * pair), near_one(2 * pair + 1)
            out_ref[pl.ds(pair * BLK, BLK), :] = jnp.where(upper, odd, swap_halves(even)).astype(BF16)
        return carry

    lax.fori_loop(0, nquery // (2 * unroll), near_step, 0)

    def long_body(query, block, chunks):
        def chunk_step(chunk, state):
            top, total, accum = state
            kv, scores = scores_of(query, *long_slots(place, table_ref, block, chunk, nrows))
            new_top = jnp.maximum(top, jnp.max(scores, axis=1, keepdims=True))
            weights = jnp.exp(scores - new_top)
            decay = jnp.exp(top - new_top)
            total = total * decay + jnp.sum(weights, axis=1, keepdims=True)
            accum = accum * decay + jnp.dot(weights.astype(BF16), kv, preferred_element_type=F32)
            return new_top, total, accum

        start = (
            jnp.full((BLK, 1), NEG, F32),
            jnp.zeros((BLK, 1), F32),
            jnp.zeros((BLK, WIDE), F32),
        )
        value = finish(query, *lax.fori_loop(0, chunks, chunk_step, start))
        spot = pl.ds(pl.multiple_of((query >> 1) * BLK, BLK), BLK)
        is_odd = (query & 1) == 1
        moved = jnp.where(is_odd, value, swap_halves(value))
        out_ref[spot, :] = jnp.where(upper == is_odd, moved, out_ref[spot, :].astype(F32)).astype(BF16)

    for_long(place, table_ref, nquery, nrows, long_body)


def backward_kernel(
    dims, nrows, unroll, table_ref, q_ref, do_ref, res_ref, kv_ref, dq_ref, dkv_ref, sum_ref
):
    place = Place(dims)
    nquery = q_ref.shape[0] // BLK
    upper = lax.broadcasted_iota(jnp.int32, (BLK, WIDE), 1) >= HEAD_DIM
    sum_ref[...] = jnp.zeros_like(sum_ref)

    def load(query, packed, is_odd):
        moved = jnp.where(is_odd, packed, swap_halves(packed))
        grad = jnp.where(upper, moved, 0.0)
        rows = pl.ds(query * BLK, BLK)
        both = jnp.concatenate([q_ref[rows, :], grad.astype(BF16)], axis=0)
        res = res_ref[rows, :]
        delta = jnp.sum(res * grad, axis=1, keepdims=True)
        return both, res[:, :1], delta

    def terms(both, log_total, delta, slots, lives):
        kv = take(kv_ref, slots)
        pair = lax.dot_general(both, kv, NT, preferred_element_type=F32)
        probs = jnp.exp(pair[:BLK] + bias_row(lives) - log_total)
        grad_scores = (probs * (pair[BLK:] - delta)).astype(BF16)
        weights = jnp.concatenate([grad_scores, probs.astype(BF16)], axis=0)
        dkv = lax.dot_general(weights, both, TN, preferred_element_type=F32)
        dq = jnp.dot(grad_scores, kv, preferred_element_type=F32)
        return dq, dkv

    def scatter(slots, dkv):
        for index, slot in enumerate(slots):
            sum_ref[pl.ds(slot, BLK), :] += dkv[index * BLK : (index + 1) * BLK]

    def near_step(index, carry):
        done = []
        for offset in range(unroll):
            pair = index * unroll + offset
            packed = do_ref[pl.ds(pair * BLK, BLK), :].astype(F32)
            grads = []
            for is_odd in (False, True):
                query = 2 * pair + int(is_odd)
                slots, lives = near_slots(table_ref, block_of(place, query, nrows))
                dq, dkv = terms(*load(query, packed, is_odd), slots, lives)
                grads.append(dq)
                done.append((slots, dkv))
            dq_ref[pl.ds(pair * BLK, BLK), :] = jnp.where(
                upper, swap_halves(grads[1]), grads[0]
            ).astype(BF16)
        for slots, dkv in done:
            scatter(slots, dkv)
        return carry

    lax.fori_loop(0, nquery // (2 * unroll), near_step, 0)

    def long_body(query, block, chunks):
        is_odd = (query & 1) == 1
        spot = pl.ds(pl.multiple_of((query >> 1) * BLK, BLK), BLK)
        loaded = load(query, do_ref[spot, :].astype(F32), is_odd)

        def chunk_step(chunk, total):
            slots, lives = long_slots(place, table_ref, block, chunk, nrows)
            dq, dkv = terms(*loaded, slots, lives)
            scatter(slots, dkv)
            return total + dq

        total = lax.fori_loop(0, chunks, chunk_step, jnp.zeros((BLK, WIDE), F32))
        moved = jnp.where(is_odd, swap_halves(total), total)
        dq_ref[spot, :] = jnp.where(upper == is_odd, moved, dq_ref[spot, :].astype(F32)).astype(BF16)

    for_long(place, table_ref, nquery, nrows, long_body)
    dkv_ref[...] = sum_ref[...].astype(BF16)


def local_call(kernel, name, out_shape, nvmem, scratch=()):
    return pl.pallas_call(
        kernel,
        out_shape=out_shape,
        in_specs=[IN_SMEM] + [IN_VMEM] * nvmem,
        out_specs=jax.tree.map(lambda _: IN_VMEM, out_shape),
        scratch_shapes=list(scratch),
        name=name,
        cost_estimate=pl.CostEstimate(flops=30 << 30, bytes_accessed=8 << 20, transcendentals=0),
        compiler_params=pltpu.CompilerParams(vmem_limit_bytes=56 << 20),
    )


class GradScatter:
    def __init__(self, place, source, bufs, sems):
        self.place, self.source = place, source
        self.land, self.pair, self.far = bufs
        self.send1, self.recv1, self.send2, self.recv2 = sems

    @staticmethod
    def buffers(dims, band, cols):
        heads, share = dims[:2]
        return [
            vmem(max(share - 1, 1), heads, band, cols),
            vmem(heads, band, cols),
            vmem(max(heads - 1, 1), band, cols),
        ]

    @staticmethod
    def semaphores(dims, count):
        return [dma(count, dims[1] - 1)] * 2 + [dma(count, dims[0] - 1)] * 2

    def near(self, step):
        other, device = self.place.partner(step)
        return remote(
            self.source.at[:, other], self.land.at[step - 1],
            self.send1.at[step - 1], self.recv1.at[step - 1], device,
        )

    def across(self, step):
        other, device = self.place.across(step)
        return remote(
            self.pair.at[other], self.far.at[step - 1],
            self.send2.at[step - 1], self.recv2.at[step - 1], device,
        )

    def start_near(self):
        for step in range(1, self.place.share):
            self.near(step).start()

    def sum_near(self):
        place = self.place
        for step in range(1, place.share):
            self.near(step).wait_recv()

        def body(head, carry):
            parts = [self.source[head, place.part]]
            parts += [self.land[step, head] for step in range(place.share - 1)]
            self.pair[head] = add_up(*parts).astype(BF16)
            return carry

        lax.fori_loop(0, place.heads, body, 0)

    def start_across(self):
        self.sum_near()
        for step in range(1, self.place.heads):
            self.across(step).start()

    def result(self):
        heads = self.place.heads
        for step in range(1, heads):
            self.across(step).wait_recv()
        return add_up(self.pair[self.place.head], *[self.far[step] for step in range(heads - 1)])

    def finish_near(self):
        for step in range(1, self.place.share):
            self.near(step).wait_send()

    def finish(self):
        self.finish_near()
        for step in range(1, self.place.heads):
            self.across(step).wait_send()


def gelu_pair(value):
    root = math.sqrt(2.0 / math.pi)
    square = value * value
    curve = jnp.tanh(root * value * (1.0 + 0.044715 * square))
    half = 0.5 * (1.0 + curve)
    slope = half + 0.5 * value * (1.0 - curve * curve) * (root * (1.0 + 3 * 0.044715 * square))
    return value * half, slope


def middle_kernel(
    dims,
    o_ref, g0_hbm, g1_hbm, wo_hbm, wi_hbm, wu_hbm, xt_ref, ob_ref, gain_ref, shift_ref, ib_ref, ub_ref,
    sum_out, do_out, da_out, mixed_out, vec_out, gi_out, gu_out,
    g_ref, wo_ref, wi_ref, wu_ref, o_in, x1, xhat, scale, h2, act, dpre, outb, terms, from_left, from_right, do_buf, ib_sum, gi, gu, land_i, land_u, pair_i, pair_u, far_i, far_u,
    *rest,
):
    place = Place(dims)
    heads, share, nseq, ntp = dims
    head, part, seq, tp = place.head, place.part, place.seq, place.tp
    sems = rest
    (o_s, o_r, hr_s, hr_r, hl_s, hl_r, tr_s, tr_r, tl_s, tl_r, do_s, do_r,
     g1_s, g1_r, g2_s, g2_r, local) = sems
    rows, width = g_ref.shape[1:]
    features = width * ntp
    tokens = rows // ntp
    rounds = ROUNDS
    span = tokens // rounds
    pieces = tokens // (2 * BLK)
    places = 2 * ntp - 1
    band = features // heads
    per = features // WIDE

    def packed_rows(index, count=tokens // 2):
        return pl.ds(pl.multiple_of(index * count, count), count)

    def span_of(index):
        return pl.ds(pl.multiple_of(index * span, span), span)

    def o_copy(step):
        to_head, to_tp, device = place.apart(step)
        return remote(
            o_ref.at[to_head, packed_rows(to_tp)], o_in.at[tp * heads + head],
            o_s.at[step], o_r.at[step], device,
        )

    def do_copy(index, step):
        to_head, to_tp, device = place.apart(step)
        return remote(
            do_buf.at[to_tp * heads + to_head, packed_rows(index, BLK)],
            do_out.at[head, packed_rows(tp * pieces + index, BLK)],
            do_s.at[index, step], do_r.at[index, step], device,
        )

    def h2_copy(index, owner, right):
        spot = h2.at[owner, span_of(index)]
        if right:
            return remote(spot, spot, hr_s.at[index, owner], hr_r.at[index, owner], (seq, tp + 1))
        return remote(spot, spot, hl_s.at[index, owner], hl_r.at[index, owner], (seq, tp - 1))

    def term_rows(index):
        return pl.ds(pl.multiple_of(index * (span // SPLIT), span // SPLIT), span // SPLIT)

    def term_copy(index, owner, right):
        here = term_rows(index)
        if right:
            return remote(
                terms.at[owner, here], from_left.at[owner, here],
                tr_s.at[index, owner], tr_r.at[index, owner], (seq, tp + 1),
            )
        return remote(
            terms.at[owner, here], from_right.at[owner, here],
            tl_s.at[index, owner], tl_r.at[index, owner], (seq, tp - 1),
        )

    scatters = [
        GradScatter(place, source, bufs, (g1_s.at[k], g1_r.at[k], g2_s.at[k], g2_r.at[k]))
        for k, (source, bufs) in enumerate(
            ((gi, (land_i, pair_i, far_i)), (gu, (land_u, pair_u, far_u)))
        )
    ]

    first_rows = g0_hbm.shape[1]
    loads = [
        pltpu.make_async_copy(o_ref.at[head, packed_rows(tp)], o_in.at[tp * heads + head], local.at[2]),
        pltpu.make_async_copy(wo_hbm, wo_ref, local.at[3]),
        pltpu.make_async_copy(wi_hbm, wi_ref, local.at[4]),
        pltpu.make_async_copy(wu_hbm, wu_ref, local.at[5]),
        pltpu.make_async_copy(g0_hbm, g_ref.at[:, pl.ds(0, first_rows)], local.at[6]),
        pltpu.make_async_copy(
            g1_hbm, g_ref.at[:, pl.ds(first_rows, rows - first_rows)], local.at[7]
        ),
    ]
    for load in loads:
        load.start()
    greet(
        [place.partner(step)[1] for step in range(1, share)]
        + [place.apart(step)[2] for step in range(1, heads * ntp)]
    )
    for step in range(heads * ntp - 1, 0, -1):
        o_copy(step).start()
    ib_sum[...] = jnp.zeros_like(ib_sum)
    for load in loads:
        load.wait()
    for step in range(1, heads * ntp):
        o_copy(step).wait_recv()

    for index in range(pieces):
        here = slice(index * 2 * BLK, (index + 1) * 2 * BLK)
        half = slice(index * BLK, (index + 1) * BLK)
        mixed = jnp.concatenate(
            [unpack_pair(o_in[i, half], o_in[i + 1, half]) for i in range(0, heads * ntp, 2)], axis=1
        )
        mixed_out[here] = mixed
        base = jnp.concatenate([xt_ref[i, here] for i in range(ntp)], axis=1).astype(F32)
        value = base + ob_ref[...] + jnp.dot(mixed, wo_ref[...].reshape(features, features), preferred_element_type=F32)
        x1[here] = value
        centered = value - jnp.sum(value, axis=1, keepdims=True) * (1.0 / features)
        spread = jnp.sum(centered * centered, axis=1, keepdims=True) * (1.0 / features)
        inverse = lax.rsqrt(spread + 1e-05)
        normed = centered * inverse
        xhat[here] = normed
        scale[here] = jnp.broadcast_to(inverse, (2 * BLK, WIDE))
        h2[tp, here] = (normed * gain_ref[...] + shift_ref[...]).astype(BF16)
        for part_index in range(index * rounds // pieces, (index + 1) * rounds // pieces):

            @pl.when(tp < ntp - 1)
            def _():
                h2_copy(part_index, tp, True).start()

            @pl.when(tp > 0)
            def _():
                h2_copy(part_index, tp, False).start()

    def spot_of(position):
        hop = (position + 1) // 2
        owner = tp + jnp.where(position % 2 == 1, -hop, hop)
        return owner, (owner >= 0) & (owner < ntp)

    def feed(index, owner):
        here = span_of(index)
        wide = span_of(owner * rounds + index)
        pre = jnp.dot(h2[owner, here], wi_ref[...], preferred_element_type=F32) + ib_ref[...]
        value, slope = gelu_pair(pre)
        value = value.astype(BF16)
        act[wide] = value
        grad = jnp.concatenate([g_ref[i, wide] for i in range(ntp)], axis=1)
        back = lax.dot_general(grad, wu_ref[...], NT, preferred_element_type=F32) * slope
        back = back.astype(BF16)
        dpre[wide] = back
        ib_sum[0:1, :] += jnp.sum(back.astype(F32), axis=0, keepdims=True)
        terms[owner, here] = lax.dot_general(
            back, wi_ref[...], NT, preferred_element_type=F32
        ).astype(BF16)

        @pl.when((owner > tp) & (tp == 0))
        def _():
            for sub in range(SPLIT):
                term_copy(index * SPLIT + sub, owner, True).start()

        @pl.when((owner < tp) & (tp == ntp - 1))
        def _():
            for sub in range(SPLIT):
                term_copy(index * SPLIT + sub, owner, False).start()

        out = jnp.dot(value, wu_ref[...], preferred_element_type=F32)
        out = out + jnp.where(owner == tp, x1[here] + ub_ref[...], 0.0)
        for i in range(ntp):
            outb[i, wide] = out[:, i * width : (i + 1) * width].astype(BF16)

    def relay_right(index):
        for owner in range(1, ntp):

            @pl.when((owner > tp) & (tp > 0))
            def _():
                for sub in range(SPLIT):
                    piece = index * SPLIT + sub
                    here = term_rows(piece)
                    term_copy(piece, owner, True).wait_recv()
                    terms[owner, here] = add_up(terms[owner, here], from_left[owner, here]).astype(BF16)
                    term_copy(piece, owner, True).start()

    def relay_left(index):
        for owner in range(ntp - 2, -1, -1):

            @pl.when((owner < tp) & (tp < ntp - 1))
            def _():
                for sub in range(SPLIT):
                    piece = index * SPLIT + sub
                    here = term_rows(piece)
                    term_copy(piece, owner, False).wait_recv()
                    terms[owner, here] = add_up(terms[owner, here], from_right[owner, here]).astype(BF16)
                    term_copy(piece, owner, False).start()

    def relay(index, first):
        @pl.when((tp < ntp // 2) == first)
        def _():
            relay_right(index)

        @pl.when((tp < ntp // 2) != first)
        def _():
            relay_left(index)

    def pass_on(index, hop):
        below, above = tp - hop, tp + hop

        @pl.when(below >= 0)
        def _():
            h2_copy(index, below, True).wait_recv()

            @pl.when(tp < ntp - 1)
            def _():
                h2_copy(index, below, True).start()

        @pl.when(above < ntp)
        def _():
            h2_copy(index, above, False).wait_recv()

            @pl.when(tp > 0)
            def _():
                h2_copy(index, above, False).start()

    def feed_step(count, carry):
        index, position = count // places, count % places
        owner, inside = spot_of(position)

        @pl.when(position % 2 == 1)
        def _():
            pass_on(index, (position + 1) // 2)

        @pl.when(inside)
        def _():
            feed(index, owner)

        @pl.when((index > 0) & (position == 2))
        def _():
            relay(index - 1, True)

        @pl.when((index > 0) & (position == places - 1))
        def _():
            relay(index - 1, False)

        return carry

    lax.fori_loop(0, rounds * places, feed_step, 0)
    save = pltpu.make_async_copy(outb, sum_out, local.at[0])
    save.start()

    def inner_grad(index):
        left = h2[:, :, index * band : (index + 1) * band].reshape(rows, band)
        value = lax.dot_general(left, dpre[...], TN, preferred_element_type=F32)
        gi[index] = value.astype(BF16).reshape(gi.shape[1:])

    def outer_grad(index):
        many = ntp // heads
        left = jnp.concatenate([g_ref[i] for i in range(index * many, (index + 1) * many)], axis=1)
        value = lax.dot_general(left, act[...], TN, preferred_element_type=F32)
        gu[index] = value.astype(BF16).reshape(gu.shape[1:])

    work = [functools.partial(inner_grad, index) for index in range(heads)]
    work += [functools.partial(outer_grad, index) for index in range(heads)]
    def finish(index):
        here = slice(index * 2 * BLK, (index + 1) * 2 * BLK)
        half = slice(index * BLK, (index + 1) * BLK)
        wide = pl.ds(pl.multiple_of(tp * tokens + index * 2 * BLK, 2 * BLK), 2 * BLK)
        finer = rounds * SPLIT
        for part_index in range(index * finer // pieces, (index + 1) * finer // pieces):

            @pl.when(tp > 0)
            def _():
                term_copy(part_index, tp, True).wait_recv()

            @pl.when(tp < ntp - 1)
            def _():
                term_copy(part_index, tp, False).wait_recv()

        grad = terms[tp, here].astype(F32)
        grad = grad + jnp.where(tp > 0, from_left[tp, here].astype(F32), 0.0)
        grad = grad + jnp.where(tp < ntp - 1, from_right[tp, here].astype(F32), 0.0)
        hat = xhat[here]
        inner = grad * gain_ref[...]
        mean0 = jnp.sum(inner, axis=1, keepdims=True) * (1.0 / features)
        mean1 = jnp.sum(inner * hat, axis=1, keepdims=True) * (1.0 / features)
        tail = scale[here, 0:1] * (inner - mean0 - hat * mean1)
        cot = jnp.concatenate([g_ref[i, wide] for i in range(ntp)], axis=1).astype(F32)
        branch = (cot + tail).astype(BF16)
        da_out[here] = branch
        do = lax.dot_general(
            branch, wo_ref[...].reshape(features, features), NT, preferred_element_type=F32
        )
        for i in range(0, heads * ntp, 2):
            pair = pack_pair(do[:, i * HEAD_DIM : (i + 2) * HEAD_DIM])
            do_buf[i, half] = pair[0]
            do_buf[i + 1, half] = pair[1]
        for step in range(heads * ntp - 1, 0, -1):
            do_copy(index, step).start()
        sums = (
            jnp.sum(branch.astype(F32), axis=0, keepdims=True),
            jnp.sum(grad * hat, axis=0, keepdims=True),
            jnp.sum(grad, axis=0, keepdims=True),
        )
        for kind, value in enumerate(sums):
            for sub in range(per):
                row = slice(kind * per + sub, kind * per + sub + 1)
                piece = value[:, sub * WIDE : (sub + 1) * WIDE]
                if index == 0:
                    vec_out[row, :] = piece
                else:
                    vec_out[row, :] += piece
    early = pieces * (rounds - 1) // rounds
    for item in work[:heads]:
        item()
    scatters[0].start_near()
    for index in range(early):
        finish(index)
    relay(rounds - 1, True)
    scatters[0].start_across()
    for item in work[heads:]:
        item()
    scatters[1].start_near()
    relay(rounds - 1, False)
    for index in range(early, pieces):
        finish(index)
    own = pltpu.make_async_copy(
        do_buf.at[tp * heads + head], do_out.at[head, packed_rows(tp)], local.at[1]
    )
    own.start()
    scatters[1].start_across()
    cot = jnp.sum(g_ref[tp].astype(F32), axis=0, keepdims=True)
    for sub in range(per):
        owner, lane = divmod(sub * WIDE, width)
        vec_out[3 * per + sub : 3 * per + sub + 1, :] = jnp.where(
            tp == owner, cot[:, lane : lane + WIDE], 0.0
        )
    for sub in range(ib_sum.shape[1] // WIDE):
        row = 4 * per + sub
        vec_out[row : row + 1, :] = ib_sum[0:1, sub * WIDE : (sub + 1) * WIDE]
    gi_out[...] = scatters[0].result()
    gu_out[...] = scatters[1].result().T
    save.wait()
    own.wait()
    for step in range(1, heads * ntp):
        for index in range(pieces):
            do_copy(index, step).wait_recv()
    for step in range(1, heads * ntp):
        o_copy(step).wait_send()
        for index in range(pieces):
            do_copy(index, step).wait_send()
    for index in range(rounds):
        for owner in range(ntp):
            @pl.when((tp >= owner) & (tp < ntp - 1))
            def _():
                h2_copy(index, owner, True).wait_send()

            @pl.when((tp <= owner) & (tp > 0))
            def _():
                h2_copy(index, owner, False).wait_send()

            for sub in range(SPLIT):
                @pl.when(tp < owner)
                def _():
                    term_copy(index * SPLIT + sub, owner, True).wait_send()

                @pl.when(tp > owner)
                def _():
                    term_copy(index * SPLIT + sub, owner, False).wait_send()

    for scatter in scatters:
        scatter.finish()


def run_middle(dims, o, g0, g1, wo, wi, wu, xt, ob, gain, shift, ib, ub):
    heads, share, nseq, ntp = dims
    rows, width = g0.shape[1] + g1.shape[1], g0.shape[2]
    features, hidden = width * ntp, wi.shape[1]
    tokens, band = rows // ntp, features // nseq
    per = features // WIDE
    rounds, pieces = ROUNDS, tokens // (2 * BLK)
    sds = jax.ShapeDtypeStruct
    outs = [
        sds((ntp, rows, width), BF16),
        sds((heads, rows // 2, WIDE), BF16),
        sds((tokens, features), BF16),
        sds((tokens, features), BF16),
        sds((4 * per + hidden // WIDE, WIDE), F32),
        sds((band, hidden), F32),
        sds((hidden, band), F32),
    ]
    count = heads * ntp
    scratch = [
        vmem(ntp, rows, width),
        vmem(*wo.shape),
        vmem(*wi.shape),
        vmem(*wu.shape),
        vmem(count, tokens // 2, WIDE),
        vmem(tokens, features, dtype=F32),
        vmem(tokens, features, dtype=F32),
        vmem(tokens, WIDE, dtype=F32),
        vmem(ntp, tokens, features),
        vmem(rows, hidden),
        vmem(rows, hidden),
        vmem(ntp, rows, width),
        vmem(ntp, tokens, features),
        vmem(ntp, tokens, features),
        vmem(ntp, tokens, features),
        vmem(count, tokens // 2, WIDE),
        vmem(8, hidden, dtype=F32),
        vmem(heads, share, band, hidden),
        vmem(heads, share, band, hidden),
        vmem(max(share - 1, 1), heads, band, hidden),
        vmem(max(share - 1, 1), heads, band, hidden),
        vmem(heads, band, hidden),
        vmem(heads, band, hidden),
        vmem(max(heads - 1, 1), band, hidden),
        vmem(max(heads - 1, 1), band, hidden),
    ]
    sems = (
        [dma(count)] * 2 + [dma(rounds, ntp)] * 4 + [dma(rounds * SPLIT, ntp)] * 4 + [dma(pieces, count)] * 2
        + GradScatter.semaphores(dims, 2) + [dma(8)]
    )
    return pl.pallas_call(
        functools.partial(middle_kernel, dims),
        out_shape=outs,
        in_specs=[ANYWHERE] * 6 + [IN_VMEM] * 6,
        out_specs=[ANYWHERE] * 2 + [IN_VMEM] * 5,
        scratch_shapes=scratch + sems,
        name="middle",
        cost_estimate=pl.CostEstimate(flops=110 << 30, bytes_accessed=8 << 20, transcendentals=0),
        compiler_params=pltpu.CompilerParams(
            collective_id=2, has_side_effects=True, vmem_limit_bytes=63 << 20
        ),
    )(o, g0, g1, wo, wi, wu, xt, ob, gain, shift, ib, ub)


def tail_kernel(
    dims,
    dq_ref, dkv_hbm, h1_hbm, x_hbm, da_ref, mixed_ref, stat_ref, gain_ref, wq_ref, wk_ref, wv_ref, vec_ref,
    gx_ref, ow_ref, oq_ref, ok_ref, ov_ref, vout_ref,
    dkv_own, h1_ref, x_ref, dq_in, dkv_in, dkv_land, dkv_sum, all3, pbuf, from_left, from_right,
    sums, sums_land, vbuf, vec_land, vsum, vec_far, gw, g3, wbuf, wfar,
    *rest,
):
    place = Place(dims)
    heads, share, nseq, ntp = dims
    head, part, seq, tp = place.head, place.part, place.seq, place.tp
    lands, sems = rest[:6], rest[6:]
    (dq_s, dq_r, kv1_s, kv1_r, kv2_s, kv2_r, right_s, right_r, left_s, left_r,
     st_s, st_r, v1_s, v1_r, v2_s, v2_r, w_s, w_r, g1_s, g1_r, g2_s, g2_r, load_s) = sems
    rows, features = h1_ref.shape
    width = features // ntp
    tokens = rows // ntp
    local_width = wq_ref.shape[1]
    chunk_rows = rows // CHUNKS
    band = features // heads
    per = features // WIDE

    def chunk_of(chunk):
        return pl.ds(chunk * chunk_rows, chunk_rows)

    def half_of(chunk):
        return pl.ds(chunk * chunk_rows // 2, chunk_rows // 2)

    def columns_of(index):
        return pl.ds(pl.multiple_of(index * width, width), width)

    def dq_copy(chunk, step):
        other, device = place.across(step)
        return remote(
            dq_ref.at[other, half_of(chunk)], dq_in.at[head, half_of(chunk)],
            dq_s.at[chunk, step - 1], dq_r.at[chunk, step - 1], device,
        )

    def dkv_near(chunk, step):
        other, device = place.partner(step)
        here = chunk_of(chunk)
        return remote(
            dkv_hbm.at[other, :, here], dkv_land.at[step - 1, :, here],
            kv1_s.at[chunk, step - 1], kv1_r.at[chunk, step - 1], device,
        )

    def dkv_copy(chunk, step):
        other, device = place.across(step)
        return remote(
            dkv_sum.at[other, chunk_of(chunk)], dkv_in.at[head, chunk_of(chunk)],
            kv2_s.at[chunk, step - 1], kv2_r.at[chunk, step - 1], device,
        )

    def rightward(chunk, index):
        return remote(
            pbuf.at[chunk, index], from_left.at[chunk, index],
            right_s.at[chunk, index], right_r.at[chunk, index], (seq, tp + 1),
        )

    def leftward(chunk, index):
        return remote(
            pbuf.at[chunk, index], from_right.at[chunk, index],
            left_s.at[chunk, index], left_r.at[chunk, index], (seq, tp - 1),
        )

    def sums_copy(step):
        return remote(
            sums, sums_land.at[step - 1], st_s.at[step - 1], st_r.at[step - 1], place.along(step)[1]
        )

    def vec_copy(step):
        return remote(
            vbuf, vec_land.at[step - 1], v1_s.at[step - 1], v1_r.at[step - 1],
            (lax.rem(seq + step, nseq), tp),
        )

    def vec_far_copy(step):
        return remote(
            vsum, vec_far.at[step - 1], v2_s.at[step - 1], v2_r.at[step - 1], place.along(step)[1]
        )

    def w_copy(step):
        other, device = place.along(step)
        return remote(wbuf.at[other], wfar.at[step - 1], w_s.at[step - 1], w_r.at[step - 1], device)

    scatters = [
        GradScatter(
            place, source, lands[3 * k : 3 * k + 3], (g1_s.at[k], g1_r.at[k], g2_s.at[k], g2_r.at[k])
        )
        for k, source in enumerate((gw, g3))
    ]

    loads = [
        pltpu.make_async_copy(dkv_hbm.at[part], dkv_own, load_s.at[0]),
        pltpu.make_async_copy(dq_ref.at[head], dq_in.at[head], load_s.at[1]),
        pltpu.make_async_copy(x_hbm, x_ref, load_s.at[2]),
        pltpu.make_async_copy(h1_hbm, h1_ref, load_s.at[3]),
    ]
    for load in loads:
        load.start()
    greet(
        [(lax.rem(seq + step, nseq), tp) for step in range(1, nseq)]
        + [place.along(step)[1] for step in range(1, ntp)]
    )
    for chunk in range(CHUNKS):
        for step in range(1, share):
            dkv_near(chunk, step).start()
    vbuf[: 2 * per] = jnp.zeros((2 * per, WIDE), F32)
    vbuf[2 * per : 6 * per] = vec_ref[: 4 * per]
    narrow = 3 * local_width // WIDE
    vbuf[6 * per : 6 * per + narrow] = jnp.zeros((narrow, WIDE), F32)
    vbuf[6 * per + narrow :] = vec_ref[4 * per :]
    loads[0].wait()
    for chunk in range(CHUNKS):
        for step in range(1, heads):
            dq_copy(chunk, step).start()
        for step in range(1, share):
            dkv_near(chunk, step).wait_recv()
        for target in range(heads):
            where = (target, chunk_of(chunk))
            parts = [dkv_own[where]] + [dkv_land[(step,) + where] for step in range(share - 1)]
            dkv_sum[where] = add_up(*parts).astype(BF16)
        for step in range(1, heads):
            dkv_copy(chunk, step).start()
    dkv_in[head] = dkv_sum[head]
    for load in loads[1:]:
        load.wait()

    def output_grad(index):
        value = lax.dot_general(
            da_ref[:, index * band : (index + 1) * band], mixed_ref[...], TN, preferred_element_type=F32
        )
        gw[index] = value.astype(BF16).reshape(gw.shape[1:])

    gain = gain_ref[...]
    lane = lax.broadcasted_iota(jnp.int32, (chunk_rows, WIDE), 1)

    def partial_step(chunk):
        here, half = chunk_of(chunk), half_of(chunk)
        for step in range(1, heads):
            dq_copy(chunk, step).wait_recv()
            dkv_copy(chunk, step).wait_recv()
        three = [[], [], []]
        for i in range(0, heads, 2):
            three[0].append(unpack_pair(dq_in[i, half], dq_in[i + 1, half]))
            k, v = mix_pair(dkv_in[i, here].astype(F32), dkv_in[i + 1, here].astype(F32))
            three[1].append(k.astype(BF16))
            three[2].append(v.astype(BF16))
        three = [jnp.concatenate(item, axis=1) for item in three]
        grad = 0.125 * lax.dot_general(three[0], wq_ref[...], NT, preferred_element_type=F32)
        grad = grad + lax.dot_general(three[1], wk_ref[...], NT, preferred_element_type=F32)
        grad = grad + lax.dot_general(three[2], wv_ref[...], NT, preferred_element_type=F32)
        row = 6 * per
        for kind, value in enumerate(three):
            all3[here, kind * local_width : (kind + 1) * local_width] = value
            column = jnp.sum(value.astype(F32), axis=0, keepdims=True)
            for start in range(0, local_width, WIDE):
                vbuf[row : row + 1, :] += column[:, start : start + WIDE]
                row += 1
        mean, scale = stat_ref[here, 0:1], stat_ref[here, 1:2]
        sum0 = jnp.zeros((chunk_rows, 1), F32)
        sum1 = jnp.zeros((chunk_rows, 1), F32)
        for index in range(ntp):
            cols = slice(index * width, (index + 1) * width)
            piece = grad[:, cols]
            xhat = (x_ref[index, here].astype(F32) - mean) * scale
            weighted = piece * gain[:, cols]
            sum0 = sum0 + jnp.sum(weighted, axis=1, keepdims=True)
            sum1 = sum1 + jnp.sum(weighted * xhat, axis=1, keepdims=True)
            col0 = jnp.sum(piece * xhat, axis=0, keepdims=True)
            col1 = jnp.sum(piece, axis=0, keepdims=True)
            for sub in range(width // WIDE):
                row = index * (width // WIDE) + sub
                lanes = slice(sub * WIDE, (sub + 1) * WIDE)
                vbuf[row : row + 1, :] += col0[:, lanes]
                vbuf[per + row : per + row + 1, :] += col1[:, lanes]
            pbuf[chunk, index] = piece.astype(BF16)
            for sub in range(max(chunk_rows // tokens, 1)):
                rows_here = slice(sub * tokens, sub * tokens + min(tokens, chunk_rows))

                @pl.when(tp == chunk * chunk_rows // tokens + sub)
                def _():
                    start = chunk * chunk_rows % tokens
                    carried = da_ref[start : start + min(tokens, chunk_rows), cols].astype(F32)
                    carried = carried / (scale[rows_here] * gain[:, cols])
                    pbuf[chunk, index, rows_here] = (piece[rows_here] + carried).astype(BF16)

        both = jnp.where(lane == 0, sum0, jnp.where(lane == 1, sum1, 0.0))
        sums[:, here] = both.T[:8]

    def set_off(chunk):
        for step in range(ntp - 1):
            far = ntp - 1 - step

            @pl.when(tp == 0)
            def _():
                rightward(chunk, far).start()

            @pl.when(tp == ntp - 1)
            def _():
                leftward(chunk, step).start()

    def relay_right(chunk):
        for step in range(ntp - 1):
            far = ntp - 1 - step

            @pl.when((tp < far) & (tp > 0))
            def _():
                rightward(chunk, far).wait_recv()
                pbuf[chunk, far] = add_up(pbuf[chunk, far], from_left[chunk, far]).astype(BF16)
                rightward(chunk, far).start()

    def relay_left(chunk):
        for step in range(ntp - 1):

            @pl.when((tp > step) & (tp < ntp - 1))
            def _():
                leftward(chunk, step).wait_recv()
                pbuf[chunk, step] = add_up(pbuf[chunk, step], from_right[chunk, step]).astype(BF16)
                leftward(chunk, step).start()

    def relay(chunk):
        @pl.when(tp < ntp // 2)
        def _():
            relay_right(chunk)
            relay_left(chunk)

        @pl.when(tp >= ntp // 2)
        def _():
            relay_left(chunk)
            relay_right(chunk)

    def projection_grad(index):
        left = h1_ref[:, pl.ds(index * band, band)]
        value = lax.dot_general(left, all3[...], TN, preferred_element_type=F32)
        g3[index] = value.astype(BF16).reshape(g3.shape[1:])

    for index in range(heads):
        output_grad(index)
    scatters[0].start_near()
    for chunk in range(CHUNKS):
        partial_step(chunk)
        set_off(chunk)
        if chunk == 0:
            scatters[0].start_across()
        if chunk > 1:
            relay(chunk - 2)
    for step in range(1, ntp):
        sums_copy(step).start()
    for step in range(1, nseq):
        vec_copy(step).start()
    for index in range(heads // 2):
        projection_grad(index)
    relay(CHUNKS - 2)
    for index in range(heads // 2, heads):
        projection_grad(index)
    scatters[1].start_near()
    for step in range(1, nseq):
        vec_copy(step).wait_recv()
    total = vbuf[...]
    for step in range(nseq - 1):
        total = total + vec_land[step]
    vsum[...] = total
    for step in range(1, ntp):
        vec_far_copy(step).start()
    scatters[1].start_across()
    relay(CHUNKS - 1)
    value = scatters[0].result().astype(BF16)
    for index in range(ntp):
        wbuf[index] = value[:, index * local_width : (index + 1) * local_width]
    for step in range(1, ntp):
        w_copy(step).start()

    for step in range(1, ntp):
        sums_copy(step).wait_recv()
    my_gain = gain_ref[:, columns_of(tp)]
    for chunk in range(CHUNKS):
        here = chunk_of(chunk)
        both = sums[:, here]
        for step in range(ntp - 1):
            both = both + sums_land[step, :, here]
        both = jnp.concatenate([both, jnp.zeros((WIDE - 8, chunk_rows), F32)], axis=0).T
        both = both * (1.0 / features)

        @pl.when(tp > 0)
        def _():
            rightward(chunk, tp).wait_recv()

        @pl.when(tp < ntp - 1)
        def _():
            leftward(chunk, tp).wait_recv()

        grad = pbuf[chunk, tp].astype(F32)
        grad = grad + jnp.where(tp > 0, from_left[chunk, tp].astype(F32), 0.0)
        grad = grad + jnp.where(tp < ntp - 1, from_right[chunk, tp].astype(F32), 0.0)
        mean, scale = stat_ref[here, 0:1], stat_ref[here, 1:2]
        xhat = (x_ref[tp, here].astype(F32) - mean) * scale
        gx_ref[here] = scale * (grad * my_gain - both[:, 0:1] - xhat * both[:, 1:2])
    value = scatters[1].result()
    oq_ref[...] = 0.125 * value[:, :local_width]
    ok_ref[...] = value[:, local_width : 2 * local_width]
    ov_ref[...] = value[:, 2 * local_width :]
    for step in range(1, ntp):
        vec_far_copy(step).wait_recv()
        w_copy(step).wait_recv()
    vout_ref[...] = vsum[...]
    for step in range(ntp - 1):
        vout_ref[: 6 * per] += vec_far[step, : 6 * per]
    ow_ref[...] = add_up(wbuf[tp], *[wfar[step] for step in range(ntp - 1)]).T

    for chunk in range(CHUNKS):
        for step in range(1, share):
            dkv_near(chunk, step).wait_send()
        for step in range(1, heads):
            dq_copy(chunk, step).wait_send()
            dkv_copy(chunk, step).wait_send()
        for index in range(ntp):
            @pl.when(tp < index)
            def _():
                rightward(chunk, index).wait_send()

            @pl.when(tp > index)
            def _():
                leftward(chunk, index).wait_send()

    for step in range(1, ntp):
        sums_copy(step).wait_send()
        vec_far_copy(step).wait_send()
        w_copy(step).wait_send()
    for step in range(1, nseq):
        vec_copy(step).wait_send()
    for scatter in scatters:
        scatter.finish()


def run_tail(dims, dq, dkv, h1, x_parts, da, mixed, stats, gain, wq, wk, wv, vec):
    heads, share, nseq, ntp = dims
    rows, features = h1.shape
    width, tokens = features // ntp, rows // ntp
    band = features // nseq
    local_width = wq.shape[1]
    per = features // WIDE
    sds = jax.ShapeDtypeStruct
    nvec = vec.shape[0] + 2 * per + 3 * local_width // WIDE
    outs = [
        sds((rows, width), F32),
        sds((local_width, band), F32),
        sds((band, local_width), F32),
        sds((band, local_width), F32),
        sds((band, local_width), F32),
        sds((nvec, WIDE), F32),
    ]
    pieces = (CHUNKS, ntp, rows // CHUNKS, width)
    scratch = [
        vmem(heads, rows, WIDE),
        vmem(rows, features),
        vmem(ntp, rows, width),
        vmem(heads, rows // 2, WIDE),
        vmem(heads, rows, WIDE),
        vmem(max(share - 1, 1), heads, rows, WIDE),
        vmem(heads, rows, WIDE),
        vmem(rows, 3 * local_width),
        vmem(*pieces),
        vmem(*pieces),
        vmem(*pieces),
        vmem(8, rows, dtype=F32),
        vmem(ntp - 1, 8, rows, dtype=F32),
        vmem(nvec, WIDE, dtype=F32),
        vmem(nseq - 1, nvec, WIDE, dtype=F32),
        vmem(nvec, WIDE, dtype=F32),
        vmem(ntp - 1, nvec, WIDE, dtype=F32),
        vmem(heads, share, band, features),
        vmem(heads, share, band, 3 * local_width),
        vmem(ntp, band, local_width),
        vmem(ntp - 1, band, local_width),
        *GradScatter.buffers(dims, band, features),
        *GradScatter.buffers(dims, band, 3 * local_width),
    ]
    sems = (
        [dma(CHUNKS, heads - 1)] * 2 + [dma(CHUNKS, share - 1)] * 2 + [dma(CHUNKS, heads - 1)] * 2
        + [dma(CHUNKS, ntp)] * 4 + [dma(ntp - 1)] * 2 + [dma(nseq - 1)] * 2 + [dma(ntp - 1)] * 4
        + GradScatter.semaphores(dims, 2) + [dma(4)]
    )
    return pl.pallas_call(
        functools.partial(tail_kernel, dims),
        out_shape=outs,
        in_specs=[ANYWHERE] * 4 + [IN_VMEM] * 8,
        out_specs=[IN_VMEM] * len(outs),
        scratch_shapes=scratch + sems,
        name="tail",
        cost_estimate=pl.CostEstimate(flops=70 << 30, bytes_accessed=8 << 20, transcendentals=0),
        compiler_params=pltpu.CompilerParams(
            collective_id=3, has_side_effects=True, vmem_limit_bytes=60 << 20
        ),
    )(dq, dkv, h1, x_parts, da, mixed, stats, gain, wq, wk, wv, vec)


def deliver_kernel(sizes, *refs):
    many = (len(refs) - 2 - len(sizes)) // 3
    vec, sources = refs[0], refs[1 : 1 + many]
    pieces, targets = refs[1 + many : 1 + many + len(sizes)], refs[1 + many + len(sizes) : 1 + 2 * many + len(sizes)]
    held, sems = refs[1 + 2 * many + len(sizes) : -1], refs[-1]
    loads = [
        pltpu.make_async_copy(source, buf, sems.at[0, index])
        for index, (source, buf) in enumerate(zip(sources, held))
    ]
    saves = [
        pltpu.make_async_copy(buf, target, sems.at[1, index])
        for index, (target, buf) in enumerate(zip(targets, held))
    ]
    for load in loads:
        load.start()
    start = 0
    for index, (size, factor) in enumerate(sizes):
        pieces[index][...] = factor * vec[start : start + size]
        start += size
    for load, save in zip(loads, saves):
        load.wait()
        save.start()
    for save in saves:
        save.wait()


def deliver(vec, sizes, arrays):
    sds = jax.ShapeDtypeStruct
    outs = [sds((size, WIDE), F32) for size, _ in sizes] + [sds(a.shape, a.dtype) for a in arrays]
    results = pl.pallas_call(
        functools.partial(deliver_kernel, sizes),
        out_shape=outs,
        in_specs=[IN_VMEM] + [ANYWHERE] * len(arrays),
        out_specs=[IN_VMEM] * len(sizes) + [ANYWHERE] * len(arrays),
        scratch_shapes=[vmem(*a.shape, dtype=a.dtype) for a in arrays] + [dma(2, len(arrays))],
        name="deliver",
        compiler_params=pltpu.CompilerParams(vmem_limit_bytes=60 << 20),
    )(vec, *arrays)
    return [item.reshape(-1) for item in results[: len(sizes)]], results[len(sizes) :]


def on_device(
    hidden_in,
    norm_gain,
    norm_shift,
    query_weight,
    query_bias,
    key_weight,
    value_weight,
    value_bias,
    output_weight,
    output_bias,
    feed_gain,
    feed_shift,
    inner_weight,
    inner_bias,
    outer_weight,
    outer_bias,
    doc_blocks,
    doc_padding,
    random_picks,
    cotangent,
):
    nrows, block_len, width = hidden_in.shape
    rows = nrows * block_len
    nseq, ntp = lax.axis_size("seq"), lax.axis_size("tp")
    local_width = query_weight.shape[1]
    heads = local_width // HEAD_DIM
    share = nseq // heads
    dims = (heads, share, nseq, ntp)
    features = width * ntp
    per = features // WIDE
    cot = cotangent.reshape(rows, width)
    q, kv, h1, x_parts, g_first, rest, output_full, x_mine, stats, table = run_head(
        dims, nrows, doc_blocks, doc_padding, random_picks.T, hidden_in.reshape(rows, width),
        norm_gain[None, :], norm_shift[None, :], query_weight, query_bias[None, :],
        key_weight, value_weight, value_bias[None, :], cot, output_weight,
    )
    g_rest = lax.all_gather(rest, "tp", axis=0)
    q = q.reshape(heads * rows, WIDE)
    kv = kv.reshape(nseq * rows, WIDE)
    sds = jax.ShapeDtypeStruct
    packed, res = local_call(
        functools.partial(forward_kernel, dims, nrows, 4),
        "attention_forward",
        (sds((heads * rows // 2, WIDE), BF16), sds((heads * rows, WIDE), F32)),
        2,
    )(table, q, kv)
    out_sum, do, da, mixed, vec, inner_part, outer_part = run_middle(
        dims, packed.reshape(heads, rows // 2, WIDE), g_first, g_rest, output_full,
        inner_weight, outer_weight, x_mine, output_bias[None, :], feed_gain[None, :],
        feed_shift[None, :], inner_bias[None, :], outer_bias[None, :],
    )
    result = lax.psum_scatter(out_sum, "tp", scatter_dimension=0)
    dq, dkv = local_call(
        functools.partial(backward_kernel, dims, nrows, 4),
        "attention_backward",
        (sds((heads * rows // 2, WIDE), BF16), sds((nseq * rows, WIDE), BF16)),
        4,
        [pltpu.VMEM((nseq * rows, WIDE), F32)],
    )(table, q, do.reshape(heads * rows // 2, WIDE), res, kv)
    grad_x, output_part, query_part, key_part, value_part, vectors = run_tail(
        dims, dq.reshape(heads, rows // 2, WIDE), dkv.reshape(share, heads, rows, WIDE), h1,
        x_parts, da, mixed, stats, norm_gain[None, :], query_weight, key_weight, value_weight, vec,
    )
    lines = local_width // WIDE
    sizes = [(per, 1.0)] * 6 + [(lines, 0.125), (lines, 1.0), (lines, 1.0)]
    sizes += [(vectors.shape[0] - 6 * per - 3 * lines, 1.0)]
    sums, arrays = deliver(
        vectors,
        tuple(sizes),
        [grad_x, output_part, query_part, key_part, value_part, inner_part, outer_part],
    )
    grad_x, output_part, query_part, key_part, value_part, inner_part, outer_part = arrays
    return (
        result.reshape(hidden_in.shape),
        grad_x.reshape(hidden_in.shape),
        sums[0],
        sums[1],
        query_part,
        sums[6],
        key_part,
        value_part,
        sums[8],
        output_part,
        sums[2],
        sums[3],
        sums[4],
        inner_part,
        sums[9],
        outer_part,
        sums[5],
    )


def solution(mesh):
    return jax.shard_map(
        on_device,
        mesh=mesh,
        in_specs=(
            P(None, "seq", "tp"),
            P(),
            P(),
            P(None, "tp"),
            P("tp"),
            P(None, "tp"),
            P(None, "tp"),
            P("tp"),
            P("tp", None),
            P(),
            P(),
            P(),
            P(None, "tp"),
            P("tp"),
            P("tp", None),
            P(),
            P(),
            P(),
            P(),
            P(None, "seq", "tp"),
        ),
        out_specs=(
            P(None, "seq", "tp"),
            P(None, "seq", "tp"),
            P(),
            P(),
            P("seq", "tp"),
            P("tp"),
            P("seq", "tp"),
            P("seq", "tp"),
            P("tp"),
            P("tp", "seq"),
            P(),
            P(),
            P(),
            P("seq", "tp"),
            P("tp"),
            P("tp", "seq"),
            P(),
        ),
        check_vma=False,
    )
```

```python
import functools
import math

import jax
import jax.numpy as jnp
from jax import lax
from jax.experimental import pallas as pl
from jax.experimental.pallas import tpu as pltpu
from jax.sharding import PartitionSpec as P

HEAD_DIM = 64
BLK = 64
GLOBAL = 2
SLOTS = 8
WIDE = 2 * HEAD_DIM
CHUNKS = 4
COT_CHUNKS = 1
ROUNDS = 2
SPLIT = 2
NEG = -1e30
NT = (((1,), (1,)), ((), ()))
TN = (((0,), (0,)), ((), ()))
MESH = pl.DeviceIdType.MESH
F32, BF16 = jnp.float32, jnp.bfloat16


def split_by(value, count):
    if count & (count - 1) == 0:
        return value >> (count.bit_length() - 1), value & (count - 1)
    return value // count, value % count


def remote(src, dst, send_sem, recv_sem, device):
    return pltpu.make_async_remote_copy(
        src_ref=src, dst_ref=dst, send_sem=send_sem, recv_sem=recv_sem,
        device_id=device, device_id_type=MESH,
    )


def greet(peers):
    barrier = pltpu.get_barrier_semaphore()
    for peer in peers:
        pl.semaphore_signal(barrier, inc=1, device_id=peer, device_id_type=MESH)
    pl.semaphore_wait(barrier, len(peers))


def add_up(*terms):
    total = terms[0].astype(F32)
    for term in terms[1:]:
        total = total + term.astype(F32)
    return total


def swap_halves(value):
    return pltpu.roll(value, HEAD_DIM, 1)


def low_half(value):
    return lax.broadcasted_iota(jnp.int32, value.shape, 1) < HEAD_DIM


def mix_pair(left, right):
    low = low_half(left)
    return (
        jnp.where(low, left, swap_halves(right)),
        jnp.where(low, swap_halves(left), right),
    )


def unpack_pair(left, right):
    even, odd = mix_pair(left.astype(F32), right.astype(F32))
    tiles = []
    for start in range(0, left.shape[0], BLK):
        tiles += [even[start : start + BLK], odd[start : start + BLK]]
    return jnp.concatenate(tiles, axis=0).astype(BF16)


def pack_pair(value):
    lefts, rights = [], []
    for start in range(0, value.shape[0], 2 * BLK):
        left, right = mix_pair(value[start : start + BLK], value[start + BLK : start + 2 * BLK])
        lefts.append(left)
        rights.append(right)
    return jnp.concatenate(lefts, axis=0).astype(BF16), jnp.concatenate(rights, axis=0).astype(BF16)


def dma(*shape):
    return pltpu.SemaphoreType.DMA(tuple(max(size, 1) for size in shape))


def vmem(*shape, dtype=BF16):
    return pltpu.VMEM(shape, dtype)


IN_VMEM = pl.BlockSpec(memory_space=pltpu.VMEM)
IN_SMEM = pl.BlockSpec(memory_space=pltpu.SMEM)
ANYWHERE = pl.BlockSpec(memory_space=pl.ANY)


class Place:
    def __init__(self, dims):
        self.heads, self.share, self.nseq, self.ntp = dims
        self.seq, self.tp = lax.axis_index("seq"), lax.axis_index("tp")
        self.head, self.part = self.seq // self.share, lax.rem(self.seq, self.share)

    def partner(self, step):
        other = lax.rem(self.part + step, self.share)
        return other, (self.head * self.share + other, self.tp)

    def across(self, step):
        other = lax.rem(self.head + step, self.heads)
        return other, (other * self.share + self.part, self.tp)

    def along(self, step):
        other = lax.rem(self.tp + step, self.ntp)
        return other, (self.seq, other)

    def apart(self, step):
        far, near = step // self.heads, step % self.heads
        head = lax.rem(self.head + near, self.heads)
        tp = lax.rem(self.tp + far, self.ntp)
        return head, tp, (head * self.share + self.part, tp)


def fill_table(place, docs_ref, pads_ref, picks_ref, table_ref, nrows):
    nblocks = table_ref.shape[1]
    block = lax.broadcasted_iota(jnp.int32, (1, nblocks), 1)

    def doc_step(doc, state):
        start, first, last, pad = state
        stop = start + docs_ref[doc]
        inside = (block >= start) & (block < stop)
        first = jnp.where(inside, start, first)
        last = jnp.where(inside, stop - 1, last)
        pad = jnp.where(inside, pads_ref[doc], pad)
        return stop, first, last, pad

    zero = jnp.zeros((1, nblocks), jnp.int32)
    _, first, last, pad = lax.fori_loop(
        0, docs_ref.shape[0], doc_step, (jnp.int32(0), zero, zero, zero)
    )
    length = last - first + 1
    picks = []
    for index in range(picks_ref.shape[0]):
        pick = picks_ref[index : index + 1, :]
        whole = (pick.astype(F32) / length.astype(F32)).astype(jnp.int32)
        left = pick - whole * length
        left = jnp.where(left < 0, left + length, left)
        left = jnp.where(left >= length, left - length, left)
        picks.append(first + left)
    glob = block - first < GLOBAL
    is_long = glob & (last - first >= SLOTS)
    never = block < 0
    p0, p1, p2 = picks
    fresh = lambda pick: (pick >= first + GLOBAL) & ((pick > block + 1) | (pick < block - 1))
    near = [
        (block - 1, ~never),
        (block, ~never),
        (block + 1, block < last),
        (first, ~never),
        (first + 1, block - 1 > first + 1),
        (p0, fresh(p0)),
        (p1, fresh(p1) & (p1 != p0)),
        (p2, fresh(p2) & (p2 != p0) & (p2 != p1)),
    ]
    for index, (other, use) in enumerate(near):
        whole = first + index
        use = (glob & (whole <= last) & ~is_long) | (~glob & use)
        other = jnp.where(use, jnp.where(glob, whole, other), block)
        live = jnp.where(use, jnp.where(other == last, BLK - pad, BLK), 0)
        table_ref[index : index + 1, :] = row_of(place, other, nrows) * WIDE + live
    table_ref[SLOTS : SLOTS + 1, :] = first
    table_ref[SLOTS + 1 : SLOTS + 2, :] = last
    table_ref[SLOTS + 2 : SLOTS + 3, :] = pad


def head_kernel(
    dims, nrows, docs_ref, pads_ref, picks_ref, x_ref, gain_ref, shift_ref,
    wq_ref, bq_ref, wk_ref, wv_ref, bv_ref, cot_ref, wo_ref,
    q_out, kv_out, h1_out, xs_out, g_out, rest_out, wo_out, xt_out, stat_out, table_out,
    xs, h1, qbuf, kvbuf, right_s, right_r, left_s, left_r, q_s, q_r, kv_s, kv_r, on_s, on_r,
    wz_s, wz_r, wa_s, wa_r, wp_s, wp_r, local,
):
    place = Place(dims)
    heads, share, nseq, ntp = dims
    head, part, seq, tp = place.head, place.part, place.seq, place.tp
    rows, width = x_ref.shape
    features = width * ntp
    chunk_rows = rows // CHUNKS

    def chunk_of(chunk):
        return pl.ds(chunk * chunk_rows, chunk_rows)

    def traveller(chunk, index):
        if chunk < CHUNKS:
            return xs.at[index, chunk_of(chunk)]
        return g_out.at[index, chunk_of(chunk - CHUNKS)]

    def rightward(chunk, index):
        spot = traveller(chunk, index)
        return remote(
            spot, spot, right_s.at[chunk, index], right_r.at[chunk, index], (seq, tp + 1)
        )

    def leftward(chunk, index):
        spot = traveller(chunk, index)
        return remote(spot, spot, left_s.at[chunk, index], left_r.at[chunk, index], (seq, tp - 1))

    def q_copy(chunk, step):
        other, device = place.across(step)
        return remote(
            qbuf.at[other, chunk_of(chunk)], q_out.at[head, chunk_of(chunk)],
            q_s.at[chunk, step - 1], q_r.at[chunk, step - 1], device,
        )

    def kv_copy(chunk, step):
        other, device = place.across(step)
        return remote(
            kvbuf.at[other, chunk_of(chunk)], kv_out.at[part, head, chunk_of(chunk)],
            kv_s.at[chunk, step - 1], kv_r.at[chunk, step - 1], device,
        )

    def kv_on(chunk, hop, step):
        owner = lax.rem(head + heads - hop, heads)
        spot = kv_out.at[part, owner, chunk_of(chunk)]
        source = kvbuf.at[head, chunk_of(chunk)] if hop == 0 else spot
        return remote(
            source, spot, on_s.at[chunk, hop, step - 1], on_r.at[chunk, hop, step - 1],
            place.partner(step)[1],
        )

    def own_send(chunk):
        @pl.when(tp < ntp - 1)
        def _():
            rightward(chunk, tp).start()

        @pl.when(tp > 0)
        def _():
            leftward(chunk, tp).start()

    def pass_on(chunk):
        for hop in range(1, ntp):
            below, above = tp - hop, tp + hop

            @pl.when(below >= 0)
            def _():
                rightward(chunk, below).wait_recv()

                @pl.when(tp < ntp - 1)
                def _():
                    rightward(chunk, below).start()

            @pl.when(above < ntp)
            def _():
                leftward(chunk, above).wait_recv()

                @pl.when(tp > 0)
                def _():
                    leftward(chunk, above).start()

    def compute(chunk):
        here = chunk_of(chunk)
        x = jnp.concatenate([xs[index, here] for index in range(ntp)], axis=1).astype(F32)
        mean = jnp.sum(x, axis=1, keepdims=True) * (1.0 / features)
        centered = x - mean
        spread = jnp.sum(centered * centered, axis=1, keepdims=True) * (1.0 / features)
        scale = lax.rsqrt(spread + 1e-05)
        normed = (centered * scale * gain_ref[...] + shift_ref[...]).astype(BF16)
        h1[here] = normed
        stat_out[here, 0:1] = mean
        stat_out[here, 1:2] = scale
        q = (jnp.dot(normed, wq_ref[...], preferred_element_type=F32) + bq_ref[...]) * 0.125
        k = jnp.dot(normed, wk_ref[...], preferred_element_type=F32)
        v = jnp.dot(normed, wv_ref[...], preferred_element_type=F32) + bv_ref[...]
        for index in range(0, heads, 2):
            lanes = slice(index * HEAD_DIM, (index + 2) * HEAD_DIM)
            kv = mix_pair(k[:, lanes], v[:, lanes])
            low = low_half(q[:, lanes])
            qs = (q[:, lanes], swap_halves(q[:, lanes]))
            for off in range(2):
                kvbuf[index + off, here] = kv[off].astype(BF16)
                qbuf[index + off, here] = jnp.where(low, qs[off], 0.0).astype(BF16)

    def hand_on(chunk):
        for hop in range(heads):
            if hop:
                kv_copy(chunk, hop).wait_recv()
            for step in range(1, share):
                kv_on(chunk, hop, step).start()

    slice_rows = wo_out.shape[3]
    half = lax.rem(part, 2)

    def wo_along(step):
        start = pl.multiple_of((head * 2 + half) * slice_rows, slice_rows)
        return remote(
            wo_ref.at[pl.ds(start, slice_rows)], wo_out.at[tp, head, half],
            wz_s.at[step - 1], wz_r.at[step - 1], place.along(step)[1],
        )

    def wo_across(step):
        spot = wo_out.at[:, head, half]
        return remote(spot, spot, wa_s.at[step - 1], wa_r.at[step - 1], place.across(step)[1])

    def wo_swap():
        spot = wo_out.at[:, :, half]
        return remote(spot, spot, wp_s.at[0], wp_r.at[0], (seq + 1 - 2 * half, tp))

    xs[tp] = x_ref[...]
    own_rows = pl.ds(pl.multiple_of((head * 2 + half) * slice_rows, slice_rows), slice_rows)
    early = [
        pltpu.make_async_copy(wo_ref.at[own_rows], wo_out.at[tp, head, half], local.at[5]),
        pltpu.make_async_copy(cot_ref.at[pl.ds(0, g_out.shape[1])], g_out.at[tp], local.at[6]),
    ]
    for copy in early:
        copy.start()
    copies = [
        pltpu.make_async_copy(
            cot_ref.at[pl.ds(g_out.shape[1], rest_out.shape[0])], rest_out, local.at[2]
        )
    ]
    copies[0].start()
    greet(
        [place.partner(step)[1] for step in range(1, share)]
        + [place.across(step)[1] for step in range(1, heads)]
        + [place.along(step)[1] for step in range(1, ntp)]
    )
    for step in range(1, ntp):
        wo_along(step).start()
    own_send(0)
    own_send(1)
    fill_table(place, docs_ref, pads_ref, picks_ref, table_out, nrows)
    for copy in early:
        copy.wait()
    for step in range(1, ntp):
        wo_along(step).wait_recv()
    for step in range(1, heads):
        wo_across(step).start()
    for chunk in range(CHUNKS):
        if chunk > 0:
            own_send(chunk + 1)
        pass_on(chunk)
        compute(chunk)
        here = chunk_of(chunk)
        for index, (source, target) in enumerate(
            [(h1.at[here], h1_out.at[here]), (xs.at[:, here], xs_out.at[:, here])]
        ):
            copies.append(pltpu.make_async_copy(source, target, local.at[7 + 2 * chunk + index]))
            copies[-1].start()
        for step in range(1, heads):
            kv_copy(chunk, step).start()
        for step in range(1, heads):
            q_copy(chunk, step).start()
        if chunk > 0:
            hand_on(chunk - 1)
        if chunk == 2:
            for step in range(1, heads):
                wo_across(step).wait_recv()
            wo_swap().start()
    for index, (source, target) in enumerate(
        [(qbuf.at[head], q_out.at[head]), (kvbuf.at[head], kv_out.at[part, head])]
    ):
        copies.append(pltpu.make_async_copy(source, target, local.at[index]))
        copies[-1].start()
    mine = pl.ds(pl.multiple_of(tp * (rows // ntp), rows // ntp), rows // ntp)
    xt_out[...] = xs[:, mine]
    hand_on(CHUNKS - 1)
    for chunk in range(CHUNKS, CHUNKS + COT_CHUNKS):
        if chunk + 1 < CHUNKS + COT_CHUNKS:
            own_send(chunk + 1)
        pass_on(chunk)
    wo_swap().wait()
    for step in range(1, ntp):
        wo_along(step).wait_send()
    for step in range(1, heads):
        wo_across(step).wait_send()
    for copy in copies:
        copy.wait()
    for chunk in range(CHUNKS):
        for step in range(1, heads):
            q_copy(chunk, step).wait_recv()
        for hop in range(heads):
            for step in range(1, share):
                kv_on(chunk, hop, step).wait_recv()
    for chunk in range(CHUNKS):
        for step in range(1, heads):
            q_copy(chunk, step).wait_send()
            kv_copy(chunk, step).wait_send()
        for hop in range(heads):
            for step in range(1, share):
                kv_on(chunk, hop, step).wait_send()
    for chunk in range(CHUNKS + COT_CHUNKS):
        for index in range(ntp):
            @pl.when((tp >= index) & (tp < ntp - 1))
            def _():
                rightward(chunk, index).wait_send()

            @pl.when((tp <= index) & (tp > 0))
            def _():
                leftward(chunk, index).wait_send()


def run_head(dims, nrows, docs, pads, picks, x, *params):
    heads, share, nseq, ntp = dims
    rows, width = x.shape
    nblocks = picks.shape[1]
    first = rows // CHUNKS * COT_CHUNKS
    sds = jax.ShapeDtypeStruct
    outs = [
        sds((heads, rows, WIDE), BF16),
        sds((share, heads, rows, WIDE), BF16),
        sds((rows, width * ntp), BF16),
        sds((ntp, rows, width), BF16),
        sds((ntp, first, width), BF16),
        sds((rows - first, width), BF16),
        sds((ntp, heads, 2, params[-1].shape[0] // (2 * heads), params[-1].shape[1]), BF16),
        sds((ntp, rows // ntp, width), BF16),
        sds((rows, 2), F32),
        sds((16, nblocks), jnp.int32),
    ]
    scratch = [
        vmem(ntp, rows, width),
        vmem(rows, width * ntp),
        vmem(heads, rows, WIDE),
        vmem(heads, rows, WIDE),
    ]
    sems = (
        [dma(CHUNKS + COT_CHUNKS, ntp)] * 4 + [dma(CHUNKS, heads - 1)] * 4
        + [dma(CHUNKS, heads, share - 1)] * 2 + [dma(ntp - 1)] * 2 + [dma(heads - 1)] * 2
        + [dma(1)] * 2 + [dma(7 + 2 * CHUNKS)]
    )
    return pl.pallas_call(
        functools.partial(head_kernel, dims, nrows),
        out_shape=outs,
        in_specs=[IN_SMEM, IN_SMEM] + [IN_VMEM] * (2 + len(params)),
        out_specs=[ANYWHERE] * 7 + [IN_VMEM] * 3,
        scratch_shapes=scratch + sems,
        name="head",
        cost_estimate=pl.CostEstimate(flops=60 << 30, bytes_accessed=8 << 20, transcendentals=0),
        compiler_params=pltpu.CompilerParams(
            collective_id=1, has_side_effects=True, vmem_limit_bytes=60 << 20
        ),
    )(docs, pads, picks, x, *params)


def block_of(place, query, nrows):
    source, row = split_by(query, nrows)
    return row * place.nseq + source * place.share + place.part


def row_of(place, block, nrows):
    row, holder = split_by(block, place.nseq)
    head, part = split_by(holder, place.share)
    return ((part * place.heads + head) * nrows + row) * BLK


def near_slots(table_ref, block):
    entries = [table_ref[index, block] for index in range(SLOTS)]
    slots = [pl.multiple_of(entry >> 7, BLK) for entry in entries]
    return slots, [entry & (WIDE - 1) for entry in entries]


def long_slots(place, table_ref, block, chunk, nrows):
    first, last = table_ref[SLOTS, block], table_ref[SLOTS + 1, block]
    final = BLK - table_ref[SLOTS + 2, block]
    slots, lives = [], []
    for index in range(SLOTS):
        wanted = first + chunk * SLOTS + index
        slots.append(pl.multiple_of(row_of(place, jnp.minimum(wanted, last), nrows), BLK))
        lives.append(jnp.where(wanted < last, BLK, jnp.where(wanted == last, final, 0)))
    return slots, lives


def for_long(place, table_ref, nquery, nrows, body):
    def step(query, carry):
        block = block_of(place, query, nrows)
        first, last = table_ref[SLOTS, block], table_ref[SLOTS + 1, block]

        @pl.when((block - first < GLOBAL) & (last - first >= SLOTS))
        def _():
            body(query, block, (last - first + SLOTS) >> 3)

        return carry

    lax.fori_loop(0, nquery, step, 0)


def bias_row(lives):
    lane = lax.broadcasted_iota(jnp.int32, (1, WIDE), 1)
    parts = []
    for index in range(0, SLOTS, 2):
        bound = jnp.where(lane < BLK, lives[index], lives[index + 1] + BLK)
        parts.append(jnp.where(lane < bound, 0.0, NEG))
    return jnp.concatenate(parts, axis=1)


def take(ref, slots):
    return jnp.concatenate([ref[pl.ds(slot, BLK), :] for slot in slots], axis=0)


def forward_kernel(dims, nrows, unroll, table_ref, q_ref, kv_ref, out_ref, res_ref):
    place = Place(dims)
    nquery = q_ref.shape[0] // BLK
    upper = lax.broadcasted_iota(jnp.int32, (BLK, WIDE), 1) >= HEAD_DIM

    def finish(query, top, total, accum):
        value = accum / total
        res_ref[pl.ds(query * BLK, BLK), :] = jnp.where(upper, value, top + jnp.log(total))
        return value

    def scores_of(query, slots, lives):
        kv = take(kv_ref, slots)
        scores = lax.dot_general(
            q_ref[pl.ds(query * BLK, BLK), :], kv, NT, preferred_element_type=F32
        )
        return kv, scores + bias_row(lives)

    def near_one(query):
        kv, scores = scores_of(query, *near_slots(table_ref, block_of(place, query, nrows)))
        top = jnp.max(scores, axis=1, keepdims=True)
        weights = jnp.exp(scores - top)
        total = jnp.sum(weights, axis=1, keepdims=True)
        accum = jnp.dot(weights.astype(BF16), kv, preferred_element_type=F32)
        return finish(query, top, total, accum)

    def near_step(index, carry):
        for offset in range(unroll):
            pair = index * unroll + offset
            even, odd = near_one(2 * pair), near_one(2 * pair + 1)
            out_ref[pl.ds(pair * BLK, BLK), :] = jnp.where(upper, odd, swap_halves(even)).astype(BF16)
        return carry

    lax.fori_loop(0, nquery // (2 * unroll), near_step, 0)

    def long_body(query, block, chunks):
        def chunk_step(chunk, state):
            top, total, accum = state
            kv, scores = scores_of(query, *long_slots(place, table_ref, block, chunk, nrows))
            new_top = jnp.maximum(top, jnp.max(scores, axis=1, keepdims=True))
            weights = jnp.exp(scores - new_top)
            decay = jnp.exp(top - new_top)
            total = total * decay + jnp.sum(weights, axis=1, keepdims=True)
            accum = accum * decay + jnp.dot(weights.astype(BF16), kv, preferred_element_type=F32)
            return new_top, total, accum

        start = (
            jnp.full((BLK, 1), NEG, F32),
            jnp.zeros((BLK, 1), F32),
            jnp.zeros((BLK, WIDE), F32),
        )
        value = finish(query, *lax.fori_loop(0, chunks, chunk_step, start))
        spot = pl.ds(pl.multiple_of((query >> 1) * BLK, BLK), BLK)
        is_odd = (query & 1) == 1
        moved = jnp.where(is_odd, value, swap_halves(value))
        out_ref[spot, :] = jnp.where(upper == is_odd, moved, out_ref[spot, :].astype(F32)).astype(BF16)

    for_long(place, table_ref, nquery, nrows, long_body)


def backward_kernel(
    dims, nrows, unroll, table_ref, q_ref, do_ref, res_ref, kv_ref, dq_ref, dkv_ref, sum_ref
):
    place = Place(dims)
    nquery = q_ref.shape[0] // BLK
    upper = lax.broadcasted_iota(jnp.int32, (BLK, WIDE), 1) >= HEAD_DIM
    sum_ref[...] = jnp.zeros_like(sum_ref)

    def load(query, packed, is_odd):
        moved = jnp.where(is_odd, packed, swap_halves(packed))
        grad = jnp.where(upper, moved, 0.0)
        rows = pl.ds(query * BLK, BLK)
        both = jnp.concatenate([q_ref[rows, :], grad.astype(BF16)], axis=0)
        res = res_ref[rows, :]
        delta = jnp.sum(res * grad, axis=1, keepdims=True)
        return both, res[:, :1], delta

    def terms(both, log_total, delta, slots, lives):
        kv = take(kv_ref, slots)
        pair = lax.dot_general(both, kv, NT, preferred_element_type=F32)
        probs = jnp.exp(pair[:BLK] + bias_row(lives) - log_total)
        grad_scores = (probs * (pair[BLK:] - delta)).astype(BF16)
        weights = jnp.concatenate([grad_scores, probs.astype(BF16)], axis=0)
        dkv = lax.dot_general(weights, both, TN, preferred_element_type=F32)
        dq = jnp.dot(grad_scores, kv, preferred_element_type=F32)
        return dq, dkv

    def scatter(slots, dkv):
        for index, slot in enumerate(slots):
            sum_ref[pl.ds(slot, BLK), :] += dkv[index * BLK : (index + 1) * BLK]

    def near_step(index, carry):
        done = []
        for offset in range(unroll):
            pair = index * unroll + offset
            packed = do_ref[pl.ds(pair * BLK, BLK), :].astype(F32)
            grads = []
            for is_odd in (False, True):
                query = 2 * pair + int(is_odd)
                slots, lives = near_slots(table_ref, block_of(place, query, nrows))
                dq, dkv = terms(*load(query, packed, is_odd), slots, lives)
                grads.append(dq)
                done.append((slots, dkv))
            dq_ref[pl.ds(pair * BLK, BLK), :] = jnp.where(
                upper, swap_halves(grads[1]), grads[0]
            ).astype(BF16)
        for slots, dkv in done:
            scatter(slots, dkv)
        return carry

    lax.fori_loop(0, nquery // (2 * unroll), near_step, 0)

    def long_body(query, block, chunks):
        is_odd = (query & 1) == 1
        spot = pl.ds(pl.multiple_of((query >> 1) * BLK, BLK), BLK)
        loaded = load(query, do_ref[spot, :].astype(F32), is_odd)

        def chunk_step(chunk, total):
            slots, lives = long_slots(place, table_ref, block, chunk, nrows)
            dq, dkv = terms(*loaded, slots, lives)
            scatter(slots, dkv)
            return total + dq

        total = lax.fori_loop(0, chunks, chunk_step, jnp.zeros((BLK, WIDE), F32))
        moved = jnp.where(is_odd, swap_halves(total), total)
        dq_ref[spot, :] = jnp.where(upper == is_odd, moved, dq_ref[spot, :].astype(F32)).astype(BF16)

    for_long(place, table_ref, nquery, nrows, long_body)
    dkv_ref[...] = sum_ref[...].astype(BF16)


def local_call(kernel, name, out_shape, nvmem, scratch=()):
    return pl.pallas_call(
        kernel,
        out_shape=out_shape,
        in_specs=[IN_SMEM] + [IN_VMEM] * nvmem,
        out_specs=jax.tree.map(lambda _: IN_VMEM, out_shape),
        scratch_shapes=list(scratch),
        name=name,
        cost_estimate=pl.CostEstimate(flops=30 << 30, bytes_accessed=8 << 20, transcendentals=0),
        compiler_params=pltpu.CompilerParams(vmem_limit_bytes=56 << 20),
    )


class GradScatter:
    def __init__(self, place, source, bufs, sems):
        self.place, self.source = place, source
        self.land, self.pair, self.far = bufs
        self.send1, self.recv1, self.send2, self.recv2 = sems

    @staticmethod
    def buffers(dims, band, cols):
        heads, share = dims[:2]
        return [
            vmem(max(share - 1, 1), heads, band, cols),
            vmem(heads, band, cols),
            vmem(max(heads - 1, 1), band, cols),
        ]

    @staticmethod
    def semaphores(dims, count):
        return [dma(count, dims[1] - 1)] * 2 + [dma(count, dims[0] - 1)] * 2

    def near(self, step):
        other, device = self.place.partner(step)
        return remote(
            self.source.at[:, other], self.land.at[step - 1],
            self.send1.at[step - 1], self.recv1.at[step - 1], device,
        )

    def across(self, step):
        other, device = self.place.across(step)
        return remote(
            self.pair.at[other], self.far.at[step - 1],
            self.send2.at[step - 1], self.recv2.at[step - 1], device,
        )

    def start_near(self):
        for step in range(1, self.place.share):
            self.near(step).start()

    def sum_near(self):
        place = self.place
        for step in range(1, place.share):
            self.near(step).wait_recv()

        def body(head, carry):
            parts = [self.source[head, place.part]]
            parts += [self.land[step, head] for step in range(place.share - 1)]
            self.pair[head] = add_up(*parts).astype(BF16)
            return carry

        lax.fori_loop(0, place.heads, body, 0)

    def start_across(self):
        self.sum_near()
        for step in range(1, self.place.heads):
            self.across(step).start()

    def result(self):
        heads = self.place.heads
        for step in range(1, heads):
            self.across(step).wait_recv()
        return add_up(self.pair[self.place.head], *[self.far[step] for step in range(heads - 1)])

    def finish_near(self):
        for step in range(1, self.place.share):
            self.near(step).wait_send()

    def finish(self):
        self.finish_near()
        for step in range(1, self.place.heads):
            self.across(step).wait_send()


def gelu_pair(value):
    root = math.sqrt(2.0 / math.pi)
    square = value * value
    curve = jnp.tanh(root * value * (1.0 + 0.044715 * square))
    half = 0.5 * (1.0 + curve)
    slope = half + 0.5 * value * (1.0 - curve * curve) * (root * (1.0 + 3 * 0.044715 * square))
    return value * half, slope


def middle_kernel(
    dims,
    o_ref, g0_hbm, g1_hbm, wo_hbm, wi_hbm, wu_hbm, xt_ref, ob_ref, gain_ref, shift_ref, ib_ref, ub_ref,
    sum_out, do_out, da_out, mixed_out, vec_out, gi_out, gu_out,
    g_ref, wo_ref, wi_ref, wu_ref, o_in, x1, xhat, scale, h2, act, dpre, outb, terms, from_left, from_right, do_buf, ib_sum, gi, gu, land_i, land_u, pair_i, pair_u, far_i, far_u,
    *rest,
):
    place = Place(dims)
    heads, share, nseq, ntp = dims
    head, part, seq, tp = place.head, place.part, place.seq, place.tp
    sems = rest
    (o_s, o_r, hr_s, hr_r, hl_s, hl_r, tr_s, tr_r, tl_s, tl_r, do_s, do_r,
     g1_s, g1_r, g2_s, g2_r, local) = sems
    rows, width = g_ref.shape[1:]
    features = width * ntp
    tokens = rows // ntp
    rounds = ROUNDS
    span = tokens // rounds
    pieces = tokens // (2 * BLK)
    places = 2 * ntp - 1
    band = features // heads
    per = features // WIDE

    def packed_rows(index, count=tokens // 2):
        return pl.ds(pl.multiple_of(index * count, count), count)

    def span_of(index):
        return pl.ds(pl.multiple_of(index * span, span), span)

    def o_copy(step):
        to_head, to_tp, device = place.apart(step)
        return remote(
            o_ref.at[to_head, packed_rows(to_tp)], o_in.at[tp * heads + head],
            o_s.at[step], o_r.at[step], device,
        )

    def do_copy(index, step):
        to_head, to_tp, device = place.apart(step)
        return remote(
            do_buf.at[to_tp * heads + to_head, packed_rows(index, BLK)],
            do_out.at[head, packed_rows(tp * pieces + index, BLK)],
            do_s.at[index, step], do_r.at[index, step], device,
        )

    def h2_copy(index, owner, right):
        spot = h2.at[owner, span_of(index)]
        if right:
            return remote(spot, spot, hr_s.at[index, owner], hr_r.at[index, owner], (seq, tp + 1))
        return remote(spot, spot, hl_s.at[index, owner], hl_r.at[index, owner], (seq, tp - 1))

    def term_rows(index):
        return pl.ds(pl.multiple_of(index * (span // SPLIT), span // SPLIT), span // SPLIT)

    def term_copy(index, owner, right):
        here = term_rows(index)
        if right:
            return remote(
                terms.at[owner, here], from_left.at[owner, here],
                tr_s.at[index, owner], tr_r.at[index, owner], (seq, tp + 1),
            )
        return remote(
            terms.at[owner, here], from_right.at[owner, here],
            tl_s.at[index, owner], tl_r.at[index, owner], (seq, tp - 1),
        )

    scatters = [
        GradScatter(place, source, bufs, (g1_s.at[k], g1_r.at[k], g2_s.at[k], g2_r.at[k]))
        for k, (source, bufs) in enumerate(
            ((gi, (land_i, pair_i, far_i)), (gu, (land_u, pair_u, far_u)))
        )
    ]

    first_rows = g0_hbm.shape[1]
    loads = [
        pltpu.make_async_copy(o_ref.at[head, packed_rows(tp)], o_in.at[tp * heads + head], local.at[2]),
        pltpu.make_async_copy(wo_hbm, wo_ref, local.at[3]),
        pltpu.make_async_copy(wi_hbm, wi_ref, local.at[4]),
        pltpu.make_async_copy(wu_hbm, wu_ref, local.at[5]),
        pltpu.make_async_copy(g0_hbm, g_ref.at[:, pl.ds(0, first_rows)], local.at[6]),
        pltpu.make_async_copy(
            g1_hbm, g_ref.at[:, pl.ds(first_rows, rows - first_rows)], local.at[7]
        ),
    ]
    for load in loads:
        load.start()
    greet(
        [place.partner(step)[1] for step in range(1, share)]
        + [place.apart(step)[2] for step in range(1, heads * ntp)]
    )
    for step in range(heads * ntp - 1, 0, -1):
        o_copy(step).start()
    ib_sum[...] = jnp.zeros_like(ib_sum)
    for load in loads:
        load.wait()
    for step in range(1, heads * ntp):
        o_copy(step).wait_recv()

    for index in range(pieces):
        here = slice(index * 2 * BLK, (index + 1) * 2 * BLK)
        half = slice(index * BLK, (index + 1) * BLK)
        mixed = jnp.concatenate(
            [unpack_pair(o_in[i, half], o_in[i + 1, half]) for i in range(0, heads * ntp, 2)], axis=1
        )
        mixed_out[here] = mixed
        base = jnp.concatenate([xt_ref[i, here] for i in range(ntp)], axis=1).astype(F32)
        value = base + ob_ref[...] + jnp.dot(mixed, wo_ref[...].reshape(features, features), preferred_element_type=F32)
        x1[here] = value
        centered = value - jnp.sum(value, axis=1, keepdims=True) * (1.0 / features)
        spread = jnp.sum(centered * centered, axis=1, keepdims=True) * (1.0 / features)
        inverse = lax.rsqrt(spread + 1e-05)
        normed = centered * inverse
        xhat[here] = normed
        scale[here] = jnp.broadcast_to(inverse, (2 * BLK, WIDE))
        h2[tp, here] = (normed * gain_ref[...] + shift_ref[...]).astype(BF16)
        for part_index in range(index * rounds // pieces, (index + 1) * rounds // pieces):

            @pl.when(tp < ntp - 1)
            def _():
                h2_copy(part_index, tp, True).start()

            @pl.when(tp > 0)
            def _():
                h2_copy(part_index, tp, False).start()

    def spot_of(position):
        hop = (position + 1) // 2
        owner = tp + jnp.where(position % 2 == 1, -hop, hop)
        return owner, (owner >= 0) & (owner < ntp)

    def feed(index, owner):
        here = span_of(index)
        wide = span_of(owner * rounds + index)
        pre = jnp.dot(h2[owner, here], wi_ref[...], preferred_element_type=F32) + ib_ref[...]
        value, slope = gelu_pair(pre)
        value = value.astype(BF16)
        act[wide] = value
        grad = jnp.concatenate([g_ref[i, wide] for i in range(ntp)], axis=1)
        back = lax.dot_general(grad, wu_ref[...], NT, preferred_element_type=F32) * slope
        back = back.astype(BF16)
        dpre[wide] = back
        ib_sum[0:1, :] += jnp.sum(back.astype(F32), axis=0, keepdims=True)
        terms[owner, here] = lax.dot_general(
            back, wi_ref[...], NT, preferred_element_type=F32
        ).astype(BF16)

        @pl.when((owner > tp) & (tp == 0))
        def _():
            for sub in range(SPLIT):
                term_copy(index * SPLIT + sub, owner, True).start()

        @pl.when((owner < tp) & (tp == ntp - 1))
        def _():
            for sub in range(SPLIT):
                term_copy(index * SPLIT + sub, owner, False).start()

        out = jnp.dot(value, wu_ref[...], preferred_element_type=F32)
        out = out + jnp.where(owner == tp, x1[here] + ub_ref[...], 0.0)
        for i in range(ntp):
            outb[i, wide] = out[:, i * width : (i + 1) * width].astype(BF16)

    def relay_right(index):
        for owner in range(1, ntp):

            @pl.when((owner > tp) & (tp > 0))
            def _():
                for sub in range(SPLIT):
                    piece = index * SPLIT + sub
                    here = term_rows(piece)
                    term_copy(piece, owner, True).wait_recv()
                    terms[owner, here] = add_up(terms[owner, here], from_left[owner, here]).astype(BF16)
                    term_copy(piece, owner, True).start()

    def relay_left(index):
        for owner in range(ntp - 2, -1, -1):

            @pl.when((owner < tp) & (tp < ntp - 1))
            def _():
                for sub in range(SPLIT):
                    piece = index * SPLIT + sub
                    here = term_rows(piece)
                    term_copy(piece, owner, False).wait_recv()
                    terms[owner, here] = add_up(terms[owner, here], from_right[owner, here]).astype(BF16)
                    term_copy(piece, owner, False).start()

    def relay(index, first):
        @pl.when((tp < ntp // 2) == first)
        def _():
            relay_right(index)

        @pl.when((tp < ntp // 2) != first)
        def _():
            relay_left(index)

    def pass_on(index, hop):
        below, above = tp - hop, tp + hop

        @pl.when(below >= 0)
        def _():
            h2_copy(index, below, True).wait_recv()

            @pl.when(tp < ntp - 1)
            def _():
                h2_copy(index, below, True).start()

        @pl.when(above < ntp)
        def _():
            h2_copy(index, above, False).wait_recv()

            @pl.when(tp > 0)
            def _():
                h2_copy(index, above, False).start()

    def feed_step(count, carry):
        index, position = count // places, count % places
        owner, inside = spot_of(position)

        @pl.when(position % 2 == 1)
        def _():
            pass_on(index, (position + 1) // 2)

        @pl.when(inside)
        def _():
            feed(index, owner)

        @pl.when((index > 0) & (position == 2))
        def _():
            relay(index - 1, True)

        @pl.when((index > 0) & (position == places - 1))
        def _():
            relay(index - 1, False)

        return carry

    lax.fori_loop(0, rounds * places, feed_step, 0)
    save = pltpu.make_async_copy(outb, sum_out, local.at[0])
    save.start()

    def inner_grad(index):
        left = h2[:, :, index * band : (index + 1) * band].reshape(rows, band)
        value = lax.dot_general(left, dpre[...], TN, preferred_element_type=F32)
        gi[index] = value.astype(BF16).reshape(gi.shape[1:])

    def outer_grad(index):
        many = ntp // heads
        left = jnp.concatenate([g_ref[i] for i in range(index * many, (index + 1) * many)], axis=1)
        value = lax.dot_general(left, act[...], TN, preferred_element_type=F32)
        gu[index] = value.astype(BF16).reshape(gu.shape[1:])

    work = [functools.partial(inner_grad, index) for index in range(heads)]
    work += [functools.partial(outer_grad, index) for index in range(heads)]
    def finish(index):
        here = slice(index * 2 * BLK, (index + 1) * 2 * BLK)
        half = slice(index * BLK, (index + 1) * BLK)
        wide = pl.ds(pl.multiple_of(tp * tokens + index * 2 * BLK, 2 * BLK), 2 * BLK)
        finer = rounds * SPLIT
        for part_index in range(index * finer // pieces, (index + 1) * finer // pieces):

            @pl.when(tp > 0)
            def _():
                term_copy(part_index, tp, True).wait_recv()

            @pl.when(tp < ntp - 1)
            def _():
                term_copy(part_index, tp, False).wait_recv()

        grad = terms[tp, here].astype(F32)
        grad = grad + jnp.where(tp > 0, from_left[tp, here].astype(F32), 0.0)
        grad = grad + jnp.where(tp < ntp - 1, from_right[tp, here].astype(F32), 0.0)
        hat = xhat[here]
        inner = grad * gain_ref[...]
        mean0 = jnp.sum(inner, axis=1, keepdims=True) * (1.0 / features)
        mean1 = jnp.sum(inner * hat, axis=1, keepdims=True) * (1.0 / features)
        tail = scale[here, 0:1] * (inner - mean0 - hat * mean1)
        cot = jnp.concatenate([g_ref[i, wide] for i in range(ntp)], axis=1).astype(F32)
        branch = (cot + tail).astype(BF16)
        da_out[here] = branch
        do = lax.dot_general(
            branch, wo_ref[...].reshape(features, features), NT, preferred_element_type=F32
        )
        for i in range(0, heads * ntp, 2):
            pair = pack_pair(do[:, i * HEAD_DIM : (i + 2) * HEAD_DIM])
            do_buf[i, half] = pair[0]
            do_buf[i + 1, half] = pair[1]
        for step in range(heads * ntp - 1, 0, -1):
            do_copy(index, step).start()
        sums = (
            jnp.sum(branch.astype(F32), axis=0, keepdims=True),
            jnp.sum(grad * hat, axis=0, keepdims=True),
            jnp.sum(grad, axis=0, keepdims=True),
        )
        for kind, value in enumerate(sums):
            for sub in range(per):
                row = slice(kind * per + sub, kind * per + sub + 1)
                piece = value[:, sub * WIDE : (sub + 1) * WIDE]
                if index == 0:
                    vec_out[row, :] = piece
                else:
                    vec_out[row, :] += piece
    early = pieces * (rounds - 1) // rounds
    for item in work[:heads]:
        item()
    scatters[0].start_near()
    for index in range(early):
        finish(index)
    relay(rounds - 1, True)
    scatters[0].start_across()
    for item in work[heads:]:
        item()
    scatters[1].start_near()
    relay(rounds - 1, False)
    for index in range(early, pieces):
        finish(index)
    own = pltpu.make_async_copy(
        do_buf.at[tp * heads + head], do_out.at[head, packed_rows(tp)], local.at[1]
    )
    own.start()
    scatters[1].start_across()
    cot = jnp.sum(g_ref[tp].astype(F32), axis=0, keepdims=True)
    for sub in range(per):
        owner, lane = divmod(sub * WIDE, width)
        vec_out[3 * per + sub : 3 * per + sub + 1, :] = jnp.where(
            tp == owner, cot[:, lane : lane + WIDE], 0.0
        )
    for sub in range(ib_sum.shape[1] // WIDE):
        row = 4 * per + sub
        vec_out[row : row + 1, :] = ib_sum[0:1, sub * WIDE : (sub + 1) * WIDE]
    gi_out[...] = scatters[0].result()
    gu_out[...] = scatters[1].result().T
    save.wait()
    own.wait()
    for step in range(1, heads * ntp):
        for index in range(pieces):
            do_copy(index, step).wait_recv()
    for step in range(1, heads * ntp):
        o_copy(step).wait_send()
        for index in range(pieces):
            do_copy(index, step).wait_send()
    for index in range(rounds):
        for owner in range(ntp):
            @pl.when((tp >= owner) & (tp < ntp - 1))
            def _():
                h2_copy(index, owner, True).wait_send()

            @pl.when((tp <= owner) & (tp > 0))
            def _():
                h2_copy(index, owner, False).wait_send()

            for sub in range(SPLIT):
                @pl.when(tp < owner)
                def _():
                    term_copy(index * SPLIT + sub, owner, True).wait_send()

                @pl.when(tp > owner)
                def _():
                    term_copy(index * SPLIT + sub, owner, False).wait_send()

    for scatter in scatters:
        scatter.finish()


def run_middle(dims, o, g0, g1, wo, wi, wu, xt, ob, gain, shift, ib, ub):
    heads, share, nseq, ntp = dims
    rows, width = g0.shape[1] + g1.shape[1], g0.shape[2]
    features, hidden = width * ntp, wi.shape[1]
    tokens, band = rows // ntp, features // nseq
    per = features // WIDE
    rounds, pieces = ROUNDS, tokens // (2 * BLK)
    sds = jax.ShapeDtypeStruct
    outs = [
        sds((ntp, rows, width), BF16),
        sds((heads, rows // 2, WIDE), BF16),
        sds((tokens, features), BF16),
        sds((tokens, features), BF16),
        sds((4 * per + hidden // WIDE, WIDE), F32),
        sds((band, hidden), F32),
        sds((hidden, band), F32),
    ]
    count = heads * ntp
    scratch = [
        vmem(ntp, rows, width),
        vmem(*wo.shape),
        vmem(*wi.shape),
        vmem(*wu.shape),
        vmem(count, tokens // 2, WIDE),
        vmem(tokens, features, dtype=F32),
        vmem(tokens, features, dtype=F32),
        vmem(tokens, WIDE, dtype=F32),
        vmem(ntp, tokens, features),
        vmem(rows, hidden),
        vmem(rows, hidden),
        vmem(ntp, rows, width),
        vmem(ntp, tokens, features),
        vmem(ntp, tokens, features),
        vmem(ntp, tokens, features),
        vmem(count, tokens // 2, WIDE),
        vmem(8, hidden, dtype=F32),
        vmem(heads, share, band, hidden),
        vmem(heads, share, band, hidden),
        vmem(max(share - 1, 1), heads, band, hidden),
        vmem(max(share - 1, 1), heads, band, hidden),
        vmem(heads, band, hidden),
        vmem(heads, band, hidden),
        vmem(max(heads - 1, 1), band, hidden),
        vmem(max(heads - 1, 1), band, hidden),
    ]
    sems = (
        [dma(count)] * 2 + [dma(rounds, ntp)] * 4 + [dma(rounds * SPLIT, ntp)] * 4 + [dma(pieces, count)] * 2
        + GradScatter.semaphores(dims, 2) + [dma(8)]
    )
    return pl.pallas_call(
        functools.partial(middle_kernel, dims),
        out_shape=outs,
        in_specs=[ANYWHERE] * 6 + [IN_VMEM] * 6,
        out_specs=[ANYWHERE] * 2 + [IN_VMEM] * 5,
        scratch_shapes=scratch + sems,
        name="middle",
        cost_estimate=pl.CostEstimate(flops=110 << 30, bytes_accessed=8 << 20, transcendentals=0),
        compiler_params=pltpu.CompilerParams(
            collective_id=2, has_side_effects=True, vmem_limit_bytes=63 << 20
        ),
    )(o, g0, g1, wo, wi, wu, xt, ob, gain, shift, ib, ub)


def tail_kernel(
    dims,
    dq_ref, dkv_hbm, h1_hbm, x_hbm, da_ref, mixed_ref, stat_ref, gain_ref, wq_ref, wk_ref, wv_ref, vec_ref,
    gx_ref, ow_ref, oq_ref, ok_ref, ov_ref, vout_ref,
    dkv_own, h1_ref, x_ref, dq_in, dkv_in, dkv_land, dkv_sum, all3, pbuf, from_left, from_right,
    sums, sums_land, vbuf, vec_land, vsum, vec_far, gw, g3, wbuf, wfar,
    *rest,
):
    place = Place(dims)
    heads, share, nseq, ntp = dims
    head, part, seq, tp = place.head, place.part, place.seq, place.tp
    lands, sems = rest[:6], rest[6:]
    (dq_s, dq_r, kv1_s, kv1_r, kv2_s, kv2_r, right_s, right_r, left_s, left_r,
     st_s, st_r, v1_s, v1_r, v2_s, v2_r, w_s, w_r, g1_s, g1_r, g2_s, g2_r, load_s) = sems
    rows, features = h1_ref.shape
    width = features // ntp
    tokens = rows // ntp
    local_width = wq_ref.shape[1]
    chunk_rows = rows // CHUNKS
    band = features // heads
    per = features // WIDE

    def chunk_of(chunk):
        return pl.ds(chunk * chunk_rows, chunk_rows)

    def half_of(chunk):
        return pl.ds(chunk * chunk_rows // 2, chunk_rows // 2)

    def columns_of(index):
        return pl.ds(pl.multiple_of(index * width, width), width)

    def dq_copy(chunk, step):
        other, device = place.across(step)
        return remote(
            dq_ref.at[other, half_of(chunk)], dq_in.at[head, half_of(chunk)],
            dq_s.at[chunk, step - 1], dq_r.at[chunk, step - 1], device,
        )

    def dkv_near(chunk, step):
        other, device = place.partner(step)
        here = chunk_of(chunk)
        return remote(
            dkv_hbm.at[other, :, here], dkv_land.at[step - 1, :, here],
            kv1_s.at[chunk, step - 1], kv1_r.at[chunk, step - 1], device,
        )

    def dkv_copy(chunk, step):
        other, device = place.across(step)
        return remote(
            dkv_sum.at[other, chunk_of(chunk)], dkv_in.at[head, chunk_of(chunk)],
            kv2_s.at[chunk, step - 1], kv2_r.at[chunk, step - 1], device,
        )

    def rightward(chunk, index):
        return remote(
            pbuf.at[chunk, index], from_left.at[chunk, index],
            right_s.at[chunk, index], right_r.at[chunk, index], (seq, tp + 1),
        )

    def leftward(chunk, index):
        return remote(
            pbuf.at[chunk, index], from_right.at[chunk, index],
            left_s.at[chunk, index], left_r.at[chunk, index], (seq, tp - 1),
        )

    def sums_copy(step):
        return remote(
            sums, sums_land.at[step - 1], st_s.at[step - 1], st_r.at[step - 1], place.along(step)[1]
        )

    def vec_copy(step):
        return remote(
            vbuf, vec_land.at[step - 1], v1_s.at[step - 1], v1_r.at[step - 1],
            (lax.rem(seq + step, nseq), tp),
        )

    def vec_far_copy(step):
        return remote(
            vsum, vec_far.at[step - 1], v2_s.at[step - 1], v2_r.at[step - 1], place.along(step)[1]
        )

    def w_copy(step):
        other, device = place.along(step)
        return remote(wbuf.at[other], wfar.at[step - 1], w_s.at[step - 1], w_r.at[step - 1], device)

    scatters = [
        GradScatter(
            place, source, lands[3 * k : 3 * k + 3], (g1_s.at[k], g1_r.at[k], g2_s.at[k], g2_r.at[k])
        )
        for k, source in enumerate((gw, g3))
    ]

    loads = [
        pltpu.make_async_copy(dkv_hbm.at[part], dkv_own, load_s.at[0]),
        pltpu.make_async_copy(dq_ref.at[head], dq_in.at[head], load_s.at[1]),
        pltpu.make_async_copy(x_hbm, x_ref, load_s.at[2]),
        pltpu.make_async_copy(h1_hbm, h1_ref, load_s.at[3]),
    ]
    for load in loads:
        load.start()
    greet(
        [(lax.rem(seq + step, nseq), tp) for step in range(1, nseq)]
        + [place.along(step)[1] for step in range(1, ntp)]
    )
    for chunk in range(CHUNKS):
        for step in range(1, share):
            dkv_near(chunk, step).start()
    vbuf[: 2 * per] = jnp.zeros((2 * per, WIDE), F32)
    vbuf[2 * per : 6 * per] = vec_ref[: 4 * per]
    narrow = 3 * local_width // WIDE
    vbuf[6 * per : 6 * per + narrow] = jnp.zeros((narrow, WIDE), F32)
    vbuf[6 * per + narrow :] = vec_ref[4 * per :]
    loads[0].wait()
    for chunk in range(CHUNKS):
        for step in range(1, heads):
            dq_copy(chunk, step).start()
        for step in range(1, share):
            dkv_near(chunk, step).wait_recv()
        for target in range(heads):
            where = (target, chunk_of(chunk))
            parts = [dkv_own[where]] + [dkv_land[(step,) + where] for step in range(share - 1)]
            dkv_sum[where] = add_up(*parts).astype(BF16)
        for step in range(1, heads):
            dkv_copy(chunk, step).start()
    dkv_in[head] = dkv_sum[head]
    for load in loads[1:]:
        load.wait()

    def output_grad(index):
        value = lax.dot_general(
            da_ref[:, index * band : (index + 1) * band], mixed_ref[...], TN, preferred_element_type=F32
        )
        gw[index] = value.astype(BF16).reshape(gw.shape[1:])

    gain = gain_ref[...]
    lane = lax.broadcasted_iota(jnp.int32, (chunk_rows, WIDE), 1)

    def partial_step(chunk):
        here, half = chunk_of(chunk), half_of(chunk)
        for step in range(1, heads):
            dq_copy(chunk, step).wait_recv()
            dkv_copy(chunk, step).wait_recv()
        three = [[], [], []]
        for i in range(0, heads, 2):
            three[0].append(unpack_pair(dq_in[i, half], dq_in[i + 1, half]))
            k, v = mix_pair(dkv_in[i, here].astype(F32), dkv_in[i + 1, here].astype(F32))
            three[1].append(k.astype(BF16))
            three[2].append(v.astype(BF16))
        three = [jnp.concatenate(item, axis=1) for item in three]
        grad = 0.125 * lax.dot_general(three[0], wq_ref[...], NT, preferred_element_type=F32)
        grad = grad + lax.dot_general(three[1], wk_ref[...], NT, preferred_element_type=F32)
        grad = grad + lax.dot_general(three[2], wv_ref[...], NT, preferred_element_type=F32)
        row = 6 * per
        for kind, value in enumerate(three):
            all3[here, kind * local_width : (kind + 1) * local_width] = value
            column = jnp.sum(value.astype(F32), axis=0, keepdims=True)
            for start in range(0, local_width, WIDE):
                vbuf[row : row + 1, :] += column[:, start : start + WIDE]
                row += 1
        mean, scale = stat_ref[here, 0:1], stat_ref[here, 1:2]
        sum0 = jnp.zeros((chunk_rows, 1), F32)
        sum1 = jnp.zeros((chunk_rows, 1), F32)
        for index in range(ntp):
            cols = slice(index * width, (index + 1) * width)
            piece = grad[:, cols]
            xhat = (x_ref[index, here].astype(F32) - mean) * scale
            weighted = piece * gain[:, cols]
            sum0 = sum0 + jnp.sum(weighted, axis=1, keepdims=True)
            sum1 = sum1 + jnp.sum(weighted * xhat, axis=1, keepdims=True)
            col0 = jnp.sum(piece * xhat, axis=0, keepdims=True)
            col1 = jnp.sum(piece, axis=0, keepdims=True)
            for sub in range(width // WIDE):
                row = index * (width // WIDE) + sub
                lanes = slice(sub * WIDE, (sub + 1) * WIDE)
                vbuf[row : row + 1, :] += col0[:, lanes]
                vbuf[per + row : per + row + 1, :] += col1[:, lanes]
            pbuf[chunk, index] = piece.astype(BF16)
            for sub in range(max(chunk_rows // tokens, 1)):
                rows_here = slice(sub * tokens, sub * tokens + min(tokens, chunk_rows))

                @pl.when(tp == chunk * chunk_rows // tokens + sub)
                def _():
                    start = chunk * chunk_rows % tokens
                    carried = da_ref[start : start + min(tokens, chunk_rows), cols].astype(F32)
                    carried = carried / (scale[rows_here] * gain[:, cols])
                    pbuf[chunk, index, rows_here] = (piece[rows_here] + carried).astype(BF16)

        both = jnp.where(lane == 0, sum0, jnp.where(lane == 1, sum1, 0.0))
        sums[:, here] = both.T[:8]

    def set_off(chunk):
        for step in range(ntp - 1):
            far = ntp - 1 - step

            @pl.when(tp == 0)
            def _():
                rightward(chunk, far).start()

            @pl.when(tp == ntp - 1)
            def _():
                leftward(chunk, step).start()

    def relay_right(chunk):
        for step in range(ntp - 1):
            far = ntp - 1 - step

            @pl.when((tp < far) & (tp > 0))
            def _():
                rightward(chunk, far).wait_recv()
                pbuf[chunk, far] = add_up(pbuf[chunk, far], from_left[chunk, far]).astype(BF16)
                rightward(chunk, far).start()

    def relay_left(chunk):
        for step in range(ntp - 1):

            @pl.when((tp > step) & (tp < ntp - 1))
            def _():
                leftward(chunk, step).wait_recv()
                pbuf[chunk, step] = add_up(pbuf[chunk, step], from_right[chunk, step]).astype(BF16)
                leftward(chunk, step).start()

    def relay(chunk):
        @pl.when(tp < ntp // 2)
        def _():
            relay_right(chunk)
            relay_left(chunk)

        @pl.when(tp >= ntp // 2)
        def _():
            relay_left(chunk)
            relay_right(chunk)

    def projection_grad(index):
        left = h1_ref[:, pl.ds(index * band, band)]
        value = lax.dot_general(left, all3[...], TN, preferred_element_type=F32)
        g3[index] = value.astype(BF16).reshape(g3.shape[1:])

    for index in range(heads):
        output_grad(index)
    scatters[0].start_near()
    for chunk in range(CHUNKS):
        partial_step(chunk)
        set_off(chunk)
        if chunk == 0:
            scatters[0].start_across()
        if chunk > 1:
            relay(chunk - 2)
    for step in range(1, ntp):
        sums_copy(step).start()
    for step in range(1, nseq):
        vec_copy(step).start()
    for index in range(heads // 2):
        projection_grad(index)
    relay(CHUNKS - 2)
    for index in range(heads // 2, heads):
        projection_grad(index)
    scatters[1].start_near()
    for step in range(1, nseq):
        vec_copy(step).wait_recv()
    total = vbuf[...]
    for step in range(nseq - 1):
        total = total + vec_land[step]
    vsum[...] = total
    for step in range(1, ntp):
        vec_far_copy(step).start()
    scatters[1].start_across()
    relay(CHUNKS - 1)
    value = scatters[0].result().astype(BF16)
    for index in range(ntp):
        wbuf[index] = value[:, index * local_width : (index + 1) * local_width]
    for step in range(1, ntp):
        w_copy(step).start()

    for step in range(1, ntp):
        sums_copy(step).wait_recv()
    my_gain = gain_ref[:, columns_of(tp)]
    for chunk in range(CHUNKS):
        here = chunk_of(chunk)
        both = sums[:, here]
        for step in range(ntp - 1):
            both = both + sums_land[step, :, here]
        both = jnp.concatenate([both, jnp.zeros((WIDE - 8, chunk_rows), F32)], axis=0).T
        both = both * (1.0 / features)

        @pl.when(tp > 0)
        def _():
            rightward(chunk, tp).wait_recv()

        @pl.when(tp < ntp - 1)
        def _():
            leftward(chunk, tp).wait_recv()

        grad = pbuf[chunk, tp].astype(F32)
        grad = grad + jnp.where(tp > 0, from_left[chunk, tp].astype(F32), 0.0)
        grad = grad + jnp.where(tp < ntp - 1, from_right[chunk, tp].astype(F32), 0.0)
        mean, scale = stat_ref[here, 0:1], stat_ref[here, 1:2]
        xhat = (x_ref[tp, here].astype(F32) - mean) * scale
        gx_ref[here] = scale * (grad * my_gain - both[:, 0:1] - xhat * both[:, 1:2])
    value = scatters[1].result()
    oq_ref[...] = 0.125 * value[:, :local_width]
    ok_ref[...] = value[:, local_width : 2 * local_width]
    ov_ref[...] = value[:, 2 * local_width :]
    for step in range(1, ntp):
        vec_far_copy(step).wait_recv()
        w_copy(step).wait_recv()
    vout_ref[...] = vsum[...]
    for step in range(ntp - 1):
        vout_ref[: 6 * per] += vec_far[step, : 6 * per]
    ow_ref[...] = add_up(wbuf[tp], *[wfar[step] for step in range(ntp - 1)]).T

    for chunk in range(CHUNKS):
        for step in range(1, share):
            dkv_near(chunk, step).wait_send()
        for step in range(1, heads):
            dq_copy(chunk, step).wait_send()
            dkv_copy(chunk, step).wait_send()
        for index in range(ntp):
            @pl.when(tp < index)
            def _():
                rightward(chunk, index).wait_send()

            @pl.when(tp > index)
            def _():
                leftward(chunk, index).wait_send()

    for step in range(1, ntp):
        sums_copy(step).wait_send()
        vec_far_copy(step).wait_send()
        w_copy(step).wait_send()
    for step in range(1, nseq):
        vec_copy(step).wait_send()
    for scatter in scatters:
        scatter.finish()


def run_tail(dims, dq, dkv, h1, x_parts, da, mixed, stats, gain, wq, wk, wv, vec):
    heads, share, nseq, ntp = dims
    rows, features = h1.shape
    width, tokens = features // ntp, rows // ntp
    band = features // nseq
    local_width = wq.shape[1]
    per = features // WIDE
    sds = jax.ShapeDtypeStruct
    nvec = vec.shape[0] + 2 * per + 3 * local_width // WIDE
    outs = [
        sds((rows, width), F32),
        sds((local_width, band), F32),
        sds((band, local_width), F32),
        sds((band, local_width), F32),
        sds((band, local_width), F32),
        sds((nvec, WIDE), F32),
    ]
    pieces = (CHUNKS, ntp, rows // CHUNKS, width)
    scratch = [
        vmem(heads, rows, WIDE),
        vmem(rows, features),
        vmem(ntp, rows, width),
        vmem(heads, rows // 2, WIDE),
        vmem(heads, rows, WIDE),
        vmem(max(share - 1, 1), heads, rows, WIDE),
        vmem(heads, rows, WIDE),
        vmem(rows, 3 * local_width),
        vmem(*pieces),
        vmem(*pieces),
        vmem(*pieces),
        vmem(8, rows, dtype=F32),
        vmem(ntp - 1, 8, rows, dtype=F32),
        vmem(nvec, WIDE, dtype=F32),
        vmem(nseq - 1, nvec, WIDE, dtype=F32),
        vmem(nvec, WIDE, dtype=F32),
        vmem(ntp - 1, nvec, WIDE, dtype=F32),
        vmem(heads, share, band, features),
        vmem(heads, share, band, 3 * local_width),
        vmem(ntp, band, local_width),
        vmem(ntp - 1, band, local_width),
        *GradScatter.buffers(dims, band, features),
        *GradScatter.buffers(dims, band, 3 * local_width),
    ]
    sems = (
        [dma(CHUNKS, heads - 1)] * 2 + [dma(CHUNKS, share - 1)] * 2 + [dma(CHUNKS, heads - 1)] * 2
        + [dma(CHUNKS, ntp)] * 4 + [dma(ntp - 1)] * 2 + [dma(nseq - 1)] * 2 + [dma(ntp - 1)] * 4
        + GradScatter.semaphores(dims, 2) + [dma(4)]
    )
    return pl.pallas_call(
        functools.partial(tail_kernel, dims),
        out_shape=outs,
        in_specs=[ANYWHERE] * 4 + [IN_VMEM] * 8,
        out_specs=[IN_VMEM] * len(outs),
        scratch_shapes=scratch + sems,
        name="tail",
        cost_estimate=pl.CostEstimate(flops=70 << 30, bytes_accessed=8 << 20, transcendentals=0),
        compiler_params=pltpu.CompilerParams(
            collective_id=3, has_side_effects=True, vmem_limit_bytes=60 << 20
        ),
    )(dq, dkv, h1, x_parts, da, mixed, stats, gain, wq, wk, wv, vec)


def deliver_kernel(sizes, *refs):
    many = (len(refs) - 2 - len(sizes)) // 3
    vec, sources = refs[0], refs[1 : 1 + many]
    pieces, targets = refs[1 + many : 1 + many + len(sizes)], refs[1 + many + len(sizes) : 1 + 2 * many + len(sizes)]
    held, sems = refs[1 + 2 * many + len(sizes) : -1], refs[-1]
    loads = [
        pltpu.make_async_copy(source, buf, sems.at[0, index])
        for index, (source, buf) in enumerate(zip(sources, held))
    ]
    saves = [
        pltpu.make_async_copy(buf, target, sems.at[1, index])
        for index, (target, buf) in enumerate(zip(targets, held))
    ]
    for load in loads:
        load.start()
    start = 0
    for index, (size, factor) in enumerate(sizes):
        pieces[index][...] = factor * vec[start : start + size]
        start += size
    for load, save in zip(loads, saves):
        load.wait()
        save.start()
    for save in saves:
        save.wait()


def deliver(vec, sizes, arrays):
    sds = jax.ShapeDtypeStruct
    outs = [sds((size, WIDE), F32) for size, _ in sizes] + [sds(a.shape, a.dtype) for a in arrays]
    results = pl.pallas_call(
        functools.partial(deliver_kernel, sizes),
        out_shape=outs,
        in_specs=[IN_VMEM] + [ANYWHERE] * len(arrays),
        out_specs=[IN_VMEM] * len(sizes) + [ANYWHERE] * len(arrays),
        scratch_shapes=[vmem(*a.shape, dtype=a.dtype) for a in arrays] + [dma(2, len(arrays))],
        name="deliver",
        compiler_params=pltpu.CompilerParams(vmem_limit_bytes=60 << 20),
    )(vec, *arrays)
    return [item.reshape(-1) for item in results[: len(sizes)]], results[len(sizes) :]


def on_device(
    hidden_in,
    norm_gain,
    norm_shift,
    query_weight,
    query_bias,
    key_weight,
    value_weight,
    value_bias,
    output_weight,
    output_bias,
    feed_gain,
    feed_shift,
    inner_weight,
    inner_bias,
    outer_weight,
    outer_bias,
    doc_blocks,
    doc_padding,
    random_picks,
    cotangent,
):
    nrows, block_len, width = hidden_in.shape
    rows = nrows * block_len
    nseq, ntp = lax.axis_size("seq"), lax.axis_size("tp")
    local_width = query_weight.shape[1]
    heads = local_width // HEAD_DIM
    share = nseq // heads
    dims = (heads, share, nseq, ntp)
    features = width * ntp
    per = features // WIDE
    cot = cotangent.reshape(rows, width)
    q, kv, h1, x_parts, g_first, rest, output_full, x_mine, stats, table = run_head(
        dims, nrows, doc_blocks, doc_padding, random_picks.T, hidden_in.reshape(rows, width),
        norm_gain[None, :], norm_shift[None, :], query_weight, query_bias[None, :],
        key_weight, value_weight, value_bias[None, :], cot, output_weight,
    )
    g_rest = lax.all_gather(rest, "tp", axis=0)
    q = q.reshape(heads * rows, WIDE)
    kv = kv.reshape(nseq * rows, WIDE)
    sds = jax.ShapeDtypeStruct
    packed, res = local_call(
        functools.partial(forward_kernel, dims, nrows, 4),
        "attention_forward",
        (sds((heads * rows // 2, WIDE), BF16), sds((heads * rows, WIDE), F32)),
        2,
    )(table, q, kv)
    out_sum, do, da, mixed, vec, inner_part, outer_part = run_middle(
        dims, packed.reshape(heads, rows // 2, WIDE), g_first, g_rest, output_full,
        inner_weight, outer_weight, x_mine, output_bias[None, :], feed_gain[None, :],
        feed_shift[None, :], inner_bias[None, :], outer_bias[None, :],
    )
    result = lax.psum_scatter(out_sum, "tp", scatter_dimension=0)
    dq, dkv = local_call(
        functools.partial(backward_kernel, dims, nrows, 8),
        "attention_backward",
        (sds((heads * rows // 2, WIDE), BF16), sds((nseq * rows, WIDE), BF16)),
        4,
        [pltpu.VMEM((nseq * rows, WIDE), F32)],
    )(table, q, do.reshape(heads * rows // 2, WIDE), res, kv)
    grad_x, output_part, query_part, key_part, value_part, vectors = run_tail(
        dims, dq.reshape(heads, rows // 2, WIDE), dkv.reshape(share, heads, rows, WIDE), h1,
        x_parts, da, mixed, stats, norm_gain[None, :], query_weight, key_weight, value_weight, vec,
    )
    lines = local_width // WIDE
    sizes = [(per, 1.0)] * 6 + [(lines, 0.125), (lines, 1.0), (lines, 1.0)]
    sizes += [(vectors.shape[0] - 6 * per - 3 * lines, 1.0)]
    sums, arrays = deliver(
        vectors,
        tuple(sizes),
        [grad_x, output_part, query_part, key_part, value_part, inner_part, outer_part],
    )
    grad_x, output_part, query_part, key_part, value_part, inner_part, outer_part = arrays
    return (
        result.reshape(hidden_in.shape),
        grad_x.reshape(hidden_in.shape),
        sums[0],
        sums[1],
        query_part,
        sums[6],
        key_part,
        value_part,
        sums[8],
        output_part,
        sums[2],
        sums[3],
        sums[4],
        inner_part,
        sums[9],
        outer_part,
        sums[5],
    )


def solution(mesh):
    return jax.shard_map(
        on_device,
        mesh=mesh,
        in_specs=(
            P(None, "seq", "tp"),
            P(),
            P(),
            P(None, "tp"),
            P("tp"),
            P(None, "tp"),
            P(None, "tp"),
            P("tp"),
            P("tp", None),
            P(),
            P(),
            P(),
            P(None, "tp"),
            P("tp"),
            P("tp", None),
            P(),
            P(),
            P(),
            P(),
            P(None, "seq", "tp"),
        ),
        out_specs=(
            P(None, "seq", "tp"),
            P(None, "seq", "tp"),
            P(),
            P(),
            P("seq", "tp"),
            P("tp"),
            P("seq", "tp"),
            P("seq", "tp"),
            P("tp"),
            P("tp", "seq"),
            P(),
            P(),
            P(),
            P("seq", "tp"),
            P("tp"),
            P("tp", "seq"),
            P(),
        ),
        check_vma=False,
    )
```
